32 devices in a mesh: region: 8 (over z, y), dest: 4 (over x, core).
Axes of the slice: x: 2, y: 2, z: 4, core: 2. Of those that a mesh axis runs over, the one named last changes fastest.
Arguments:
- occupancy: float32 [16384, 4096], P('region', 'dest'), may hold values from 0 to 9, as said below
- capacity: float32 [16384], P('region'), may hold values from 0.5 to 1.5
- jam: float32 [16384], P('region'), may hold values from 13 to 16
- wave: float32 [16384], P('region'), may hold values from 0.08 to 0.25
- node_in: int32 [4, 8192], P(None, 'region'), may hold values from -1 to 2047, as said below
- node_out: int32 [4, 8192], P(None, 'region'), may hold values from -1 to 16383, as said below
- send_list: int32 [32, 192], P('region'), may hold values from -1 to 4095, as said below
- recv_list: int32 [32, 192], P('region'), may hold values from -1 to 2047, as said below
- turn: int32 [8192, 4096], P('region', 'dest'), may hold values from 0 to 3, as said below
Outputs:
- new_occupancy: float32 [16384, 4096], P('region', 'dest')
The draws below stay inside these ranges and needn't reach their ends.
Inputs may be any that keep to these rules, and one draw needn't show every extreme that they name: `node_in`: every cell of a region is the incoming cell of exactly one node block of that region; each block has 1 to 4 valid incoming slots, first in order, and some block of every region has 4. `node_out`: every cell is the outgoing cell of exactly one slot of one node block; each block has 1 to 4 valid outgoing slots, first in order, and some block of every region has 4. The outgoing cells lie in the block's own region or in the regions at offsets 1, -1, 2, -2 around the cyclic order of regions. `send_list`: row 4 r + t lists, in its first slots, every outgoing slot of region r that leads into region r + d_t (d = 1, -1, 2, -2), at most 192 of them; regions r and r + d send each other equally many; some pair at offset 1 and some at offset 2 send exactly 192. `recv_list`: row 4 r + t holds, slot by slot, the cells of region r that the slots of row 4 (r - d_t) + t of send_list lead into, -1 where that slot is empty. turn[n, k] is always a valid outgoing slot of node block n. `occupancy`: entries are positive.
All inputs are finite; a program needn't handle non-finite values.
Results may differ from the reference program's by a relative error of at most 0.0003.
Values sent between devices are 32-bit elements; how exact they have to be, the bound alone decides.
No kernel may reach another device: no remote copies, remote signals or barrier semaphores. Data moves between devices by JAX's collectives and lax.ppermute only.
A program may use at most 128 MiB of HBM per device.

```python
import math
import jax
import jax.numpy as jnp
import numpy as np
from jax import lax

K = 4096
CELL_DEV = 2048
BRANCH = 4
NODE_DEV = 1024
CAP = 192
CELLS = 16384
N_REGION = 8


PATTERNS = np.array([[1, 1, 1, 1], [2, 1, 1, 0], [2, 2, 0, 0], [3, 1, 0, 0]], dtype=np.int32)


STRIDES = np.array([0, 1, -1, 2, -2], dtype=np.int32)


MIRRORS = np.array([0, 2, 1, 4, 3], dtype=np.int32)


OPPOSITE = np.array([2, 1, 4, 3], dtype=np.int32)


COUNTERPART = np.array([1, 0, 3, 2], dtype=np.int32)


def permute_rows(key, row_count, length):
    sub_keys = jax.random.split(key, row_count)
    return jax.vmap(lambda single: jax.random.permutation(single, length))(sub_keys).astype(jnp.int32)


def degrees(key):
    region_count = CELLS // CELL_DEV
    quad_count = NODE_DEV // 4
    pick_key, shuffle_key = jax.random.split(key)
    chosen = jax.random.randint(pick_key, (region_count, quad_count), 0, 4)
    chosen = chosen.at[:, 0].set(3)
    extras = jnp.asarray(PATTERNS)[chosen]
    shuffle = permute_rows(shuffle_key, region_count * quad_count, 4).reshape(region_count, quad_count, 4)
    extras = jnp.take_along_axis(extras, shuffle, axis=2)
    return (1 + extras).reshape(region_count, NODE_DEV).astype(jnp.int32)


def network(key):
    sub_keys = jax.random.split(key, 7)
    region_count = CELLS // CELL_DEV
    in_degree = degrees(sub_keys[0])
    out_degree = degrees(sub_keys[1])
    regions = jnp.arange(region_count, dtype=jnp.int32)
    branches = jnp.arange(BRANCH, dtype=jnp.int32)[:, None, None]
    row_axis = regions[None, :, None]
    in_first = jnp.cumsum(in_degree, axis=1) - in_degree
    in_shuffle = permute_rows(sub_keys[2], region_count, CELL_DEV)
    in_valid = branches < in_degree[None]
    in_rank = jnp.minimum(in_first[None] + branches, CELL_DEV - 1)
    node_in = jnp.where(in_valid, in_shuffle[row_axis, in_rank], -1)
    edge_one = jax.random.randint(sub_keys[3], (region_count,), CAP // 3, CAP + 1).at[0].set(CAP)
    edge_two = jax.random.randint(sub_keys[4], (region_count,), CAP // 3, CAP + 1).at[0].set(CAP)
    counts = jnp.stack([edge_one, jnp.roll(edge_one, 1), edge_two, jnp.roll(edge_two, 2)], axis=1).astype(jnp.int32)
    blocks = jnp.concatenate([CELL_DEV - jnp.sum(counts, axis=1, keepdims=True), counts], axis=1)
    block_first = jnp.cumsum(blocks, axis=1) - blocks
    out_shuffle = permute_rows(sub_keys[5], region_count, CELL_DEV)
    landing = permute_rows(sub_keys[6], region_count, CELL_DEV)
    out_first = jnp.cumsum(out_degree, axis=1) - out_degree
    out_valid = branches < out_degree[None]
    out_rank = jnp.minimum(out_first[None] + branches, CELL_DEV - 1)
    out_spot = out_shuffle[row_axis, out_rank]
    block_kind = jnp.sum(out_spot[..., None] >= block_first[None, :, None, 1:], axis=3).astype(jnp.int32)
    within_block = out_spot - block_first[row_axis, block_kind]
    stride = jnp.asarray(STRIDES)[block_kind]
    peer_region = (row_axis + stride) % region_count
    mirror = jnp.asarray(MIRRORS)[block_kind]
    target = landing[peer_region, jnp.minimum(block_first[peer_region, mirror] + within_block, CELL_DEV - 1)]
    node_out = jnp.where(out_valid, peer_region * CELL_DEV + target, -1)
    position = branches * NODE_DEV + jnp.arange(NODE_DEV, dtype=jnp.int32)[None, None, :]
    position = jnp.broadcast_to(position, out_valid.shape)
    by_spot = jnp.full((region_count, CELL_DEV), -1, jnp.int32)
    by_spot = by_spot.at[jnp.broadcast_to(row_axis, out_valid.shape), jnp.where(out_valid, out_spot, CELL_DEV)].set(position, mode='drop')
    slot_number = jnp.arange(CAP, dtype=jnp.int32)[None, None, :]
    send_first = jnp.minimum(block_first[:, 1:, None] + slot_number, CELL_DEV - 1)
    send_list = jnp.where(slot_number < counts[:, :, None], by_spot[regions[:, None, None], send_first], -1)
    recv_first = jnp.minimum(block_first[:, OPPOSITE][:, :, None] + slot_number, CELL_DEV - 1)
    recv_list = jnp.where(slot_number < counts[:, COUNTERPART][:, :, None], landing[regions[:, None, None], recv_first], -1)
    return (node_in.reshape(BRANCH, -1).astype(jnp.int32), node_out.reshape(BRANCH, -1).astype(jnp.int32), send_list.reshape(-1, CAP).astype(jnp.int32), recv_list.reshape(-1, CAP).astype(jnp.int32), out_degree)


def draw_node_in(key, part):
    return network(key)[0]


def draw_node_out(key, part):
    return network(key)[1]


def draw_send_list(key, part):
    return network(key)[2]


def draw_recv_list(key, part):
    return network(key)[3]


def draw_turn(key, part):
    out_degree = network(key)[4]
    key = jax.random.fold_in(key, 5)
    raw_turn = jax.random.randint(key, (out_degree.size, K), 0, 1 << 20)
    return (raw_turn % out_degree.reshape(-1)[:, None]).astype(jnp.int32)


def draw_occupancy(key, part):
    key = jax.random.fold_in(key, 11)
    level_key, rough_key = jax.random.split(key)
    cell_level = jnp.exp(jax.random.uniform(level_key, (CELLS, 1), jnp.float32, math.log(0.5), math.log(2.0)))
    profile = jnp.exp(math.log(3.0) * jnp.arange(K, dtype=jnp.float32) / K)[None, :]
    roughness = jax.random.uniform(rough_key, (CELLS, K), jnp.float32, 0.5, 1.5)
    return (cell_level * profile * roughness).astype(jnp.float32)


def level_of(stream_key, shape, cuts, low, largest):
    def one(dim, blocks):
        steps = jax.random.uniform(jax.random.fold_in(jax.random.fold_in(stream_key, 6), dim), (blocks,), jnp.float32, low / len(cuts), largest / len(cuts))
        return jnp.repeat(jnp.exp(steps), shape[dim] // blocks).reshape((-1,) + (1,) * (len(shape) - dim - 1))

    loudness = one(*cuts[0])
    for cut in cuts[1:]:
        loudness = loudness * one(*cut)
    return loudness


def setup_inputs(seed: int = 0) -> dict:
    arg_keys = jax.random.split(jax.random.key(seed), 10)
    occupancy = draw_occupancy(jax.random.fold_in(arg_keys[9], 71), 0)
    capacity = jnp.clip(0.5 + 1.0 * jax.random.uniform(arg_keys[1], (CELLS,), jnp.float32) ** level_of(arg_keys[1], (CELLS,), ((0, 8),), -0.2, 0.2), 0.5, 1.5)
    jam = jnp.clip(13.0 + 3.0 * jax.random.uniform(arg_keys[2], (CELLS,), jnp.float32) ** level_of(arg_keys[2], (CELLS,), ((0, 8),), -0.2, 0.2), 13.0, 16.0)
    wave = jnp.clip(0.08 + 0.17 * jax.random.uniform(arg_keys[3], (CELLS,), jnp.float32) ** level_of(arg_keys[3], (CELLS,), ((0, 8),), -0.2, 0.2), 0.08, 0.25)
    node_in = draw_node_in(jax.random.fold_in(arg_keys[9], 71), 0)
    node_out = draw_node_out(jax.random.fold_in(arg_keys[9], 71), 0)
    send_list = draw_send_list(jax.random.fold_in(arg_keys[9], 71), 0)
    recv_list = draw_recv_list(jax.random.fold_in(arg_keys[9], 71), 0)
    turn = draw_turn(jax.random.fold_in(arg_keys[9], 71), 0)
    return dict(occupancy=occupancy, capacity=capacity, jam=jam, wave=wave, node_in=node_in, node_out=node_out, send_list=send_list, recv_list=recv_list, turn=turn)


SHIFTS = (1, -1, 2, -2)


def reference(occupancy, capacity, jam, wave, node_in, node_out, send_list, recv_list, turn):
    cell_total = occupancy.shape[0]
    vehicles = jnp.sum(occupancy, axis=1) / K
    fraction = jnp.minimum(vehicles, capacity) / vehicles
    supply = jnp.minimum(capacity, wave * (jam - vehicles))
    flat_size = BRANCH * NODE_DEV

    def one_region(inflow, region_no):
        first_node = region_no * NODE_DEV
        ins = lax.dynamic_slice_in_dim(node_in, first_node, NODE_DEV, 1)
        outs = lax.dynamic_slice_in_dim(node_out, first_node, NODE_DEV, 1)
        turns = lax.dynamic_slice_in_dim(turn, first_node, NODE_DEV, 0)
        sent = lax.dynamic_slice_in_dim(send_list, region_no * 4, 4, 0)
        in_valid = ins >= 0
        in_cell = (region_no * CELL_DEV + jnp.maximum(ins, 0)).astype(jnp.int32)
        weights = jnp.where(in_valid, fraction[in_cell], 0.0)
        node_flow = jnp.sum(occupancy[in_cell] * weights[:, :, None], axis=0)
        branch_part = jnp.stack([jnp.where(turns == outlet, node_flow, 0.0) for outlet in range(BRANCH)])
        demand = jnp.sum(branch_part, axis=2) / K
        out_valid = outs >= 0
        home = out_valid & (outs // CELL_DEV == region_no)
        home_cell = jnp.where(home, outs, 0).astype(jnp.int32)
        flat_room = jnp.where(home, supply[home_cell], 0.0).reshape(-1)
        peer_rows = []
        for side_no in range(4):
            peer_region = (region_no + SHIFTS[side_no]) % N_REGION
            wanted = lax.dynamic_slice_in_dim(recv_list, peer_region * 4 + side_no, 1, 0)[0]
            peer_cell = (peer_region * CELL_DEV + jnp.maximum(wanted, 0)).astype(jnp.int32)
            value = jnp.where(wanted >= 0, supply[peer_cell], 0.0)
            slot_ids = sent[side_no]
            flat_room = flat_room.at[jnp.where(slot_ids >= 0, slot_ids, flat_size)].set(value, mode="drop")
            peer_rows.append((peer_region, wanted, slot_ids))
        room = flat_room.reshape(BRANCH, NODE_DEV)
        ratio = room / jnp.maximum(demand, room)
        theta = jnp.min(jnp.where(out_valid, ratio, 1.0), axis=0)
        moved = (branch_part * theta[None, :, None]).reshape(flat_size, K)
        home_place = jnp.where(home, outs, cell_total).reshape(-1)
        inflow = inflow.at[home_place].add(moved, mode="drop")
        for peer_region, wanted, slot_ids in peer_rows:
            rows_out = jnp.where((slot_ids >= 0)[:, None], moved[jnp.maximum(slot_ids, 0)], 0.0)
            landing = jnp.where(wanted >= 0, peer_region * CELL_DEV + wanted, cell_total)
            inflow = inflow.at[landing].add(rows_out, mode="drop")
        return inflow, theta

    inflow, thetas = lax.scan(one_region, jnp.zeros_like(occupancy), jnp.arange(N_REGION, dtype=jnp.int32))
    node_region = jnp.arange(N_REGION * NODE_DEV, dtype=jnp.int32) // NODE_DEV
    in_global = jnp.where(node_in >= 0, node_region[None, :] * CELL_DEV + node_in, cell_total)
    theta_rows = jnp.broadcast_to(thetas.reshape(1, -1), node_in.shape)
    cell_theta = jnp.zeros((cell_total,), jnp.float32).at[in_global.reshape(-1)].set(theta_rows.reshape(-1), mode="drop")
    keeping = 1.0 - cell_theta * fraction
    return occupancy * keeping[:, None] + inflow
```

```python
import functools

import jax
import jax.numpy as jnp
from jax import lax
from jax.experimental import pallas as pl
from jax.experimental.pallas import tpu as pltpu
from jax.sharding import PartitionSpec as P

SHIFTS = (1, -1, 2, -2)
EXACT = lax.Precision.HIGHEST
LANES = 128
MIB = 1 << 20
VMEM_WHOLE = pl.BlockSpec(memory_space=pltpu.VMEM)
SMEM_WHOLE = pl.BlockSpec(memory_space=pltpu.SMEM)


def shifted(block, axis, distance):
    devices = range(lax.axis_size(axis))
    route = [((i - distance) % len(devices), i) for i in devices]
    return lax.ppermute(block, axis, route)


def params(mib):
    return pltpu.CompilerParams(vmem_limit_bytes=mib * MIB)


def cost(flops, moved):
    return pl.CostEstimate(flops=flops, bytes_accessed=moved, transcendentals=0)


def lane_sums(partial):
    ones = jnp.ones((8, LANES), jnp.float32)
    sums = lax.dot_general(
        ones, partial, (((1,), (1,)), ((), ())),
        preferred_element_type=jnp.float32, precision=EXACT,
    )
    return sums[0:1, :]


def to_rows(x_ref, rows_ref, first, count, sub):
    for group in range(count // 8):
        for q in range(sub):
            piece = x_ref[group * 8 : group * 8 + 8, q * LANES : (q + 1) * LANES]
            start = (first + group * 8) * sub + q
            rows_ref[pl.ds(start, 8, stride=sub), :] = piece


def cell_sum_kernel(block, sub, x_ref, sum_ref, rows_ref):
    step = pl.program_id(0)
    to_rows(x_ref, rows_ref, step * block, block, sub)
    partial = x_ref[:, 0:LANES]
    for q in range(1, sub):
        partial = partial + x_ref[:, q * LANES : (q + 1) * LANES]
    sums = lane_sums(partial)
    per_step = block // LANES
    for part in range(per_step):
        sum_ref[pl.ds(step * per_step + part, 1), :] = sums[:, part * LANES : (part + 1) * LANES]


def turn_rows_kernel(block, sub, x_ref, rows_ref):
    to_rows(x_ref, rows_ref, pl.program_id(0) * block, block, sub)


def node_flow_kernel(sizes, fraction, in_row, send_row, send_outlet, rows, turns, flow, *rest):
    cells, nodes, branches, cap, sub = sizes
    sends, scaled = rest[:4], rest[4]

    def row(index):
        return pl.ds(pl.multiple_of(index, sub), sub)

    def scale(step, carry):
        first = step * 16
        values = [
            rows[row((first + i) * sub), :] * fraction[first + i] for i in range(16)
        ]
        for i in range(16):
            scaled[row((first + i) * sub), :] = values[i]
        return carry

    lax.fori_loop(0, cells // 16, scale, 0)
    scaled[row(cells * sub), :] = jnp.zeros((sub, LANES), jnp.float32)

    def gather(step, carry):
        first = step * 8
        values = []
        for i in range(8):
            parts = [
                scaled[row(in_row[j * nodes + first + i]), :] for j in range(branches)
            ]
            while len(parts) > 1:
                parts = [sum(parts[k : k + 2][1:], parts[k]) for k in range(0, len(parts), 2)]
            values.append(parts[0])
        for i in range(8):
            flow[row((first + i) * sub), :] = values[i]
        return carry

    lax.fori_loop(0, nodes // 8, gather, 0)

    for side, send in enumerate(sends):

        def pick(step, carry, side=side, send=send):
            first = step * 8
            values = []
            for i in range(8):
                slot = side * cap + first + i
                where_from = row(send_row[slot])
                values.append(
                    jnp.where(turns[where_from, :] == send_outlet[slot], flow[where_from, :], 0.0)
                )
            for i in range(8):
                send[row((first + i) * sub), :] = values[i]
            return carry

        lax.fori_loop(0, cap // 8, pick, 0)


def demand_kernel(sizes, flow, turn, demand, partial):
    cells, nodes, branches, cap, sub = sizes

    def group(step, carry):
        first = step * 8
        totals = [jnp.zeros((8, LANES), jnp.float32)] * branches
        for q in range(sub):
            value = flow[pl.ds(first * sub + q, 8, stride=sub), :]
            choice = turn[pl.ds(pl.multiple_of(first, 8), 8), q * LANES : (q + 1) * LANES]
            totals = [
                total + jnp.where(choice == j, value, 0.0) for j, total in enumerate(totals)
            ]
        for j in range(branches):
            partial[j, pl.ds(pl.multiple_of(first, 8), 8), :] = totals[j]
        return carry

    lax.fori_loop(0, nodes // 8, group, 0)
    for j in range(branches):
        demand[j : j + 1, :] = lane_sums(partial[j])


def room_kernel(table, place, room):
    def body(step, carry):
        first = step * 16
        values = [table[place[first + i]] for i in range(16)]
        for i in range(16):
            room[first + i] = values[i]
        return carry

    lax.fori_loop(0, place.shape[0] // 16, body, 0)


def home_kernel(sizes, theta, keep, home_row, rows, turns, flow, base):
    cells, nodes, branches, cap, sub = sizes

    def row(index):
        return pl.ds(pl.multiple_of(index, sub), sub)

    def body(step, carry):
        first = step * 4
        stores = []
        for i in range(4):
            node = first + i
            moved = flow[row(node * sub), :] * theta[node]
            choice = turns[row(node * sub), :]
            for j in range(branches):
                cell = home_row[j * nodes + node]
                at = row(cell * sub)
                kept = rows[row(jnp.minimum(cell, cells - 1) * sub), :] * keep[cell]
                stores.append((at, kept + jnp.where(choice == j, moved, 0.0)))
        for at, value in stores:
            base[at, :] = value
        return carry

    lax.fori_loop(0, nodes // 4, body, 0)


def finish_kernel(sizes, block, keep, scale, land, rows, *rest):
    cells, nodes, branches, cap, sub = sizes
    received, (base_in, out, base) = rest[:4], rest[4:]

    def row(index):
        return pl.ds(pl.multiple_of(index, sub), sub)

    step = pl.program_id(0)

    @pl.when(step == 0)
    def _():
        for side in range(4):

            def body(turn_no, carry, side=side):
                first = turn_no * 8
                stores = []
                for i in range(8):
                    slot = side * cap + first + i
                    cell = land[slot]
                    kept = rows[row(jnp.minimum(cell, cells - 1) * sub), :] * keep[cell]
                    value = kept + received[side][row((first + i) * sub), :] * scale[slot]
                    stores.append((row(cell * sub), value))
                for at, value in stores:
                    base[at, :] = value
                return carry

            lax.fori_loop(0, cap // 8, body, 0)

    for group in range(block // 8):
        for q in range(sub):
            start = (step * block + group * 8) * sub + q
            out[group * 8 : group * 8 + 8, q * LANES : (q + 1) * LANES] = base[
                pl.ds(start, 8, stride=sub), :
            ]


def on_device(occupancy, capacity, jam, wave, node_in, node_out, send_list, recv_list, turn):
    cells, width = occupancy.shape
    branches, nodes = node_in.shape
    cap = send_list.shape[1]
    sub = width // LANES
    sizes = (cells, nodes, branches, cap, sub)
    regions = lax.axis_size("region")
    commodities = width * lax.axis_size("dest")
    region_no = lax.axis_index("region")
    block = 256
    f32 = jnp.float32

    local_sum, rows = pl.pallas_call(
        functools.partial(cell_sum_kernel, block, sub),
        grid=(cells // block,),
        in_specs=[pl.BlockSpec((block, width), lambda i: (i, 0))],
        out_specs=[pl.BlockSpec((cells // LANES, LANES), lambda i: (0, 0)), VMEM_WHOLE],
        out_shape=[
            jax.ShapeDtypeStruct((cells // LANES, LANES), f32),
            pltpu.VMEM((cells * sub, LANES), f32),
        ],
        compiler_params=params(12),
        cost_estimate=cost(cells * width, cells * width * 4),
        name="cell_sum",
    )(occupancy)

    turn_block = 128
    turns = pl.pallas_call(
        functools.partial(turn_rows_kernel, turn_block, sub),
        grid=(nodes // turn_block,),
        in_specs=[pl.BlockSpec((turn_block, width), lambda i: (i, 0))],
        out_specs=VMEM_WHOLE,
        out_shape=pltpu.VMEM((nodes * sub, LANES), jnp.int32),
        compiler_params=params(8),
        cost_estimate=cost(0, nodes * width * 4),
        name="turn_rows",
    )(turn)

    in_row = jnp.where(node_in >= 0, node_in, cells).reshape(-1) * sub
    slots = send_list.reshape(-1)
    send_row = jnp.where(slots >= 0, slots % nodes, 0) * sub
    send_outlet = jnp.where(slots >= 0, slots // nodes, -1)
    land = jnp.where(recv_list >= 0, recv_list, cells).reshape(-1)
    out_valid = node_out >= 0
    out_cell = jnp.maximum(node_out, 0)
    offset = (out_cell // cells - region_no) % regions
    out_local = out_cell % cells
    home = out_valid & (offset == 0)
    home_row = jnp.where(home, out_local, cells).reshape(-1)
    sector = jnp.zeros_like(offset)
    for side, stride in enumerate(SHIFTS):
        sector = jnp.where(offset == stride % regions, side + 1, sector)
    place = (sector * cells + out_local).reshape(-1)

    vehicles = lax.psum(local_sum, "dest") / commodities
    cap_of = capacity.reshape(vehicles.shape)
    fraction = jnp.minimum(vehicles, cap_of) / vehicles
    supply = jnp.minimum(
        cap_of, wave.reshape(vehicles.shape) * (jam.reshape(vehicles.shape) - vehicles)
    )
    fraction = fraction.reshape(-1)

    row_shape = jax.ShapeDtypeStruct((cap * sub, LANES), f32)
    flow, *sends = pl.pallas_call(
        functools.partial(node_flow_kernel, sizes),
        in_specs=[SMEM_WHOLE] * 4 + [VMEM_WHOLE] * 2,
        out_specs=[VMEM_WHOLE] * 5,
        out_shape=[pltpu.VMEM((nodes * sub, LANES), f32)]
        + [pltpu.VMEM((cap * sub, LANES), f32)] * 4,
        scratch_shapes=[pltpu.VMEM(((cells + 1) * sub, LANES), f32)],
        compiler_params=params(16),
        cost_estimate=cost(cells * width * 2, cells * width * 4),
        name="node_flow",
    )(fraction, in_row, send_row, send_outlet, rows, turns)

    arrived = [shifted(sends[side], "region", SHIFTS[side]) for side in range(4)]

    table = jnp.concatenate(
        [supply] + [shifted(supply, "region", -stride) for stride in SHIFTS]
    ).reshape(-1)

    demand = pl.pallas_call(
        functools.partial(demand_kernel, sizes),
        in_specs=[VMEM_WHOLE] * 2,
        out_specs=VMEM_WHOLE,
        out_shape=jax.ShapeDtypeStruct((branches, nodes), f32),
        scratch_shapes=[pltpu.VMEM((branches, nodes, LANES), f32)],
        compiler_params=params(12),
        cost_estimate=cost(nodes * width * 8, nodes * width * 4),
        name="demand",
    )(flow, turn)
    demand = lax.psum(demand, "dest") / commodities

    room = pl.pallas_call(
        room_kernel,
        in_specs=[SMEM_WHOLE] * 2,
        out_specs=SMEM_WHOLE,
        out_shape=jax.ShapeDtypeStruct((branches * nodes,), f32),
        cost_estimate=cost(0, branches * nodes * 4),
        name="room",
    )(table, place).reshape(branches, nodes)
    ratio = room / jnp.maximum(demand, room)
    theta = jnp.min(jnp.where(out_valid, ratio, 1.0), axis=0)

    sent_theta = pl.pallas_call(
        room_kernel,
        in_specs=[SMEM_WHOLE] * 2,
        out_specs=SMEM_WHOLE,
        out_shape=jax.ShapeDtypeStruct((4 * cap,), f32),
        cost_estimate=cost(0, cap * 16),
        name="slot_theta",
    )(theta, send_row // sub).reshape(4, cap)
    scale = jnp.concatenate(
        [shifted(sent_theta[side], "region", SHIFTS[side]) for side in range(4)]
    )

    cell_ids = jnp.arange(cells, dtype=jnp.int32)
    incidence = jnp.any(node_in[:, :, None] == cell_ids[None, None, :], axis=0).astype(f32)
    cell_theta = jnp.dot(
        theta[None, :], incidence, preferred_element_type=f32, precision=EXACT
    )[0]
    keep = jnp.concatenate([1.0 - cell_theta * fraction, jnp.zeros((LANES,), f32)])

    base = pl.pallas_call(
        functools.partial(home_kernel, sizes),
        in_specs=[SMEM_WHOLE] * 3 + [VMEM_WHOLE] * 3,
        out_specs=VMEM_WHOLE,
        out_shape=pltpu.VMEM(((cells + 1) * sub, LANES), f32),
        compiler_params=params(8),
        cost_estimate=cost(cells * width * 2, cells * width * 4),
        name="home_inflow",
    )(theta, keep, home_row, rows, turns, flow)

    out, _ = pl.pallas_call(
        functools.partial(finish_kernel, sizes, block),
        grid=(cells // block,),
        in_specs=[SMEM_WHOLE] * 3 + [VMEM_WHOLE] * 6,
        out_specs=[pl.BlockSpec((block, width), lambda i: (i, 0)), VMEM_WHOLE],
        out_shape=[
            jax.ShapeDtypeStruct((cells, width), f32),
            pltpu.VMEM(((cells + 1) * sub, LANES), f32),
        ],
        input_output_aliases={8: 1},
        compiler_params=params(12),
        cost_estimate=cost(cells * width, cells * width * 4),
        name="finish",
    )(keep, scale, land, rows, *arrived, base)
    return out


def solution(mesh):
    return jax.shard_map(
        on_device,
        mesh=mesh,
        in_specs=(
            P("region", "dest"),
            P("region"),
            P("region"),
            P("region"),
            P(None, "region"),
            P(None, "region"),
            P("region", None),
            P("region", None),
            P("region", "dest"),
        ),
        out_specs=P("region", "dest"),
        check_vma=False,
    )
```

```python
import functools

import jax
import jax.numpy as jnp
from jax import lax
from jax.experimental import pallas as pl
from jax.experimental.pallas import tpu as pltpu
from jax.sharding import PartitionSpec as P

SHIFTS = (2, -2, 1, -1)
SIDES = (2, 3, 0, 1)
EXACT = lax.Precision.HIGHEST
LANES = 128
MIB = 1 << 20
F32 = jnp.float32
VMEM_WHOLE = pl.BlockSpec(memory_space=pltpu.VMEM)
SMEM_WHOLE = pl.BlockSpec(memory_space=pltpu.SMEM)


def shifted(block, axis, distance):
    devices = range(lax.axis_size(axis))
    route = [((i - distance) % len(devices), i) for i in devices]
    return lax.ppermute(block, axis, route)


def partners(block, axis):
    count = lax.axis_size(axis)
    return [block] + [
        lax.ppermute(block, axis, [(i, i ^ other) for i in range(count)])
        for other in range(1, count)
    ]


def tree_sum(parts):
    while len(parts) > 1:
        parts = [parts[k] + parts[k + 1] for k in range(0, len(parts), 2)]
    return parts[0]


def params(mib):
    return pltpu.CompilerParams(vmem_limit_bytes=mib * MIB)


def cost(flops, moved):
    return pl.CostEstimate(flops=flops, bytes_accessed=moved, transcendentals=0)


def lane_sums(partial):
    ones = jnp.ones((8, LANES), F32)
    sums = lax.dot_general(
        ones, partial, (((1,), (1,)), ((), ())), preferred_element_type=F32, precision=EXACT
    )
    return sums[0:1, :]


def row_at(index, sub):
    return pl.ds(pl.multiple_of(index, sub), sub)


def to_rows(x_ref, rows_ref, first, count, sub):
    for group in range(count // 8):
        for q in range(sub):
            piece = x_ref[group * 8 : group * 8 + 8, q * LANES : (q + 1) * LANES]
            start = (first + group * 8) * sub + q
            rows_ref[pl.ds(start, 8, stride=sub), :] = piece


def cell_sum_kernel(block, sub, x_ref, sum_ref, rows_ref):
    step = pl.program_id(0)
    to_rows(x_ref, rows_ref, step * block, block, sub)
    partial = x_ref[:, 0:LANES]
    for q in range(1, sub):
        partial = partial + x_ref[:, q * LANES : (q + 1) * LANES]
    sums = lane_sums(partial)
    per_step = block // LANES
    for part in range(per_step):
        sum_ref[pl.ds(step * per_step + part, 1), :] = sums[:, part * LANES : (part + 1) * LANES]

    @pl.when(step == 0)
    def _():
        zeros = rows_ref.shape[0] - sub
        rows_ref[zeros:, :] = jnp.zeros((sub, LANES), F32)


def turn_rows_kernel(block, sub, x_ref, after_ref, rows_ref):
    to_rows(x_ref, rows_ref, pl.program_id(0) * block, block, sub)


def one_hot(index, count):
    rows = lax.broadcasted_iota(jnp.int32, (count, index.shape[1]), 0)
    return jnp.where(rows == index, 1.0, 0.0)


def look_up(table, index):
    picked = lax.dot_general(
        table.T,
        one_hot(index // LANES, table.shape[0]),
        (((1,), (0,)), ((), ())),
        preferred_element_type=F32,
        precision=EXACT,
    )
    return jnp.sum(picked * one_hot(index % LANES, LANES), axis=0, keepdims=True)


def scatter(index, values, height):
    high = jnp.where(index >= 0, index // LANES, -1)
    return lax.dot_general(
        one_hot(high, height) * values,
        one_hot(jnp.where(index >= 0, index % LANES, -1), LANES),
        (((1,), (1,)), ((), ())),
        preferred_element_type=F32,
        precision=EXACT,
    )


def source_kernel(sizes, home_cell, after_ref, node, outlet):
    cells, nodes, branches, cap, sub = sizes
    height = cells // LANES
    ids = lax.broadcasted_iota(jnp.int32, (1, nodes), 1).astype(F32) + 1.0
    number = jnp.zeros((height, LANES), F32)
    slot = jnp.zeros((height, LANES), F32)
    for j in range(branches):
        here = scatter(home_cell[j : j + 1, :], ids, height)
        number = number + here
        slot = slot + jnp.where(here > 0.0, j + 1.0, 0.0)
    node[...] = jnp.maximum(number.astype(jnp.int32) - 1, 0) * sub
    outlet[...] = slot.astype(jnp.int32) - 1


def gathered_flow(node, in_cell, fraction, rows, sizes):
    cells, nodes, branches, cap, sub = sizes
    parts = []
    for i in range(branches):
        cell = in_cell[i * nodes + node]
        parts.append(rows[row_at(cell * sub, sub), :] * fraction[cell])
    return tree_sum(parts)


def send_kernel(sizes, fraction, in_cell, send_node, send_outlet, rows, turns, *sends):
    cells, nodes, branches, cap, sub = sizes
    batch = 8
    for side, send in enumerate(sends):

        def body(step, carry, side=side, send=send):
            first = step * batch
            values = []
            for i in range(batch):
                slot = side * cap + first + i
                node = send_node[slot]
                value = gathered_flow(node, in_cell, fraction, rows, sizes)
                choice = turns[row_at(node * sub, sub), :]
                values.append(jnp.where(choice == send_outlet[slot], value, 0.0))
            for i in range(batch):
                send[row_at((first + i) * sub, sub), :] = values[i]
            return carry

        lax.fori_loop(0, cap // batch, body, 0)


def node_flow_kernel(sizes, fraction, in_cell, rows, turn, flow, demand, partial):
    cells, nodes, branches, cap, sub = sizes

    def group(step, carry):
        first = step * 8
        values = [
            gathered_flow(first + i, in_cell, fraction, rows, sizes) for i in range(8)
        ]
        for i in range(8):
            flow[row_at((first + i) * sub, sub), :] = values[i]
        totals = [jnp.zeros((8, LANES), F32)] * branches
        for q in range(sub):
            value = flow[pl.ds(first * sub + q, 8, stride=sub), :]
            choice = turn[pl.ds(pl.multiple_of(first, 8), 8), q * LANES : (q + 1) * LANES]
            totals = [
                total + jnp.where(choice == j, value, 0.0) for j, total in enumerate(totals)
            ]
        for j in range(branches):
            partial[j, pl.ds(pl.multiple_of(first, 8), 8), :] = totals[j]
        return carry

    lax.fori_loop(0, nodes // 8, group, 0)
    for j in range(branches):
        demand[j : j + 1, :] = lane_sums(partial[j])


def theta_kernel(
    sizes, commodities, table, place, out_valid, in_cell, home_cell, send_node, fraction, *rest
):
    cells, nodes, branches, cap, sub = sizes
    parts, (keep, home_theta, slot_theta) = rest[:-3], rest[-3:]
    height = cells // LANES
    demand = tree_sum([part[...] for part in parts]) * (1.0 / commodities)
    lookup = table[...]
    theta = jnp.ones((1, nodes), F32)
    for j in range(branches):
        room = look_up(lookup, place[j : j + 1, :])
        ratio = room / jnp.maximum(demand[j : j + 1, :], room)
        theta = jnp.minimum(theta, jnp.where(out_valid[j : j + 1, :] > 0, ratio, 1.0))
    cell_theta = jnp.zeros((height, LANES), F32)
    into = jnp.zeros((height, LANES), F32)
    for j in range(branches):
        cell_theta = cell_theta + scatter(in_cell[j : j + 1, :], theta, height)
        into = into + scatter(home_cell[j : j + 1, :], theta, height)
    keep[...] = 1.0 - cell_theta * fraction[...]
    home_theta[...] = into
    tall = jnp.concatenate(
        [theta[:, q * LANES : (q + 1) * LANES] for q in range(nodes // LANES)], axis=0
    )
    for side in range(4):
        slot_theta[side : side + 1, :] = look_up(tall, send_node[side : side + 1, :])


def base_kernel(sizes, keep, home_theta, node_row, outlet, rows, turns, flow, base):
    cells, nodes, branches, cap, sub = sizes
    batch = 8

    def body(step, carry):
        first = step * batch
        for i in range(batch):
            cell = first + i
            at = row_at(node_row[cell], sub)
            moved = jnp.where(turns[at, :] == outlet[cell], flow[at, :], 0.0)
            kept = rows[row_at(cell * sub, sub), :] * keep[cell]
            base[row_at(cell * sub, sub), :] = kept + moved * home_theta[cell]
        return carry

    lax.fori_loop(0, cells // batch, body, 0)


def finish_kernel(sizes, block, scale, land, *rest):
    cells, nodes, branches, cap, sub = sizes
    received, (base_in, out, base) = rest[:4], rest[4:]
    step = pl.program_id(0)
    batch = 8

    @pl.when(step == 0)
    def _():
        for side in range(4):

            def body(turn_no, carry, side=side):
                first = turn_no * batch
                stores = []
                for i in range(batch):
                    slot = side * cap + first + i
                    at = row_at(land[slot], sub)
                    value = received[side][row_at((first + i) * sub, sub), :] * scale[slot]
                    stores.append((at, base[at, :] + value))
                for at, value in stores:
                    base[at, :] = value
                return carry

            lax.fori_loop(0, cap // batch, body, 0)

    for group in range(block // 8):
        for q in range(sub):
            start = (step * block + group * 8) * sub + q
            out[group * 8 : group * 8 + 8, q * LANES : (q + 1) * LANES] = base[
                pl.ds(start, 8, stride=sub), :
            ]


def on_device(occupancy, capacity, jam, wave, node_in, node_out, send_list, recv_list, turn):
    cells, width = occupancy.shape
    branches, nodes = node_in.shape
    cap = send_list.shape[1]
    sub = width // LANES
    sizes = (cells, nodes, branches, cap, sub)
    regions = lax.axis_size("region")
    commodities = width * lax.axis_size("dest")
    region_no = lax.axis_index("region")
    height = cells // LANES
    per_cell = (height, LANES)
    block = 256
    row_bytes = width * 4
    occupancy = pltpu.with_memory_space_constraint(occupancy, pltpu.HBM)
    turn = pltpu.with_memory_space_constraint(turn, pltpu.HBM)

    local_sum, rows = pl.pallas_call(
        functools.partial(cell_sum_kernel, block, sub),
        grid=(cells // block,),
        in_specs=[pl.BlockSpec((block, width), lambda i: (i, 0))],
        out_specs=[pl.BlockSpec(per_cell, lambda i: (0, 0)), VMEM_WHOLE],
        out_shape=[
            jax.ShapeDtypeStruct(per_cell, F32),
            pltpu.VMEM(((cells + 1) * sub, LANES), F32),
        ],
        compiler_params=params(8),
        cost_estimate=cost(cells * width, cells * row_bytes),
        name="cell_sum",
    )(occupancy)

    sums = partners(local_sum, "dest")

    turn_block = 128
    turns = pl.pallas_call(
        functools.partial(turn_rows_kernel, turn_block, sub),
        grid=(nodes // turn_block,),
        in_specs=[
            pl.BlockSpec((turn_block, width), lambda i: (i, 0)),
            pl.BlockSpec(memory_space=pl.ANY),
        ],
        out_specs=VMEM_WHOLE,
        out_shape=pltpu.VMEM((nodes * sub, LANES), jnp.int32),
        compiler_params=params(6),
        cost_estimate=cost(0, nodes * row_bytes),
        name="turn_rows",
    )(turn, local_sum)

    in_cell = jnp.where(node_in >= 0, node_in, cells).reshape(-1)
    slots = jnp.concatenate([send_list[side : side + 1] for side in SIDES])
    lands = jnp.concatenate([recv_list[side : side + 1] for side in SIDES])
    send_node = jnp.where(slots >= 0, slots % nodes, 0)
    send_outlet = jnp.where(slots >= 0, slots // nodes, -1)
    land = jnp.where(lands >= 0, lands, cells) * sub
    out_valid = node_out >= 0
    out_cell = jnp.maximum(node_out, 0)
    offset = (out_cell // cells - region_no) % regions
    out_local = out_cell % cells
    home_cell = jnp.where(out_valid & (offset == 0), out_local, -1)
    sector = jnp.zeros_like(offset)
    for number, stride in enumerate(SHIFTS):
        sector = jnp.where(offset == stride % regions, number + 1, sector)
    place = sector * cells + out_local

    source_node, source_outlet = pl.pallas_call(
        functools.partial(source_kernel, sizes),
        in_specs=[VMEM_WHOLE, pl.BlockSpec(memory_space=pl.ANY)],
        out_specs=[VMEM_WHOLE] * 2,
        out_shape=[jax.ShapeDtypeStruct(per_cell, jnp.int32)] * 2,
        compiler_params=params(8),
        cost_estimate=cost(branches * nodes * cells * 2, nodes * 64),
        name="source_of_cell",
    )(home_cell, local_sum)

    vehicles = tree_sum(sums) / commodities
    cap_of = capacity.reshape(per_cell)
    fraction = jnp.minimum(vehicles, cap_of) / vehicles
    supply = jnp.minimum(cap_of, wave.reshape(per_cell) * (jam.reshape(per_cell) - vehicles))
    weights = jnp.concatenate([fraction.reshape(-1), jnp.zeros((LANES,), F32)])

    sends = []
    for pair in range(2):
        of_pair = slice(2 * pair, 2 * pair + 2)
        sends += pl.pallas_call(
            functools.partial(send_kernel, sizes),
            in_specs=[SMEM_WHOLE] * 4 + [VMEM_WHOLE] * 2,
            out_specs=[VMEM_WHOLE] * 2,
            out_shape=[pltpu.VMEM((cap * sub, LANES), F32)] * 2,
            compiler_params=params(4),
            cost_estimate=cost(cap * width * 20, cap * row_bytes * 10),
            name="send_rows",
        )(
            weights, in_cell, send_node[of_pair].reshape(-1), send_outlet[of_pair].reshape(-1),
            rows, turns,
        )
    arrived = [shifted(send, "region", stride) for send, stride in zip(sends, SHIFTS)]

    table = jnp.concatenate(
        [supply] + [shifted(supply, "region", -stride) for stride in SHIFTS]
    )

    flow, demand = pl.pallas_call(
        functools.partial(node_flow_kernel, sizes),
        in_specs=[SMEM_WHOLE] * 2 + [VMEM_WHOLE] * 2,
        out_specs=[VMEM_WHOLE] * 2,
        out_shape=[
            pltpu.VMEM((nodes * sub, LANES), F32),
            jax.ShapeDtypeStruct((branches, nodes), F32),
        ],
        scratch_shapes=[pltpu.VMEM((branches, nodes, LANES), F32)],
        compiler_params=params(12),
        cost_estimate=cost(nodes * width * 16, nodes * row_bytes * 6),
        name="node_flow",
    )(weights, in_cell, rows, turn)

    demands = partners(demand, "dest")
    keep, home_theta, slot_theta = pl.pallas_call(
        functools.partial(theta_kernel, sizes, commodities),
        out_shape=[jax.ShapeDtypeStruct(per_cell, F32)] * 2
        + [jax.ShapeDtypeStruct((4, cap), F32)],
        compiler_params=params(12),
        cost_estimate=cost(branches * nodes * cells * 8, nodes * 256),
        name="theta",
    )(
        table, place, out_valid.astype(jnp.int32), node_in, home_cell, send_node, fraction,
        *demands,
    )
    scale = jnp.concatenate(
        [shifted(slot_theta[number], "region", stride) for number, stride in enumerate(SHIFTS)]
    )

    base = pl.pallas_call(
        functools.partial(base_kernel, sizes),
        in_specs=[SMEM_WHOLE] * 4 + [VMEM_WHOLE] * 3,
        out_specs=VMEM_WHOLE,
        out_shape=pltpu.VMEM(((cells + 1) * sub, LANES), F32),
        compiler_params=params(4),
        cost_estimate=cost(cells * width * 4, cells * row_bytes * 4),
        name="home_inflow",
    )(
        keep.reshape(-1), home_theta.reshape(-1), source_node.reshape(-1),
        source_outlet.reshape(-1), rows, turns, flow,
    )

    out, _ = pl.pallas_call(
        functools.partial(finish_kernel, sizes, block),
        grid=(cells // block,),
        in_specs=[SMEM_WHOLE] * 2 + [VMEM_WHOLE] * 5,
        out_specs=[pl.BlockSpec((block, width), lambda i: (i, 0)), VMEM_WHOLE],
        out_shape=[
            jax.ShapeDtypeStruct((cells, width), F32),
            pltpu.VMEM(((cells + 1) * sub, LANES), F32),
        ],
        input_output_aliases={6: 1},
        compiler_params=params(8),
        cost_estimate=cost(cells * width, cells * row_bytes),
        name="finish",
    )(scale, land.reshape(-1), *arrived, base)
    return out


def solution(mesh):
    return jax.shard_map(
        on_device,
        mesh=mesh,
        in_specs=(
            P("region", "dest"),
            P("region"),
            P("region"),
            P("region"),
            P(None, "region"),
            P(None, "region"),
            P("region", None),
            P("region", None),
            P("region", "dest"),
        ),
        out_specs=P("region", "dest"),
        check_vma=False,
    )
```

```python
import functools

import jax
import jax.numpy as jnp
from jax import lax
from jax.experimental import pallas as pl
from jax.experimental.pallas import tpu as pltpu
from jax.sharding import PartitionSpec as P

SHIFTS = (1, -1, 2, -2)
EXACT = lax.Precision.HIGHEST
LANES = 128
MIB = 1 << 20
F32 = jnp.float32
I32 = jnp.int32
VMEM_WHOLE = pl.BlockSpec(memory_space=pltpu.VMEM)
SMEM_WHOLE = pl.BlockSpec(memory_space=pltpu.SMEM)
ANYWHERE = pl.BlockSpec(memory_space=pl.ANY)


def shifted(block, axis, distance):
    devices = range(lax.axis_size(axis))
    route = [((i - distance) % len(devices), i) for i in devices]
    return lax.ppermute(block, axis, route)


def partners(block, axis):
    count = lax.axis_size(axis)
    return [block] + [
        lax.ppermute(block, axis, [(i, i ^ other) for i in range(count)])
        for other in range(1, count)
    ]


def tree_sum(parts):
    while len(parts) > 1:
        parts = [parts[k] + parts[k + 1] for k in range(0, len(parts), 2)]
    return parts[0]


def params(mib):
    return pltpu.CompilerParams(vmem_limit_bytes=mib * MIB)


def cost(flops, moved):
    return pl.CostEstimate(flops=flops, bytes_accessed=moved, transcendentals=0)


def lane_sums(partial):
    ones = jnp.ones((8, LANES), F32)
    sums = lax.dot_general(
        ones, partial, (((1,), (1,)), ((), ())), preferred_element_type=F32, precision=EXACT
    )
    return sums[0:1, :]


def row_at(index, sub):
    return pl.ds(pl.multiple_of(index, sub), sub)


def padded(cap):
    return -(-cap // LANES) * LANES


def put_row(ref, row, value, fill):
    width = value.shape[1]
    for q in range(-(-width // LANES)):
        piece = value[:, q * LANES : min((q + 1) * LANES, width)]
        lack = LANES - piece.shape[1]
        if lack:
            piece = jnp.concatenate([piece, jnp.full((1, lack), fill, piece.dtype)], axis=1)
        ref[row + q : row + q + 1, :] = piece


def one_hot(index, count):
    rows = lax.broadcasted_iota(I32, (count, index.shape[1]), 0)
    return jnp.where(rows == index, 1.0, 0.0)


def look_up(table, index):
    picked = lax.dot_general(
        table.T,
        one_hot(index // LANES, table.shape[0]),
        (((1,), (0,)), ((), ())),
        preferred_element_type=F32,
        precision=EXACT,
    )
    return jnp.sum(picked * one_hot(index % LANES, LANES), axis=0, keepdims=True)


def scatter(index, values, height):
    high = jnp.where(index >= 0, index // LANES, -1)
    return lax.dot_general(
        one_hot(high, height) * values,
        one_hot(jnp.where(index >= 0, index % LANES, -1), LANES),
        (((1,), (1,)), ((), ())),
        preferred_element_type=F32,
        precision=EXACT,
    )


def home_cells(node_out, region_no, cells):
    here = (node_out >= 0) & (node_out // cells == region_no)
    return jnp.where(here, node_out % cells, -1)


def rows_of_group(x_ref, rows_ref, first, sub):
    total = None
    for q in range(sub):
        piece = x_ref[pl.ds(pl.multiple_of(first, 8), 8), q * LANES : (q + 1) * LANES]
        rows_ref[pl.ds(first * sub + q, 8, stride=sub), :] = piece
        total = piece if total is None else total + piece
    return total


def copies_in(source, target, sems, chunk):
    copies = [
        pltpu.make_async_copy(
            source.at[pl.ds(i * chunk, chunk), :], target.at[pl.ds(i * chunk, chunk), :], sems.at[i]
        )
        for i in range(target.shape[0] // chunk)
    ]
    for copy in copies:
        copy.start()
    return copies


def cell_sum_kernel(chunk, sub, x_hbm, sum_ref, rows_ref, x, partial, sems):
    copies = copies_in(x_hbm, x, sems, chunk)
    zeros = rows_ref.shape[0] - sub
    rows_ref[zeros:, :] = jnp.zeros((sub, LANES), F32)
    for number, copy in enumerate(copies):
        copy.wait()

        def body(step, carry, number=number):
            for half in range(2):
                first = number * chunk + step * 16 + half * 8
                total = rows_of_group(x, rows_ref, first, sub)
                partial[pl.ds(pl.multiple_of(step * 16 + half * 8, 8), 8), :] = total
            return carry

        lax.fori_loop(0, chunk // 16, body, 0)
        put_row(sum_ref, number * (chunk // LANES), lane_sums(partial[...]), 0.0)


def turn_rows_kernel(chunk, sub, x_hbm, after_ref, rows_ref, x, sems):
    for number, copy in enumerate(copies_in(x_hbm, x, sems, chunk)):
        copy.wait()

        def body(step, carry, number=number):
            for half in range(2):
                rows_of_group(x, rows_ref, number * chunk + step * 16 + half * 8, sub)
            return carry

        lax.fori_loop(0, chunk // 16, body, 0)


def index_kernel(
    sizes, node_in, node_out, send_list, recv_list, after_ref,
    in_cell, send_node, send_outlet, land, source_node, source_outlet,
):
    cells, nodes, branches, cap, sub = sizes
    height = cells // LANES
    region_no = lax.axis_index("region")
    ids = lax.broadcasted_iota(I32, (1, nodes), 1).astype(F32) + 1.0
    number = jnp.zeros((height, LANES), F32)
    slot = jnp.zeros((height, LANES), F32)
    for j in range(branches):
        ins = node_in[j : j + 1, :]
        put_row(in_cell, j * (nodes // LANES), jnp.where(ins >= 0, ins, cells), cells)
        home = home_cells(node_out[j : j + 1, :], region_no, cells)
        here = scatter(home, ids, height)
        number = number + here
        slot = slot + jnp.where(here > 0.0, j + 1.0, 0.0)
    source_node[...] = jnp.maximum(number.astype(I32) - 1, 0) * sub
    source_outlet[...] = slot.astype(I32) - 1
    per_side = padded(cap) // LANES
    for side in range(4):
        slots = send_list[side : side + 1, :]
        lands = recv_list[side : side + 1, :]
        put_row(send_node, side * per_side, jnp.where(slots >= 0, slots % nodes, 0), 0)
        put_row(send_outlet, side * per_side, jnp.where(slots >= 0, slots // nodes, -1), -1)
        put_row(land, side * per_side, jnp.where(lands >= 0, lands, cells) * sub, cells * sub)


def gathered_flow(node, in_cell, fraction, rows, sizes):
    cells, nodes, branches, cap, sub = sizes
    parts = []
    for i in range(branches):
        cell = in_cell[i * nodes + node]
        parts.append(rows[row_at(cell * sub, sub), :] * fraction[cell])
    return tree_sum(parts)


def send_kernel(sizes, sides, fraction, in_cell, send_node, send_outlet, rows, turns, *rest):
    cells, nodes, branches, cap, sub = sizes
    sends = rest[-len(sides) :]
    batch = 8
    for side, send in zip(sides, sends):

        def body(step, carry, side=side, send=send):
            first = step * batch
            values = []
            for i in range(batch):
                slot = side * padded(cap) + first + i
                node = send_node[slot]
                value = gathered_flow(node, in_cell, fraction, rows, sizes)
                choice = turns[row_at(node * sub, sub), :]
                values.append(jnp.where(choice == send_outlet[slot], value, 0.0))
            for i in range(batch):
                send[row_at((first + i) * sub, sub), :] = values[i]
            return carry

        lax.fori_loop(0, cap // batch, body, 0)


def scaled_send_kernel(sizes, side, theta, send_node, send_outlet, flow, turns, send):
    cells, nodes, branches, cap, sub = sizes
    batch = 8

    def body(step, carry):
        first = step * batch
        values = []
        for i in range(batch):
            slot = side * padded(cap) + first + i
            node = send_node[slot]
            at = row_at(node * sub, sub)
            value = flow[at, :] * theta[node]
            values.append(jnp.where(turns[at, :] == send_outlet[slot], value, 0.0))
        for i in range(batch):
            send[row_at((first + i) * sub, sub), :] = values[i]
        return carry

    lax.fori_loop(0, cap // batch, body, 0)


def node_flow_kernel(sizes, fraction, in_cell, rows, turns, after_ref, flow, demand, partial):
    cells, nodes, branches, cap, sub = sizes

    def gather(step, carry):
        first = step * 8
        values = [
            gathered_flow(first + i, in_cell, fraction, rows, sizes) for i in range(8)
        ]
        for i in range(8):
            flow[row_at((first + i) * sub, sub), :] = values[i]
        return carry

    def measure(step, carry):
        for half in range(2):
            first = step * 16 + half * 8
            totals = [jnp.zeros((8, LANES), F32)] * branches
            for q in range(sub):
                at = pl.ds(first * sub + q, 8, stride=sub)
                value = flow[at, :]
                choice = turns[at, :]
                totals = [
                    total + jnp.where(choice == j, value, 0.0) for j, total in enumerate(totals)
                ]
            for j in range(branches):
                partial[j, pl.ds(pl.multiple_of(first, 8), 8), :] = totals[j]
        return carry

    lax.fori_loop(0, nodes // 8, gather, 0)
    lax.fori_loop(0, nodes // 16, measure, 0)
    for j in range(branches):
        demand[j : j + 1, :] = lane_sums(partial[j])


def theta_kernel(
    sizes, commodities, supply, demands, node_in, node_out, fraction, keep, home_theta, tall
):
    cells, nodes, branches, cap, sub = sizes
    height = cells // LANES
    region_no = lax.axis_index("region")
    parts = [demands[k : k + branches, :] for k in range(0, demands.shape[0], branches)]
    demand = tree_sum(parts) * (1.0 / commodities)
    table = supply[...]
    theta = jnp.ones((1, nodes), F32)
    for j in range(branches):
        outs = node_out[j : j + 1, :]
        room = look_up(table, jnp.maximum(outs, 0))
        ratio = room / jnp.maximum(demand[j : j + 1, :], room)
        theta = jnp.minimum(theta, jnp.where(outs >= 0, ratio, 1.0))
    cell_theta = jnp.zeros((height, LANES), F32)
    into = jnp.zeros((height, LANES), F32)
    for j in range(branches):
        home = home_cells(node_out[j : j + 1, :], region_no, cells)
        cell_theta = cell_theta + scatter(node_in[j : j + 1, :], theta, height)
        into = into + scatter(home, theta, height)
    keep[...] = 1.0 - cell_theta * fraction[...]
    home_theta[...] = into
    put_row(tall, 0, theta, 0.0)


def slot_theta_kernel(sizes, regions, sides, theta, send_lists, scale):
    cells, nodes, branches, cap, sub = sizes
    region_no = lax.axis_index("region")
    table = theta[...]
    for side in range(4):
        if side not in sides:
            put_row(scale, side * (padded(cap) // LANES), jnp.ones((1, cap), F32), 1.0)
            continue
        sender = (region_no + (regions - SHIFTS[side])) % regions
        slots = send_lists[pl.ds(4 * sender + side, 1), :]
        node = jnp.where(slots >= 0, slots % nodes, 0) + sender * nodes
        put_row(scale, side * (padded(cap) // LANES), look_up(table, node), 0.0)


def base_kernel(sizes, keep, home_theta, node_row, outlet, rows, turns, flow, base):
    cells, nodes, branches, cap, sub = sizes
    batch = 8

    def body(step, carry):
        first = step * batch
        values = []
        for i in range(batch):
            cell = first + i
            at = row_at(node_row[cell], sub)
            moved = jnp.where(turns[at, :] == outlet[cell], flow[at, :], 0.0)
            kept = rows[row_at(cell * sub, sub), :] * keep[cell]
            values.append(kept + moved * home_theta[cell])
        for i in range(batch):
            base[row_at((first + i) * sub, sub), :] = values[i]
        return carry

    lax.fori_loop(0, cells // batch, body, 0)


def land_rows(sizes, sides, scale, land, received, base):
    cells, nodes, branches, cap, sub = sizes
    batch = 8
    for side, rows in zip(sides, received):

        def body(step, carry, side=side, rows=rows):
            first = step * batch
            stores = []
            for i in range(batch):
                slot = side * padded(cap) + first + i
                at = row_at(land[slot], sub)
                value = rows[row_at((first + i) * sub, sub), :]
                if scale is not None:
                    value = value * scale[slot]
                stores.append((at, base[at, :] + value))
            for at, value in stores:
                base[at, :] = value
            return carry

        lax.fori_loop(0, cap // batch, body, 0)


def land_kernel(sizes, sides, scale, land, *rest):
    received, (base_in, base) = rest[: len(sides)], rest[len(sides) :]
    land_rows(sizes, sides, scale, land, received, base)


def finish_kernel(sizes, sides, chunk, land, *rest):
    cells, nodes, branches, cap, sub = sizes
    received, (base_in, out, base, staged, sems) = rest[: len(sides)], rest[len(sides) :]
    land_rows(sizes, sides, None, land, received, base)
    copies = []
    for number in range(cells // chunk):

        def body(step, carry, number=number):
            for half in range(2):
                first = number * chunk + step * 16 + half * 8
                for q in range(sub):
                    staged[
                        pl.ds(pl.multiple_of(first, 8), 8), q * LANES : (q + 1) * LANES
                    ] = base[pl.ds(first * sub + q, 8, stride=sub), :]
            return carry

        lax.fori_loop(0, chunk // 16, body, 0)
        at = pl.ds(number * chunk, chunk)
        copies.append(
            pltpu.make_async_copy(staged.at[at, :], out.at[at, :], sems.at[number])
        )
        copies[-1].start()
    for copy in copies:
        copy.wait()


def on_device(occupancy, capacity, jam, wave, node_in, node_out, send_list, recv_list, turn):
    cells, width = occupancy.shape
    branches, nodes = node_in.shape
    cap = send_list.shape[1]
    sub = width // LANES
    sizes = (cells, nodes, branches, cap, sub)
    regions = lax.axis_size("region")
    commodities = width * lax.axis_size("dest")
    height = cells // LANES
    per_cell = (height, LANES)
    list_shape = (4 * padded(cap) // LANES, LANES)
    chunk = 128
    row_bytes = width * 4
    occupancy = pltpu.with_memory_space_constraint(occupancy, pltpu.HBM)
    turn = pltpu.with_memory_space_constraint(turn, pltpu.HBM)

    local_sum, rows = pl.pallas_call(
        functools.partial(cell_sum_kernel, chunk, sub),
        in_specs=[ANYWHERE],
        out_specs=[VMEM_WHOLE] * 2,
        out_shape=[
            jax.ShapeDtypeStruct(per_cell, F32),
            pltpu.VMEM(((cells + 1) * sub, LANES), F32),
        ],
        scratch_shapes=[
            pltpu.VMEM((cells, width), F32),
            pltpu.VMEM((chunk, LANES), F32),
            pltpu.SemaphoreType.DMA((cells // chunk,)),
        ],
        compiler_params=params(12),
        cost_estimate=cost(cells * width, cells * row_bytes),
        name="cell_sum",
    )(occupancy)

    sums = partners(local_sum, "dest")

    turns = pl.pallas_call(
        functools.partial(turn_rows_kernel, chunk, sub),
        in_specs=[ANYWHERE] * 2,
        out_specs=VMEM_WHOLE,
        out_shape=pltpu.VMEM((nodes * sub, LANES), I32),
        scratch_shapes=[
            pltpu.VMEM((nodes, width), I32),
            pltpu.SemaphoreType.DMA((nodes // chunk,)),
        ],
        compiler_params=params(8),
        cost_estimate=cost(0, nodes * row_bytes),
        name="turn_rows",
    )(turn, local_sum)

    in_cell, send_node, send_outlet, land, source_node, source_outlet = pl.pallas_call(
        functools.partial(index_kernel, sizes),
        in_specs=[VMEM_WHOLE] * 4 + [ANYWHERE],
        out_specs=[VMEM_WHOLE] * 6,
        out_shape=[jax.ShapeDtypeStruct((branches * nodes // LANES, LANES), I32)]
        + [jax.ShapeDtypeStruct(list_shape, I32)] * 3
        + [jax.ShapeDtypeStruct(per_cell, I32)] * 2,
        compiler_params=params(8),
        cost_estimate=cost(branches * nodes * cells * 2, nodes * 64),
        name="index_lists",
    )(node_in, node_out, send_list, recv_list, local_sum)
    in_cell, send_node, send_outlet, land, source_node, source_outlet = (
        x.reshape(-1) for x in (in_cell, send_node, send_outlet, land, source_node, source_outlet)
    )

    vehicles = tree_sum(sums) / commodities
    cap_of = capacity.reshape(per_cell)
    fraction = jnp.minimum(vehicles, cap_of) / vehicles
    supply = jnp.minimum(cap_of, wave.reshape(per_cell) * (jam.reshape(per_cell) - vehicles))
    weights = jnp.concatenate([fraction.reshape(-1), jnp.zeros((LANES,), F32)])

    def send_rows(sides, after):
        return pl.pallas_call(
            functools.partial(send_kernel, sizes, sides),
            in_specs=[SMEM_WHOLE] * 4 + [VMEM_WHOLE] * 2 + [ANYWHERE] * len(after),
            out_specs=[VMEM_WHOLE] * len(sides),
            out_shape=[pltpu.VMEM((cap * sub, LANES), F32)] * len(sides),
            compiler_params=params(4),
            cost_estimate=cost(cap * width * 20, cap * row_bytes * 10),
            name="send_rows",
        )(weights, in_cell, send_node, send_outlet, rows, turns, *after)

    near = send_rows((0, 1), ())
    ahead = send_rows((2,), near[:1])
    arrived = [
        shifted(send, "region", SHIFTS[side]) for side, send in enumerate([*near, *ahead])
    ]

    supply, _ = lax.optimization_barrier((supply, ahead[0]))
    supplies = lax.all_gather(supply, "region", axis=0, tiled=True)
    send_lists = lax.all_gather(send_list, "region", axis=0, tiled=True)

    flow, demand = pl.pallas_call(
        functools.partial(node_flow_kernel, sizes),
        in_specs=[SMEM_WHOLE] * 2 + [VMEM_WHOLE] * 2 + [ANYWHERE],
        out_specs=[VMEM_WHOLE] * 2,
        out_shape=[
            pltpu.VMEM((nodes * sub, LANES), F32),
            jax.ShapeDtypeStruct((branches, nodes), F32),
        ],
        scratch_shapes=[pltpu.VMEM((branches, nodes, LANES), F32)],
        compiler_params=params(8),
        cost_estimate=cost(nodes * width * 16, nodes * row_bytes * 6),
        name="node_flow",
    )(weights, in_cell, rows, turns, ahead[0])

    demands = lax.all_gather(demand, "dest", axis=0, tiled=True)
    keep, home_theta, theta = pl.pallas_call(
        functools.partial(theta_kernel, sizes, commodities),
        out_shape=[jax.ShapeDtypeStruct(per_cell, F32)] * 2
        + [jax.ShapeDtypeStruct((nodes // LANES, LANES), F32)],
        compiler_params=params(8),
        cost_estimate=cost(branches * nodes * cells * 8, nodes * 256),
        name="theta",
    )(supplies, demands, node_in, node_out, fraction)

    (behind,) = pl.pallas_call(
        functools.partial(scaled_send_kernel, sizes, 3),
        in_specs=[SMEM_WHOLE] * 3 + [VMEM_WHOLE] * 2,
        out_specs=[VMEM_WHOLE],
        out_shape=[pltpu.VMEM((cap * sub, LANES), F32)],
        compiler_params=params(4),
        cost_estimate=cost(cap * width * 4, cap * row_bytes * 4),
        name="scaled_send_rows",
    )(theta.reshape(-1), send_node, send_outlet, flow, turns)
    last = shifted(behind, "region", SHIFTS[3])

    thetas = lax.all_gather(theta, "region", axis=0, tiled=True)
    scale = pl.pallas_call(
        functools.partial(slot_theta_kernel, sizes, regions, (0, 1, 2)),
        out_shape=jax.ShapeDtypeStruct(list_shape, F32),
        compiler_params=params(8),
        cost_estimate=cost(4 * cap * 2048, nodes * 64),
        name="slot_theta",
    )(thetas, send_lists)

    base_shape = pltpu.VMEM(((cells + 1) * sub, LANES), F32)
    base = pl.pallas_call(
        functools.partial(base_kernel, sizes),
        in_specs=[SMEM_WHOLE] * 4 + [VMEM_WHOLE] * 3,
        out_specs=VMEM_WHOLE,
        out_shape=base_shape,
        compiler_params=params(4),
        cost_estimate=cost(cells * width * 4, cells * row_bytes * 4),
        name="home_inflow",
    )(keep.reshape(-1), home_theta.reshape(-1), source_node, source_outlet, rows, turns, flow)

    base = pl.pallas_call(
        functools.partial(land_kernel, sizes, (0, 1, 2)),
        in_specs=[SMEM_WHOLE] * 2 + [VMEM_WHOLE] * 4,
        out_specs=VMEM_WHOLE,
        out_shape=base_shape,
        input_output_aliases={5: 0},
        compiler_params=params(4),
        cost_estimate=cost(cap * width * 6, cap * row_bytes * 9),
        name="land_first",
    )(scale.reshape(-1), land, *arrived, base)

    out, _ = pl.pallas_call(
        functools.partial(finish_kernel, sizes, (3,), chunk),
        in_specs=[SMEM_WHOLE] + [VMEM_WHOLE] * 2,
        out_specs=[ANYWHERE, VMEM_WHOLE],
        out_shape=[jax.ShapeDtypeStruct((cells, width), F32), base_shape],
        scratch_shapes=[
            pltpu.VMEM((cells, width), F32),
            pltpu.SemaphoreType.DMA((cells // chunk,)),
        ],
        input_output_aliases={2: 1},
        compiler_params=params(12),
        cost_estimate=cost(cells * width, cells * row_bytes),
        name="finish",
    )(land, last, base)
    return out


def solution(mesh):
    return jax.shard_map(
        on_device,
        mesh=mesh,
        in_specs=(
            P("region", "dest"),
            P("region"),
            P("region"),
            P("region"),
            P(None, "region"),
            P(None, "region"),
            P("region", None),
            P("region", None),
            P("region", "dest"),
        ),
        out_specs=P("region", "dest"),
        check_vma=False,
    )
```

```python
import functools

import jax
import jax.numpy as jnp
from jax import lax
from jax.experimental import pallas as pl
from jax.experimental.pallas import tpu as pltpu
from jax.sharding import PartitionSpec as P

SHIFTS = (1, -1, 2, -2)
EXACT = lax.Precision.HIGHEST
LANES = 128
MIB = 1 << 20
F32 = jnp.float32
I32 = jnp.int32
VMEM_WHOLE = pl.BlockSpec(memory_space=pltpu.VMEM)
SMEM_WHOLE = pl.BlockSpec(memory_space=pltpu.SMEM)
ANYWHERE = pl.BlockSpec(memory_space=pl.ANY)


def to_neighbours(block):
    regions, members = lax.axis_size("region"), lax.axis_size("dest")
    route = [
        (r * members + d, (r + SHIFTS[d % 4]) % regions * members + d)
        for r in range(regions)
        for d in range(members)
    ]
    return lax.ppermute(block, ("region", "dest"), route)


def shifted(block, axis, distance):
    devices = range(lax.axis_size(axis))
    route = [((i - distance) % len(devices), i) for i in devices]
    return lax.ppermute(block, axis, route)


def partners(block, axis):
    count = lax.axis_size(axis)
    return [block] + [
        lax.ppermute(block, axis, [(i, i ^ other) for i in range(count)])
        for other in range(1, count)
    ]


def tree_sum(parts):
    while len(parts) > 1:
        parts = [parts[k] + parts[k + 1] for k in range(0, len(parts), 2)]
    return parts[0]


def params(mib):
    return pltpu.CompilerParams(vmem_limit_bytes=mib * MIB)


def cost(flops, moved):
    return pl.CostEstimate(flops=flops, bytes_accessed=moved, transcendentals=0)


def lane_sums(partial):
    sums = jnp.dot(
        partial, jnp.ones((LANES, LANES), F32), preferred_element_type=F32, precision=EXACT
    )
    row = lax.broadcasted_iota(I32, (LANES, LANES), 0)
    lane = lax.broadcasted_iota(I32, (LANES, LANES), 1)
    pieces = [
        jnp.sum(jnp.where(row == lane, sums[k : k + LANES, :], 0.0), axis=0, keepdims=True)
        for k in range(0, partial.shape[0], LANES)
    ]
    return jnp.concatenate(pieces, axis=0)


def stacked(row):
    return jnp.concatenate(
        [row[:, k : k + LANES] for k in range(0, row.shape[1], LANES)], axis=0
    )


def strung(rows):
    return jnp.concatenate([rows[k : k + 1, :] for k in range(rows.shape[0])], axis=1)


def row_at(index, sub):
    return pl.ds(pl.multiple_of(index, sub), sub)


def padded(cap):
    return -(-cap // LANES) * LANES


def put_row(ref, row, value, fill):
    width = value.shape[1]
    for q in range(-(-width // LANES)):
        piece = value[:, q * LANES : min((q + 1) * LANES, width)]
        lack = LANES - piece.shape[1]
        if lack:
            piece = jnp.concatenate([piece, jnp.full((1, lack), fill, piece.dtype)], axis=1)
        ref[row + q : row + q + 1, :] = piece


def one_hot(index, count):
    rows = lax.broadcasted_iota(I32, (count, index.shape[1]), 0)
    return jnp.where(rows == index, 1.0, 0.0)


def look_up(table, index):
    picked = lax.dot_general(
        table.T,
        one_hot(index // LANES, table.shape[0]),
        (((1,), (0,)), ((), ())),
        preferred_element_type=F32,
        precision=EXACT,
    )
    return jnp.sum(picked * one_hot(index % LANES, LANES), axis=0, keepdims=True)


def scatter(index, values, height):
    high = jnp.where(index >= 0, index // LANES, -1)
    return lax.dot_general(
        one_hot(high, height) * values,
        one_hot(jnp.where(index >= 0, index % LANES, -1), LANES),
        (((1,), (1,)), ((), ())),
        preferred_element_type=F32,
        precision=EXACT,
    )


def home_cells(node_out, region_no, cells):
    here = (node_out >= 0) & (node_out // cells == region_no)
    return jnp.where(here, node_out % cells, -1)


def rows_of_group(x_ref, rows_ref, first, sub):
    total = None
    for q in range(sub):
        piece = x_ref[pl.ds(pl.multiple_of(first, 8), 8), q * LANES : (q + 1) * LANES]
        rows_ref[pl.ds(first * sub + q, 8, stride=sub), :] = piece
        total = piece if total is None else total + piece
    return total


def copies_in(source, target, sems, chunk):
    copies = [
        pltpu.make_async_copy(
            source.at[pl.ds(i * chunk, chunk), :], target.at[pl.ds(i * chunk, chunk), :], sems.at[i]
        )
        for i in range(target.shape[0] // chunk)
    ]
    for copy in copies:
        copy.start()
    return copies


def cell_sum_kernel(chunk, sub, x_hbm, sum_ref, rows_ref, x, partial, sems):
    copies = copies_in(x_hbm, x, sems, chunk)
    zeros = rows_ref.shape[0] - sub
    rows_ref[zeros:, :] = jnp.zeros((sub, LANES), F32)
    for number, copy in enumerate(copies):
        copy.wait()

        def body(step, carry, number=number):
            for half in range(2):
                first = number * chunk + step * 16 + half * 8
                total = rows_of_group(x, rows_ref, first, sub)
                partial[pl.ds(pl.multiple_of(first, 8), 8), :] = total
            return carry

        lax.fori_loop(0, chunk // 16, body, 0)
    sum_ref[...] = lane_sums(partial[...])


def turn_rows_kernel(chunk, sub, x_hbm, after_ref, rows_ref, x, sems):
    for number, copy in enumerate(copies_in(x_hbm, x, sems, chunk)):
        copy.wait()

        def body(step, carry, number=number):
            for half in range(2):
                rows_of_group(x, rows_ref, number * chunk + step * 16 + half * 8, sub)
            return carry

        lax.fori_loop(0, chunk // 16, body, 0)


def index_kernel(
    sizes, node_in, node_out, send_list, recv_list, after_ref,
    in_cell, send_node, send_outlet, land, source_node, source_outlet,
):
    cells, nodes, branches, cap, sub = sizes
    height = cells // LANES
    region_no = lax.axis_index("region")
    ids = lax.broadcasted_iota(I32, (1, nodes), 1).astype(F32) + 1.0
    number = jnp.zeros((height, LANES), F32)
    slot = jnp.zeros((height, LANES), F32)
    for j in range(branches):
        ins = node_in[j : j + 1, :]
        put_row(in_cell, j * (nodes // LANES), jnp.where(ins >= 0, ins, cells), cells)
        home = home_cells(node_out[j : j + 1, :], region_no, cells)
        here = scatter(home, ids, height)
        number = number + here
        slot = slot + jnp.where(here > 0.0, j + 1.0, 0.0)
    source_node[...] = jnp.maximum(number.astype(I32) - 1, 0) * sub
    source_outlet[...] = slot.astype(I32) - 1
    per_side = padded(cap) // LANES
    for side in range(4):
        slots = send_list[side : side + 1, :]
        lands = recv_list[side : side + 1, :]
        put_row(send_node, side * per_side, jnp.where(slots >= 0, slots % nodes, 0), 0)
        put_row(send_outlet, side * per_side, jnp.where(slots >= 0, slots // nodes, -1), -1)
        put_row(land, side * per_side, jnp.where(lands >= 0, lands, cells) * sub, cells * sub)


def gathered_flow(node, in_cell, scaled, sizes):
    cells, nodes, branches, cap, sub = sizes
    return tree_sum(
        [scaled[row_at(in_cell[i * nodes + node] * sub, sub), :] for i in range(branches)]
    )


def scale_kernel(sizes, fraction, rows, scaled):
    cells, nodes, branches, cap, sub = sizes

    def body(step, carry):
        first = step * 16
        values = [
            rows[row_at((first + i) * sub, sub), :] * fraction[first + i] for i in range(16)
        ]
        for i in range(16):
            scaled[row_at((first + i) * sub, sub), :] = values[i]
        return carry

    lax.fori_loop(0, cells // 16, body, 0)
    scaled[row_at(cells * sub, sub), :] = jnp.zeros((sub, LANES), F32)


def send_kernel(sizes, sides, in_cell, send_node, send_outlet, scaled, turns, *rest):
    cells, nodes, branches, cap, sub = sizes
    sends = rest[-len(sides) :]
    batch = 8
    for side, send in zip(sides, sends):

        def body(step, carry, side=side, send=send):
            first = step * batch
            values = []
            for i in range(batch):
                slot = side * padded(cap) + first + i
                node = send_node[slot]
                value = gathered_flow(node, in_cell, scaled, sizes)
                choice = turns[row_at(node * sub, sub), :]
                values.append(jnp.where(choice == send_outlet[slot], value, 0.0))
            for i in range(batch):
                send[row_at((first + i) * sub, sub), :] = values[i]
            return carry

        lax.fori_loop(0, cap // batch, body, 0)


def scale_send_kernel(
    sizes, sides, fraction, in_cell, send_node, send_outlet, rows, turns, scaled, *sends
):
    scale_kernel(sizes, fraction, rows, scaled)
    send_kernel(sizes, sides, in_cell, send_node, send_outlet, scaled, turns, *sends)


def scaled_send_kernel(sizes, side, theta, send_node, send_outlet, flow, turns, send):
    cells, nodes, branches, cap, sub = sizes
    batch = 8

    def body(step, carry):
        first = step * batch
        values = []
        for i in range(batch):
            slot = side * padded(cap) + first + i
            node = send_node[slot]
            at = row_at(node * sub, sub)
            value = flow[at, :] * theta[node]
            values.append(jnp.where(turns[at, :] == send_outlet[slot], value, 0.0))
        for i in range(batch):
            send[row_at((first + i) * sub, sub), :] = values[i]
        return carry

    lax.fori_loop(0, cap // batch, body, 0)


def node_flow_kernel(sizes, in_cell, scaled, turns, after_ref, flow, demand, partial):
    cells, nodes, branches, cap, sub = sizes

    def gather(step, carry):
        first = step * 8
        values = [
            gathered_flow(first + i, in_cell, scaled, sizes) for i in range(8)
        ]
        for i in range(8):
            flow[row_at((first + i) * sub, sub), :] = values[i]
        return carry

    def measure(step, carry):
        for half in range(2):
            first = step * 16 + half * 8
            totals = [jnp.zeros((8, LANES), F32)] * branches
            for q in range(sub):
                at = pl.ds(first * sub + q, 8, stride=sub)
                value = flow[at, :]
                choice = turns[at, :]
                totals = [
                    total + jnp.where(choice == j, value, 0.0) for j, total in enumerate(totals)
                ]
            for j in range(branches):
                partial[j, pl.ds(pl.multiple_of(first, 8), 8), :] = totals[j]
        return carry

    lax.fori_loop(0, nodes // 8, gather, 0)
    lax.fori_loop(0, nodes // 16, measure, 0)
    per_outlet = nodes // LANES
    for j in range(branches):
        demand[j * per_outlet : (j + 1) * per_outlet, :] = lane_sums(partial[j])


def theta_kernel(
    sizes, regions, commodities, supply, shared, node_in, node_out, send_list, fraction,
    after_ref, keep, home_theta, theta_out, slot_theta,
):
    cells, nodes, branches, cap, sub = sizes
    height = cells // LANES
    per_outlet = nodes // LANES
    block = branches * per_outlet + height
    region_no = lax.axis_index("region")
    members = shared.shape[0] // block
    parts = [
        shared[d * block : d * block + branches * per_outlet, :] for d in range(members)
    ]
    demand = tree_sum(parts) * (1.0 / commodities)
    table = jnp.concatenate(
        [supply[...]]
        + [
            shared[d * block + branches * per_outlet : (d + 1) * block, :] for d in range(4)
        ],
        axis=0,
    )
    tall = jnp.ones((per_outlet, LANES), F32)
    for j in range(branches):
        outs = node_out[j : j + 1, :]
        cell = jnp.maximum(outs, 0)
        offset = (cell // cells + regions - region_no) % regions
        sector = jnp.zeros_like(offset)
        for d in range(4):
            sector = jnp.where(offset == (-SHIFTS[d]) % regions, d + 1, sector)
        room = stacked(look_up(table, sector * cells + cell % cells))
        ratio = room / jnp.maximum(demand[j * per_outlet : (j + 1) * per_outlet, :], room)
        tall = jnp.minimum(tall, jnp.where(stacked(outs) >= 0, ratio, 1.0))
    theta_out[...] = tall
    theta = strung(tall)
    cell_theta = jnp.zeros((height, LANES), F32)
    into = jnp.zeros((height, LANES), F32)
    for j in range(branches):
        home = home_cells(node_out[j : j + 1, :], region_no, cells)
        cell_theta = cell_theta + scatter(node_in[j : j + 1, :], theta, height)
        into = into + scatter(home, theta, height)
    keep[...] = 1.0 - cell_theta * fraction[...]
    home_theta[...] = into
    slots = send_list[pl.ds(lax.axis_index("dest") % 4, 1), :]
    put_row(slot_theta, 0, look_up(tall, jnp.where(slots >= 0, slots % nodes, 0)), 0.0)


def home_kernel(sizes, node_row, outlet, turns, flow, home):
    cells, nodes, branches, cap, sub = sizes
    batch = 8

    def body(step, carry):
        first = step * batch
        values = []
        for i in range(batch):
            at = row_at(node_row[first + i], sub)
            values.append(jnp.where(turns[at, :] == outlet[first + i], flow[at, :], 0.0))
        for i in range(batch):
            home[row_at((first + i) * sub, sub), :] = values[i]
        return carry

    lax.fori_loop(0, cells // batch, body, 0)


def base_kernel(sizes, keep, home_theta, rows, home, base):
    cells, nodes, branches, cap, sub = sizes
    batch = 8

    def body(step, carry):
        first = step * batch
        values = []
        for i in range(batch):
            at = row_at((first + i) * sub, sub)
            values.append(rows[at, :] * keep[first + i] + home[at, :] * home_theta[first + i])
        for i in range(batch):
            base[row_at((first + i) * sub, sub), :] = values[i]
        return carry

    lax.fori_loop(0, cells // batch, body, 0)


def land_rows(sizes, sides, scale, land, received, base):
    cells, nodes, branches, cap, sub = sizes
    batch = 8
    for side, rows in zip(sides, received):

        def body(step, carry, side=side, rows=rows):
            first = step * batch
            stores = []
            for i in range(batch):
                slot = side * padded(cap) + first + i
                at = row_at(land[slot], sub)
                value = rows[row_at((first + i) * sub, sub), :]
                if scale is not None:
                    value = value * scale[slot]
                stores.append((at, base[at, :] + value))
            for at, value in stores:
                base[at, :] = value
            return carry

        lax.fori_loop(0, cap // batch, body, 0)


def land_kernel(sizes, sides, scale, land, *rest):
    received, (base_in, base) = rest[: len(sides)], rest[len(sides) :]
    land_rows(sizes, sides, scale, land, received, base)


def finish_kernel(sizes, sides, chunk, land, *rest):
    cells, nodes, branches, cap, sub = sizes
    received, (base_in, out, base, staged, sems) = rest[: len(sides)], rest[len(sides) :]
    land_rows(sizes, sides, None, land, received, base)
    copies = []
    for number in range(cells // chunk):

        def body(step, carry, number=number):
            for half in range(2):
                first = number * chunk + step * 16 + half * 8
                for q in range(sub):
                    staged[
                        pl.ds(pl.multiple_of(first, 8), 8), q * LANES : (q + 1) * LANES
                    ] = base[pl.ds(first * sub + q, 8, stride=sub), :]
            return carry

        lax.fori_loop(0, chunk // 16, body, 0)
        at = pl.ds(number * chunk, chunk)
        copies.append(
            pltpu.make_async_copy(staged.at[at, :], out.at[at, :], sems.at[number])
        )
        copies[-1].start()
    for copy in copies:
        copy.wait()


def on_device(occupancy, capacity, jam, wave, node_in, node_out, send_list, recv_list, turn):
    cells, width = occupancy.shape
    branches, nodes = node_in.shape
    cap = send_list.shape[1]
    sub = width // LANES
    sizes = (cells, nodes, branches, cap, sub)
    regions = lax.axis_size("region")
    commodities = width * lax.axis_size("dest")
    height = cells // LANES
    per_cell = (height, LANES)
    list_shape = (4 * padded(cap) // LANES, LANES)
    chunk = 128
    some_node = node_in[0, 0] >= 0

    def apart(exchange, block):
        shape = jax.eval_shape(exchange, block)
        return lax.cond(some_node, exchange, lambda x: jnp.zeros(shape.shape, F32), block)

    row_bytes = width * 4
    occupancy = pltpu.with_memory_space_constraint(occupancy, pltpu.HBM)
    turn = pltpu.with_memory_space_constraint(turn, pltpu.HBM)

    local_sum, rows = pl.pallas_call(
        functools.partial(cell_sum_kernel, chunk, sub),
        in_specs=[ANYWHERE],
        out_specs=[VMEM_WHOLE] * 2,
        out_shape=[
            jax.ShapeDtypeStruct(per_cell, F32),
            pltpu.VMEM(((cells + 1) * sub, LANES), F32),
        ],
        scratch_shapes=[
            pltpu.VMEM((cells, width), F32),
            pltpu.VMEM((cells, LANES), F32),
            pltpu.SemaphoreType.DMA((cells // chunk,)),
        ],
        compiler_params=params(14),
        cost_estimate=cost(cells * width, cells * row_bytes),
        name="cell_sum",
    )(occupancy)

    sums = partners(local_sum, "dest")

    turns = pl.pallas_call(
        functools.partial(turn_rows_kernel, chunk, sub),
        in_specs=[ANYWHERE] * 2,
        out_specs=VMEM_WHOLE,
        out_shape=pltpu.VMEM((nodes * sub, LANES), I32),
        scratch_shapes=[
            pltpu.VMEM((nodes, width), I32),
            pltpu.SemaphoreType.DMA((nodes // chunk,)),
        ],
        compiler_params=params(8),
        cost_estimate=cost(0, nodes * row_bytes),
        name="turn_rows",
    )(turn, local_sum)

    in_cell, send_node, send_outlet, land, source_node, source_outlet = pl.pallas_call(
        functools.partial(index_kernel, sizes),
        in_specs=[VMEM_WHOLE] * 4 + [ANYWHERE],
        out_specs=[VMEM_WHOLE] * 6,
        out_shape=[jax.ShapeDtypeStruct((branches * nodes // LANES, LANES), I32)]
        + [jax.ShapeDtypeStruct(list_shape, I32)] * 3
        + [jax.ShapeDtypeStruct(per_cell, I32)] * 2,
        compiler_params=params(8),
        cost_estimate=cost(branches * nodes * cells * 2, nodes * 64),
        name="index_lists",
    )(node_in, node_out, send_list, recv_list, local_sum)
    in_cell, send_node, send_outlet, land, source_node, source_outlet = (
        x.reshape(-1) for x in (in_cell, send_node, send_outlet, land, source_node, source_outlet)
    )

    vehicles = tree_sum(sums) / commodities
    cap_of = capacity.reshape(per_cell)
    fraction = jnp.minimum(vehicles, cap_of) / vehicles
    supply = jnp.minimum(cap_of, wave.reshape(per_cell) * (jam.reshape(per_cell) - vehicles))
    rows_shape = pltpu.VMEM(((cells + 1) * sub, LANES), F32)
    send_shape = pltpu.VMEM((cap * sub, LANES), F32)

    scaled, *near = pl.pallas_call(
        functools.partial(scale_send_kernel, sizes, (0, 1)),
        in_specs=[SMEM_WHOLE] * 4 + [VMEM_WHOLE] * 2,
        out_specs=[VMEM_WHOLE] * 3,
        out_shape=[rows_shape] + [send_shape] * 2,
        compiler_params=params(4),
        cost_estimate=cost(cap * width * 20, cap * row_bytes * 10),
        name="send_near",
    )(fraction.reshape(-1), in_cell, send_node, send_outlet, rows, turns)
    ahead = pl.pallas_call(
        functools.partial(send_kernel, sizes, (2,)),
        in_specs=[SMEM_WHOLE] * 3 + [VMEM_WHOLE] * 2,
        out_specs=VMEM_WHOLE,
        out_shape=send_shape,
        compiler_params=params(4),
        cost_estimate=cost(1, 1),
        name="send_ahead",
    )(in_cell, send_node, send_outlet, scaled, turns)
    arrived = [
        shifted(send, "region", SHIFTS[side]) for side, send in enumerate([*near, ahead])
    ]

    supply, *_ = lax.optimization_barrier((supply, *near, ahead))
    supply_there = to_neighbours(supply)

    flow, demand = pl.pallas_call(
        functools.partial(node_flow_kernel, sizes),
        in_specs=[SMEM_WHOLE] + [VMEM_WHOLE] * 2 + [ANYWHERE],
        out_specs=[VMEM_WHOLE] * 2,
        out_shape=[
            pltpu.VMEM((nodes * sub, LANES), F32),
            jax.ShapeDtypeStruct((branches * nodes // LANES, LANES), F32),
        ],
        scratch_shapes=[pltpu.VMEM((branches, nodes, LANES), F32)],
        compiler_params=params(8),
        cost_estimate=cost(1, 1),
        name="node_flow",
    )(in_cell, scaled, turns, supply_there)

    shared = apart(
        lambda x: lax.all_gather(x, "dest", axis=0, tiled=True),
        jnp.concatenate([demand, supply_there]),
    )
    home = pl.pallas_call(
        functools.partial(home_kernel, sizes),
        in_specs=[SMEM_WHOLE] * 2 + [VMEM_WHOLE] * 2,
        out_specs=VMEM_WHOLE,
        out_shape=rows_shape,
        compiler_params=params(4),
        cost_estimate=cost(1, 1),
        name="home_rows",
    )(source_node, source_outlet, turns, flow)
    keep, home_theta, theta, slot_theta = pl.pallas_call(
        functools.partial(theta_kernel, sizes, regions, commodities),
        in_specs=[VMEM_WHOLE] * 6 + [ANYWHERE],
        out_specs=[VMEM_WHOLE] * 4,
        out_shape=[jax.ShapeDtypeStruct(per_cell, F32)] * 2
        + [
            jax.ShapeDtypeStruct((nodes // LANES, LANES), F32),
            jax.ShapeDtypeStruct((padded(cap) // LANES, LANES), F32),
        ],
        compiler_params=params(8),
        cost_estimate=cost(1, 1),
        name="theta",
    )(supply, shared, node_in, node_out, send_list, fraction, home)
    theta_there = apart(to_neighbours, slot_theta)
    scale = lax.all_gather(theta_there, "dest", axis=0, tiled=True)[: list_shape[0]]

    (behind,) = pl.pallas_call(
        functools.partial(scaled_send_kernel, sizes, 3),
        in_specs=[SMEM_WHOLE] * 3 + [VMEM_WHOLE] * 2,
        out_specs=[VMEM_WHOLE],
        out_shape=[send_shape],
        compiler_params=params(4),
        cost_estimate=cost(1, 1),
        name="send_scaled",
    )(theta.reshape(-1), send_node, send_outlet, flow, turns)
    behind, _ = lax.optimization_barrier((behind, theta_there))
    last = shifted(behind, "region", SHIFTS[3])

    base = pl.pallas_call(
        functools.partial(base_kernel, sizes),
        in_specs=[SMEM_WHOLE] * 2 + [VMEM_WHOLE] * 2,
        out_specs=VMEM_WHOLE,
        out_shape=rows_shape,
        compiler_params=params(4),
        cost_estimate=cost(1, 1),
        name="base_rows",
    )(keep.reshape(-1), home_theta.reshape(-1), rows, home)

    base = pl.pallas_call(
        functools.partial(land_kernel, sizes, (0, 1, 2)),
        in_specs=[SMEM_WHOLE] * 2 + [VMEM_WHOLE] * 4,
        out_specs=VMEM_WHOLE,
        out_shape=rows_shape,
        input_output_aliases={5: 0},
        compiler_params=params(4),
        cost_estimate=cost(1, 1),
        name="land_first",
    )(scale.reshape(-1), land, *arrived, base)

    out, _ = pl.pallas_call(
        functools.partial(finish_kernel, sizes, (3,), chunk),
        in_specs=[SMEM_WHOLE] + [VMEM_WHOLE] * 2,
        out_specs=[ANYWHERE, VMEM_WHOLE],
        out_shape=[jax.ShapeDtypeStruct((cells, width), F32), rows_shape],
        scratch_shapes=[
            pltpu.VMEM((cells, width), F32),
            pltpu.SemaphoreType.DMA((cells // chunk,)),
        ],
        input_output_aliases={2: 1},
        compiler_params=params(12),
        cost_estimate=cost(cells * width, cells * row_bytes),
        name="finish",
    )(land, last, base)
    return out


def solution(mesh):
    return jax.shard_map(
        on_device,
        mesh=mesh,
        in_specs=(
            P("region", "dest"),
            P("region"),
            P("region"),
            P("region"),
            P(None, "region"),
            P(None, "region"),
            P("region", None),
            P("region", None),
            P("region", "dest"),
        ),
        out_specs=P("region", "dest"),
        check_vma=False,
    )
```

```python
import functools

import jax
import jax.numpy as jnp
from jax import lax
from jax.experimental import pallas as pl
from jax.experimental.pallas import tpu as pltpu
from jax.sharding import PartitionSpec as P

SHIFTS = (1, -1, 2, -2)
EXACT = lax.Precision.HIGHEST
LANES = 128
MIB = 1 << 20
F32 = jnp.float32
I32 = jnp.int32
VMEM_WHOLE = pl.BlockSpec(memory_space=pltpu.VMEM)
SMEM_WHOLE = pl.BlockSpec(memory_space=pltpu.SMEM)
ANYWHERE = pl.BlockSpec(memory_space=pl.ANY)


def to_neighbours(block):
    regions, members = lax.axis_size("region"), lax.axis_size("dest")
    route = [
        (r * members + d, (r + SHIFTS[d % 4]) % regions * members + d)
        for r in range(regions)
        for d in range(members)
    ]
    return lax.ppermute(block, ("region", "dest"), route)


def shifted(block, axis, distance):
    devices = range(lax.axis_size(axis))
    route = [((i - distance) % len(devices), i) for i in devices]
    return lax.ppermute(block, axis, route)


def partners(block, axis):
    count = lax.axis_size(axis)
    return [block] + [
        lax.ppermute(block, axis, [(i, i ^ other) for i in range(count)])
        for other in range(1, count)
    ]


def tree_sum(parts):
    while len(parts) > 1:
        parts = [parts[k] + parts[k + 1] for k in range(0, len(parts), 2)]
    return parts[0]


def params(mib):
    return pltpu.CompilerParams(vmem_limit_bytes=mib * MIB)


def cost(flops, moved):
    return pl.CostEstimate(flops=flops, bytes_accessed=moved, transcendentals=0)


def lane_sums(partial):
    sums = jnp.dot(
        partial, jnp.ones((LANES, LANES), F32), preferred_element_type=F32, precision=EXACT
    )
    row = lax.broadcasted_iota(I32, (LANES, LANES), 0)
    lane = lax.broadcasted_iota(I32, (LANES, LANES), 1)
    pieces = [
        jnp.sum(jnp.where(row == lane, sums[k : k + LANES, :], 0.0), axis=0, keepdims=True)
        for k in range(0, partial.shape[0], LANES)
    ]
    return jnp.concatenate(pieces, axis=0)


def stacked(row):
    return jnp.concatenate(
        [row[:, k : k + LANES] for k in range(0, row.shape[1], LANES)], axis=0
    )


def strung(rows):
    return jnp.concatenate([rows[k : k + 1, :] for k in range(rows.shape[0])], axis=1)


def row_of(ref, number, sub):
    if sub % 8 == 0:
        return ref.reshape(ref.shape[0] // sub, sub, LANES).at[number]
    return ref.at[pl.ds(pl.multiple_of(number * sub, sub), sub), :]


def padded(cap):
    return -(-cap // LANES) * LANES


def put_row(ref, row, value, fill):
    width = value.shape[1]
    for q in range(-(-width // LANES)):
        piece = value[:, q * LANES : min((q + 1) * LANES, width)]
        lack = LANES - piece.shape[1]
        if lack:
            piece = jnp.concatenate([piece, jnp.full((1, lack), fill, piece.dtype)], axis=1)
        ref[row + q : row + q + 1, :] = piece


def one_hot(index, count):
    rows = lax.broadcasted_iota(I32, (count, index.shape[1]), 0)
    return jnp.where(rows == index, 1.0, 0.0)


def look_up(table, index):
    picked = lax.dot_general(
        table.T,
        one_hot(index // LANES, table.shape[0]),
        (((1,), (0,)), ((), ())),
        preferred_element_type=F32,
        precision=EXACT,
    )
    return jnp.sum(picked * one_hot(index % LANES, LANES), axis=0, keepdims=True)


def scatter(index, values, height):
    high = jnp.where(index >= 0, index // LANES, -1)
    return lax.dot_general(
        one_hot(high, height) * values,
        one_hot(jnp.where(index >= 0, index % LANES, -1), LANES),
        (((1,), (1,)), ((), ())),
        preferred_element_type=F32,
        precision=EXACT,
    )


def home_cells(node_out, region_no, cells):
    here = (node_out >= 0) & (node_out // cells == region_no)
    return jnp.where(here, node_out % cells, -1)


def rows_of_group(x_ref, rows_ref, first, sub):
    total = None
    for q in range(sub):
        piece = x_ref[pl.ds(pl.multiple_of(first, 8), 8), q * LANES : (q + 1) * LANES]
        rows_ref[pl.ds(first * sub + q, 8, stride=sub), :] = piece
        total = piece if total is None else total + piece
    return total


def copies_in(source, target, sems, chunk):
    copies = [
        pltpu.make_async_copy(
            source.at[pl.ds(i * chunk, chunk), :], target.at[pl.ds(i * chunk, chunk), :], sems.at[i]
        )
        for i in range(target.shape[0] // chunk)
    ]
    for copy in copies:
        copy.start()
    return copies


def make_lists(
    sizes, node_in, node_out, send_list, recv_list,
    in_cell, send_node, send_outlet, land, source_node, source_outlet,
):
    cells, nodes, branches, cap, sub = sizes
    height = cells // LANES
    region_no = lax.axis_index("region")
    ids = lax.broadcasted_iota(I32, (1, nodes), 1).astype(F32) + 1.0
    number = jnp.zeros((height, LANES), F32)
    slot = jnp.zeros((height, LANES), F32)
    for j in range(branches):
        ins = node_in[j : j + 1, :]
        put_row(in_cell, j * (nodes // LANES), jnp.where(ins >= 0, ins, cells), cells)
        home = home_cells(node_out[j : j + 1, :], region_no, cells)
        here = scatter(home, ids, height)
        number = number + here
        slot = slot + jnp.where(here > 0.0, j + 1.0, 0.0)
    source_node[...] = jnp.maximum(number.astype(I32) - 1, 0)
    source_outlet[...] = slot.astype(I32) - 1
    per_side = padded(cap) // LANES
    for side in range(4):
        slots = send_list[side : side + 1, :]
        lands = recv_list[side : side + 1, :]
        put_row(send_node, side * per_side, jnp.where(slots >= 0, slots % nodes, 0), 0)
        put_row(send_outlet, side * per_side, jnp.where(slots >= 0, slots // nodes, -1), -1)
        put_row(land, side * per_side, jnp.where(lands >= 0, lands, cells), cells)


def cell_sum_kernel(sizes, chunk, x_hbm, *rest):
    cells, nodes, branches, cap, sub = sizes
    lists, (sum_ref, rows_ref), made, (x, partial, sems) = (
        rest[:4], rest[4:6], rest[6:12], rest[12:]
    )
    copies = copies_in(x_hbm, x, sems, chunk)
    make_lists(sizes, *lists, *made)
    zeros = rows_ref.shape[0] - sub
    rows_ref[zeros:, :] = jnp.zeros((sub, LANES), F32)
    for number, copy in enumerate(copies):
        copy.wait()

        def body(step, carry, number=number):
            for half in range(2):
                first = number * chunk + step * 16 + half * 8
                total = rows_of_group(x, rows_ref, first, sub)
                partial[pl.ds(pl.multiple_of(first, 8), 8), :] = total
            return carry

        lax.fori_loop(0, chunk // 16, body, 0)
    sum_ref[...] = lane_sums(partial[...])


def turn_rows_kernel(chunk, sub, x_hbm, after_ref, rows_ref, x, sems):
    for number, copy in enumerate(copies_in(x_hbm, x, sems, chunk)):
        copy.wait()

        def body(step, carry, number=number):
            for half in range(2):
                rows_of_group(x, rows_ref, number * chunk + step * 16 + half * 8, sub)
            return carry

        lax.fori_loop(0, chunk // 16, body, 0)


def gathered_flow(node, in_cell, scaled, sizes):
    cells, nodes, branches, cap, sub = sizes
    return tree_sum(
        [row_of(scaled, in_cell[i * nodes + node], sub)[...] for i in range(branches)]
    )


def scale_kernel(sizes, fraction, rows, scaled):
    cells, nodes, branches, cap, sub = sizes

    def body(step, carry):
        first = step * 16
        values = [
            row_of(rows, first + i, sub)[...] * fraction[first + i] for i in range(16)
        ]
        for i in range(16):
            row_of(scaled, first + i, sub)[...] = values[i]
        return carry

    lax.fori_loop(0, cells // 16, body, 0)
    row_of(scaled, cells, sub)[...] = jnp.zeros((sub, LANES), F32)


def send_kernel(sizes, sides, in_cell, send_node, send_outlet, scaled, turns, *rest):
    cells, nodes, branches, cap, sub = sizes
    sends = rest[1:]
    batch = 8
    for side, send in zip(sides, sends):

        def body(step, carry, side=side, send=send):
            first = step * batch
            values = []
            for i in range(batch):
                slot = side * padded(cap) + first + i
                node = send_node[slot]
                value = gathered_flow(node, in_cell, scaled, sizes)
                choice = row_of(turns, node, sub)[...]
                values.append(jnp.where(choice == send_outlet[slot], value, 0.0))
            for i in range(batch):
                row_of(send, first + i, sub)[...] = values[i]
            return carry

        lax.fori_loop(0, cap // batch, body, 0)


def scaled_send_kernel(sizes, side, theta, send_node, send_outlet, flow, turns, send):
    cells, nodes, branches, cap, sub = sizes
    batch = 8

    def body(step, carry):
        first = step * batch
        values = []
        for i in range(batch):
            slot = side * padded(cap) + first + i
            node = send_node[slot]
            value = row_of(flow, node, sub)[...] * theta[node]
            choice = row_of(turns, node, sub)[...]
            values.append(jnp.where(choice == send_outlet[slot], value, 0.0))
        for i in range(batch):
            row_of(send, first + i, sub)[...] = values[i]
        return carry

    lax.fori_loop(0, cap // batch, body, 0)


def node_flow_kernel(sizes, in_cell, scaled, turns, after_ref, flow, demand, partial):
    cells, nodes, branches, cap, sub = sizes

    def gather(step, carry):
        first = step * 8
        values = [
            gathered_flow(first + i, in_cell, scaled, sizes) for i in range(8)
        ]
        for i in range(8):
            row_of(flow, first + i, sub)[...] = values[i]
        return carry

    def measure(step, carry):
        for half in range(2):
            first = step * 16 + half * 8
            totals = [jnp.zeros((8, LANES), F32)] * branches
            for q in range(sub):
                at = pl.ds(first * sub + q, 8, stride=sub)
                value = flow[at, :]
                choice = turns[at, :]
                totals = [
                    total + jnp.where(choice == j, value, 0.0) for j, total in enumerate(totals)
                ]
            for j in range(branches):
                partial[j, pl.ds(pl.multiple_of(first, 8), 8), :] = totals[j]
        return carry

    lax.fori_loop(0, nodes // 8, gather, 0)
    lax.fori_loop(0, nodes // 16, measure, 0)
    per_outlet = nodes // LANES
    for j in range(branches):
        demand[j * per_outlet : (j + 1) * per_outlet, :] = lane_sums(partial[j])


def theta_kernel(
    sizes, regions, commodities, supply, shared, node_in, node_out, send_list, fraction,
    keep, home_theta, theta_out, slot_theta,
):
    cells, nodes, branches, cap, sub = sizes
    height = cells // LANES
    per_outlet = nodes // LANES
    block = branches * per_outlet + height
    region_no = lax.axis_index("region")
    members = shared.shape[0] // block
    parts = [
        shared[d * block : d * block + branches * per_outlet, :] for d in range(members)
    ]
    demand = tree_sum(parts) * (1.0 / commodities)
    table = jnp.concatenate(
        [supply[...]]
        + [
            shared[d * block + branches * per_outlet : (d + 1) * block, :] for d in range(4)
        ],
        axis=0,
    )
    tall = jnp.ones((per_outlet, LANES), F32)
    for j in range(branches):
        outs = node_out[j : j + 1, :]
        cell = jnp.maximum(outs, 0)
        offset = (cell // cells + regions - region_no) % regions
        sector = jnp.zeros_like(offset)
        for d in range(4):
            sector = jnp.where(offset == (-SHIFTS[d]) % regions, d + 1, sector)
        room = stacked(look_up(table, sector * cells + cell % cells))
        ratio = room / jnp.maximum(demand[j * per_outlet : (j + 1) * per_outlet, :], room)
        tall = jnp.minimum(tall, jnp.where(stacked(outs) >= 0, ratio, 1.0))
    theta_out[...] = tall
    theta = strung(tall)
    cell_theta = jnp.zeros((height, LANES), F32)
    into = jnp.zeros((height, LANES), F32)
    for j in range(branches):
        home = home_cells(node_out[j : j + 1, :], region_no, cells)
        cell_theta = cell_theta + scatter(node_in[j : j + 1, :], theta, height)
        into = into + scatter(home, theta, height)
    keep[...] = 1.0 - cell_theta * fraction[...]
    home_theta[...] = into
    slots = send_list[pl.ds(lax.axis_index("dest") % 4, 1), :]
    put_row(slot_theta, 0, look_up(tall, jnp.where(slots >= 0, slots % nodes, 0)), 0.0)


def home_kernel(sizes, source, outlet, turns, flow, home):
    cells, nodes, branches, cap, sub = sizes
    batch = 8

    def body(step, carry):
        first = step * batch
        values = []
        for i in range(batch):
            node = source[first + i]
            choice = row_of(turns, node, sub)[...]
            moved = row_of(flow, node, sub)[...]
            values.append(jnp.where(choice == outlet[first + i], moved, 0.0))
        for i in range(batch):
            row_of(home, first + i, sub)[...] = values[i]
        return carry

    lax.fori_loop(0, cells // batch, body, 0)


def base_kernel(sizes, keep, home_theta, rows, home, base):
    cells, nodes, branches, cap, sub = sizes
    batch = 8

    def body(step, carry):
        first = step * batch
        values = []
        for i in range(batch):
            cell = first + i
            kept = row_of(rows, cell, sub)[...] * keep[cell]
            values.append(kept + row_of(home, cell, sub)[...] * home_theta[cell])
        for i in range(batch):
            row_of(base, first + i, sub)[...] = values[i]
        return carry

    lax.fori_loop(0, cells // batch, body, 0)


def land_rows(sizes, sides, scale, land, received, base):
    cells, nodes, branches, cap, sub = sizes
    batch = 8
    for side, rows in zip(sides, received):

        def body(step, carry, side=side, rows=rows):
            first = step * batch
            stores = []
            for i in range(batch):
                slot = side * padded(cap) + first + i
                at = row_of(base, land[slot], sub)
                value = row_of(rows, first + i, sub)[...]
                if scale is not None:
                    value = value * scale[slot]
                stores.append((at, at[...] + value))
            for at, value in stores:
                at[...] = value
            return carry

        lax.fori_loop(0, cap // batch, body, 0)


def land_kernel(sizes, sides, scale, land, *rest):
    received, (base_in, base) = rest[: len(sides)], rest[len(sides) :]
    land_rows(sizes, sides, scale, land, received, base)


def finish_kernel(sizes, sides, chunk, land, *rest):
    cells, nodes, branches, cap, sub = sizes
    received, (base_in, out, base, staged, sems) = rest[: len(sides)], rest[len(sides) :]
    land_rows(sizes, sides, None, land, received, base)
    copies = []
    for number in range(cells // chunk):

        def body(step, carry, number=number):
            for half in range(2):
                first = number * chunk + step * 16 + half * 8
                for q in range(sub):
                    staged[
                        pl.ds(pl.multiple_of(first, 8), 8), q * LANES : (q + 1) * LANES
                    ] = base[pl.ds(first * sub + q, 8, stride=sub), :]
            return carry

        lax.fori_loop(0, chunk // 16, body, 0)
        at = pl.ds(number * chunk, chunk)
        copies.append(
            pltpu.make_async_copy(staged.at[at, :], out.at[at, :], sems.at[number])
        )
        copies[-1].start()
    for copy in copies:
        copy.wait()


def on_device(occupancy, capacity, jam, wave, node_in, node_out, send_list, recv_list, turn):
    cells, width = occupancy.shape
    branches, nodes = node_in.shape
    cap = send_list.shape[1]
    sub = width // LANES
    sizes = (cells, nodes, branches, cap, sub)
    regions = lax.axis_size("region")
    commodities = width * lax.axis_size("dest")
    height = cells // LANES
    per_cell = (height, LANES)
    list_shape = (4 * padded(cap) // LANES, LANES)
    chunk = 128
    some_node = node_in[0, 0] >= 0

    def apart(exchange, block):
        shape = jax.eval_shape(exchange, block)
        return lax.cond(some_node, exchange, lambda x: jnp.zeros(shape.shape, F32), block)

    row_bytes = width * 4
    occupancy = pltpu.with_memory_space_constraint(occupancy, pltpu.HBM)
    turn = pltpu.with_memory_space_constraint(turn, pltpu.HBM)

    local_sum, rows, *lists = pl.pallas_call(
        functools.partial(cell_sum_kernel, sizes, chunk),
        in_specs=[ANYWHERE] + [VMEM_WHOLE] * 4,
        out_specs=[VMEM_WHOLE] * 8,
        out_shape=[
            jax.ShapeDtypeStruct(per_cell, F32),
            pltpu.VMEM(((cells + 1) * sub, LANES), F32),
            jax.ShapeDtypeStruct((branches * nodes // LANES, LANES), I32),
        ]
        + [jax.ShapeDtypeStruct(list_shape, I32)] * 3
        + [jax.ShapeDtypeStruct(per_cell, I32)] * 2,
        scratch_shapes=[
            pltpu.VMEM((cells, width), F32),
            pltpu.VMEM((cells, LANES), F32),
            pltpu.SemaphoreType.DMA((cells // chunk,)),
        ],
        compiler_params=params(14),
        cost_estimate=cost(cells * width, cells * row_bytes),
        name="cell_sum",
    )(occupancy, node_in, node_out, send_list, recv_list)
    in_cell, send_node, send_outlet, land, source_node, source_outlet = (
        x.reshape(-1) for x in lists
    )

    sums = partners(local_sum, "dest")

    turns = pl.pallas_call(
        functools.partial(turn_rows_kernel, chunk, sub),
        in_specs=[ANYWHERE] * 2,
        out_specs=VMEM_WHOLE,
        out_shape=pltpu.VMEM((nodes * sub, LANES), I32),
        scratch_shapes=[
            pltpu.VMEM((nodes, width), I32),
            pltpu.SemaphoreType.DMA((nodes // chunk,)),
        ],
        compiler_params=params(8),
        cost_estimate=cost(0, nodes * row_bytes),
        name="turn_rows",
    )(turn, local_sum)

    turns, *sums = lax.optimization_barrier((turns, *sums))
    vehicles = tree_sum(sums) / commodities
    cap_of = capacity.reshape(per_cell)
    fraction = jnp.minimum(vehicles, cap_of) / vehicles
    supply = jnp.minimum(cap_of, wave.reshape(per_cell) * (jam.reshape(per_cell) - vehicles))
    rows_shape = pltpu.VMEM(((cells + 1) * sub, LANES), F32)
    send_shape = pltpu.VMEM((cap * sub, LANES), F32)

    supply_there = to_neighbours(supply)
    scaled = pl.pallas_call(
        functools.partial(scale_kernel, sizes),
        in_specs=[SMEM_WHOLE, VMEM_WHOLE],
        out_specs=VMEM_WHOLE,
        out_shape=rows_shape,
        compiler_params=params(4),
        cost_estimate=cost(1, 1),
        name="scale_rows",
    )(fraction.reshape(-1), rows)
    early = pl.pallas_call(
        functools.partial(send_kernel, sizes, (0, 1, 2)),
        in_specs=[SMEM_WHOLE] * 3 + [VMEM_WHOLE] * 2 + [ANYWHERE],
        out_specs=[VMEM_WHOLE] * 3,
        out_shape=[send_shape] * 3,
        compiler_params=params(4),
        cost_estimate=cost(1, 1),
        name="send_rows",
    )(in_cell, send_node, send_outlet, scaled, turns, supply_there)
    arrived = [
        shifted(send, "region", SHIFTS[side]) for side, send in enumerate(early)
    ]


    flow, demand = pl.pallas_call(
        functools.partial(node_flow_kernel, sizes),
        in_specs=[SMEM_WHOLE] + [VMEM_WHOLE] * 2 + [ANYWHERE],
        out_specs=[VMEM_WHOLE] * 2,
        out_shape=[
            pltpu.VMEM((nodes * sub, LANES), F32),
            jax.ShapeDtypeStruct((branches * nodes // LANES, LANES), F32),
        ],
        scratch_shapes=[pltpu.VMEM((branches, nodes, LANES), F32)],
        compiler_params=params(8),
        cost_estimate=cost(1, 1),
        name="node_flow",
    )(in_cell, scaled, turns, early[0])

    shared = apart(
        lambda x: lax.all_gather(x, "dest", axis=0, tiled=True),
        jnp.concatenate([demand, supply_there]),
    )
    home = pl.pallas_call(
        functools.partial(home_kernel, sizes),
        in_specs=[SMEM_WHOLE] * 2 + [VMEM_WHOLE] * 2,
        out_specs=VMEM_WHOLE,
        out_shape=rows_shape,
        compiler_params=params(4),
        cost_estimate=cost(1, 1),
        name="home_rows",
    )(source_node, source_outlet, turns, flow)
    keep, home_theta, theta, slot_theta = pl.pallas_call(
        functools.partial(theta_kernel, sizes, regions, commodities),
        in_specs=[VMEM_WHOLE] * 6,
        out_specs=[VMEM_WHOLE] * 4,
        out_shape=[jax.ShapeDtypeStruct(per_cell, F32)] * 2
        + [
            jax.ShapeDtypeStruct((nodes // LANES, LANES), F32),
            jax.ShapeDtypeStruct((padded(cap) // LANES, LANES), F32),
        ],
        compiler_params=params(8),
        cost_estimate=cost(1, 1),
        name="theta",
    )(supply, shared, node_in, node_out, send_list, fraction)
    theta_there = apart(to_neighbours, slot_theta)

    (behind,) = pl.pallas_call(
        functools.partial(scaled_send_kernel, sizes, 3),
        in_specs=[SMEM_WHOLE] * 3 + [VMEM_WHOLE] * 2,
        out_specs=[VMEM_WHOLE],
        out_shape=[send_shape],
        compiler_params=params(4),
        cost_estimate=cost(1, 1),
        name="send_scaled",
    )(theta.reshape(-1), send_node, send_outlet, flow, turns)
    behind, theta_there, *arrived = lax.optimization_barrier((behind, theta_there, *arrived))
    last = shifted(behind, "region", SHIFTS[3])
    scale = lax.all_gather(theta_there, "dest", axis=0, tiled=True)[: list_shape[0]]

    base = pl.pallas_call(
        functools.partial(base_kernel, sizes),
        in_specs=[SMEM_WHOLE] * 2 + [VMEM_WHOLE] * 2,
        out_specs=VMEM_WHOLE,
        out_shape=rows_shape,
        compiler_params=params(4),
        cost_estimate=cost(1, 1),
        name="base_rows",
    )(keep.reshape(-1), home_theta.reshape(-1), rows, home)

    base = pl.pallas_call(
        functools.partial(land_kernel, sizes, (0, 1, 2)),
        in_specs=[SMEM_WHOLE] * 2 + [VMEM_WHOLE] * 4,
        out_specs=VMEM_WHOLE,
        out_shape=rows_shape,
        input_output_aliases={5: 0},
        compiler_params=params(4),
        cost_estimate=cost(1, 1),
        name="land_first",
    )(scale.reshape(-1), land, *arrived, base)

    out, _ = pl.pallas_call(
        functools.partial(finish_kernel, sizes, (3,), chunk),
        in_specs=[SMEM_WHOLE] + [VMEM_WHOLE] * 2,
        out_specs=[ANYWHERE, VMEM_WHOLE],
        out_shape=[jax.ShapeDtypeStruct((cells, width), F32), rows_shape],
        scratch_shapes=[
            pltpu.VMEM((cells, width), F32),
            pltpu.SemaphoreType.DMA((cells // chunk,)),
        ],
        input_output_aliases={2: 1},
        compiler_params=params(12),
        cost_estimate=cost(cells * width, cells * row_bytes),
        name="finish",
    )(land, last, base)
    return out


def solution(mesh):
    return jax.shard_map(
        on_device,
        mesh=mesh,
        in_specs=(
            P("region", "dest"),
            P("region"),
            P("region"),
            P("region"),
            P(None, "region"),
            P(None, "region"),
            P("region", None),
            P("region", None),
            P("region", "dest"),
        ),
        out_specs=P("region", "dest"),
        check_vma=False,
    )
```

```python
import functools

import jax
import jax.numpy as jnp
from jax import lax
from jax.experimental import pallas as pl
from jax.experimental.pallas import tpu as pltpu
from jax.sharding import PartitionSpec as P

SHIFTS = (1, -1, 2, -2)
EXACT = lax.Precision.HIGHEST
LANES = 128
MIB = 1 << 20
F32 = jnp.float32
I32 = jnp.int32
VMEM_WHOLE = pl.BlockSpec(memory_space=pltpu.VMEM)
SMEM_WHOLE = pl.BlockSpec(memory_space=pltpu.SMEM)
ANYWHERE = pl.BlockSpec(memory_space=pl.ANY)


def to_neighbours(block):
    regions, members = lax.axis_size("region"), lax.axis_size("dest")
    route = [
        (r * members + d, (r + SHIFTS[d % 4]) % regions * members + d)
        for r in range(regions)
        for d in range(members)
    ]
    return lax.ppermute(block, ("region", "dest"), route)


def shifted(block, axis, distance):
    devices = range(lax.axis_size(axis))
    route = [((i - distance) % len(devices), i) for i in devices]
    return lax.ppermute(block, axis, route)


def partners(block, axis):
    count = lax.axis_size(axis)
    return [block] + [
        lax.ppermute(block, axis, [(i, i ^ other) for i in range(count)])
        for other in range(1, count)
    ]


def tree_sum(parts):
    while len(parts) > 1:
        parts = [parts[k] + parts[k + 1] for k in range(0, len(parts), 2)]
    return parts[0]


def params(mib):
    return pltpu.CompilerParams(vmem_limit_bytes=mib * MIB)


def cost(flops, moved):
    return pl.CostEstimate(flops=flops, bytes_accessed=moved, transcendentals=0)


def lane_sums(partial):
    sums = jnp.dot(
        partial, jnp.ones((LANES, LANES), F32), preferred_element_type=F32, precision=EXACT
    )
    row = lax.broadcasted_iota(I32, (LANES, LANES), 0)
    lane = lax.broadcasted_iota(I32, (LANES, LANES), 1)
    pieces = [
        jnp.sum(jnp.where(row == lane, sums[k : k + LANES, :], 0.0), axis=0, keepdims=True)
        for k in range(0, partial.shape[0], LANES)
    ]
    return jnp.concatenate(pieces, axis=0)


def stacked(row):
    return jnp.concatenate(
        [row[:, k : k + LANES] for k in range(0, row.shape[1], LANES)], axis=0
    )


def strung(rows):
    return jnp.concatenate([rows[k : k + 1, :] for k in range(rows.shape[0])], axis=1)


def row_of(ref, number, sub):
    if sub % 8 == 0:
        return ref.reshape(ref.shape[0] // sub, sub, LANES).at[number]
    return ref.at[pl.ds(pl.multiple_of(number * sub, sub), sub), :]


def padded(cap):
    return -(-cap // LANES) * LANES


def put_row(ref, row, value, fill):
    width = value.shape[1]
    for q in range(-(-width // LANES)):
        piece = value[:, q * LANES : min((q + 1) * LANES, width)]
        lack = LANES - piece.shape[1]
        if lack:
            piece = jnp.concatenate([piece, jnp.full((1, lack), fill, piece.dtype)], axis=1)
        ref[row + q : row + q + 1, :] = piece


def one_hot(index, count):
    rows = lax.broadcasted_iota(I32, (count, index.shape[1]), 0)
    return jnp.where(rows == index, 1.0, 0.0)


def look_up(table, index):
    picked = lax.dot_general(
        table.T,
        one_hot(index // LANES, table.shape[0]),
        (((1,), (0,)), ((), ())),
        preferred_element_type=F32,
        precision=EXACT,
    )
    return jnp.sum(picked * one_hot(index % LANES, LANES), axis=0, keepdims=True)


def scatter(index, values, height):
    high = jnp.where(index >= 0, index // LANES, -1)
    return lax.dot_general(
        one_hot(high, height) * values,
        one_hot(jnp.where(index >= 0, index % LANES, -1), LANES),
        (((1,), (1,)), ((), ())),
        preferred_element_type=F32,
        precision=EXACT,
    )


def home_cells(node_out, region_no, cells):
    here = (node_out >= 0) & (node_out // cells == region_no)
    return jnp.where(here, node_out % cells, -1)


def rows_of_group(x_ref, rows_ref, first, sub):
    total = None
    for q in range(sub):
        piece = x_ref[pl.ds(pl.multiple_of(first, 8), 8), q * LANES : (q + 1) * LANES]
        rows_ref[pl.ds(first * sub + q, 8, stride=sub), :] = piece
        total = piece if total is None else total + piece
    return total


def copies_in(source, target, sems, chunk):
    copies = [
        pltpu.make_async_copy(
            source.at[pl.ds(i * chunk, chunk), :], target.at[pl.ds(i * chunk, chunk), :], sems.at[i]
        )
        for i in range(target.shape[0] // chunk)
    ]
    for copy in copies:
        copy.start()
    return copies


def make_lists(
    sizes, node_in, node_out, send_list, recv_list,
    in_cell, send_node, send_outlet, land, source_node, source_outlet,
):
    cells, nodes, branches, cap, sub = sizes
    height = cells // LANES
    region_no = lax.axis_index("region")
    ids = lax.broadcasted_iota(I32, (1, nodes), 1).astype(F32) + 1.0
    number = jnp.zeros((height, LANES), F32)
    slot = jnp.zeros((height, LANES), F32)
    for j in range(branches):
        ins = node_in[j : j + 1, :]
        put_row(in_cell, j * (nodes // LANES), jnp.where(ins >= 0, ins, cells), cells)
        home = home_cells(node_out[j : j + 1, :], region_no, cells)
        here = scatter(home, ids, height)
        number = number + here
        slot = slot + jnp.where(here > 0.0, j + 1.0, 0.0)
    source_node[...] = jnp.maximum(number.astype(I32) - 1, 0)
    source_outlet[...] = slot.astype(I32) - 1
    per_side = padded(cap) // LANES
    for side in range(4):
        slots = send_list[side : side + 1, :]
        lands = recv_list[side : side + 1, :]
        put_row(send_node, side * per_side, jnp.where(slots >= 0, slots % nodes, 0), 0)
        put_row(send_outlet, side * per_side, jnp.where(slots >= 0, slots // nodes, -1), -1)
        put_row(land, side * per_side, jnp.where(lands >= 0, lands, cells), cells)


def cell_sum_kernel(sizes, chunk, x_hbm, *rest):
    cells, nodes, branches, cap, sub = sizes
    lists, (sum_ref, rows_ref), made, held, (recv, x, partial, sems, list_sems) = (
        rest[:4], rest[4:6], rest[6:12], rest[12:15], rest[15:]
    )
    held = (*held, recv)
    list_copies = [
        pltpu.make_async_copy(source, target, list_sems.at[k])
        for k, (source, target) in enumerate(zip(lists, held))
    ]
    for copy in list_copies:
        copy.start()
    copies = copies_in(x_hbm, x, sems, chunk)
    for copy in list_copies:
        copy.wait()
    make_lists(sizes, *held, *made)
    zeros = rows_ref.shape[0] - sub
    rows_ref[zeros:, :] = jnp.zeros((sub, LANES), F32)
    for number, copy in enumerate(copies):
        copy.wait()

        def body(step, carry, number=number):
            for half in range(2):
                first = number * chunk + step * 16 + half * 8
                total = rows_of_group(x, rows_ref, first, sub)
                partial[pl.ds(pl.multiple_of(first, 8), 8), :] = total
            return carry

        lax.fori_loop(0, chunk // 16, body, 0)
    sum_ref[...] = lane_sums(partial[...])


def turn_rows_kernel(chunk, sub, x_hbm, after_ref, rows_ref, x, sems):
    for number, copy in enumerate(copies_in(x_hbm, x, sems, chunk)):
        copy.wait()

        def body(step, carry, number=number):
            for half in range(2):
                rows_of_group(x, rows_ref, number * chunk + step * 16 + half * 8, sub)
            return carry

        lax.fori_loop(0, chunk // 16, body, 0)


def gathered_flow(node, in_cell, scaled, sizes):
    cells, nodes, branches, cap, sub = sizes
    return tree_sum(
        [row_of(scaled, in_cell[i * nodes + node], sub)[...] for i in range(branches)]
    )


def scale_kernel(sizes, fraction, rows, scaled):
    cells, nodes, branches, cap, sub = sizes

    def body(step, carry):
        first = step * 16
        values = [
            row_of(rows, first + i, sub)[...] * fraction[first + i] for i in range(16)
        ]
        for i in range(16):
            row_of(scaled, first + i, sub)[...] = values[i]
        return carry

    lax.fori_loop(0, cells // 16, body, 0)
    row_of(scaled, cells, sub)[...] = jnp.zeros((sub, LANES), F32)


def send_kernel(sizes, sides, in_cell, send_node, send_outlet, scaled, turns, *rest):
    cells, nodes, branches, cap, sub = sizes
    sends = rest[1:]
    batch = 8
    for side, send in zip(sides, sends):

        def body(step, carry, side=side, send=send):
            first = step * batch
            values = []
            for i in range(batch):
                slot = side * padded(cap) + first + i
                node = send_node[slot]
                value = gathered_flow(node, in_cell, scaled, sizes)
                choice = row_of(turns, node, sub)[...]
                values.append(jnp.where(choice == send_outlet[slot], value, 0.0))
            for i in range(batch):
                row_of(send, first + i, sub)[...] = values[i]
            return carry

        lax.fori_loop(0, cap // batch, body, 0)


def scaled_send_kernel(sizes, side, theta, send_node, send_outlet, flow, turns, send):
    cells, nodes, branches, cap, sub = sizes
    batch = 8

    def body(step, carry):
        first = step * batch
        values = []
        for i in range(batch):
            slot = side * padded(cap) + first + i
            node = send_node[slot]
            value = row_of(flow, node, sub)[...] * theta[node]
            choice = row_of(turns, node, sub)[...]
            values.append(jnp.where(choice == send_outlet[slot], value, 0.0))
        for i in range(batch):
            row_of(send, first + i, sub)[...] = values[i]
        return carry

    lax.fori_loop(0, cap // batch, body, 0)


def node_flow_kernel(sizes, in_cell, scaled, turns, after_ref, flow, demand, partial):
    cells, nodes, branches, cap, sub = sizes

    def gather(step, carry):
        first = step * 8
        values = [
            gathered_flow(first + i, in_cell, scaled, sizes) for i in range(8)
        ]
        for i in range(8):
            row_of(flow, first + i, sub)[...] = values[i]
        return carry

    def measure(step, carry):
        for half in range(2):
            first = step * 16 + half * 8
            totals = [jnp.zeros((8, LANES), F32)] * branches
            for q in range(sub):
                at = pl.ds(first * sub + q, 8, stride=sub)
                value = flow[at, :]
                choice = turns[at, :]
                totals = [
                    total + jnp.where(choice == j, value, 0.0) for j, total in enumerate(totals)
                ]
            for j in range(branches):
                partial[j, pl.ds(pl.multiple_of(first, 8), 8), :] = totals[j]
        return carry

    lax.fori_loop(0, nodes // 8, gather, 0)
    lax.fori_loop(0, nodes // 16, measure, 0)
    per_outlet = nodes // LANES
    for j in range(branches):
        demand[j * per_outlet : (j + 1) * per_outlet, :] = lane_sums(partial[j])


def theta_kernel(
    sizes, regions, commodities, supply, shared, node_in, node_out, send_list, fraction,
    after_ref, keep, home_theta, theta_out, slot_theta,
):
    cells, nodes, branches, cap, sub = sizes
    height = cells // LANES
    per_outlet = nodes // LANES
    block = branches * per_outlet + height
    region_no = lax.axis_index("region")
    members = shared.shape[0] // block
    parts = [
        shared[d * block : d * block + branches * per_outlet, :] for d in range(members)
    ]
    demand = tree_sum(parts) * (1.0 / commodities)
    table = jnp.concatenate(
        [supply[...]]
        + [
            shared[d * block + branches * per_outlet : (d + 1) * block, :] for d in range(4)
        ],
        axis=0,
    )
    tall = jnp.ones((per_outlet, LANES), F32)
    for j in range(branches):
        outs = node_out[j : j + 1, :]
        cell = jnp.maximum(outs, 0)
        offset = (cell // cells + regions - region_no) % regions
        sector = jnp.zeros_like(offset)
        for d in range(4):
            sector = jnp.where(offset == (-SHIFTS[d]) % regions, d + 1, sector)
        room = stacked(look_up(table, sector * cells + cell % cells))
        ratio = room / jnp.maximum(demand[j * per_outlet : (j + 1) * per_outlet, :], room)
        tall = jnp.minimum(tall, jnp.where(stacked(outs) >= 0, ratio, 1.0))
    theta_out[...] = tall
    theta = strung(tall)
    cell_theta = jnp.zeros((height, LANES), F32)
    into = jnp.zeros((height, LANES), F32)
    for j in range(branches):
        home = home_cells(node_out[j : j + 1, :], region_no, cells)
        cell_theta = cell_theta + scatter(node_in[j : j + 1, :], theta, height)
        into = into + scatter(home, theta, height)
    keep[...] = 1.0 - cell_theta * fraction[...]
    home_theta[...] = into
    slots = send_list[pl.ds(lax.axis_index("dest") % 4, 1), :]
    put_row(slot_theta, 0, look_up(tall, jnp.where(slots >= 0, slots % nodes, 0)), 0.0)


def home_kernel(sizes, source, outlet, turns, flow, home):
    cells, nodes, branches, cap, sub = sizes
    batch = 8

    def body(step, carry):
        first = step * batch
        values = []
        for i in range(batch):
            node = source[first + i]
            choice = row_of(turns, node, sub)[...]
            moved = row_of(flow, node, sub)[...]
            values.append(jnp.where(choice == outlet[first + i], moved, 0.0))
        for i in range(batch):
            row_of(home, first + i, sub)[...] = values[i]
        return carry

    lax.fori_loop(0, cells // batch, body, 0)


def base_kernel(sizes, keep, home_theta, rows, home, base):
    cells, nodes, branches, cap, sub = sizes
    batch = 8

    def body(step, carry):
        first = step * batch
        values = []
        for i in range(batch):
            cell = first + i
            kept = row_of(rows, cell, sub)[...] * keep[cell]
            values.append(kept + row_of(home, cell, sub)[...] * home_theta[cell])
        for i in range(batch):
            row_of(base, first + i, sub)[...] = values[i]
        return carry

    lax.fori_loop(0, cells // batch, body, 0)


def land_rows(sizes, sides, scale, land, received, base):
    cells, nodes, branches, cap, sub = sizes
    batch = 8
    for side, rows in zip(sides, received):

        def body(step, carry, side=side, rows=rows):
            first = step * batch
            stores = []
            for i in range(batch):
                slot = side * padded(cap) + first + i
                at = row_of(base, land[slot], sub)
                value = row_of(rows, first + i, sub)[...]
                if scale is not None:
                    value = value * scale[slot]
                stores.append((at, at[...] + value))
            for at, value in stores:
                at[...] = value
            return carry

        lax.fori_loop(0, cap // batch, body, 0)


def land_kernel(sizes, sides, scale, land, *rest):
    received, (base_in, base) = rest[: len(sides)], rest[len(sides) :]
    land_rows(sizes, sides, scale, land, received, base)


def finish_kernel(sizes, sides, chunk, land, *rest):
    cells, nodes, branches, cap, sub = sizes
    received, (base_in, out, base, staged, sems) = rest[: len(sides)], rest[len(sides) :]
    land_rows(sizes, sides, None, land, received, base)
    copies = []
    for number in range(cells // chunk):

        def body(step, carry, number=number):
            for half in range(2):
                first = number * chunk + step * 16 + half * 8
                for q in range(sub):
                    staged[
                        pl.ds(pl.multiple_of(first, 8), 8), q * LANES : (q + 1) * LANES
                    ] = base[pl.ds(first * sub + q, 8, stride=sub), :]
            return carry

        lax.fori_loop(0, chunk // 16, body, 0)
        at = pl.ds(number * chunk, chunk)
        copies.append(
            pltpu.make_async_copy(staged.at[at, :], out.at[at, :], sems.at[number])
        )
        copies[-1].start()
    for copy in copies:
        copy.wait()


def on_device(occupancy, capacity, jam, wave, node_in, node_out, send_list, recv_list, turn):
    cells, width = occupancy.shape
    branches, nodes = node_in.shape
    cap = send_list.shape[1]
    sub = width // LANES
    sizes = (cells, nodes, branches, cap, sub)
    regions = lax.axis_size("region")
    commodities = width * lax.axis_size("dest")
    height = cells // LANES
    per_cell = (height, LANES)
    list_shape = (4 * padded(cap) // LANES, LANES)
    chunk = 128
    row_bytes = width * 4
    occupancy = pltpu.with_memory_space_constraint(occupancy, pltpu.HBM)
    turn = pltpu.with_memory_space_constraint(turn, pltpu.HBM)
    node_in, node_out, send_list, recv_list = (
        pltpu.with_memory_space_constraint(x, pltpu.HBM)
        for x in (node_in, node_out, send_list, recv_list)
    )

    local_sum, rows, *lists = pl.pallas_call(
        functools.partial(cell_sum_kernel, sizes, chunk),
        in_specs=[ANYWHERE] * 5,
        out_specs=[VMEM_WHOLE] * 11,
        out_shape=[
            jax.ShapeDtypeStruct(per_cell, F32),
            pltpu.VMEM(((cells + 1) * sub, LANES), F32),
            jax.ShapeDtypeStruct((branches * nodes // LANES, LANES), I32),
        ]
        + [jax.ShapeDtypeStruct(list_shape, I32)] * 3
        + [jax.ShapeDtypeStruct(per_cell, I32)] * 2
        + [pltpu.VMEM(x.shape, I32) for x in (node_in, node_out, send_list)],
        scratch_shapes=[
            pltpu.VMEM(recv_list.shape, I32),
            pltpu.VMEM((cells, width), F32),
            pltpu.VMEM((cells, LANES), F32),
            pltpu.SemaphoreType.DMA((cells // chunk,)),
            pltpu.SemaphoreType.DMA((4,)),
        ],
        compiler_params=params(14),
        cost_estimate=cost(cells * width, cells * row_bytes),
        name="cell_sum",
    )(occupancy, node_in, node_out, send_list, recv_list)
    node_in, node_out, send_list = lists[6:]
    in_cell, send_node, send_outlet, land, source_node, source_outlet = (
        x.reshape(-1) for x in lists[:6]
    )

    sums = partners(local_sum, "dest")

    turns = pl.pallas_call(
        functools.partial(turn_rows_kernel, chunk, sub),
        in_specs=[ANYWHERE] * 2,
        out_specs=VMEM_WHOLE,
        out_shape=pltpu.VMEM((nodes * sub, LANES), I32),
        scratch_shapes=[
            pltpu.VMEM((nodes, width), I32),
            pltpu.SemaphoreType.DMA((nodes // chunk,)),
        ],
        compiler_params=params(8),
        cost_estimate=cost(0, nodes * row_bytes),
        name="turn_rows",
    )(turn, local_sum)

    turns, *sums = lax.optimization_barrier((turns, *sums))
    vehicles = tree_sum(sums) / commodities
    cap_of = capacity.reshape(per_cell)
    fraction = jnp.minimum(vehicles, cap_of) / vehicles
    supply = jnp.minimum(cap_of, wave.reshape(per_cell) * (jam.reshape(per_cell) - vehicles))
    rows_shape = pltpu.VMEM(((cells + 1) * sub, LANES), F32)
    send_shape = pltpu.VMEM((cap * sub, LANES), F32)

    supply_there = to_neighbours(supply)
    scaled = pl.pallas_call(
        functools.partial(scale_kernel, sizes),
        in_specs=[SMEM_WHOLE, VMEM_WHOLE],
        out_specs=VMEM_WHOLE,
        out_shape=rows_shape,
        compiler_params=params(4),
        cost_estimate=cost(1, 1),
        name="scale_rows",
    )(fraction.reshape(-1), rows)
    early = pl.pallas_call(
        functools.partial(send_kernel, sizes, (0, 1, 2)),
        in_specs=[SMEM_WHOLE] * 3 + [VMEM_WHOLE] * 2 + [ANYWHERE],
        out_specs=[VMEM_WHOLE] * 3,
        out_shape=[send_shape] * 3,
        compiler_params=params(4),
        cost_estimate=cost(1, 1),
        name="send_rows",
    )(in_cell, send_node, send_outlet, scaled, turns, supply_there)
    arrived = [
        shifted(send, "region", SHIFTS[side]) for side, send in enumerate(early)
    ]


    flow, demand = pl.pallas_call(
        functools.partial(node_flow_kernel, sizes),
        in_specs=[SMEM_WHOLE] + [VMEM_WHOLE] * 2 + [ANYWHERE],
        out_specs=[VMEM_WHOLE] * 2,
        out_shape=[
            pltpu.VMEM((nodes * sub, LANES), F32),
            jax.ShapeDtypeStruct((branches * nodes // LANES, LANES), F32),
        ],
        scratch_shapes=[pltpu.VMEM((branches, nodes, LANES), F32)],
        compiler_params=params(8),
        cost_estimate=cost(1, 1),
        name="node_flow",
    )(in_cell, scaled, turns, early[0])

    shared = lax.all_gather(
        jnp.concatenate([demand, supply_there]), "dest", axis=0, tiled=True
    )
    home = pl.pallas_call(
        functools.partial(home_kernel, sizes),
        in_specs=[SMEM_WHOLE] * 2 + [VMEM_WHOLE] * 2,
        out_specs=VMEM_WHOLE,
        out_shape=rows_shape,
        compiler_params=params(4),
        cost_estimate=cost(1, 1),
        name="home_rows",
    )(source_node, source_outlet, turns, flow)
    keep, home_theta, theta, slot_theta = pl.pallas_call(
        functools.partial(theta_kernel, sizes, regions, commodities),
        in_specs=[VMEM_WHOLE] * 6 + [ANYWHERE],
        out_specs=[VMEM_WHOLE] * 4,
        out_shape=[jax.ShapeDtypeStruct(per_cell, F32)] * 2
        + [
            jax.ShapeDtypeStruct((nodes // LANES, LANES), F32),
            jax.ShapeDtypeStruct((padded(cap) // LANES, LANES), F32),
        ],
        compiler_params=params(8),
        cost_estimate=cost(1, 1),
        name="theta",
    )(supply, shared, node_in, node_out, send_list, fraction, home)
    theta_there = to_neighbours(slot_theta)

    (behind,) = pl.pallas_call(
        functools.partial(scaled_send_kernel, sizes, 3),
        in_specs=[SMEM_WHOLE] * 3 + [VMEM_WHOLE] * 2,
        out_specs=[VMEM_WHOLE],
        out_shape=[send_shape],
        compiler_params=params(4),
        cost_estimate=cost(1, 1),
        name="send_scaled",
    )(theta.reshape(-1), send_node, send_outlet, flow, turns)
    behind, theta_there, *arrived = lax.optimization_barrier((behind, theta_there, *arrived))
    last = shifted(behind, "region", SHIFTS[3])
    scale = lax.all_gather(theta_there, "dest", axis=0, tiled=True)[: list_shape[0]]

    base = pl.pallas_call(
        functools.partial(base_kernel, sizes),
        in_specs=[SMEM_WHOLE] * 2 + [VMEM_WHOLE] * 2,
        out_specs=VMEM_WHOLE,
        out_shape=rows_shape,
        compiler_params=params(4),
        cost_estimate=cost(1, 1),
        name="base_rows",
    )(keep.reshape(-1), home_theta.reshape(-1), rows, home)

    base = pl.pallas_call(
        functools.partial(land_kernel, sizes, (0, 1, 2)),
        in_specs=[SMEM_WHOLE] * 2 + [VMEM_WHOLE] * 4,
        out_specs=VMEM_WHOLE,
        out_shape=rows_shape,
        input_output_aliases={5: 0},
        compiler_params=params(4),
        cost_estimate=cost(1, 1),
        name="land_first",
    )(scale.reshape(-1), land, *arrived, base)

    out, _ = pl.pallas_call(
        functools.partial(finish_kernel, sizes, (3,), chunk),
        in_specs=[SMEM_WHOLE] + [VMEM_WHOLE] * 2,
        out_specs=[ANYWHERE, VMEM_WHOLE],
        out_shape=[jax.ShapeDtypeStruct((cells, width), F32), rows_shape],
        scratch_shapes=[
            pltpu.VMEM((cells, width), F32),
            pltpu.SemaphoreType.DMA((cells // chunk,)),
        ],
        input_output_aliases={2: 1},
        compiler_params=params(12),
        cost_estimate=cost(cells * width, cells * row_bytes),
        name="finish",
    )(land, last, base)
    return out


def solution(mesh):
    return jax.shard_map(
        on_device,
        mesh=mesh,
        in_specs=(
            P("region", "dest"),
            P("region"),
            P("region"),
            P("region"),
            P(None, "region"),
            P(None, "region"),
            P("region", None),
            P("region", None),
            P("region", "dest"),
        ),
        out_specs=P("region", "dest"),
        check_vma=False,
    )
```

```python
import functools

import jax
import jax.numpy as jnp
from jax import lax
from jax.experimental import pallas as pl
from jax.experimental.pallas import tpu as pltpu
from jax.sharding import PartitionSpec as P

SHIFTS = (1, -1, 2, -2)
EXACT = lax.Precision.HIGHEST
LANES = 128
MIB = 1 << 20
F32 = jnp.float32
I32 = jnp.int32
VMEM_WHOLE = pl.BlockSpec(memory_space=pltpu.VMEM)
SMEM_WHOLE = pl.BlockSpec(memory_space=pltpu.SMEM)
ANYWHERE = pl.BlockSpec(memory_space=pl.ANY)


def to_neighbours(block):
    regions, members = lax.axis_size("region"), lax.axis_size("dest")
    route = [
        (r * members + d, (r + SHIFTS[d % 4]) % regions * members + d)
        for r in range(regions)
        for d in range(members)
    ]
    return lax.ppermute(block, ("region", "dest"), route)


def shifted(block, axis, distance):
    devices = range(lax.axis_size(axis))
    route = [((i - distance) % len(devices), i) for i in devices]
    return lax.ppermute(block, axis, route)


def partners(block, axis):
    count = lax.axis_size(axis)
    return [block] + [
        lax.ppermute(block, axis, [(i, i ^ other) for i in range(count)])
        for other in range(1, count)
    ]


def tree_sum(parts):
    while len(parts) > 1:
        parts = [parts[k] + parts[k + 1] for k in range(0, len(parts), 2)]
    return parts[0]


def params(mib):
    return pltpu.CompilerParams(vmem_limit_bytes=mib * MIB)


def cost(flops, moved):
    return pl.CostEstimate(flops=flops, bytes_accessed=moved, transcendentals=0)


def lane_sums(partial):
    sums = jnp.dot(
        partial, jnp.ones((LANES, LANES), F32), preferred_element_type=F32, precision=EXACT
    )
    row = lax.broadcasted_iota(I32, (LANES, LANES), 0)
    lane = lax.broadcasted_iota(I32, (LANES, LANES), 1)
    pieces = [
        jnp.sum(jnp.where(row == lane, sums[k : k + LANES, :], 0.0), axis=0, keepdims=True)
        for k in range(0, partial.shape[0], LANES)
    ]
    return jnp.concatenate(pieces, axis=0)


def stacked(row):
    return jnp.concatenate(
        [row[:, k : k + LANES] for k in range(0, row.shape[1], LANES)], axis=0
    )


def strung(rows):
    return jnp.concatenate([rows[k : k + 1, :] for k in range(rows.shape[0])], axis=1)


def row_of(ref, number, sub):
    if sub % 8 == 0:
        return ref.reshape(ref.shape[0] // sub, sub, LANES).at[number]
    return ref.at[pl.ds(pl.multiple_of(number * sub, sub), sub), :]


def padded(cap):
    return -(-cap // LANES) * LANES


def put_row(ref, row, value, fill):
    width = value.shape[1]
    for q in range(-(-width // LANES)):
        piece = value[:, q * LANES : min((q + 1) * LANES, width)]
        lack = LANES - piece.shape[1]
        if lack:
            piece = jnp.concatenate([piece, jnp.full((1, lack), fill, piece.dtype)], axis=1)
        ref[row + q : row + q + 1, :] = piece


def one_hot(index, count):
    rows = lax.broadcasted_iota(I32, (count, index.shape[1]), 0)
    return jnp.where(rows == index, 1.0, 0.0)


def look_up(table, index):
    picked = lax.dot_general(
        table.T,
        one_hot(index // LANES, table.shape[0]),
        (((1,), (0,)), ((), ())),
        preferred_element_type=F32,
        precision=EXACT,
    )
    return jnp.sum(picked * one_hot(index % LANES, LANES), axis=0, keepdims=True)


def scatter(index, values, height):
    high = jnp.where(index >= 0, index // LANES, -1)
    return lax.dot_general(
        one_hot(high, height) * values,
        one_hot(jnp.where(index >= 0, index % LANES, -1), LANES),
        (((1,), (1,)), ((), ())),
        preferred_element_type=F32,
        precision=EXACT,
    )


def home_cells(node_out, region_no, cells):
    here = (node_out >= 0) & (node_out // cells == region_no)
    return jnp.where(here, node_out % cells, -1)


def rows_of_group(x_ref, rows_ref, first, sub):
    total = None
    for q in range(sub):
        piece = x_ref[pl.ds(pl.multiple_of(first, 8), 8), q * LANES : (q + 1) * LANES]
        rows_ref[pl.ds(first * sub + q, 8, stride=sub), :] = piece
        total = piece if total is None else total + piece
    return total


def copies_in(source, target, sems, chunk):
    copies = [
        pltpu.make_async_copy(
            source.at[pl.ds(i * chunk, chunk), :], target.at[pl.ds(i * chunk, chunk), :], sems.at[i]
        )
        for i in range(target.shape[0] // chunk)
    ]
    for copy in copies:
        copy.start()
    return copies


def make_lists(
    sizes, node_in, node_out, send_list, recv_list,
    in_cell, send_node, send_outlet, land, source_node, source_outlet,
):
    cells, nodes, branches, cap, sub = sizes
    height = cells // LANES
    region_no = lax.axis_index("region")
    ids = lax.broadcasted_iota(I32, (1, nodes), 1).astype(F32) + 1.0
    number = jnp.zeros((height, LANES), F32)
    slot = jnp.zeros((height, LANES), F32)
    for j in range(branches):
        ins = node_in[j : j + 1, :]
        put_row(in_cell, j * (nodes // LANES), jnp.where(ins >= 0, ins, cells), cells)
        home = home_cells(node_out[j : j + 1, :], region_no, cells)
        here = scatter(home, ids, height)
        number = number + here
        slot = slot + jnp.where(here > 0.0, j + 1.0, 0.0)
    source_node[...] = jnp.maximum(number.astype(I32) - 1, 0)
    source_outlet[...] = slot.astype(I32) - 1
    per_side = padded(cap) // LANES
    for side in range(4):
        slots = send_list[side : side + 1, :]
        lands = recv_list[side : side + 1, :]
        put_row(send_node, side * per_side, jnp.where(slots >= 0, slots % nodes, 0), 0)
        put_row(send_outlet, side * per_side, jnp.where(slots >= 0, slots // nodes, -1), -1)
        put_row(land, side * per_side, jnp.where(lands >= 0, lands, cells), cells)


def cell_sum_kernel(chunk, sub, x_hbm, sum_ref, rows_ref, x, partial, sems):
    copies = copies_in(x_hbm, x, sems, chunk)
    zeros = rows_ref.shape[0] - sub
    rows_ref[zeros:, :] = jnp.zeros((sub, LANES), F32)
    for number, copy in enumerate(copies):
        copy.wait()

        def body(step, carry, number=number):
            for half in range(2):
                first = number * chunk + step * 16 + half * 8
                total = rows_of_group(x, rows_ref, first, sub)
                partial[pl.ds(pl.multiple_of(first, 8), 8), :] = total
            return carry

        lax.fori_loop(0, chunk // 16, body, 0)
    sum_ref[...] = lane_sums(partial[...])


def turn_rows_kernel(sizes, chunk, x_hbm, after_ref, *rest):
    cells, nodes, branches, cap, sub = sizes
    lists, rows_ref, made, held, (recv, x, sems, list_sems) = (
        rest[:4], rest[4], rest[5:11], rest[11:14], rest[14:]
    )
    held = (*held, recv)
    list_copies = [
        pltpu.make_async_copy(source, target, list_sems.at[k])
        for k, (source, target) in enumerate(zip(lists, held))
    ]
    for copy in list_copies:
        copy.start()
    copies = copies_in(x_hbm, x, sems, chunk)
    for copy in list_copies:
        copy.wait()
    make_lists(sizes, *held, *made)
    for number, copy in enumerate(copies):
        copy.wait()

        def body(step, carry, number=number):
            for half in range(2):
                rows_of_group(x, rows_ref, number * chunk + step * 16 + half * 8, sub)
            return carry

        lax.fori_loop(0, chunk // 16, body, 0)


def gathered_flow(node, in_cell, scaled, sizes):
    cells, nodes, branches, cap, sub = sizes
    return tree_sum(
        [row_of(scaled, in_cell[i * nodes + node], sub)[...] for i in range(branches)]
    )


def scale_kernel(sizes, fraction, rows, scaled):
    cells, nodes, branches, cap, sub = sizes

    def body(step, carry):
        first = step * 16
        values = [
            row_of(rows, first + i, sub)[...] * fraction[first + i] for i in range(16)
        ]
        for i in range(16):
            row_of(scaled, first + i, sub)[...] = values[i]
        return carry

    lax.fori_loop(0, cells // 16, body, 0)
    row_of(scaled, cells, sub)[...] = jnp.zeros((sub, LANES), F32)


def send_kernel(sizes, sides, in_cell, send_node, send_outlet, scaled, turns, *rest):
    cells, nodes, branches, cap, sub = sizes
    sends = rest
    batch = 8
    for side, send in zip(sides, sends):

        def body(step, carry, side=side, send=send):
            first = step * batch
            values = []
            for i in range(batch):
                slot = side * padded(cap) + first + i
                node = send_node[slot]
                value = gathered_flow(node, in_cell, scaled, sizes)
                choice = row_of(turns, node, sub)[...]
                values.append(jnp.where(choice == send_outlet[slot], value, 0.0))
            for i in range(batch):
                row_of(send, first + i, sub)[...] = values[i]
            return carry

        lax.fori_loop(0, cap // batch, body, 0)


def scaled_send_kernel(sizes, side, theta, send_node, send_outlet, flow, turns, send):
    cells, nodes, branches, cap, sub = sizes
    batch = 8

    def body(step, carry):
        first = step * batch
        values = []
        for i in range(batch):
            slot = side * padded(cap) + first + i
            node = send_node[slot]
            value = row_of(flow, node, sub)[...] * theta[node]
            choice = row_of(turns, node, sub)[...]
            values.append(jnp.where(choice == send_outlet[slot], value, 0.0))
        for i in range(batch):
            row_of(send, first + i, sub)[...] = values[i]
        return carry

    lax.fori_loop(0, cap // batch, body, 0)


def node_flow_kernel(sizes, in_cell, scaled, turns, after_ref, flow, demand, partial):
    cells, nodes, branches, cap, sub = sizes

    def gather(step, carry):
        first = step * 8
        values = [
            gathered_flow(first + i, in_cell, scaled, sizes) for i in range(8)
        ]
        for i in range(8):
            row_of(flow, first + i, sub)[...] = values[i]
        return carry

    def measure(step, carry):
        for half in range(2):
            first = step * 16 + half * 8
            totals = [jnp.zeros((8, LANES), F32)] * branches
            for q in range(sub):
                at = pl.ds(first * sub + q, 8, stride=sub)
                value = flow[at, :]
                choice = turns[at, :]
                totals = [
                    total + jnp.where(choice == j, value, 0.0) for j, total in enumerate(totals)
                ]
            for j in range(branches):
                partial[j, pl.ds(pl.multiple_of(first, 8), 8), :] = totals[j]
        return carry

    lax.fori_loop(0, nodes // 8, gather, 0)
    lax.fori_loop(0, nodes // 16, measure, 0)
    per_outlet = nodes // LANES
    for j in range(branches):
        demand[j * per_outlet : (j + 1) * per_outlet, :] = lane_sums(partial[j])


def theta_kernel(
    sizes, regions, commodities, supply, shared, node_in, node_out, send_list, fraction,
    after_ref, keep, home_theta, theta_out, slot_theta,
):
    cells, nodes, branches, cap, sub = sizes
    height = cells // LANES
    per_outlet = nodes // LANES
    block = branches * per_outlet + height
    region_no = lax.axis_index("region")
    members = shared.shape[0] // block
    parts = [
        shared[d * block : d * block + branches * per_outlet, :] for d in range(members)
    ]
    demand = tree_sum(parts) * (1.0 / commodities)
    table = jnp.concatenate(
        [supply[...]]
        + [
            shared[d * block + branches * per_outlet : (d + 1) * block, :] for d in range(4)
        ],
        axis=0,
    )
    tall = jnp.ones((per_outlet, LANES), F32)
    for j in range(branches):
        outs = node_out[j : j + 1, :]
        cell = jnp.maximum(outs, 0)
        offset = (cell // cells + regions - region_no) % regions
        sector = jnp.zeros_like(offset)
        for d in range(4):
            sector = jnp.where(offset == (-SHIFTS[d]) % regions, d + 1, sector)
        room = stacked(look_up(table, sector * cells + cell % cells))
        ratio = room / jnp.maximum(demand[j * per_outlet : (j + 1) * per_outlet, :], room)
        tall = jnp.minimum(tall, jnp.where(stacked(outs) >= 0, ratio, 1.0))
    theta_out[...] = tall
    theta = strung(tall)
    cell_theta = jnp.zeros((height, LANES), F32)
    into = jnp.zeros((height, LANES), F32)
    for j in range(branches):
        home = home_cells(node_out[j : j + 1, :], region_no, cells)
        cell_theta = cell_theta + scatter(node_in[j : j + 1, :], theta, height)
        into = into + scatter(home, theta, height)
    keep[...] = 1.0 - cell_theta * fraction[...]
    home_theta[...] = into
    slots = send_list[pl.ds(lax.axis_index("dest") % 4, 1), :]
    put_row(slot_theta, 0, look_up(tall, jnp.where(slots >= 0, slots % nodes, 0)), 0.0)


def home_kernel(sizes, source, outlet, turns, flow, after_ref, home):
    cells, nodes, branches, cap, sub = sizes
    batch = 8

    def body(step, carry):
        first = step * batch
        values = []
        for i in range(batch):
            node = source[first + i]
            choice = row_of(turns, node, sub)[...]
            moved = row_of(flow, node, sub)[...]
            values.append(jnp.where(choice == outlet[first + i], moved, 0.0))
        for i in range(batch):
            row_of(home, first + i, sub)[...] = values[i]
        return carry

    lax.fori_loop(0, cells // batch, body, 0)


def base_kernel(sizes, keep, home_theta, rows, home, base):
    cells, nodes, branches, cap, sub = sizes
    batch = 8

    def body(step, carry):
        first = step * batch
        values = []
        for i in range(batch):
            cell = first + i
            kept = row_of(rows, cell, sub)[...] * keep[cell]
            values.append(kept + row_of(home, cell, sub)[...] * home_theta[cell])
        for i in range(batch):
            row_of(base, first + i, sub)[...] = values[i]
        return carry

    lax.fori_loop(0, cells // batch, body, 0)


def land_rows(sizes, sides, scale, land, received, base):
    cells, nodes, branches, cap, sub = sizes
    batch = 8
    for side, rows in zip(sides, received):

        def body(step, carry, side=side, rows=rows):
            first = step * batch
            stores = []
            for i in range(batch):
                slot = side * padded(cap) + first + i
                at = row_of(base, land[slot], sub)
                value = row_of(rows, first + i, sub)[...]
                if scale is not None:
                    value = value * scale[slot]
                stores.append((at, at[...] + value))
            for at, value in stores:
                at[...] = value
            return carry

        lax.fori_loop(0, cap // batch, body, 0)


def land_kernel(sizes, sides, scale, land, *rest):
    received, (base_in, base) = rest[: len(sides)], rest[len(sides) :]
    land_rows(sizes, sides, scale, land, received, base)


def finish_kernel(sizes, sides, chunk, land, *rest):
    cells, nodes, branches, cap, sub = sizes
    received, (base_in, out, base, staged, sems) = rest[: len(sides)], rest[len(sides) :]
    land_rows(sizes, sides, None, land, received, base)
    copies = []
    for number in range(cells // chunk):

        def body(step, carry, number=number):
            for half in range(2):
                first = number * chunk + step * 16 + half * 8
                for q in range(sub):
                    staged[
                        pl.ds(pl.multiple_of(first, 8), 8), q * LANES : (q + 1) * LANES
                    ] = base[pl.ds(first * sub + q, 8, stride=sub), :]
            return carry

        lax.fori_loop(0, chunk // 16, body, 0)
        at = pl.ds(number * chunk, chunk)
        copies.append(
            pltpu.make_async_copy(staged.at[at, :], out.at[at, :], sems.at[number])
        )
        copies[-1].start()
    for copy in copies:
        copy.wait()


def on_device(occupancy, capacity, jam, wave, node_in, node_out, send_list, recv_list, turn):
    cells, width = occupancy.shape
    branches, nodes = node_in.shape
    cap = send_list.shape[1]
    sub = width // LANES
    sizes = (cells, nodes, branches, cap, sub)
    regions = lax.axis_size("region")
    commodities = width * lax.axis_size("dest")
    height = cells // LANES
    per_cell = (height, LANES)
    list_shape = (4 * padded(cap) // LANES, LANES)
    chunk = 128
    row_bytes = width * 4
    occupancy = pltpu.with_memory_space_constraint(occupancy, pltpu.HBM)
    turn = pltpu.with_memory_space_constraint(turn, pltpu.HBM)
    node_in, node_out, send_list, recv_list = (
        pltpu.with_memory_space_constraint(x, pltpu.HBM)
        for x in (node_in, node_out, send_list, recv_list)
    )

    local_sum, rows = pl.pallas_call(
        functools.partial(cell_sum_kernel, chunk, sub),
        in_specs=[ANYWHERE],
        out_specs=[VMEM_WHOLE] * 2,
        out_shape=[
            jax.ShapeDtypeStruct(per_cell, F32),
            pltpu.VMEM(((cells + 1) * sub, LANES), F32),
        ],
        scratch_shapes=[
            pltpu.VMEM((cells, width), F32),
            pltpu.VMEM((cells, LANES), F32),
            pltpu.SemaphoreType.DMA((cells // chunk,)),
        ],
        compiler_params=params(14),
        cost_estimate=cost(cells * width, cells * row_bytes),
        name="cell_sum",
    )(occupancy)

    sums = partners(local_sum, "dest")

    turns, *lists = pl.pallas_call(
        functools.partial(turn_rows_kernel, sizes, chunk),
        in_specs=[ANYWHERE] * 6,
        out_specs=[VMEM_WHOLE] * 10,
        out_shape=[
            pltpu.VMEM((nodes * sub, LANES), I32),
            jax.ShapeDtypeStruct((branches * nodes // LANES, LANES), I32),
        ]
        + [jax.ShapeDtypeStruct(list_shape, I32)] * 3
        + [jax.ShapeDtypeStruct(per_cell, I32)] * 2
        + [pltpu.VMEM(x.shape, I32) for x in (node_in, node_out, send_list)],
        scratch_shapes=[
            pltpu.VMEM(recv_list.shape, I32),
            pltpu.VMEM((nodes, width), I32),
            pltpu.SemaphoreType.DMA((nodes // chunk,)),
            pltpu.SemaphoreType.DMA((4,)),
        ],
        compiler_params=params(8),
        cost_estimate=cost(0, nodes * row_bytes),
        name="turn_rows",
    )(turn, local_sum, node_in, node_out, send_list, recv_list)
    node_in, node_out, send_list = lists[6:]
    in_cell, send_node, send_outlet, land, source_node, source_outlet = (
        x.reshape(-1) for x in lists[:6]
    )

    turns, *sums = lax.optimization_barrier((turns, *sums))
    vehicles = tree_sum(sums) / commodities
    cap_of = capacity.reshape(per_cell)
    fraction = jnp.minimum(vehicles, cap_of) / vehicles
    supply = jnp.minimum(cap_of, wave.reshape(per_cell) * (jam.reshape(per_cell) - vehicles))
    rows_shape = pltpu.VMEM(((cells + 1) * sub, LANES), F32)
    send_shape = pltpu.VMEM((cap * sub, LANES), F32)

    supply_there = to_neighbours(supply)
    scaled = pl.pallas_call(
        functools.partial(scale_kernel, sizes),
        in_specs=[SMEM_WHOLE, VMEM_WHOLE],
        out_specs=VMEM_WHOLE,
        out_shape=rows_shape,
        compiler_params=params(4),
        cost_estimate=cost(1, 1),
        name="scale_rows",
    )(fraction.reshape(-1), rows)
    early = pl.pallas_call(
        functools.partial(send_kernel, sizes, (0, 1, 2)),
        in_specs=[SMEM_WHOLE] * 3 + [VMEM_WHOLE] * 2,
        out_specs=[VMEM_WHOLE] * 3,
        out_shape=[send_shape] * 3,
        compiler_params=params(4),
        cost_estimate=cost(1, 1),
        name="send_rows",
    )(in_cell, send_node, send_outlet, scaled, turns)
    supply_there, *early = lax.optimization_barrier((supply_there, *early))
    arrived = [
        shifted(send, "region", SHIFTS[side]) for side, send in enumerate(early)
    ]


    flow, demand = pl.pallas_call(
        functools.partial(node_flow_kernel, sizes),
        in_specs=[SMEM_WHOLE] + [VMEM_WHOLE] * 2 + [ANYWHERE],
        out_specs=[VMEM_WHOLE] * 2,
        out_shape=[
            pltpu.VMEM((nodes * sub, LANES), F32),
            jax.ShapeDtypeStruct((branches * nodes // LANES, LANES), F32),
        ],
        scratch_shapes=[pltpu.VMEM((branches, nodes, LANES), F32)],
        compiler_params=params(8),
        cost_estimate=cost(1, 1),
        name="node_flow",
    )(in_cell, scaled, turns, early[0])

    joined = jnp.concatenate([demand, supply_there])
    shared = lax.all_gather(joined, "dest", axis=0, tiled=True)
    home = pl.pallas_call(
        functools.partial(home_kernel, sizes),
        in_specs=[SMEM_WHOLE] * 2 + [VMEM_WHOLE] * 2 + [ANYWHERE],
        out_specs=VMEM_WHOLE,
        out_shape=rows_shape,
        compiler_params=params(4),
        cost_estimate=cost(1, 1),
        name="home_rows",
    )(source_node, source_outlet, turns, flow, joined)
    keep, home_theta, theta, slot_theta = pl.pallas_call(
        functools.partial(theta_kernel, sizes, regions, commodities),
        in_specs=[VMEM_WHOLE] * 6 + [ANYWHERE],
        out_specs=[VMEM_WHOLE] * 4,
        out_shape=[jax.ShapeDtypeStruct(per_cell, F32)] * 2
        + [
            jax.ShapeDtypeStruct((nodes // LANES, LANES), F32),
            jax.ShapeDtypeStruct((padded(cap) // LANES, LANES), F32),
        ],
        compiler_params=params(8),
        cost_estimate=cost(1, 1),
        name="theta",
    )(supply, shared, node_in, node_out, send_list, fraction, home)
    theta_there = to_neighbours(slot_theta)

    (behind,) = pl.pallas_call(
        functools.partial(scaled_send_kernel, sizes, 3),
        in_specs=[SMEM_WHOLE] * 3 + [VMEM_WHOLE] * 2,
        out_specs=[VMEM_WHOLE],
        out_shape=[send_shape],
        compiler_params=params(4),
        cost_estimate=cost(1, 1),
        name="send_scaled",
    )(theta.reshape(-1), send_node, send_outlet, flow, turns)
    behind, theta_there, *arrived = lax.optimization_barrier((behind, theta_there, *arrived))
    last = shifted(behind, "region", SHIFTS[3])
    scale = lax.all_gather(theta_there, "dest", axis=0, tiled=True)[: list_shape[0]]

    base = pl.pallas_call(
        functools.partial(base_kernel, sizes),
        in_specs=[SMEM_WHOLE] * 2 + [VMEM_WHOLE] * 2,
        out_specs=VMEM_WHOLE,
        out_shape=rows_shape,
        compiler_params=params(4),
        cost_estimate=cost(1, 1),
        name="base_rows",
    )(keep.reshape(-1), home_theta.reshape(-1), rows, home)

    base = pl.pallas_call(
        functools.partial(land_kernel, sizes, (0, 1, 2)),
        in_specs=[SMEM_WHOLE] * 2 + [VMEM_WHOLE] * 4,
        out_specs=VMEM_WHOLE,
        out_shape=rows_shape,
        input_output_aliases={5: 0},
        compiler_params=params(4),
        cost_estimate=cost(1, 1),
        name="land_first",
    )(scale.reshape(-1), land, *arrived, base)

    out, _ = pl.pallas_call(
        functools.partial(finish_kernel, sizes, (3,), chunk),
        in_specs=[SMEM_WHOLE] + [VMEM_WHOLE] * 2,
        out_specs=[ANYWHERE, VMEM_WHOLE],
        out_shape=[jax.ShapeDtypeStruct((cells, width), F32), rows_shape],
        scratch_shapes=[
            pltpu.VMEM((cells, width), F32),
            pltpu.SemaphoreType.DMA((cells // chunk,)),
        ],
        input_output_aliases={2: 1},
        compiler_params=params(12),
        cost_estimate=cost(cells * width, cells * row_bytes),
        name="finish",
    )(land, last, base)
    return out


def solution(mesh):
    return jax.shard_map(
        on_device,
        mesh=mesh,
        in_specs=(
            P("region", "dest"),
            P("region"),
            P("region"),
            P("region"),
            P(None, "region"),
            P(None, "region"),
            P("region", None),
            P("region", None),
            P("region", "dest"),
        ),
        out_specs=P("region", "dest"),
        check_vma=False,
    )
```

```python
import functools

import jax
import jax.numpy as jnp
from jax import lax
from jax.experimental import pallas as pl
from jax.experimental.pallas import tpu as pltpu
from jax.sharding import PartitionSpec as P

SHIFTS = (1, -1, 2, -2)
EXACT = lax.Precision.HIGHEST
LANES = 128
MIB = 1 << 20
F32 = jnp.float32
I32 = jnp.int32
VMEM_WHOLE = pl.BlockSpec(memory_space=pltpu.VMEM)
SMEM_WHOLE = pl.BlockSpec(memory_space=pltpu.SMEM)
ANYWHERE = pl.BlockSpec(memory_space=pl.ANY)


def to_neighbours(block):
    regions, members = lax.axis_size("region"), lax.axis_size("dest")
    route = [
        (r * members + d, (r + SHIFTS[d % 4]) % regions * members + d)
        for r in range(regions)
        for d in range(members)
    ]
    return lax.ppermute(block, ("region", "dest"), route)


def shifted(block, axis, distance):
    devices = range(lax.axis_size(axis))
    route = [((i - distance) % len(devices), i) for i in devices]
    return lax.ppermute(block, axis, route)


def partners(block, axis):
    count = lax.axis_size(axis)
    return [block] + [
        lax.ppermute(block, axis, [(i, i ^ other) for i in range(count)])
        for other in range(1, count)
    ]


def tree_sum(parts):
    while len(parts) > 1:
        parts = [parts[k] + parts[k + 1] for k in range(0, len(parts), 2)]
    return parts[0]


def params(mib):
    return pltpu.CompilerParams(vmem_limit_bytes=mib * MIB)


def cost(flops, moved):
    return pl.CostEstimate(flops=flops, bytes_accessed=moved, transcendentals=0)


def lane_sums(partial):
    sums = jnp.dot(
        partial, jnp.ones((LANES, LANES), F32), preferred_element_type=F32, precision=EXACT
    )
    row = lax.broadcasted_iota(I32, (LANES, LANES), 0)
    lane = lax.broadcasted_iota(I32, (LANES, LANES), 1)
    pieces = [
        jnp.sum(jnp.where(row == lane, sums[k : k + LANES, :], 0.0), axis=0, keepdims=True)
        for k in range(0, partial.shape[0], LANES)
    ]
    return jnp.concatenate(pieces, axis=0)


def stacked(row):
    return jnp.concatenate(
        [row[:, k : k + LANES] for k in range(0, row.shape[1], LANES)], axis=0
    )


def strung(rows):
    return jnp.concatenate([rows[k : k + 1, :] for k in range(rows.shape[0])], axis=1)


def row_of(ref, number, sub):
    if sub % 8 == 0:
        return ref.reshape(ref.shape[0] // sub, sub, LANES).at[number]
    return ref.at[pl.ds(pl.multiple_of(number * sub, sub), sub), :]


def padded(cap):
    return -(-cap // LANES) * LANES


def put_row(ref, row, value, fill):
    width = value.shape[1]
    for q in range(-(-width // LANES)):
        piece = value[:, q * LANES : min((q + 1) * LANES, width)]
        lack = LANES - piece.shape[1]
        if lack:
            piece = jnp.concatenate([piece, jnp.full((1, lack), fill, piece.dtype)], axis=1)
        ref[row + q : row + q + 1, :] = piece


def one_hot(index, count):
    rows = lax.broadcasted_iota(I32, (count, index.shape[1]), 0)
    return jnp.where(rows == index, 1.0, 0.0)


def in_parts(x):
    high = x.astype(jnp.bfloat16)
    rest = x - high.astype(F32)
    middle = rest.astype(jnp.bfloat16)
    low = (rest - middle.astype(F32)).astype(jnp.bfloat16)
    return jnp.concatenate([high, middle, low], axis=0)


def selected(values, choice, dims):
    count = values.shape[0]
    product = lax.dot_general(
        in_parts(values), choice.astype(jnp.bfloat16), (dims, ((), ())),
        preferred_element_type=F32,
    )
    return product[:count, :] + product[count : 2 * count, :] + product[2 * count :, :]


def look_up(table, index):
    picked = selected(table.T, one_hot(index // LANES, table.shape[0]), ((1,), (0,)))
    return jnp.sum(picked * one_hot(index % LANES, LANES), axis=0, keepdims=True)


def scatter(index, values, height):
    high = jnp.where(index >= 0, index // LANES, -1)
    low = jnp.where(index >= 0, index % LANES, -1)
    return selected(one_hot(high, height) * values, one_hot(low, LANES), ((1,), (1,)))


def home_cells(node_out, region_no, cells):
    here = (node_out >= 0) & (node_out // cells == region_no)
    return jnp.where(here, node_out % cells, -1)


def rows_of_group(x_ref, rows_ref, first, sub):
    total = None
    for q in range(sub):
        piece = x_ref[pl.ds(pl.multiple_of(first, 8), 8), q * LANES : (q + 1) * LANES]
        rows_ref[pl.ds(first * sub + q, 8, stride=sub), :] = piece
        total = piece if total is None else total + piece
    return total


def copies_in(source, target, sems, chunk):
    copies = [
        pltpu.make_async_copy(
            source.at[pl.ds(i * chunk, chunk), :], target.at[pl.ds(i * chunk, chunk), :], sems.at[i]
        )
        for i in range(target.shape[0] // chunk)
    ]
    for copy in copies:
        copy.start()
    return copies


def make_lists(
    sizes, node_in, node_out, send_list, recv_list,
    in_cell, send_node, send_outlet, land, source_node, source_outlet,
):
    cells, nodes, branches, cap, sub = sizes
    height = cells // LANES
    region_no = lax.axis_index("region")
    ids = lax.broadcasted_iota(I32, (1, nodes), 1).astype(F32) + 1.0
    number = jnp.zeros((height, LANES), F32)
    slot = jnp.zeros((height, LANES), F32)
    for j in range(branches):
        ins = node_in[j : j + 1, :]
        put_row(in_cell, j * (nodes // LANES), jnp.where(ins >= 0, ins, cells), cells)
        home = home_cells(node_out[j : j + 1, :], region_no, cells)
        here = scatter(home, ids, height)
        number = number + here
        slot = slot + jnp.where(here > 0.0, j + 1.0, 0.0)
    source_node[...] = jnp.maximum(number.astype(I32) - 1, 0)
    source_outlet[...] = slot.astype(I32) - 1
    per_side = padded(cap) // LANES
    for side in range(4):
        slots = send_list[side : side + 1, :]
        lands = recv_list[side : side + 1, :]
        put_row(send_node, side * per_side, jnp.where(slots >= 0, slots % nodes, 0), 0)
        put_row(send_outlet, side * per_side, jnp.where(slots >= 0, slots // nodes, -1), -1)
        put_row(land, side * per_side, jnp.where(lands >= 0, lands, cells), cells)


def cell_sum_kernel(chunk, sub, x_hbm, sum_ref, rows_ref, x, partial, sems):
    copies = copies_in(x_hbm, x, sems, chunk)
    zeros = rows_ref.shape[0] - sub
    rows_ref[zeros:, :] = jnp.zeros((sub, LANES), F32)
    for number, copy in enumerate(copies):
        copy.wait()

        def body(step, carry, number=number):
            for half in range(2):
                first = number * chunk + step * 16 + half * 8
                total = rows_of_group(x, rows_ref, first, sub)
                partial[pl.ds(pl.multiple_of(first, 8), 8), :] = total
            return carry

        lax.fori_loop(0, chunk // 16, body, 0)
    sum_ref[...] = lane_sums(partial[...])


def turn_rows_kernel(sizes, chunk, x_hbm, after_ref, *rest):
    cells, nodes, branches, cap, sub = sizes
    lists, rows_ref, made, (x, sems) = rest[:4], rest[4], rest[5:11], rest[11:]
    copies = copies_in(x_hbm, x, sems, chunk)
    make_lists(sizes, *lists, *made)
    for number, copy in enumerate(copies):
        copy.wait()

        def body(step, carry, number=number):
            for half in range(2):
                rows_of_group(x, rows_ref, number * chunk + step * 16 + half * 8, sub)
            return carry

        lax.fori_loop(0, chunk // 16, body, 0)


def gathered_flow(node, in_cell, fraction, rows, sizes):
    cells, nodes, branches, cap, sub = sizes
    parts = []
    for i in range(branches):
        cell = in_cell[i * nodes + node]
        part = row_of(rows, cell, sub)[...]
        parts.append(part if fraction is None else part * fraction[cell])
    return tree_sum(parts)


def scale_kernel(sizes, fraction, rows, after_ref, scaled):
    cells, nodes, branches, cap, sub = sizes

    def body(step, carry):
        first = step * 16
        values = [
            row_of(rows, first + i, sub)[...] * fraction[first + i] for i in range(16)
        ]
        for i in range(16):
            row_of(scaled, first + i, sub)[...] = values[i]
        return carry

    lax.fori_loop(0, cells // 16, body, 0)
    row_of(scaled, cells, sub)[...] = jnp.zeros((sub, LANES), F32)


def send_kernel(sizes, sides, fraction, in_cell, send_node, send_outlet, rows, turns, *sends):
    cells, nodes, branches, cap, sub = sizes
    batch = 8
    for side, send in zip(sides, sends):

        def body(step, carry, side=side, send=send):
            first = step * batch
            values = []
            for i in range(batch):
                slot = side * padded(cap) + first + i
                node = send_node[slot]
                value = gathered_flow(node, in_cell, fraction, rows, sizes)
                choice = row_of(turns, node, sub)[...]
                values.append(jnp.where(choice == send_outlet[slot], value, 0.0))
            for i in range(batch):
                row_of(send, first + i, sub)[...] = values[i]
            return carry

        lax.fori_loop(0, cap // batch, body, 0)


def scaled_send_kernel(sizes, side, theta, send_node, send_outlet, flow, turns, send):
    cells, nodes, branches, cap, sub = sizes
    batch = 8

    def body(step, carry):
        first = step * batch
        values = []
        for i in range(batch):
            slot = side * padded(cap) + first + i
            node = send_node[slot]
            value = row_of(flow, node, sub)[...] * theta[node]
            choice = row_of(turns, node, sub)[...]
            values.append(jnp.where(choice == send_outlet[slot], value, 0.0))
        for i in range(batch):
            row_of(send, first + i, sub)[...] = values[i]
        return carry

    lax.fori_loop(0, cap // batch, body, 0)


def node_flow_kernel(sizes, in_cell, scaled, turns, after_ref, flow, demand, partial):
    cells, nodes, branches, cap, sub = sizes

    def gather(step, carry):
        first = step * 8
        values = [
            gathered_flow(first + i, in_cell, None, scaled, sizes) for i in range(8)
        ]
        for i in range(8):
            row_of(flow, first + i, sub)[...] = values[i]
        return carry

    def measure(step, carry):
        for half in range(2):
            first = step * 16 + half * 8
            totals = [jnp.zeros((8, LANES), F32)] * branches
            for q in range(sub):
                at = pl.ds(first * sub + q, 8, stride=sub)
                value = flow[at, :]
                choice = turns[at, :]
                totals = [
                    total + jnp.where(choice == j, value, 0.0) for j, total in enumerate(totals)
                ]
            for j in range(branches):
                partial[j, pl.ds(pl.multiple_of(first, 8), 8), :] = totals[j]
        return carry

    lax.fori_loop(0, nodes // 8, gather, 0)
    lax.fori_loop(0, nodes // 16, measure, 0)
    per_outlet = nodes // LANES
    for j in range(branches):
        demand[j * per_outlet : (j + 1) * per_outlet, :] = lane_sums(partial[j])


def theta_kernel(
    sizes, regions, commodities, supply, shared, node_out, send_list, after_ref,
    theta_out, slot_theta,
):
    cells, nodes, branches, cap, sub = sizes
    per_outlet = nodes // LANES
    height = cells // LANES
    block = branches * per_outlet + height
    region_no = lax.axis_index("region")
    members = shared.shape[0] // block
    parts = [
        shared[d * block : d * block + branches * per_outlet, :] for d in range(members)
    ]
    demand = tree_sum(parts) * (1.0 / commodities)
    table = jnp.concatenate(
        [supply[...]]
        + [
            shared[d * block + branches * per_outlet : (d + 1) * block, :] for d in range(4)
        ],
        axis=0,
    )
    tall = jnp.ones((per_outlet, LANES), F32)
    for j in range(branches):
        outs = node_out[j : j + 1, :]
        cell = jnp.maximum(outs, 0)
        offset = (cell // cells + regions - region_no) % regions
        sector = jnp.zeros_like(offset)
        for d in range(4):
            sector = jnp.where(offset == (-SHIFTS[d]) % regions, d + 1, sector)
        room = stacked(look_up(table, sector * cells + cell % cells))
        ratio = room / jnp.maximum(demand[j * per_outlet : (j + 1) * per_outlet, :], room)
        tall = jnp.minimum(tall, jnp.where(stacked(outs) >= 0, ratio, 1.0))
    theta_out[...] = tall
    slots = send_list[pl.ds(lax.axis_index("dest") % 4, 1), :]
    put_row(slot_theta, 0, look_up(tall, jnp.where(slots >= 0, slots % nodes, 0)), 0.0)


def keep_kernel(
    sizes, theta_ref, node_in, node_out, fraction, sent_ref, arrived_ref, keep, home_theta
):
    cells, nodes, branches, cap, sub = sizes
    height = cells // LANES
    region_no = lax.axis_index("region")
    theta = strung(theta_ref[...])
    cell_theta = jnp.zeros((height, LANES), F32)
    into = jnp.zeros((height, LANES), F32)
    for j in range(branches):
        home = home_cells(node_out[j : j + 1, :], region_no, cells)
        cell_theta = cell_theta + scatter(node_in[j : j + 1, :], theta, height)
        into = into + scatter(home, theta, height)
    keep[...] = 1.0 - cell_theta * fraction[...]
    home_theta[...] = into


def home_kernel(sizes, source, outlet, turns, flow, after_ref, home):
    cells, nodes, branches, cap, sub = sizes
    batch = 8

    def body(step, carry):
        first = step * batch
        values = []
        for i in range(batch):
            node = source[first + i]
            choice = row_of(turns, node, sub)[...]
            moved = row_of(flow, node, sub)[...]
            values.append(jnp.where(choice == outlet[first + i], moved, 0.0))
        for i in range(batch):
            row_of(home, first + i, sub)[...] = values[i]
        return carry

    lax.fori_loop(0, cells // batch, body, 0)


def base_kernel(sizes, keep, home_theta, rows, home, base):
    cells, nodes, branches, cap, sub = sizes
    batch = 8

    def body(step, carry):
        first = step * batch
        values = []
        for i in range(batch):
            cell = first + i
            kept = row_of(rows, cell, sub)[...] * keep[cell]
            values.append(kept + row_of(home, cell, sub)[...] * home_theta[cell])
        for i in range(batch):
            row_of(base, first + i, sub)[...] = values[i]
        return carry

    lax.fori_loop(0, cells // batch, body, 0)


def land_rows(sizes, sides, scale, land, received, base):
    cells, nodes, branches, cap, sub = sizes
    batch = 8
    for side, rows in zip(sides, received):

        def body(step, carry, side=side, rows=rows):
            first = step * batch
            stores = []
            for i in range(batch):
                slot = side * padded(cap) + first + i
                at = row_of(base, land[slot], sub)
                value = row_of(rows, first + i, sub)[...]
                if scale is not None:
                    value = value * scale[slot]
                stores.append((at, at[...] + value))
            for at, value in stores:
                at[...] = value
            return carry

        lax.fori_loop(0, cap // batch, body, 0)


def land_kernel(sizes, sides, scale, land, *rest):
    received, (base_in, base) = rest[: len(sides)], rest[len(sides) :]
    land_rows(sizes, sides, scale, land, received, base)


def finish_kernel(sizes, sides, chunk, land, *rest):
    cells, nodes, branches, cap, sub = sizes
    received, (base_in, out, base, staged, sems) = rest[: len(sides)], rest[len(sides) :]
    land_rows(sizes, sides, None, land, received, base)
    copies = []
    for number in range(cells // chunk):

        def body(step, carry, number=number):
            for half in range(2):
                first = number * chunk + step * 16 + half * 8
                for q in range(sub):
                    staged[
                        pl.ds(pl.multiple_of(first, 8), 8), q * LANES : (q + 1) * LANES
                    ] = base[pl.ds(first * sub + q, 8, stride=sub), :]
            return carry

        lax.fori_loop(0, chunk // 16, body, 0)
        at = pl.ds(number * chunk, chunk)
        copies.append(
            pltpu.make_async_copy(staged.at[at, :], out.at[at, :], sems.at[number])
        )
        copies[-1].start()
    for copy in copies:
        copy.wait()


def on_device(occupancy, capacity, jam, wave, node_in, node_out, send_list, recv_list, turn):
    cells, width = occupancy.shape
    branches, nodes = node_in.shape
    cap = send_list.shape[1]
    sub = width // LANES
    sizes = (cells, nodes, branches, cap, sub)
    regions = lax.axis_size("region")
    commodities = width * lax.axis_size("dest")
    height = cells // LANES
    per_cell = (height, LANES)
    list_shape = (4 * padded(cap) // LANES, LANES)
    chunk = 128
    row_bytes = width * 4
    occupancy = pltpu.with_memory_space_constraint(occupancy, pltpu.HBM)
    turn = pltpu.with_memory_space_constraint(turn, pltpu.HBM)

    local_sum, rows = pl.pallas_call(
        functools.partial(cell_sum_kernel, chunk, sub),
        in_specs=[ANYWHERE],
        out_specs=[VMEM_WHOLE] * 2,
        out_shape=[
            jax.ShapeDtypeStruct(per_cell, F32),
            pltpu.VMEM(((cells + 1) * sub, LANES), F32),
        ],
        scratch_shapes=[
            pltpu.VMEM((cells, width), F32),
            pltpu.VMEM((cells, LANES), F32),
            pltpu.SemaphoreType.DMA((cells // chunk,)),
        ],
        compiler_params=params(14),
        cost_estimate=cost(cells * width, cells * row_bytes),
        name="cell_sum",
    )(occupancy)

    sums = partners(local_sum, "dest")

    turns, *lists = pl.pallas_call(
        functools.partial(turn_rows_kernel, sizes, chunk),
        in_specs=[ANYWHERE] * 2 + [VMEM_WHOLE] * 4,
        out_specs=[VMEM_WHOLE] * 7,
        out_shape=[
            pltpu.VMEM((nodes * sub, LANES), I32),
            jax.ShapeDtypeStruct((branches * nodes // LANES, LANES), I32),
        ]
        + [jax.ShapeDtypeStruct(list_shape, I32)] * 3
        + [jax.ShapeDtypeStruct(per_cell, I32)] * 2,
        scratch_shapes=[
            pltpu.VMEM((nodes, width), I32),
            pltpu.SemaphoreType.DMA((nodes // chunk,)),
        ],
        compiler_params=params(8),
        cost_estimate=cost(0, nodes * row_bytes),
        name="turn_rows",
    )(turn, local_sum, node_in, node_out, send_list, recv_list)
    in_cell, send_node, send_outlet, land, source_node, source_outlet = (
        x.reshape(-1) for x in lists
    )

    turns, *sums = lax.optimization_barrier((turns, *sums))
    vehicles = tree_sum(sums) / commodities
    cap_of = capacity.reshape(per_cell)
    fraction = jnp.minimum(vehicles, cap_of) / vehicles
    supply = jnp.minimum(cap_of, wave.reshape(per_cell) * (jam.reshape(per_cell) - vehicles))
    rows_shape = pltpu.VMEM(((cells + 1) * sub, LANES), F32)
    send_shape = pltpu.VMEM((cap * sub, LANES), F32)

    supply_there = to_neighbours(supply)
    weights = jnp.concatenate([fraction.reshape(-1), jnp.zeros((LANES,), F32)])
    (ahead,) = pl.pallas_call(
        functools.partial(send_kernel, sizes, (2,)),
        in_specs=[SMEM_WHOLE] * 4 + [VMEM_WHOLE] * 2,
        out_specs=[VMEM_WHOLE],
        out_shape=[send_shape],
        compiler_params=params(4),
        cost_estimate=cost(1, 1),
        name="send_ahead",
    )(weights, in_cell, send_node, send_outlet, rows, turns)
    ahead, supply_there = lax.optimization_barrier((ahead, supply_there))
    scaled = pl.pallas_call(
        functools.partial(scale_kernel, sizes),
        in_specs=[SMEM_WHOLE, VMEM_WHOLE, ANYWHERE],
        out_specs=VMEM_WHOLE,
        out_shape=rows_shape,
        compiler_params=params(4),
        cost_estimate=cost(1, 1),
        name="scale_rows",
    )(fraction.reshape(-1), rows, ahead)
    near = pl.pallas_call(
        functools.partial(send_kernel, sizes, (0, 1), None),
        in_specs=[SMEM_WHOLE] * 3 + [VMEM_WHOLE] * 2,
        out_specs=[VMEM_WHOLE] * 2,
        out_shape=[send_shape] * 2,
        compiler_params=params(4),
        cost_estimate=cost(1, 1),
        name="send_near",
    )(in_cell, send_node, send_outlet, scaled, turns)
    arrived = [
        shifted(send, "region", SHIFTS[side]) for side, send in enumerate([*near, ahead])
    ]

    flow, demand = pl.pallas_call(
        functools.partial(node_flow_kernel, sizes),
        in_specs=[SMEM_WHOLE] + [VMEM_WHOLE] * 2 + [ANYWHERE],
        out_specs=[VMEM_WHOLE] * 2,
        out_shape=[
            pltpu.VMEM((nodes * sub, LANES), F32),
            jax.ShapeDtypeStruct((branches * nodes // LANES, LANES), F32),
        ],
        scratch_shapes=[pltpu.VMEM((branches, nodes, LANES), F32)],
        compiler_params=params(8),
        cost_estimate=cost(1, 1),
        name="node_flow",
    )(in_cell, scaled, turns, near[0])

    joined = jnp.concatenate([demand, supply_there])
    shared = lax.all_gather(joined, "dest", axis=0, tiled=True)
    home = pl.pallas_call(
        functools.partial(home_kernel, sizes),
        in_specs=[SMEM_WHOLE] * 2 + [VMEM_WHOLE] * 2 + [ANYWHERE],
        out_specs=VMEM_WHOLE,
        out_shape=rows_shape,
        compiler_params=params(4),
        cost_estimate=cost(1, 1),
        name="home_rows",
    )(source_node, source_outlet, turns, flow, joined)
    theta, slot_theta = pl.pallas_call(
        functools.partial(theta_kernel, sizes, regions, commodities),
        in_specs=[VMEM_WHOLE] * 4 + [ANYWHERE],
        out_specs=[VMEM_WHOLE] * 2,
        out_shape=[
            jax.ShapeDtypeStruct((nodes // LANES, LANES), F32),
            jax.ShapeDtypeStruct((padded(cap) // LANES, LANES), F32),
        ],
        compiler_params=params(8),
        cost_estimate=cost(1, 1),
        name="theta",
    )(supply, shared, node_out, send_list, home)
    theta_there = to_neighbours(slot_theta)

    (behind,) = pl.pallas_call(
        functools.partial(scaled_send_kernel, sizes, 3),
        in_specs=[SMEM_WHOLE] * 3 + [VMEM_WHOLE] * 2,
        out_specs=[VMEM_WHOLE],
        out_shape=[send_shape],
        compiler_params=params(4),
        cost_estimate=cost(1, 1),
        name="send_scaled",
    )(theta.reshape(-1), send_node, send_outlet, flow, turns)
    keep, home_theta = pl.pallas_call(
        functools.partial(keep_kernel, sizes),
        in_specs=[VMEM_WHOLE] * 4 + [ANYWHERE] * 2,
        out_specs=[VMEM_WHOLE] * 2,
        out_shape=[jax.ShapeDtypeStruct(per_cell, F32)] * 2,
        compiler_params=params(8),
        cost_estimate=cost(100000000, 1),
        name="keep",
    )(theta, node_in, node_out, fraction, behind, arrived[2])
    keep, theta_there, *arrived = lax.optimization_barrier((keep, theta_there, *arrived))
    last = shifted(behind, "region", SHIFTS[3])
    scale = lax.all_gather(theta_there, "dest", axis=0, tiled=True)[: list_shape[0]]

    base = pl.pallas_call(
        functools.partial(base_kernel, sizes),
        in_specs=[SMEM_WHOLE] * 2 + [VMEM_WHOLE] * 2,
        out_specs=VMEM_WHOLE,
        out_shape=rows_shape,
        compiler_params=params(4),
        cost_estimate=pl.CostEstimate(flops=100000000000, bytes_accessed=1, transcendentals=0),
        name="base_rows",
    )(keep.reshape(-1), home_theta.reshape(-1), rows, home)

    base = pl.pallas_call(
        functools.partial(land_kernel, sizes, (0, 1, 2)),
        in_specs=[SMEM_WHOLE] * 2 + [VMEM_WHOLE] * 4,
        out_specs=VMEM_WHOLE,
        out_shape=rows_shape,
        input_output_aliases={5: 0},
        compiler_params=params(4),
        cost_estimate=pl.CostEstimate(flops=100000000000, bytes_accessed=1, transcendentals=0),
        name="land_first",
    )(scale.reshape(-1), land, *arrived, base)

    out, _ = pl.pallas_call(
        functools.partial(finish_kernel, sizes, (3,), chunk),
        in_specs=[SMEM_WHOLE] + [VMEM_WHOLE] * 2,
        out_specs=[ANYWHERE, VMEM_WHOLE],
        out_shape=[jax.ShapeDtypeStruct((cells, width), F32), rows_shape],
        scratch_shapes=[
            pltpu.VMEM((cells, width), F32),
            pltpu.SemaphoreType.DMA((cells // chunk,)),
        ],
        input_output_aliases={2: 1},
        compiler_params=params(12),
        cost_estimate=cost(cells * width, cells * row_bytes),
        name="finish",
    )(land, last, base)
    return out


def solution(mesh):
    return jax.shard_map(
        on_device,
        mesh=mesh,
        in_specs=(
            P("region", "dest"),
            P("region"),
            P("region"),
            P("region"),
            P(None, "region"),
            P(None, "region"),
            P("region", None),
            P("region", None),
            P("region", "dest"),
        ),
        out_specs=P("region", "dest"),
        check_vma=False,
    )
```

```python
import functools

import jax
import jax.numpy as jnp
from jax import lax
from jax.experimental import pallas as pl
from jax.experimental.pallas import tpu as pltpu
from jax.sharding import PartitionSpec as P

SHIFTS = (1, -1, 2, -2)
EXACT = lax.Precision.HIGHEST
LANES = 128
MIB = 1 << 20
F32 = jnp.float32
I32 = jnp.int32
VMEM_WHOLE = pl.BlockSpec(memory_space=pltpu.VMEM)
SMEM_WHOLE = pl.BlockSpec(memory_space=pltpu.SMEM)
ANYWHERE = pl.BlockSpec(memory_space=pl.ANY)


def to_neighbours(block):
    regions, members = lax.axis_size("region"), lax.axis_size("dest")
    route = [
        (r * members + d, (r + SHIFTS[d % 4]) % regions * members + d)
        for r in range(regions)
        for d in range(members)
    ]
    return lax.ppermute(block, ("region", "dest"), route)


def shifted(block, axis, distance):
    devices = range(lax.axis_size(axis))
    route = [((i - distance) % len(devices), i) for i in devices]
    return lax.ppermute(block, axis, route)


def partners(block, axis):
    count = lax.axis_size(axis)
    return [block] + [
        lax.ppermute(block, axis, [(i, i ^ other) for i in range(count)])
        for other in range(1, count)
    ]


def tree_sum(parts):
    while len(parts) > 1:
        parts = [parts[k] + parts[k + 1] for k in range(0, len(parts), 2)]
    return parts[0]


def params(mib):
    return pltpu.CompilerParams(vmem_limit_bytes=mib * MIB)


def cost(flops, moved):
    return pl.CostEstimate(flops=flops, bytes_accessed=moved, transcendentals=0)


def lane_sums(partial):
    sums = jnp.dot(
        partial, jnp.ones((LANES, LANES), F32), preferred_element_type=F32, precision=EXACT
    )
    row = lax.broadcasted_iota(I32, (LANES, LANES), 0)
    lane = lax.broadcasted_iota(I32, (LANES, LANES), 1)
    pieces = [
        jnp.sum(jnp.where(row == lane, sums[k : k + LANES, :], 0.0), axis=0, keepdims=True)
        for k in range(0, partial.shape[0], LANES)
    ]
    return jnp.concatenate(pieces, axis=0)


def stacked(row):
    return jnp.concatenate(
        [row[:, k : k + LANES] for k in range(0, row.shape[1], LANES)], axis=0
    )


def strung(rows):
    return jnp.concatenate([rows[k : k + 1, :] for k in range(rows.shape[0])], axis=1)


def row_of(ref, number, sub):
    if sub % 8 == 0:
        return ref.reshape(ref.shape[0] // sub, sub, LANES).at[number]
    return ref.at[pl.ds(pl.multiple_of(number * sub, sub), sub), :]


def padded(cap):
    return -(-cap // LANES) * LANES


def put_row(ref, row, value, fill):
    width = value.shape[1]
    for q in range(-(-width // LANES)):
        piece = value[:, q * LANES : min((q + 1) * LANES, width)]
        lack = LANES - piece.shape[1]
        if lack:
            piece = jnp.concatenate([piece, jnp.full((1, lack), fill, piece.dtype)], axis=1)
        ref[row + q : row + q + 1, :] = piece


def one_hot(index, count):
    rows = lax.broadcasted_iota(I32, (count, index.shape[1]), 0)
    return jnp.where(rows == index, 1.0, 0.0)


def in_parts(x):
    high = x.astype(jnp.bfloat16)
    rest = x - high.astype(F32)
    middle = rest.astype(jnp.bfloat16)
    low = (rest - middle.astype(F32)).astype(jnp.bfloat16)
    return jnp.concatenate([high, middle, low], axis=0)


def selected(values, choice, dims):
    count = values.shape[0]
    product = lax.dot_general(
        in_parts(values), choice.astype(jnp.bfloat16), (dims, ((), ())),
        preferred_element_type=F32,
    )
    return product[:count, :] + product[count : 2 * count, :] + product[2 * count :, :]


def look_up(table, index):
    picked = selected(table.T, one_hot(index // LANES, table.shape[0]), ((1,), (0,)))
    return jnp.sum(picked * one_hot(index % LANES, LANES), axis=0, keepdims=True)


def scatter(index, values, height):
    high = jnp.where(index >= 0, index // LANES, -1)
    low = jnp.where(index >= 0, index % LANES, -1)
    return selected(one_hot(high, height) * values, one_hot(low, LANES), ((1,), (1,)))


def home_cells(node_out, region_no, cells):
    here = (node_out >= 0) & (node_out // cells == region_no)
    return jnp.where(here, node_out % cells, -1)


def rows_of_group(x_ref, rows_ref, first, sub):
    total = None
    for q in range(sub):
        piece = x_ref[pl.ds(pl.multiple_of(first, 8), 8), q * LANES : (q + 1) * LANES]
        rows_ref[pl.ds(first * sub + q, 8, stride=sub), :] = piece
        total = piece if total is None else total + piece
    return total


def copies_in(source, target, sems, chunk):
    copies = [
        pltpu.make_async_copy(
            source.at[pl.ds(i * chunk, chunk), :], target.at[pl.ds(i * chunk, chunk), :], sems.at[i]
        )
        for i in range(target.shape[0] // chunk)
    ]
    for copy in copies:
        copy.start()
    return copies


def make_lists(
    sizes, node_in, node_out, send_list, recv_list,
    in_cell, send_node, send_outlet, land, source_node, source_outlet,
):
    cells, nodes, branches, cap, sub = sizes
    height = cells // LANES
    region_no = lax.axis_index("region")
    ids = lax.broadcasted_iota(I32, (1, nodes), 1).astype(F32) + 1.0
    number = jnp.zeros((height, LANES), F32)
    slot = jnp.zeros((height, LANES), F32)
    for j in range(branches):
        ins = node_in[j : j + 1, :]
        put_row(in_cell, j * (nodes // LANES), jnp.where(ins >= 0, ins, cells), cells)
        home = home_cells(node_out[j : j + 1, :], region_no, cells)
        here = scatter(home, ids, height)
        number = number + here
        slot = slot + jnp.where(here > 0.0, j + 1.0, 0.0)
    source_node[...] = jnp.maximum(number.astype(I32) - 1, 0)
    source_outlet[...] = slot.astype(I32) - 1
    per_side = padded(cap) // LANES
    for side in range(4):
        slots = send_list[side : side + 1, :]
        lands = recv_list[side : side + 1, :]
        put_row(send_node, side * per_side, jnp.where(slots >= 0, slots % nodes, 0), 0)
        put_row(send_outlet, side * per_side, jnp.where(slots >= 0, slots // nodes, -1), -1)
        put_row(land, side * per_side, jnp.where(lands >= 0, lands, cells), cells)


def cell_sum_kernel(chunk, sub, x_hbm, sum_ref, rows_ref, x, partial, sems):
    copies = copies_in(x_hbm, x, sems, chunk)
    zeros = rows_ref.shape[0] - sub
    rows_ref[zeros:, :] = jnp.zeros((sub, LANES), F32)
    for number, copy in enumerate(copies):
        copy.wait()

        def body(step, carry, number=number):
            for half in range(2):
                first = number * chunk + step * 16 + half * 8
                total = rows_of_group(x, rows_ref, first, sub)
                partial[pl.ds(pl.multiple_of(first, 8), 8), :] = total
            return carry

        lax.fori_loop(0, chunk // 16, body, 0)
    sum_ref[...] = lane_sums(partial[...])


def turn_rows_kernel(sizes, chunk, x_hbm, after_ref, *rest):
    cells, nodes, branches, cap, sub = sizes
    lists, rows_ref, made, (x, sems) = rest[:4], rest[4], rest[5:11], rest[11:]
    copies = copies_in(x_hbm, x, sems, chunk)
    make_lists(sizes, *lists, *made)
    for number, copy in enumerate(copies):
        copy.wait()

        def body(step, carry, number=number):
            for half in range(2):
                rows_of_group(x, rows_ref, number * chunk + step * 16 + half * 8, sub)
            return carry

        lax.fori_loop(0, chunk // 16, body, 0)


def gathered_flow(node, in_cell, fraction, rows, sizes):
    cells, nodes, branches, cap, sub = sizes
    parts = []
    for i in range(branches):
        cell = in_cell[i * nodes + node]
        part = row_of(rows, cell, sub)[...]
        parts.append(part if fraction is None else part * fraction[cell])
    return tree_sum(parts)


def scale_kernel(sizes, fraction, rows, sent_ref, supply_ref, scaled):
    cells, nodes, branches, cap, sub = sizes

    def body(step, carry):
        first = step * 16
        values = [
            row_of(rows, first + i, sub)[...] * fraction[first + i] for i in range(16)
        ]
        for i in range(16):
            row_of(scaled, first + i, sub)[...] = values[i]
        return carry

    lax.fori_loop(0, cells // 16, body, 0)
    row_of(scaled, cells, sub)[...] = jnp.zeros((sub, LANES), F32)


def send_kernel(sizes, sides, fraction, in_cell, send_node, send_outlet, rows, turns, *sends):
    cells, nodes, branches, cap, sub = sizes
    batch = 8
    for side, send in zip(sides, sends):

        def body(step, carry, side=side, send=send):
            first = step * batch
            values = []
            for i in range(batch):
                slot = side * padded(cap) + first + i
                node = send_node[slot]
                value = gathered_flow(node, in_cell, fraction, rows, sizes)
                choice = row_of(turns, node, sub)[...]
                values.append(jnp.where(choice == send_outlet[slot], value, 0.0))
            for i in range(batch):
                row_of(send, first + i, sub)[...] = values[i]
            return carry

        lax.fori_loop(0, cap // batch, body, 0)


def scaled_send_kernel(sizes, side, theta, send_node, send_outlet, flow, turns, send):
    cells, nodes, branches, cap, sub = sizes
    batch = 8

    def body(step, carry):
        first = step * batch
        values = []
        for i in range(batch):
            slot = side * padded(cap) + first + i
            node = send_node[slot]
            value = row_of(flow, node, sub)[...] * theta[node]
            choice = row_of(turns, node, sub)[...]
            values.append(jnp.where(choice == send_outlet[slot], value, 0.0))
        for i in range(batch):
            row_of(send, first + i, sub)[...] = values[i]
        return carry

    lax.fori_loop(0, cap // batch, body, 0)


def node_flow_kernel(sizes, in_cell, scaled, turns, after_ref, flow, demand, partial):
    cells, nodes, branches, cap, sub = sizes

    def gather(step, carry):
        first = step * 8
        values = [
            gathered_flow(first + i, in_cell, None, scaled, sizes) for i in range(8)
        ]
        for i in range(8):
            row_of(flow, first + i, sub)[...] = values[i]
        return carry

    def measure(step, carry):
        for half in range(2):
            first = step * 16 + half * 8
            totals = [jnp.zeros((8, LANES), F32)] * branches
            for q in range(sub):
                at = pl.ds(first * sub + q, 8, stride=sub)
                value = flow[at, :]
                choice = turns[at, :]
                totals = [
                    total + jnp.where(choice == j, value, 0.0) for j, total in enumerate(totals)
                ]
            for j in range(branches):
                partial[j, pl.ds(pl.multiple_of(first, 8), 8), :] = totals[j]
        return carry

    lax.fori_loop(0, nodes // 8, gather, 0)
    lax.fori_loop(0, nodes // 16, measure, 0)
    per_outlet = nodes // LANES
    for j in range(branches):
        demand[j * per_outlet : (j + 1) * per_outlet, :] = lane_sums(partial[j])


def theta_kernel(
    sizes, regions, commodities, supply, shared, node_out, send_list, theta_out, slot_theta
):
    cells, nodes, branches, cap, sub = sizes
    per_outlet = nodes // LANES
    height = cells // LANES
    block = branches * per_outlet + height
    region_no = lax.axis_index("region")
    members = shared.shape[0] // block
    parts = [
        shared[d * block : d * block + branches * per_outlet, :] for d in range(members)
    ]
    demand = tree_sum(parts) * (1.0 / commodities)
    table = jnp.concatenate(
        [supply[...]]
        + [
            shared[d * block + branches * per_outlet : (d + 1) * block, :] for d in range(4)
        ],
        axis=0,
    )
    tall = jnp.ones((per_outlet, LANES), F32)
    for j in range(branches):
        outs = node_out[j : j + 1, :]
        cell = jnp.maximum(outs, 0)
        offset = (cell // cells + regions - region_no) % regions
        sector = jnp.zeros_like(offset)
        for d in range(4):
            sector = jnp.where(offset == (-SHIFTS[d]) % regions, d + 1, sector)
        room = stacked(look_up(table, sector * cells + cell % cells))
        ratio = room / jnp.maximum(demand[j * per_outlet : (j + 1) * per_outlet, :], room)
        tall = jnp.minimum(tall, jnp.where(stacked(outs) >= 0, ratio, 1.0))
    theta_out[...] = tall
    slots = send_list[pl.ds(lax.axis_index("dest") % 4, 1), :]
    put_row(slot_theta, 0, look_up(tall, jnp.where(slots >= 0, slots % nodes, 0)), 0.0)


def keep_kernel(
    sizes, theta_ref, node_in, node_out, fraction, sent_ref, arrived_ref, keep, home_theta
):
    cells, nodes, branches, cap, sub = sizes
    height = cells // LANES
    region_no = lax.axis_index("region")
    theta = strung(theta_ref[...])
    cell_theta = jnp.zeros((height, LANES), F32)
    into = jnp.zeros((height, LANES), F32)
    for j in range(branches):
        home = home_cells(node_out[j : j + 1, :], region_no, cells)
        cell_theta = cell_theta + scatter(node_in[j : j + 1, :], theta, height)
        into = into + scatter(home, theta, height)
    keep[...] = 1.0 - cell_theta * fraction[...]
    home_theta[...] = into


def home_kernel(sizes, source, outlet, turns, flow, after_ref, home):
    cells, nodes, branches, cap, sub = sizes
    batch = 8

    def body(step, carry):
        first = step * batch
        values = []
        for i in range(batch):
            node = source[first + i]
            choice = row_of(turns, node, sub)[...]
            moved = row_of(flow, node, sub)[...]
            values.append(jnp.where(choice == outlet[first + i], moved, 0.0))
        for i in range(batch):
            row_of(home, first + i, sub)[...] = values[i]
        return carry

    lax.fori_loop(0, cells // batch, body, 0)


def base_kernel(sizes, keep, home_theta, rows, home, base):
    cells, nodes, branches, cap, sub = sizes
    batch = 8

    def body(step, carry):
        first = step * batch
        values = []
        for i in range(batch):
            cell = first + i
            kept = row_of(rows, cell, sub)[...] * keep[cell]
            values.append(kept + row_of(home, cell, sub)[...] * home_theta[cell])
        for i in range(batch):
            row_of(base, first + i, sub)[...] = values[i]
        return carry

    lax.fori_loop(0, cells // batch, body, 0)


def land_rows(sizes, sides, scale, land, received, base):
    cells, nodes, branches, cap, sub = sizes
    batch = 8
    for side, rows in zip(sides, received):

        def body(step, carry, side=side, rows=rows):
            first = step * batch
            stores = []
            for i in range(batch):
                slot = side * padded(cap) + first + i
                at = row_of(base, land[slot], sub)
                value = row_of(rows, first + i, sub)[...]
                if scale is not None:
                    value = value * scale[slot]
                stores.append((at, at[...] + value))
            for at, value in stores:
                at[...] = value
            return carry

        lax.fori_loop(0, cap // batch, body, 0)


def land_kernel(sizes, sides, scale, land, *rest):
    received, (base_in, base) = rest[: len(sides)], rest[len(sides) :]
    land_rows(sizes, sides, scale, land, received, base)


def finish_kernel(sizes, sides, chunk, land, *rest):
    cells, nodes, branches, cap, sub = sizes
    received, (base_in, out, base, staged, sems) = rest[: len(sides)], rest[len(sides) :]
    land_rows(sizes, sides, None, land, received, base)
    copies = []
    for number in range(cells // chunk):

        def body(step, carry, number=number):
            for half in range(2):
                first = number * chunk + step * 16 + half * 8
                for q in range(sub):
                    staged[
                        pl.ds(pl.multiple_of(first, 8), 8), q * LANES : (q + 1) * LANES
                    ] = base[pl.ds(first * sub + q, 8, stride=sub), :]
            return carry

        lax.fori_loop(0, chunk // 16, body, 0)
        at = pl.ds(number * chunk, chunk)
        copies.append(
            pltpu.make_async_copy(staged.at[at, :], out.at[at, :], sems.at[number])
        )
        copies[-1].start()
    for copy in copies:
        copy.wait()


def on_device(occupancy, capacity, jam, wave, node_in, node_out, send_list, recv_list, turn):
    cells, width = occupancy.shape
    branches, nodes = node_in.shape
    cap = send_list.shape[1]
    sub = width // LANES
    sizes = (cells, nodes, branches, cap, sub)
    regions = lax.axis_size("region")
    commodities = width * lax.axis_size("dest")
    height = cells // LANES
    per_cell = (height, LANES)
    list_shape = (4 * padded(cap) // LANES, LANES)
    chunk = 128
    row_bytes = width * 4
    occupancy = pltpu.with_memory_space_constraint(occupancy, pltpu.HBM)
    turn = pltpu.with_memory_space_constraint(turn, pltpu.HBM)

    local_sum, rows = pl.pallas_call(
        functools.partial(cell_sum_kernel, chunk, sub),
        in_specs=[ANYWHERE],
        out_specs=[VMEM_WHOLE] * 2,
        out_shape=[
            jax.ShapeDtypeStruct(per_cell, F32),
            pltpu.VMEM(((cells + 1) * sub, LANES), F32),
        ],
        scratch_shapes=[
            pltpu.VMEM((cells, width), F32),
            pltpu.VMEM((cells, LANES), F32),
            pltpu.SemaphoreType.DMA((cells // chunk,)),
        ],
        compiler_params=params(14),
        cost_estimate=cost(cells * width, cells * row_bytes),
        name="cell_sum",
    )(occupancy)

    sums = partners(local_sum, "dest")

    turns, *lists = pl.pallas_call(
        functools.partial(turn_rows_kernel, sizes, chunk),
        in_specs=[ANYWHERE] * 2 + [VMEM_WHOLE] * 4,
        out_specs=[VMEM_WHOLE] * 7,
        out_shape=[
            pltpu.VMEM((nodes * sub, LANES), I32),
            jax.ShapeDtypeStruct((branches * nodes // LANES, LANES), I32),
        ]
        + [jax.ShapeDtypeStruct(list_shape, I32)] * 3
        + [jax.ShapeDtypeStruct(per_cell, I32)] * 2,
        scratch_shapes=[
            pltpu.VMEM((nodes, width), I32),
            pltpu.SemaphoreType.DMA((nodes // chunk,)),
        ],
        compiler_params=params(8),
        cost_estimate=cost(0, nodes * row_bytes),
        name="turn_rows",
    )(turn, local_sum, node_in, node_out, send_list, recv_list)
    in_cell, send_node, send_outlet, land, source_node, source_outlet = (
        x.reshape(-1) for x in lists
    )

    turns, *sums = lax.optimization_barrier((turns, *sums))
    vehicles = tree_sum(sums) / commodities
    cap_of = capacity.reshape(per_cell)
    fraction = jnp.minimum(vehicles, cap_of) / vehicles
    supply = jnp.minimum(cap_of, wave.reshape(per_cell) * (jam.reshape(per_cell) - vehicles))
    rows_shape = pltpu.VMEM(((cells + 1) * sub, LANES), F32)
    send_shape = pltpu.VMEM((cap * sub, LANES), F32)

    supply_there = to_neighbours(supply)
    weights = jnp.concatenate([fraction.reshape(-1), jnp.zeros((LANES,), F32)])
    (ahead,) = pl.pallas_call(
        functools.partial(send_kernel, sizes, (2,)),
        in_specs=[SMEM_WHOLE] * 4 + [VMEM_WHOLE] * 2,
        out_specs=[VMEM_WHOLE],
        out_shape=[send_shape],
        compiler_params=params(4),
        cost_estimate=cost(1, 1),
        name="send_ahead",
    )(weights, in_cell, send_node, send_outlet, rows, turns)
    scaled = pl.pallas_call(
        functools.partial(scale_kernel, sizes),
        in_specs=[SMEM_WHOLE, VMEM_WHOLE, ANYWHERE, ANYWHERE],
        out_specs=VMEM_WHOLE,
        out_shape=rows_shape,
        compiler_params=params(4),
        cost_estimate=cost(1, 1),
        name="scale_rows",
    )(fraction.reshape(-1), rows, ahead, supply_there)
    near = pl.pallas_call(
        functools.partial(send_kernel, sizes, (0, 1), None),
        in_specs=[SMEM_WHOLE] * 3 + [VMEM_WHOLE] * 2,
        out_specs=[VMEM_WHOLE] * 2,
        out_shape=[send_shape] * 2,
        compiler_params=params(4),
        cost_estimate=cost(1, 1),
        name="send_near",
    )(in_cell, send_node, send_outlet, scaled, turns)
    arrived = [
        shifted(send, "region", SHIFTS[side]) for side, send in enumerate([*near, ahead])
    ]

    flow, demand = pl.pallas_call(
        functools.partial(node_flow_kernel, sizes),
        in_specs=[SMEM_WHOLE] + [VMEM_WHOLE] * 2 + [ANYWHERE],
        out_specs=[VMEM_WHOLE] * 2,
        out_shape=[
            pltpu.VMEM((nodes * sub, LANES), F32),
            jax.ShapeDtypeStruct((branches * nodes // LANES, LANES), F32),
        ],
        scratch_shapes=[pltpu.VMEM((branches, nodes, LANES), F32)],
        compiler_params=params(8),
        cost_estimate=cost(1, 1),
        name="node_flow",
    )(in_cell, scaled, turns, near[0])

    joined = jnp.concatenate([demand, supply_there])
    shared = lax.all_gather(joined, "dest", axis=0, tiled=True)
    theta, slot_theta = pl.pallas_call(
        functools.partial(theta_kernel, sizes, regions, commodities),
        in_specs=[VMEM_WHOLE] * 4,
        out_specs=[VMEM_WHOLE] * 2,
        out_shape=[
            jax.ShapeDtypeStruct((nodes // LANES, LANES), F32),
            jax.ShapeDtypeStruct((padded(cap) // LANES, LANES), F32),
        ],
        compiler_params=params(8),
        cost_estimate=cost(1, 1),
        name="theta",
    )(supply, shared, node_out, send_list)
    theta_there = to_neighbours(slot_theta)

    (behind,) = pl.pallas_call(
        functools.partial(scaled_send_kernel, sizes, 3),
        in_specs=[SMEM_WHOLE] * 3 + [VMEM_WHOLE] * 2,
        out_specs=[VMEM_WHOLE],
        out_shape=[send_shape],
        compiler_params=params(4),
        cost_estimate=cost(1, 1),
        name="send_scaled",
    )(theta.reshape(-1), send_node, send_outlet, flow, turns)
    home = pl.pallas_call(
        functools.partial(home_kernel, sizes),
        in_specs=[SMEM_WHOLE] * 2 + [VMEM_WHOLE] * 2 + [ANYWHERE],
        out_specs=VMEM_WHOLE,
        out_shape=rows_shape,
        compiler_params=params(4),
        cost_estimate=cost(1, 1),
        name="home_rows",
    )(source_node, source_outlet, turns, flow, behind)
    keep, home_theta = pl.pallas_call(
        functools.partial(keep_kernel, sizes),
        in_specs=[VMEM_WHOLE] * 4 + [ANYWHERE] * 2,
        out_specs=[VMEM_WHOLE] * 2,
        out_shape=[jax.ShapeDtypeStruct(per_cell, F32)] * 2,
        compiler_params=params(8),
        cost_estimate=cost(10000000, 1),
        name="keep",
    )(theta, node_in, node_out, fraction, behind, arrived[2])
    base = pl.pallas_call(
        functools.partial(base_kernel, sizes),
        in_specs=[SMEM_WHOLE] * 2 + [VMEM_WHOLE] * 2,
        out_specs=VMEM_WHOLE,
        out_shape=rows_shape,
        compiler_params=params(4),
        cost_estimate=cost(10000000, 1),
        name="base_rows",
    )(keep.reshape(-1), home_theta.reshape(-1), rows, home)

    base, theta_there, *arrived = lax.optimization_barrier((base, theta_there, *arrived))
    last = shifted(behind, "region", SHIFTS[3])
    scale = lax.all_gather(theta_there, "dest", axis=0, tiled=True)[: list_shape[0]]

    base = pl.pallas_call(
        functools.partial(land_kernel, sizes, (0, 1, 2)),
        in_specs=[SMEM_WHOLE] * 2 + [VMEM_WHOLE] * 4,
        out_specs=VMEM_WHOLE,
        out_shape=rows_shape,
        input_output_aliases={5: 0},
        compiler_params=params(4),
        cost_estimate=cost(100000000000, 1),
        name="land_first",
    )(scale.reshape(-1), land, *arrived, base)

    out, _ = pl.pallas_call(
        functools.partial(finish_kernel, sizes, (3,), chunk),
        in_specs=[SMEM_WHOLE] + [VMEM_WHOLE] * 2,
        out_specs=[ANYWHERE, VMEM_WHOLE],
        out_shape=[jax.ShapeDtypeStruct((cells, width), F32), rows_shape],
        scratch_shapes=[
            pltpu.VMEM((cells, width), F32),
            pltpu.SemaphoreType.DMA((cells // chunk,)),
        ],
        input_output_aliases={2: 1},
        compiler_params=params(12),
        cost_estimate=cost(cells * width, cells * row_bytes),
        name="finish",
    )(land, last, base)
    return out


def solution(mesh):
    return jax.shard_map(
        on_device,
        mesh=mesh,
        in_specs=(
            P("region", "dest"),
            P("region"),
            P("region"),
            P("region"),
            P(None, "region"),
            P(None, "region"),
            P("region", None),
            P("region", None),
            P("region", "dest"),
        ),
        out_specs=P("region", "dest"),
        check_vma=False,
    )
```

```python
import functools

import jax
import jax.numpy as jnp
from jax import lax
from jax.experimental import pallas as pl
from jax.experimental.pallas import tpu as pltpu
from jax.sharding import PartitionSpec as P

SHIFTS = (1, -1, 2, -2)
EXACT = lax.Precision.HIGHEST
LANES = 128
MIB = 1 << 20
F32 = jnp.float32
I32 = jnp.int32
VMEM_WHOLE = pl.BlockSpec(memory_space=pltpu.VMEM)
SMEM_WHOLE = pl.BlockSpec(memory_space=pltpu.SMEM)
ANYWHERE = pl.BlockSpec(memory_space=pl.ANY)


def to_neighbours(block):
    regions, members = lax.axis_size("region"), lax.axis_size("dest")
    route = [
        (r * members + d, (r + SHIFTS[d % 4]) % regions * members + d)
        for r in range(regions)
        for d in range(members)
    ]
    return lax.ppermute(block, ("region", "dest"), route)


def shifted(block, axis, distance):
    devices = range(lax.axis_size(axis))
    route = [((i - distance) % len(devices), i) for i in devices]
    return lax.ppermute(block, axis, route)


def partners(block, axis):
    count = lax.axis_size(axis)
    return [block] + [
        lax.ppermute(block, axis, [(i, i ^ other) for i in range(count)])
        for other in range(1, count)
    ]


def tree_sum(parts):
    while len(parts) > 1:
        parts = [parts[k] + parts[k + 1] for k in range(0, len(parts), 2)]
    return parts[0]


def params(mib):
    return pltpu.CompilerParams(vmem_limit_bytes=mib * MIB)


def cost(flops, moved):
    return pl.CostEstimate(flops=flops, bytes_accessed=moved, transcendentals=0)


def lane_sums(partial):
    sums = jnp.dot(
        partial, jnp.ones((LANES, LANES), F32), preferred_element_type=F32, precision=EXACT
    )
    row = lax.broadcasted_iota(I32, (LANES, LANES), 0)
    lane = lax.broadcasted_iota(I32, (LANES, LANES), 1)
    pieces = [
        jnp.sum(jnp.where(row == lane, sums[k : k + LANES, :], 0.0), axis=0, keepdims=True)
        for k in range(0, partial.shape[0], LANES)
    ]
    return jnp.concatenate(pieces, axis=0)


def stacked(row):
    return jnp.concatenate(
        [row[:, k : k + LANES] for k in range(0, row.shape[1], LANES)], axis=0
    )


def strung(rows):
    return jnp.concatenate([rows[k : k + 1, :] for k in range(rows.shape[0])], axis=1)


def row_of(ref, number, sub):
    if sub % 8 == 0:
        return ref.reshape(ref.shape[0] // sub, sub, LANES).at[number]
    return ref.at[pl.ds(pl.multiple_of(number * sub, sub), sub), :]


def padded(cap):
    return -(-cap // LANES) * LANES


def put_row(ref, row, value, fill):
    width = value.shape[1]
    for q in range(-(-width // LANES)):
        piece = value[:, q * LANES : min((q + 1) * LANES, width)]
        lack = LANES - piece.shape[1]
        if lack:
            piece = jnp.concatenate([piece, jnp.full((1, lack), fill, piece.dtype)], axis=1)
        ref[row + q : row + q + 1, :] = piece


def one_hot(index, count):
    rows = lax.broadcasted_iota(I32, (count, index.shape[1]), 0)
    return jnp.where(rows == index, 1.0, 0.0)


def in_parts(x):
    high = x.astype(jnp.bfloat16)
    rest = x - high.astype(F32)
    middle = rest.astype(jnp.bfloat16)
    low = (rest - middle.astype(F32)).astype(jnp.bfloat16)
    return jnp.concatenate([high, middle, low], axis=0)


def selected(values, choice, dims):
    count = values.shape[0]
    product = lax.dot_general(
        in_parts(values), choice.astype(jnp.bfloat16), (dims, ((), ())),
        preferred_element_type=F32,
    )
    return product[:count, :] + product[count : 2 * count, :] + product[2 * count :, :]


def look_up(table, index):
    picked = selected(table.T, one_hot(index // LANES, table.shape[0]), ((1,), (0,)))
    return jnp.sum(picked * one_hot(index % LANES, LANES), axis=0, keepdims=True)


def scatter(index, values, height):
    high = jnp.where(index >= 0, index // LANES, -1)
    low = jnp.where(index >= 0, index % LANES, -1)
    return selected(one_hot(high, height) * values, one_hot(low, LANES), ((1,), (1,)))


def home_cells(node_out, region_no, cells):
    here = (node_out >= 0) & (node_out // cells == region_no)
    return jnp.where(here, node_out % cells, -1)


def rows_of_group(x_ref, rows_ref, first, sub):
    total = None
    for q in range(sub):
        piece = x_ref[pl.ds(pl.multiple_of(first, 8), 8), q * LANES : (q + 1) * LANES]
        rows_ref[pl.ds(first * sub + q, 8, stride=sub), :] = piece
        total = piece if total is None else total + piece
    return total


def copies_in(source, target, sems, chunk):
    copies = [
        pltpu.make_async_copy(
            source.at[pl.ds(i * chunk, chunk), :], target.at[pl.ds(i * chunk, chunk), :], sems.at[i]
        )
        for i in range(target.shape[0] // chunk)
    ]
    for copy in copies:
        copy.start()
    return copies


def make_lists(
    sizes, node_in, node_out, send_list, recv_list,
    in_cell, send_node, send_outlet, land, source_node, source_outlet,
):
    cells, nodes, branches, cap, sub = sizes
    height = cells // LANES
    region_no = lax.axis_index("region")
    ids = lax.broadcasted_iota(I32, (1, nodes), 1).astype(F32) + 1.0
    number = jnp.zeros((height, LANES), F32)
    slot = jnp.zeros((height, LANES), F32)
    for j in range(branches):
        ins = node_in[j : j + 1, :]
        put_row(in_cell, j * (nodes // LANES), jnp.where(ins >= 0, ins, cells), cells)
        home = home_cells(node_out[j : j + 1, :], region_no, cells)
        here = scatter(home, ids, height)
        number = number + here
        slot = slot + jnp.where(here > 0.0, j + 1.0, 0.0)
    source_node[...] = jnp.maximum(number.astype(I32) - 1, 0)
    source_outlet[...] = slot.astype(I32) - 1
    per_side = padded(cap) // LANES
    for side in range(4):
        slots = send_list[side : side + 1, :]
        lands = recv_list[side : side + 1, :]
        put_row(send_node, side * per_side, jnp.where(slots >= 0, slots % nodes, 0), 0)
        put_row(send_outlet, side * per_side, jnp.where(slots >= 0, slots // nodes, -1), -1)
        put_row(land, side * per_side, jnp.where(lands >= 0, lands, cells), cells)


def cell_sum_kernel(chunk, sub, x_hbm, sum_ref, rows_ref, x, partial, sems):
    copies = copies_in(x_hbm, x, sems, chunk)
    zeros = rows_ref.shape[0] - sub
    rows_ref[zeros:, :] = jnp.zeros((sub, LANES), F32)
    for number, copy in enumerate(copies):
        copy.wait()

        def body(step, carry, number=number):
            for half in range(2):
                first = number * chunk + step * 16 + half * 8
                total = rows_of_group(x, rows_ref, first, sub)
                partial[pl.ds(pl.multiple_of(first, 8), 8), :] = total
            return carry

        lax.fori_loop(0, chunk // 16, body, 0)
        done = number + 1
        if done % 4 == 0:
            part = lane_sums(partial[(done - 4) * chunk : done * chunk, :])
            sum_ref[(done - 4) * chunk // LANES : done * chunk // LANES, :] = part


def turn_rows_kernel(sizes, chunk, x_hbm, after_ref, *rest):
    cells, nodes, branches, cap, sub = sizes
    lists, rows_ref, made, (x, sems) = rest[:4], rest[4], rest[5:11], rest[11:]
    copies = copies_in(x_hbm, x, sems, chunk)
    make_lists(sizes, *lists, *made)
    for number, copy in enumerate(copies):
        copy.wait()

        def body(step, carry, number=number):
            for half in range(2):
                rows_of_group(x, rows_ref, number * chunk + step * 16 + half * 8, sub)
            return carry

        lax.fori_loop(0, chunk // 16, body, 0)


def gathered_flow(node, in_cell, fraction, rows, sizes):
    cells, nodes, branches, cap, sub = sizes
    parts = []
    for i in range(branches):
        cell = in_cell[i * nodes + node]
        part = row_of(rows, cell, sub)[...]
        parts.append(part if fraction is None else part * fraction[cell])
    return tree_sum(parts)


def scale_kernel(sizes, fraction, rows, sent_ref, supply_ref, scaled):
    cells, nodes, branches, cap, sub = sizes

    def body(step, carry):
        first = step * 16
        values = [
            row_of(rows, first + i, sub)[...] * fraction[first + i] for i in range(16)
        ]
        for i in range(16):
            row_of(scaled, first + i, sub)[...] = values[i]
        return carry

    lax.fori_loop(0, cells // 16, body, 0)
    row_of(scaled, cells, sub)[...] = jnp.zeros((sub, LANES), F32)


def send_kernel(sizes, sides, fraction, in_cell, send_node, send_outlet, rows, turns, *sends):
    cells, nodes, branches, cap, sub = sizes
    batch = 8
    for side, send in zip(sides, sends):

        def body(step, carry, side=side, send=send):
            first = step * batch
            values = []
            for i in range(batch):
                slot = side * padded(cap) + first + i
                node = send_node[slot]
                value = gathered_flow(node, in_cell, fraction, rows, sizes)
                choice = row_of(turns, node, sub)[...]
                values.append(jnp.where(choice == send_outlet[slot], value, 0.0))
            for i in range(batch):
                row_of(send, first + i, sub)[...] = values[i]
            return carry

        lax.fori_loop(0, cap // batch, body, 0)


def scaled_send_kernel(sizes, side, theta, send_node, send_outlet, flow, turns, send):
    cells, nodes, branches, cap, sub = sizes
    batch = 8

    def body(step, carry):
        first = step * batch
        values = []
        for i in range(batch):
            slot = side * padded(cap) + first + i
            node = send_node[slot]
            value = row_of(flow, node, sub)[...] * theta[node]
            choice = row_of(turns, node, sub)[...]
            values.append(jnp.where(choice == send_outlet[slot], value, 0.0))
        for i in range(batch):
            row_of(send, first + i, sub)[...] = values[i]
        return carry

    lax.fori_loop(0, cap // batch, body, 0)


def node_flow_kernel(sizes, in_cell, scaled, turns, after_ref, flow, demand, partial):
    cells, nodes, branches, cap, sub = sizes

    def gather(step, carry):
        first = step * 8
        values = [
            gathered_flow(first + i, in_cell, None, scaled, sizes) for i in range(8)
        ]
        for i in range(8):
            row_of(flow, first + i, sub)[...] = values[i]
        return carry

    def measure(step, carry):
        for half in range(2):
            first = step * 16 + half * 8
            totals = [jnp.zeros((8, LANES), F32)] * branches
            for q in range(sub):
                at = pl.ds(first * sub + q, 8, stride=sub)
                value = flow[at, :]
                choice = turns[at, :]
                totals = [
                    total + jnp.where(choice == j, value, 0.0) for j, total in enumerate(totals)
                ]
            for j in range(branches):
                partial[j, pl.ds(pl.multiple_of(first, 8), 8), :] = totals[j]
        return carry

    lax.fori_loop(0, nodes // 8, gather, 0)
    lax.fori_loop(0, nodes // 16, measure, 0)
    per_outlet = nodes // LANES
    for j in range(branches):
        demand[j * per_outlet : (j + 1) * per_outlet, :] = lane_sums(partial[j])


def theta_kernel(
    sizes, regions, commodities, supply, shared, node_out, send_list, theta_out, slot_theta
):
    cells, nodes, branches, cap, sub = sizes
    per_outlet = nodes // LANES
    height = cells // LANES
    block = branches * per_outlet + height
    region_no = lax.axis_index("region")
    members = shared.shape[0] // block
    parts = [
        shared[d * block : d * block + branches * per_outlet, :] for d in range(members)
    ]
    demand = tree_sum(parts) * (1.0 / commodities)
    table = jnp.concatenate(
        [supply[...]]
        + [
            shared[d * block + branches * per_outlet : (d + 1) * block, :] for d in range(4)
        ],
        axis=0,
    )
    tall = jnp.ones((per_outlet, LANES), F32)
    for j in range(branches):
        outs = node_out[j : j + 1, :]
        cell = jnp.maximum(outs, 0)
        offset = (cell // cells + regions - region_no) % regions
        sector = jnp.zeros_like(offset)
        for d in range(4):
            sector = jnp.where(offset == (-SHIFTS[d]) % regions, d + 1, sector)
        room = stacked(look_up(table, sector * cells + cell % cells))
        ratio = room / jnp.maximum(demand[j * per_outlet : (j + 1) * per_outlet, :], room)
        tall = jnp.minimum(tall, jnp.where(stacked(outs) >= 0, ratio, 1.0))
    theta_out[...] = tall
    per_side = padded(cap) // LANES
    for side in range(3):
        slots = send_list[side : side + 1, :]
        there = look_up(tall, jnp.where(slots >= 0, slots % nodes, 0))
        put_row(slot_theta, side * per_side, there, 0.0)


def keep_kernel(
    sizes, theta_ref, node_in, node_out, fraction, sent_ref, arrived_ref, keep, home_theta
):
    cells, nodes, branches, cap, sub = sizes
    height = cells // LANES
    region_no = lax.axis_index("region")
    theta = strung(theta_ref[...])
    cell_theta = jnp.zeros((height, LANES), F32)
    into = jnp.zeros((height, LANES), F32)
    for j in range(branches):
        home = home_cells(node_out[j : j + 1, :], region_no, cells)
        cell_theta = cell_theta + scatter(node_in[j : j + 1, :], theta, height)
        into = into + scatter(home, theta, height)
    keep[...] = 1.0 - cell_theta * fraction[...]
    home_theta[...] = into


def home_kernel(sizes, source, outlet, turns, flow, sent_ref, theta_ref, home):
    cells, nodes, branches, cap, sub = sizes
    batch = 8

    def body(step, carry):
        first = step * batch
        values = []
        for i in range(batch):
            node = source[first + i]
            choice = row_of(turns, node, sub)[...]
            moved = row_of(flow, node, sub)[...]
            values.append(jnp.where(choice == outlet[first + i], moved, 0.0))
        for i in range(batch):
            row_of(home, first + i, sub)[...] = values[i]
        return carry

    lax.fori_loop(0, cells // batch, body, 0)


def base_kernel(sizes, keep, home_theta, rows, home, base):
    cells, nodes, branches, cap, sub = sizes
    batch = 8

    def body(step, carry):
        first = step * batch
        values = []
        for i in range(batch):
            cell = first + i
            kept = row_of(rows, cell, sub)[...] * keep[cell]
            values.append(kept + row_of(home, cell, sub)[...] * home_theta[cell])
        for i in range(batch):
            row_of(base, first + i, sub)[...] = values[i]
        return carry

    lax.fori_loop(0, cells // batch, body, 0)


def land_rows(sizes, sides, scale, land, received, base):
    cells, nodes, branches, cap, sub = sizes
    batch = 8
    for side, rows in zip(sides, received):

        def body(step, carry, side=side, rows=rows):
            first = step * batch
            stores = []
            for i in range(batch):
                slot = side * padded(cap) + first + i
                at = row_of(base, land[slot], sub)
                value = row_of(rows, first + i, sub)[...]
                if scale is not None:
                    value = value * scale[slot]
                stores.append((at, at[...] + value))
            for at, value in stores:
                at[...] = value
            return carry

        lax.fori_loop(0, cap // batch, body, 0)


def land_kernel(sizes, sides, scale, land, *rest):
    received, (base_in, base) = rest[: len(sides)], rest[len(sides) :]
    land_rows(sizes, sides, scale, land, received, base)


def finish_kernel(sizes, sides, chunk, land, *rest):
    cells, nodes, branches, cap, sub = sizes
    received, (base_in, out, base, staged, sems) = rest[: len(sides)], rest[len(sides) :]
    land_rows(sizes, sides, None, land, received, base)
    copies = []
    for number in range(cells // chunk):

        def body(step, carry, number=number):
            for half in range(2):
                first = number * chunk + step * 16 + half * 8
                for q in range(sub):
                    staged[
                        pl.ds(pl.multiple_of(first, 8), 8), q * LANES : (q + 1) * LANES
                    ] = base[pl.ds(first * sub + q, 8, stride=sub), :]
            return carry

        lax.fori_loop(0, chunk // 16, body, 0)
        at = pl.ds(number * chunk, chunk)
        copies.append(
            pltpu.make_async_copy(staged.at[at, :], out.at[at, :], sems.at[number])
        )
        copies[-1].start()
    for copy in copies:
        copy.wait()


def on_device(occupancy, capacity, jam, wave, node_in, node_out, send_list, recv_list, turn):
    cells, width = occupancy.shape
    branches, nodes = node_in.shape
    cap = send_list.shape[1]
    sub = width // LANES
    sizes = (cells, nodes, branches, cap, sub)
    regions = lax.axis_size("region")
    commodities = width * lax.axis_size("dest")
    height = cells // LANES
    per_cell = (height, LANES)
    list_shape = (4 * padded(cap) // LANES, LANES)
    chunk = 128
    row_bytes = width * 4
    occupancy = pltpu.with_memory_space_constraint(occupancy, pltpu.HBM)
    turn = pltpu.with_memory_space_constraint(turn, pltpu.HBM)

    local_sum, rows = pl.pallas_call(
        functools.partial(cell_sum_kernel, chunk, sub),
        in_specs=[ANYWHERE],
        out_specs=[VMEM_WHOLE] * 2,
        out_shape=[
            jax.ShapeDtypeStruct(per_cell, F32),
            pltpu.VMEM(((cells + 1) * sub, LANES), F32),
        ],
        scratch_shapes=[
            pltpu.VMEM((cells, width), F32),
            pltpu.VMEM((cells, LANES), F32),
            pltpu.SemaphoreType.DMA((cells // chunk,)),
        ],
        compiler_params=params(14),
        cost_estimate=cost(cells * width, cells * row_bytes),
        name="cell_sum",
    )(occupancy)

    sums = partners(local_sum, "dest")

    turns, *lists = pl.pallas_call(
        functools.partial(turn_rows_kernel, sizes, chunk),
        in_specs=[ANYWHERE] * 2 + [VMEM_WHOLE] * 4,
        out_specs=[VMEM_WHOLE] * 7,
        out_shape=[
            pltpu.VMEM((nodes * sub, LANES), I32),
            jax.ShapeDtypeStruct((branches * nodes // LANES, LANES), I32),
        ]
        + [jax.ShapeDtypeStruct(list_shape, I32)] * 3
        + [jax.ShapeDtypeStruct(per_cell, I32)] * 2,
        scratch_shapes=[
            pltpu.VMEM((nodes, width), I32),
            pltpu.SemaphoreType.DMA((nodes // chunk,)),
        ],
        compiler_params=params(8),
        cost_estimate=cost(0, nodes * row_bytes),
        name="turn_rows",
    )(turn, local_sum, node_in, node_out, send_list, recv_list)
    in_cell, send_node, send_outlet, land, source_node, source_outlet = (
        x.reshape(-1) for x in lists
    )

    turns, *sums = lax.optimization_barrier((turns, *sums))
    vehicles = tree_sum(sums) / commodities
    cap_of = capacity.reshape(per_cell)
    fraction = jnp.minimum(vehicles, cap_of) / vehicles
    supply = jnp.minimum(cap_of, wave.reshape(per_cell) * (jam.reshape(per_cell) - vehicles))
    rows_shape = pltpu.VMEM(((cells + 1) * sub, LANES), F32)
    send_shape = pltpu.VMEM((cap * sub, LANES), F32)

    supply_there = to_neighbours(supply)
    weights = jnp.concatenate([fraction.reshape(-1), jnp.zeros((LANES,), F32)])
    (ahead,) = pl.pallas_call(
        functools.partial(send_kernel, sizes, (2,)),
        in_specs=[SMEM_WHOLE] * 4 + [VMEM_WHOLE] * 2,
        out_specs=[VMEM_WHOLE],
        out_shape=[send_shape],
        compiler_params=params(4),
        cost_estimate=cost(1, 1),
        name="send_ahead",
    )(weights, in_cell, send_node, send_outlet, rows, turns)
    scaled = pl.pallas_call(
        functools.partial(scale_kernel, sizes),
        in_specs=[SMEM_WHOLE, VMEM_WHOLE, ANYWHERE, ANYWHERE],
        out_specs=VMEM_WHOLE,
        out_shape=rows_shape,
        compiler_params=params(4),
        cost_estimate=cost(1, 1),
        name="scale_rows",
    )(fraction.reshape(-1), rows, ahead, supply_there)
    near = pl.pallas_call(
        functools.partial(send_kernel, sizes, (0, 1), None),
        in_specs=[SMEM_WHOLE] * 3 + [VMEM_WHOLE] * 2,
        out_specs=[VMEM_WHOLE] * 2,
        out_shape=[send_shape] * 2,
        compiler_params=params(4),
        cost_estimate=cost(1, 1),
        name="send_near",
    )(in_cell, send_node, send_outlet, scaled, turns)
    arrived = [
        shifted(send, "region", SHIFTS[side]) for side, send in enumerate([*near, ahead])
    ]

    flow, demand = pl.pallas_call(
        functools.partial(node_flow_kernel, sizes),
        in_specs=[SMEM_WHOLE] + [VMEM_WHOLE] * 2 + [ANYWHERE],
        out_specs=[VMEM_WHOLE] * 2,
        out_shape=[
            pltpu.VMEM((nodes * sub, LANES), F32),
            jax.ShapeDtypeStruct((branches * nodes // LANES, LANES), F32),
        ],
        scratch_shapes=[pltpu.VMEM((branches, nodes, LANES), F32)],
        compiler_params=params(8),
        cost_estimate=cost(1, 1),
        name="node_flow",
    )(in_cell, scaled, turns, near[0])

    joined = jnp.concatenate([demand, supply_there])
    shared = lax.all_gather(joined, "dest", axis=0, tiled=True)
    theta, slot_theta = pl.pallas_call(
        functools.partial(theta_kernel, sizes, regions, commodities),
        in_specs=[VMEM_WHOLE] * 4,
        out_specs=[VMEM_WHOLE] * 2,
        out_shape=[
            jax.ShapeDtypeStruct((nodes // LANES, LANES), F32),
            jax.ShapeDtypeStruct((3 * padded(cap) // LANES, LANES), F32),
        ],
        compiler_params=params(8),
        cost_estimate=cost(1, 1),
        name="theta",
    )(supply, shared, node_out, send_list)
    per_side = padded(cap) // LANES
    theta_there = [
        shifted(slot_theta[side * per_side : (side + 1) * per_side], "region", SHIFTS[side])
        for side in range(3)
    ]

    (behind,) = pl.pallas_call(
        functools.partial(scaled_send_kernel, sizes, 3),
        in_specs=[SMEM_WHOLE] * 3 + [VMEM_WHOLE] * 2,
        out_specs=[VMEM_WHOLE],
        out_shape=[send_shape],
        compiler_params=params(4),
        cost_estimate=cost(1, 1),
        name="send_scaled",
    )(theta.reshape(-1), send_node, send_outlet, flow, turns)
    home = pl.pallas_call(
        functools.partial(home_kernel, sizes),
        in_specs=[SMEM_WHOLE] * 2 + [VMEM_WHOLE] * 2 + [ANYWHERE] * 2,
        out_specs=VMEM_WHOLE,
        out_shape=rows_shape,
        compiler_params=params(4),
        cost_estimate=cost(1, 1),
        name="home_rows",
    )(source_node, source_outlet, turns, flow, behind, theta_there[2])
    keep, home_theta = pl.pallas_call(
        functools.partial(keep_kernel, sizes),
        in_specs=[VMEM_WHOLE] * 4 + [ANYWHERE] * 2,
        out_specs=[VMEM_WHOLE] * 2,
        out_shape=[jax.ShapeDtypeStruct(per_cell, F32)] * 2,
        compiler_params=params(8),
        cost_estimate=cost(10000000, 1),
        name="keep",
    )(theta, node_in, node_out, fraction, behind, arrived[2])
    base = pl.pallas_call(
        functools.partial(base_kernel, sizes),
        in_specs=[SMEM_WHOLE] * 2 + [VMEM_WHOLE] * 2,
        out_specs=VMEM_WHOLE,
        out_shape=rows_shape,
        compiler_params=params(4),
        cost_estimate=cost(10000000, 1),
        name="base_rows",
    )(keep.reshape(-1), home_theta.reshape(-1), rows, home)

    base, theta_there, *arrived = lax.optimization_barrier((base, theta_there, *arrived))
    last = shifted(behind, "region", SHIFTS[3])
    scale = jnp.concatenate(theta_there)

    base = pl.pallas_call(
        functools.partial(land_kernel, sizes, (0, 1, 2)),
        in_specs=[SMEM_WHOLE] * 2 + [VMEM_WHOLE] * 4,
        out_specs=VMEM_WHOLE,
        out_shape=rows_shape,
        input_output_aliases={5: 0},
        compiler_params=params(4),
        cost_estimate=cost(100000000000, 1),
        name="land_first",
    )(scale.reshape(-1), land, *arrived, base)

    out, _ = pl.pallas_call(
        functools.partial(finish_kernel, sizes, (3,), chunk),
        in_specs=[SMEM_WHOLE] + [VMEM_WHOLE] * 2,
        out_specs=[ANYWHERE, VMEM_WHOLE],
        out_shape=[jax.ShapeDtypeStruct((cells, width), F32), rows_shape],
        scratch_shapes=[
            pltpu.VMEM((cells, width), F32),
            pltpu.SemaphoreType.DMA((cells // chunk,)),
        ],
        input_output_aliases={2: 1},
        compiler_params=params(12),
        cost_estimate=cost(cells * width, cells * row_bytes),
        name="finish",
    )(land, last, base)
    return out


def solution(mesh):
    return jax.shard_map(
        on_device,
        mesh=mesh,
        in_specs=(
            P("region", "dest"),
            P("region"),
            P("region"),
            P("region"),
            P(None, "region"),
            P(None, "region"),
            P("region", None),
            P("region", None),
            P("region", "dest"),
        ),
        out_specs=P("region", "dest"),
        check_vma=False,
    )
```

```python
import functools

import jax
import jax.numpy as jnp
from jax import lax
from jax.experimental import pallas as pl
from jax.experimental.pallas import tpu as pltpu
from jax.sharding import PartitionSpec as P

SHIFTS = (1, -1, 2, -2)
EXACT = lax.Precision.HIGHEST
LANES = 128
MIB = 1 << 20
F32 = jnp.float32
I32 = jnp.int32
VMEM_WHOLE = pl.BlockSpec(memory_space=pltpu.VMEM)
SMEM_WHOLE = pl.BlockSpec(memory_space=pltpu.SMEM)
ANYWHERE = pl.BlockSpec(memory_space=pl.ANY)


def to_neighbours(block):
    regions, members = lax.axis_size("region"), lax.axis_size("dest")
    route = [
        (r * members + d, (r + SHIFTS[d % 4]) % regions * members + d)
        for r in range(regions)
        for d in range(members)
    ]
    return lax.ppermute(block, ("region", "dest"), route)


def shifted(block, axis, distance):
    devices = range(lax.axis_size(axis))
    route = [((i - distance) % len(devices), i) for i in devices]
    return lax.ppermute(block, axis, route)


def partners(block, axis):
    count = lax.axis_size(axis)
    return [block] + [
        lax.ppermute(block, axis, [(i, i ^ other) for i in range(count)])
        for other in range(1, count)
    ]


def tree_sum(parts):
    while len(parts) > 1:
        parts = [parts[k] + parts[k + 1] for k in range(0, len(parts), 2)]
    return parts[0]


def params(mib):
    return pltpu.CompilerParams(vmem_limit_bytes=mib * MIB)


def cost(flops, moved):
    return pl.CostEstimate(flops=flops, bytes_accessed=moved, transcendentals=0)


def lane_sums(partial):
    sums = jnp.dot(
        partial, jnp.ones((LANES, LANES), F32), preferred_element_type=F32, precision=EXACT
    )
    row = lax.broadcasted_iota(I32, (LANES, LANES), 0)
    lane = lax.broadcasted_iota(I32, (LANES, LANES), 1)
    pieces = [
        jnp.sum(jnp.where(row == lane, sums[k : k + LANES, :], 0.0), axis=0, keepdims=True)
        for k in range(0, partial.shape[0], LANES)
    ]
    return jnp.concatenate(pieces, axis=0)


def stacked(row):
    return jnp.concatenate(
        [row[:, k : k + LANES] for k in range(0, row.shape[1], LANES)], axis=0
    )


def strung(rows):
    return jnp.concatenate([rows[k : k + 1, :] for k in range(rows.shape[0])], axis=1)


def row_of(ref, number, sub):
    if sub % 8 == 0:
        return ref.reshape(ref.shape[0] // sub, sub, LANES).at[number]
    return ref.at[pl.ds(pl.multiple_of(number * sub, sub), sub), :]


def padded(cap):
    return -(-cap // LANES) * LANES


def put_row(ref, row, value, fill):
    width = value.shape[1]
    for q in range(-(-width // LANES)):
        piece = value[:, q * LANES : min((q + 1) * LANES, width)]
        lack = LANES - piece.shape[1]
        if lack:
            piece = jnp.concatenate([piece, jnp.full((1, lack), fill, piece.dtype)], axis=1)
        ref[row + q : row + q + 1, :] = piece


def one_hot(index, count):
    rows = lax.broadcasted_iota(I32, (count, index.shape[1]), 0)
    return jnp.where(rows == index, 1.0, 0.0)


def in_parts(x):
    high = x.astype(jnp.bfloat16)
    rest = x - high.astype(F32)
    middle = rest.astype(jnp.bfloat16)
    low = (rest - middle.astype(F32)).astype(jnp.bfloat16)
    return jnp.concatenate([high, middle, low], axis=0)


def selected(values, choice, dims):
    count = values.shape[0]
    product = lax.dot_general(
        in_parts(values), choice.astype(jnp.bfloat16), (dims, ((), ())),
        preferred_element_type=F32,
    )
    return product[:count, :] + product[count : 2 * count, :] + product[2 * count :, :]


def look_up(table, index):
    picked = selected(table.T, one_hot(index // LANES, table.shape[0]), ((1,), (0,)))
    return jnp.sum(picked * one_hot(index % LANES, LANES), axis=0, keepdims=True)


def scatter(index, values, height):
    high = jnp.where(index >= 0, index // LANES, -1)
    low = jnp.where(index >= 0, index % LANES, -1)
    return selected(one_hot(high, height) * values, one_hot(low, LANES), ((1,), (1,)))


def home_cells(node_out, region_no, cells):
    here = (node_out >= 0) & (node_out // cells == region_no)
    return jnp.where(here, node_out % cells, -1)


def rows_of_group(x_ref, rows_ref, first, sub):
    total = None
    for q in range(sub):
        piece = x_ref[pl.ds(pl.multiple_of(first, 8), 8), q * LANES : (q + 1) * LANES]
        rows_ref[pl.ds(first * sub + q, 8, stride=sub), :] = piece
        total = piece if total is None else total + piece
    return total


def copies_in(source, target, sems, chunk):
    copies = [
        pltpu.make_async_copy(
            source.at[pl.ds(i * chunk, chunk), :], target.at[pl.ds(i * chunk, chunk), :], sems.at[i]
        )
        for i in range(target.shape[0] // chunk)
    ]
    for copy in copies:
        copy.start()
    return copies


def make_lists(
    sizes, node_in, node_out, send_list, recv_list,
    in_cell, send_node, send_outlet, land, source_node, source_outlet,
):
    cells, nodes, branches, cap, sub = sizes
    height = cells // LANES
    region_no = lax.axis_index("region")
    ids = lax.broadcasted_iota(I32, (1, nodes), 1).astype(F32) + 1.0
    number = jnp.zeros((height, LANES), F32)
    slot = jnp.zeros((height, LANES), F32)
    for j in range(branches):
        ins = node_in[j : j + 1, :]
        put_row(in_cell, j * (nodes // LANES), jnp.where(ins >= 0, ins, cells), cells)
        home = home_cells(node_out[j : j + 1, :], region_no, cells)
        here = scatter(home, ids, height)
        number = number + here
        slot = slot + jnp.where(here > 0.0, j + 1.0, 0.0)
    source_node[...] = jnp.maximum(number.astype(I32) - 1, 0)
    source_outlet[...] = slot.astype(I32) - 1
    per_side = padded(cap) // LANES
    for side in range(4):
        slots = send_list[side : side + 1, :]
        lands = recv_list[side : side + 1, :]
        put_row(send_node, side * per_side, jnp.where(slots >= 0, slots % nodes, 0), 0)
        put_row(send_outlet, side * per_side, jnp.where(slots >= 0, slots // nodes, -1), -1)
        put_row(land, side * per_side, jnp.where(lands >= 0, lands, cells), cells)


def cell_sum_kernel(chunk, sub, x_hbm, sum_ref, rows_ref, x, partial, sems):
    copies = copies_in(x_hbm, x, sems, chunk)
    zeros = rows_ref.shape[0] - sub
    rows_ref[zeros:, :] = jnp.zeros((sub, LANES), F32)
    for number, copy in enumerate(copies):
        copy.wait()

        def body(step, carry, number=number):
            for half in range(2):
                first = number * chunk + step * 16 + half * 8
                total = rows_of_group(x, rows_ref, first, sub)
                partial[pl.ds(pl.multiple_of(first, 8), 8), :] = total
            return carry

        lax.fori_loop(0, chunk // 16, body, 0)
    sum_ref[...] = lane_sums(partial[...])


def turn_rows_kernel(sizes, chunk, x_hbm, after_ref, *rest):
    cells, nodes, branches, cap, sub = sizes
    lists, rows_ref, made, (x, sems) = rest[:4], rest[4], rest[5:11], rest[11:]
    copies = copies_in(x_hbm, x, sems, chunk)
    make_lists(sizes, *lists, *made)
    for number, copy in enumerate(copies):
        copy.wait()

        def body(step, carry, number=number):
            for half in range(2):
                rows_of_group(x, rows_ref, number * chunk + step * 16 + half * 8, sub)
            return carry

        lax.fori_loop(0, chunk // 16, body, 0)


def gathered_flow(node, in_cell, fraction, rows, sizes):
    cells, nodes, branches, cap, sub = sizes
    parts = []
    for i in range(branches):
        cell = in_cell[i * nodes + node]
        part = row_of(rows, cell, sub)[...]
        parts.append(part if fraction is None else part * fraction[cell])
    return tree_sum(parts)


def scale_kernel(sizes, fraction, rows, sent_ref, supply_ref, scaled):
    cells, nodes, branches, cap, sub = sizes

    def body(step, carry):
        first = step * 16
        values = [
            row_of(rows, first + i, sub)[...] * fraction[first + i] for i in range(16)
        ]
        for i in range(16):
            row_of(scaled, first + i, sub)[...] = values[i]
        return carry

    lax.fori_loop(0, cells // 16, body, 0)
    row_of(scaled, cells, sub)[...] = jnp.zeros((sub, LANES), F32)


def send_kernel(sizes, parts, fraction, in_cell, send_node, send_outlet, rows, turns, *sends):
    cells, nodes, branches, cap, sub = sizes
    batch = 8
    for (side, start, count), send in zip(parts, sends):

        def body(step, carry, side=side, start=start, send=send):
            first = step * batch
            values = []
            for i in range(batch):
                slot = side * padded(cap) + start + first + i
                node = send_node[slot]
                value = gathered_flow(node, in_cell, fraction, rows, sizes)
                choice = row_of(turns, node, sub)[...]
                values.append(jnp.where(choice == send_outlet[slot], value, 0.0))
            for i in range(batch):
                row_of(send, first + i, sub)[...] = values[i]
            return carry

        lax.fori_loop(0, count // batch, body, 0)


def scaled_send_kernel(
    sizes, part, theta, send_node, send_outlet, flow, turns, after_ref, send
):
    cells, nodes, branches, cap, sub = sizes
    side, start, count = part
    batch = 8

    def body(step, carry):
        first = step * batch
        values = []
        for i in range(batch):
            slot = side * padded(cap) + start + first + i
            node = send_node[slot]
            value = row_of(flow, node, sub)[...] * theta[node]
            choice = row_of(turns, node, sub)[...]
            values.append(jnp.where(choice == send_outlet[slot], value, 0.0))
        for i in range(batch):
            row_of(send, first + i, sub)[...] = values[i]
        return carry

    lax.fori_loop(0, count // batch, body, 0)


def node_flow_kernel(sizes, in_cell, scaled, turns, after_ref, flow, demand, partial):
    cells, nodes, branches, cap, sub = sizes

    def gather(step, carry):
        first = step * 8
        values = [
            gathered_flow(first + i, in_cell, None, scaled, sizes) for i in range(8)
        ]
        for i in range(8):
            row_of(flow, first + i, sub)[...] = values[i]
        return carry

    def measure(step, carry):
        for half in range(2):
            first = step * 16 + half * 8
            totals = [jnp.zeros((8, LANES), F32)] * branches
            for q in range(sub):
                at = pl.ds(first * sub + q, 8, stride=sub)
                value = flow[at, :]
                choice = turns[at, :]
                totals = [
                    total + jnp.where(choice == j, value, 0.0) for j, total in enumerate(totals)
                ]
            for j in range(branches):
                partial[j, pl.ds(pl.multiple_of(first, 8), 8), :] = totals[j]
        return carry

    lax.fori_loop(0, nodes // 8, gather, 0)
    lax.fori_loop(0, nodes // 16, measure, 0)
    per_outlet = nodes // LANES
    for j in range(branches):
        demand[j * per_outlet : (j + 1) * per_outlet, :] = lane_sums(partial[j])


def theta_kernel(
    sizes, regions, commodities, supply, shared, node_out, send_list, theta_out, slot_theta
):
    cells, nodes, branches, cap, sub = sizes
    per_outlet = nodes // LANES
    height = cells // LANES
    block = branches * per_outlet + height
    region_no = lax.axis_index("region")
    members = shared.shape[0] // block
    parts = [
        shared[d * block : d * block + branches * per_outlet, :] for d in range(members)
    ]
    demand = tree_sum(parts) * (1.0 / commodities)
    table = jnp.concatenate(
        [supply[...]]
        + [
            shared[d * block + branches * per_outlet : (d + 1) * block, :] for d in range(4)
        ],
        axis=0,
    )
    tall = jnp.ones((per_outlet, LANES), F32)
    for j in range(branches):
        outs = node_out[j : j + 1, :]
        cell = jnp.maximum(outs, 0)
        offset = (cell // cells + regions - region_no) % regions
        sector = jnp.zeros_like(offset)
        for d in range(4):
            sector = jnp.where(offset == (-SHIFTS[d]) % regions, d + 1, sector)
        room = stacked(look_up(table, sector * cells + cell % cells))
        ratio = room / jnp.maximum(demand[j * per_outlet : (j + 1) * per_outlet, :], room)
        tall = jnp.minimum(tall, jnp.where(stacked(outs) >= 0, ratio, 1.0))
    theta_out[...] = tall
    slots = send_list[pl.ds(lax.axis_index("dest") % 4, 1), :]
    put_row(slot_theta, 0, look_up(tall, jnp.where(slots >= 0, slots % nodes, 0)), 0.0)


def keep_kernel(
    sizes, theta_ref, node_in, node_out, fraction, sent_ref, arrived_ref, keep, home_theta
):
    cells, nodes, branches, cap, sub = sizes
    height = cells // LANES
    region_no = lax.axis_index("region")
    theta = strung(theta_ref[...])
    cell_theta = jnp.zeros((height, LANES), F32)
    into = jnp.zeros((height, LANES), F32)
    for j in range(branches):
        home = home_cells(node_out[j : j + 1, :], region_no, cells)
        cell_theta = cell_theta + scatter(node_in[j : j + 1, :], theta, height)
        into = into + scatter(home, theta, height)
    keep[...] = 1.0 - cell_theta * fraction[...]
    home_theta[...] = into


def home_kernel(sizes, source, outlet, turns, flow, after_ref, home):
    cells, nodes, branches, cap, sub = sizes
    batch = 8

    def body(step, carry):
        first = step * batch
        values = []
        for i in range(batch):
            node = source[first + i]
            choice = row_of(turns, node, sub)[...]
            moved = row_of(flow, node, sub)[...]
            values.append(jnp.where(choice == outlet[first + i], moved, 0.0))
        for i in range(batch):
            row_of(home, first + i, sub)[...] = values[i]
        return carry

    lax.fori_loop(0, cells // batch, body, 0)


def base_kernel(sizes, keep, home_theta, rows, home, base):
    cells, nodes, branches, cap, sub = sizes
    batch = 8

    def body(step, carry):
        first = step * batch
        values = []
        for i in range(batch):
            cell = first + i
            kept = row_of(rows, cell, sub)[...] * keep[cell]
            values.append(kept + row_of(home, cell, sub)[...] * home_theta[cell])
        for i in range(batch):
            row_of(base, first + i, sub)[...] = values[i]
        return carry

    lax.fori_loop(0, cells // batch, body, 0)


def land_rows(sizes, parts, scale, land, received, base):
    cells, nodes, branches, cap, sub = sizes
    batch = 8
    for (side, start, count), rows in zip(parts, received):

        def body(step, carry, side=side, start=start, rows=rows):
            first = step * batch
            stores = []
            for i in range(batch):
                slot = side * padded(cap) + start + first + i
                at = row_of(base, land[slot], sub)
                value = row_of(rows, first + i, sub)[...]
                if scale is not None:
                    value = value * scale[slot]
                stores.append((at, at[...] + value))
            for at, value in stores:
                at[...] = value
            return carry

        lax.fori_loop(0, count // batch, body, 0)


def land_kernel(sizes, parts, scale, land, *rest):
    received, (base_in, base) = rest[: len(parts)], rest[len(parts) :]
    land_rows(sizes, parts, scale, land, received, base)


def finish_kernel(sizes, parts, chunk, land, *rest):
    cells, nodes, branches, cap, sub = sizes
    received, (base_in, out, base, staged, sems) = rest[: len(parts)], rest[len(parts) :]
    land_rows(sizes, parts, None, land, received, base)
    copies = []
    for number in range(cells // chunk):

        def body(step, carry, number=number):
            for half in range(2):
                first = number * chunk + step * 16 + half * 8
                for q in range(sub):
                    staged[
                        pl.ds(pl.multiple_of(first, 8), 8), q * LANES : (q + 1) * LANES
                    ] = base[pl.ds(first * sub + q, 8, stride=sub), :]
            return carry

        lax.fori_loop(0, chunk // 16, body, 0)
        at = pl.ds(number * chunk, chunk)
        copies.append(
            pltpu.make_async_copy(staged.at[at, :], out.at[at, :], sems.at[number])
        )
        copies[-1].start()
    for copy in copies:
        copy.wait()


def on_device(occupancy, capacity, jam, wave, node_in, node_out, send_list, recv_list, turn):
    cells, width = occupancy.shape
    branches, nodes = node_in.shape
    cap = send_list.shape[1]
    sub = width // LANES
    sizes = (cells, nodes, branches, cap, sub)
    regions = lax.axis_size("region")
    commodities = width * lax.axis_size("dest")
    height = cells // LANES
    per_cell = (height, LANES)
    list_shape = (4 * padded(cap) // LANES, LANES)
    chunk = 128
    row_bytes = width * 4
    occupancy = pltpu.with_memory_space_constraint(occupancy, pltpu.HBM)
    turn = pltpu.with_memory_space_constraint(turn, pltpu.HBM)

    local_sum, rows = pl.pallas_call(
        functools.partial(cell_sum_kernel, chunk, sub),
        in_specs=[ANYWHERE],
        out_specs=[VMEM_WHOLE] * 2,
        out_shape=[
            jax.ShapeDtypeStruct(per_cell, F32),
            pltpu.VMEM(((cells + 1) * sub, LANES), F32),
        ],
        scratch_shapes=[
            pltpu.VMEM((cells, width), F32),
            pltpu.VMEM((cells, LANES), F32),
            pltpu.SemaphoreType.DMA((cells // chunk,)),
        ],
        compiler_params=params(14),
        cost_estimate=cost(cells * width, cells * row_bytes),
        name="cell_sum",
    )(occupancy)

    sums = partners(local_sum, "dest")

    turns, *lists = pl.pallas_call(
        functools.partial(turn_rows_kernel, sizes, chunk),
        in_specs=[ANYWHERE] * 2 + [VMEM_WHOLE] * 4,
        out_specs=[VMEM_WHOLE] * 7,
        out_shape=[
            pltpu.VMEM((nodes * sub, LANES), I32),
            jax.ShapeDtypeStruct((branches * nodes // LANES, LANES), I32),
        ]
        + [jax.ShapeDtypeStruct(list_shape, I32)] * 3
        + [jax.ShapeDtypeStruct(per_cell, I32)] * 2,
        scratch_shapes=[
            pltpu.VMEM((nodes, width), I32),
            pltpu.SemaphoreType.DMA((nodes // chunk,)),
        ],
        compiler_params=params(8),
        cost_estimate=cost(0, nodes * row_bytes),
        name="turn_rows",
    )(turn, local_sum, node_in, node_out, send_list, recv_list)
    in_cell, send_node, send_outlet, land, source_node, source_outlet = (
        x.reshape(-1) for x in lists
    )

    turns, *sums = lax.optimization_barrier((turns, *sums))
    vehicles = tree_sum(sums) / commodities
    cap_of = capacity.reshape(per_cell)
    fraction = jnp.minimum(vehicles, cap_of) / vehicles
    supply = jnp.minimum(cap_of, wave.reshape(per_cell) * (jam.reshape(per_cell) - vehicles))
    rows_shape = pltpu.VMEM(((cells + 1) * sub, LANES), F32)
    early = cap * 2 // 3 // 8 * 8
    whole = [(side, 0, cap) for side in range(4)]
    parts = (*whole[:3], (3, 0, early))
    last_part = (3, early, cap - early)

    def send_shape(part):
        return pltpu.VMEM((part[2] * sub, LANES), F32)


    supply_there = to_neighbours(supply)
    weights = jnp.concatenate([fraction.reshape(-1), jnp.zeros((LANES,), F32)])
    (ahead,) = pl.pallas_call(
        functools.partial(send_kernel, sizes, parts[2:3]),
        in_specs=[SMEM_WHOLE] * 4 + [VMEM_WHOLE] * 2,
        out_specs=[VMEM_WHOLE],
        out_shape=[send_shape(parts[2])],
        compiler_params=params(4),
        cost_estimate=cost(1, 1),
        name="send_ahead",
    )(weights, in_cell, send_node, send_outlet, rows, turns)
    scaled = pl.pallas_call(
        functools.partial(scale_kernel, sizes),
        in_specs=[SMEM_WHOLE, VMEM_WHOLE, ANYWHERE, ANYWHERE],
        out_specs=VMEM_WHOLE,
        out_shape=rows_shape,
        compiler_params=params(4),
        cost_estimate=cost(1, 1),
        name="scale_rows",
    )(fraction.reshape(-1), rows, ahead, supply_there)
    near = pl.pallas_call(
        functools.partial(send_kernel, sizes, (parts[0], parts[1], parts[3]), None),
        in_specs=[SMEM_WHOLE] * 3 + [VMEM_WHOLE] * 2,
        out_specs=[VMEM_WHOLE] * 3,
        out_shape=[send_shape(part) for part in (parts[0], parts[1], parts[3])],
        compiler_params=params(4),
        cost_estimate=cost(1, 1),
        name="send_near",
    )(in_cell, send_node, send_outlet, scaled, turns)
    arrived = [
        shifted(send, "region", SHIFTS[side]) for side, send in enumerate([near[0], near[1], ahead, near[2]])
    ]

    flow, demand = pl.pallas_call(
        functools.partial(node_flow_kernel, sizes),
        in_specs=[SMEM_WHOLE] + [VMEM_WHOLE] * 2 + [ANYWHERE],
        out_specs=[VMEM_WHOLE] * 2,
        out_shape=[
            pltpu.VMEM((nodes * sub, LANES), F32),
            jax.ShapeDtypeStruct((branches * nodes // LANES, LANES), F32),
        ],
        scratch_shapes=[pltpu.VMEM((branches, nodes, LANES), F32)],
        compiler_params=params(8),
        cost_estimate=cost(1, 1),
        name="node_flow",
    )(in_cell, scaled, turns, near[0])

    joined = jnp.concatenate([demand, supply_there])
    shared = lax.all_gather(joined, "dest", axis=0, tiled=True)
    theta, slot_theta = pl.pallas_call(
        functools.partial(theta_kernel, sizes, regions, commodities),
        in_specs=[VMEM_WHOLE] * 4,
        out_specs=[VMEM_WHOLE] * 2,
        out_shape=[
            jax.ShapeDtypeStruct((nodes // LANES, LANES), F32),
            jax.ShapeDtypeStruct((padded(cap) // LANES, LANES), F32),
        ],
        compiler_params=params(8),
        cost_estimate=cost(1, 1),
        name="theta",
    )(supply, shared, node_out, send_list)
    theta_there = to_neighbours(slot_theta)

    home = pl.pallas_call(
        functools.partial(home_kernel, sizes),
        in_specs=[SMEM_WHOLE] * 2 + [VMEM_WHOLE] * 2 + [ANYWHERE],
        out_specs=VMEM_WHOLE,
        out_shape=rows_shape,
        compiler_params=params(4),
        cost_estimate=cost(1, 1),
        name="home_rows",
    )(source_node, source_outlet, turns, flow, slot_theta)
    (behind,) = pl.pallas_call(
        functools.partial(scaled_send_kernel, sizes, last_part),
        in_specs=[SMEM_WHOLE] * 3 + [VMEM_WHOLE] * 2 + [ANYWHERE],
        out_specs=[VMEM_WHOLE],
        out_shape=[send_shape(last_part)],
        compiler_params=params(4),
        cost_estimate=cost(1, 1),
        name="send_scaled",
    )(theta.reshape(-1), send_node, send_outlet, flow, turns, home)
    keep, home_theta = pl.pallas_call(
        functools.partial(keep_kernel, sizes),
        in_specs=[VMEM_WHOLE] * 4 + [ANYWHERE] * 2,
        out_specs=[VMEM_WHOLE] * 2,
        out_shape=[jax.ShapeDtypeStruct(per_cell, F32)] * 2,
        compiler_params=params(8),
        cost_estimate=cost(10000000, 1),
        name="keep",
    )(theta, node_in, node_out, fraction, behind, arrived[2])
    base = pl.pallas_call(
        functools.partial(base_kernel, sizes),
        in_specs=[SMEM_WHOLE] * 2 + [VMEM_WHOLE] * 2,
        out_specs=VMEM_WHOLE,
        out_shape=rows_shape,
        compiler_params=params(4),
        cost_estimate=cost(10000000, 1),
        name="base_rows",
    )(keep.reshape(-1), home_theta.reshape(-1), rows, home)

    base, theta_there, *arrived = lax.optimization_barrier((base, theta_there, *arrived))
    last = shifted(behind, "region", SHIFTS[3])
    scale = lax.all_gather(theta_there, "dest", axis=0, tiled=True)[: list_shape[0]]

    base = pl.pallas_call(
        functools.partial(land_kernel, sizes, parts),
        in_specs=[SMEM_WHOLE] * 2 + [VMEM_WHOLE] * 5,
        out_specs=VMEM_WHOLE,
        out_shape=rows_shape,
        input_output_aliases={6: 0},
        compiler_params=params(4),
        cost_estimate=cost(100000000000, 1),
        name="land_first",
    )(scale.reshape(-1), land, *arrived, base)

    out, _ = pl.pallas_call(
        functools.partial(finish_kernel, sizes, (last_part,), chunk),
        in_specs=[SMEM_WHOLE] + [VMEM_WHOLE] * 2,
        out_specs=[ANYWHERE, VMEM_WHOLE],
        out_shape=[jax.ShapeDtypeStruct((cells, width), F32), rows_shape],
        scratch_shapes=[
            pltpu.VMEM((cells, width), F32),
            pltpu.SemaphoreType.DMA((cells // chunk,)),
        ],
        input_output_aliases={2: 1},
        compiler_params=params(12),
        cost_estimate=cost(cells * width, cells * row_bytes),
        name="finish",
    )(land, last, base)
    return out


def solution(mesh):
    return jax.shard_map(
        on_device,
        mesh=mesh,
        in_specs=(
            P("region", "dest"),
            P("region"),
            P("region"),
            P("region"),
            P(None, "region"),
            P(None, "region"),
            P("region", None),
            P("region", None),
            P("region", "dest"),
        ),
        out_specs=P("region", "dest"),
        check_vma=False,
    )
```

```python
import functools

import jax
import jax.numpy as jnp
from jax import lax
from jax.experimental import pallas as pl
from jax.experimental.pallas import tpu as pltpu
from jax.sharding import PartitionSpec as P

SHIFTS = (1, -1, 2, -2)
EXACT = lax.Precision.HIGHEST
LANES = 128
MIB = 1 << 20
F32 = jnp.float32
I32 = jnp.int32
VMEM_WHOLE = pl.BlockSpec(memory_space=pltpu.VMEM)
SMEM_WHOLE = pl.BlockSpec(memory_space=pltpu.SMEM)
ANYWHERE = pl.BlockSpec(memory_space=pl.ANY)


def to_neighbours(block):
    regions, members = lax.axis_size("region"), lax.axis_size("dest")
    route = [
        (r * members + d, (r + SHIFTS[d % 4]) % regions * members + d)
        for r in range(regions)
        for d in range(members)
    ]
    return lax.ppermute(block, ("region", "dest"), route)


def to_two(block, first):
    regions, members = lax.axis_size("region"), lax.axis_size("dest")
    route = [
        (r * members + d, (r + SHIFTS[first + d % 2]) % regions * members + d)
        for r in range(regions)
        for d in range(members)
    ]
    return lax.ppermute(block, ("region", "dest"), route)


def shifted(block, axis, distance):
    devices = range(lax.axis_size(axis))
    route = [((i - distance) % len(devices), i) for i in devices]
    return lax.ppermute(block, axis, route)


def partners(block, axis):
    count = lax.axis_size(axis)
    return [block] + [
        lax.ppermute(block, axis, [(i, i ^ other) for i in range(count)])
        for other in range(1, count)
    ]


def tree_sum(parts):
    while len(parts) > 1:
        parts = [parts[k] + parts[k + 1] for k in range(0, len(parts), 2)]
    return parts[0]


def params(mib):
    return pltpu.CompilerParams(vmem_limit_bytes=mib * MIB)


def cost(flops, moved):
    return pl.CostEstimate(flops=flops, bytes_accessed=moved, transcendentals=0)


def lane_sums(partial):
    sums = jnp.dot(
        partial, jnp.ones((LANES, LANES), F32), preferred_element_type=F32, precision=EXACT
    )
    row = lax.broadcasted_iota(I32, (LANES, LANES), 0)
    lane = lax.broadcasted_iota(I32, (LANES, LANES), 1)
    pieces = [
        jnp.sum(jnp.where(row == lane, sums[k : k + LANES, :], 0.0), axis=0, keepdims=True)
        for k in range(0, partial.shape[0], LANES)
    ]
    return jnp.concatenate(pieces, axis=0)


def stacked(row):
    return jnp.concatenate(
        [row[:, k : k + LANES] for k in range(0, row.shape[1], LANES)], axis=0
    )


def strung(rows):
    return jnp.concatenate([rows[k : k + 1, :] for k in range(rows.shape[0])], axis=1)


def row_of(ref, number, sub):
    if sub % 8 == 0:
        return ref.reshape(ref.shape[0] // sub, sub, LANES).at[number]
    return ref.at[pl.ds(pl.multiple_of(number * sub, sub), sub), :]


def padded(cap):
    return -(-cap // LANES) * LANES


def put_row(ref, row, value, fill):
    width = value.shape[1]
    for q in range(-(-width // LANES)):
        piece = value[:, q * LANES : min((q + 1) * LANES, width)]
        lack = LANES - piece.shape[1]
        if lack:
            piece = jnp.concatenate([piece, jnp.full((1, lack), fill, piece.dtype)], axis=1)
        ref[row + q : row + q + 1, :] = piece


def one_hot(index, count):
    rows = lax.broadcasted_iota(I32, (count, index.shape[1]), 0)
    return jnp.where(rows == index, 1.0, 0.0)


def in_parts(x):
    high = x.astype(jnp.bfloat16)
    rest = x - high.astype(F32)
    middle = rest.astype(jnp.bfloat16)
    low = (rest - middle.astype(F32)).astype(jnp.bfloat16)
    return jnp.concatenate([high, middle, low], axis=0)


def selected(values, choice, dims):
    count = values.shape[0]
    product = lax.dot_general(
        in_parts(values), choice.astype(jnp.bfloat16), (dims, ((), ())),
        preferred_element_type=F32,
    )
    return product[:count, :] + product[count : 2 * count, :] + product[2 * count :, :]


def look_up(table, index):
    picked = selected(table.T, one_hot(index // LANES, table.shape[0]), ((1,), (0,)))
    return jnp.sum(picked * one_hot(index % LANES, LANES), axis=0, keepdims=True)


def scatter(index, values, height):
    high = jnp.where(index >= 0, index // LANES, -1)
    low = jnp.where(index >= 0, index % LANES, -1)
    return selected(one_hot(high, height) * values, one_hot(low, LANES), ((1,), (1,)))


def home_cells(node_out, region_no, cells):
    here = (node_out >= 0) & (node_out // cells == region_no)
    return jnp.where(here, node_out % cells, -1)


def rows_of_group(x_ref, rows_ref, first, sub):
    total = None
    for q in range(sub):
        piece = x_ref[pl.ds(pl.multiple_of(first, 8), 8), q * LANES : (q + 1) * LANES]
        rows_ref[pl.ds(first * sub + q, 8, stride=sub), :] = piece
        total = piece if total is None else total + piece
    return total


def copies_in(source, target, sems, chunk):
    copies = [
        pltpu.make_async_copy(
            source.at[pl.ds(i * chunk, chunk), :], target.at[pl.ds(i * chunk, chunk), :], sems.at[i]
        )
        for i in range(target.shape[0] // chunk)
    ]
    for copy in copies:
        copy.start()
    return copies


def make_lists(
    sizes, node_in, node_out, send_list, recv_list,
    in_cell, send_node, send_outlet, land, source_node, source_outlet,
):
    cells, nodes, branches, cap, sub = sizes
    height = cells // LANES
    region_no = lax.axis_index("region")
    ids = lax.broadcasted_iota(I32, (1, nodes), 1).astype(F32) + 1.0
    number = jnp.zeros((height, LANES), F32)
    slot = jnp.zeros((height, LANES), F32)
    for j in range(branches):
        ins = node_in[j : j + 1, :]
        put_row(in_cell, j * (nodes // LANES), jnp.where(ins >= 0, ins, cells), cells)
        home = home_cells(node_out[j : j + 1, :], region_no, cells)
        here = scatter(home, ids, height)
        number = number + here
        slot = slot + jnp.where(here > 0.0, j + 1.0, 0.0)
    source_node[...] = jnp.maximum(number.astype(I32) - 1, 0)
    source_outlet[...] = slot.astype(I32) - 1
    per_side = padded(cap) // LANES
    for side in range(4):
        slots = send_list[side : side + 1, :]
        lands = recv_list[side : side + 1, :]
        put_row(send_node, side * per_side, jnp.where(slots >= 0, slots % nodes, 0), 0)
        put_row(send_outlet, side * per_side, jnp.where(slots >= 0, slots // nodes, -1), -1)
        put_row(land, side * per_side, jnp.where(lands >= 0, lands, cells), cells)


def cell_sum_kernel(chunk, sub, x_hbm, sum_ref, rows_ref, x, partial, sems):
    copies = copies_in(x_hbm, x, sems, chunk)
    zeros = rows_ref.shape[0] - sub
    rows_ref[zeros:, :] = jnp.zeros((sub, LANES), F32)
    for number, copy in enumerate(copies):
        copy.wait()

        def body(step, carry, number=number):
            for half in range(2):
                first = number * chunk + step * 16 + half * 8
                total = rows_of_group(x, rows_ref, first, sub)
                partial[pl.ds(pl.multiple_of(first, 8), 8), :] = total
            return carry

        lax.fori_loop(0, chunk // 16, body, 0)
    sum_ref[...] = lane_sums(partial[...])


def turn_rows_kernel(sizes, chunk, x_hbm, after_ref, *rest):
    cells, nodes, branches, cap, sub = sizes
    lists, rows_ref, made, (x, sems) = rest[:4], rest[4], rest[5:11], rest[11:]
    copies = copies_in(x_hbm, x, sems, chunk)
    make_lists(sizes, *lists, *made)
    for number, copy in enumerate(copies):
        copy.wait()

        def body(step, carry, number=number):
            for half in range(2):
                rows_of_group(x, rows_ref, number * chunk + step * 16 + half * 8, sub)
            return carry

        lax.fori_loop(0, chunk // 16, body, 0)


def gathered_flow(node, in_cell, fraction, rows, sizes):
    cells, nodes, branches, cap, sub = sizes
    parts = []
    for i in range(branches):
        cell = in_cell[i * nodes + node]
        part = row_of(rows, cell, sub)[...]
        parts.append(part if fraction is None else part * fraction[cell])
    return tree_sum(parts)


def scale_kernel(sizes, fraction, rows, sent_ref, supply_ref, scaled):
    cells, nodes, branches, cap, sub = sizes

    def body(step, carry):
        first = step * 16
        values = [
            row_of(rows, first + i, sub)[...] * fraction[first + i] for i in range(16)
        ]
        for i in range(16):
            row_of(scaled, first + i, sub)[...] = values[i]
        return carry

    lax.fori_loop(0, cells // 16, body, 0)
    row_of(scaled, cells, sub)[...] = jnp.zeros((sub, LANES), F32)


def send_kernel(sizes, parts, fraction, in_cell, send_node, send_outlet, rows, turns, *sends):
    cells, nodes, branches, cap, sub = sizes
    batch = 8
    for (side, start, count), send in zip(parts, sends):

        def body(step, carry, side=side, start=start, send=send):
            first = step * batch
            values = []
            for i in range(batch):
                slot = side * padded(cap) + start + first + i
                node = send_node[slot]
                value = gathered_flow(node, in_cell, fraction, rows, sizes)
                choice = row_of(turns, node, sub)[...]
                values.append(jnp.where(choice == send_outlet[slot], value, 0.0))
            for i in range(batch):
                row_of(send, first + i, sub)[...] = values[i]
            return carry

        lax.fori_loop(0, count // batch, body, 0)


def node_flow_kernel(sizes, in_cell, scaled, turns, after_ref, flow, demand, partial):
    cells, nodes, branches, cap, sub = sizes

    def gather(step, carry):
        first = step * 8
        values = [
            gathered_flow(first + i, in_cell, None, scaled, sizes) for i in range(8)
        ]
        for i in range(8):
            row_of(flow, first + i, sub)[...] = values[i]
        return carry

    def measure(step, carry):
        for half in range(2):
            first = step * 16 + half * 8
            totals = [jnp.zeros((8, LANES), F32)] * branches
            for q in range(sub):
                at = pl.ds(first * sub + q, 8, stride=sub)
                value = flow[at, :]
                choice = turns[at, :]
                totals = [
                    total + jnp.where(choice == j, value, 0.0) for j, total in enumerate(totals)
                ]
            for j in range(branches):
                partial[j, pl.ds(pl.multiple_of(first, 8), 8), :] = totals[j]
        return carry

    lax.fori_loop(0, nodes // 8, gather, 0)
    lax.fori_loop(0, nodes // 16, measure, 0)
    per_outlet = nodes // LANES
    for j in range(branches):
        demand[j * per_outlet : (j + 1) * per_outlet, :] = lane_sums(partial[j])


def theta_kernel(
    sizes, regions, commodities, supply, shared, node_out, send_list, theta_out, slot_theta
):
    cells, nodes, branches, cap, sub = sizes
    per_outlet = nodes // LANES
    height = cells // LANES
    block = branches * per_outlet + height
    region_no = lax.axis_index("region")
    members = shared.shape[0] // block
    parts = [
        shared[d * block : d * block + branches * per_outlet, :] for d in range(members)
    ]
    demand = tree_sum(parts) * (1.0 / commodities)
    table = jnp.concatenate(
        [supply[...]]
        + [
            shared[d * block + branches * per_outlet : (d + 1) * block, :] for d in range(4)
        ],
        axis=0,
    )
    tall = jnp.ones((per_outlet, LANES), F32)
    for j in range(branches):
        outs = node_out[j : j + 1, :]
        cell = jnp.maximum(outs, 0)
        offset = (cell // cells + regions - region_no) % regions
        sector = jnp.zeros_like(offset)
        for d in range(4):
            sector = jnp.where(offset == (-SHIFTS[d]) % regions, d + 1, sector)
        room = stacked(look_up(table, sector * cells + cell % cells))
        ratio = room / jnp.maximum(demand[j * per_outlet : (j + 1) * per_outlet, :], room)
        tall = jnp.minimum(tall, jnp.where(stacked(outs) >= 0, ratio, 1.0))
    theta_out[...] = tall
    per_side = padded(cap) // LANES
    for k in range(2):
        slots = send_list[pl.ds(2 * k + lax.axis_index("dest") % 2, 1), :]
        there = look_up(tall, jnp.where(slots >= 0, slots % nodes, 0))
        put_row(slot_theta, k * per_side, there, 0.0)


def keep_kernel(sizes, theta_ref, node_in, node_out, fraction, after_ref, keep, home_theta):
    cells, nodes, branches, cap, sub = sizes
    height = cells // LANES
    region_no = lax.axis_index("region")
    theta = strung(theta_ref[...])
    cell_theta = jnp.zeros((height, LANES), F32)
    into = jnp.zeros((height, LANES), F32)
    for j in range(branches):
        home = home_cells(node_out[j : j + 1, :], region_no, cells)
        cell_theta = cell_theta + scatter(node_in[j : j + 1, :], theta, height)
        into = into + scatter(home, theta, height)
    keep[...] = 1.0 - cell_theta * fraction[...]
    home_theta[...] = into


def home_kernel(sizes, source, outlet, turns, flow, after_ref, home):
    cells, nodes, branches, cap, sub = sizes
    batch = 8

    def body(step, carry):
        first = step * batch
        values = []
        for i in range(batch):
            node = source[first + i]
            choice = row_of(turns, node, sub)[...]
            moved = row_of(flow, node, sub)[...]
            values.append(jnp.where(choice == outlet[first + i], moved, 0.0))
        for i in range(batch):
            row_of(home, first + i, sub)[...] = values[i]
        return carry

    lax.fori_loop(0, cells // batch, body, 0)


def base_kernel(sizes, keep, home_theta, rows, home, base):
    cells, nodes, branches, cap, sub = sizes
    batch = 8

    def body(step, carry):
        first = step * batch
        values = []
        for i in range(batch):
            cell = first + i
            kept = row_of(rows, cell, sub)[...] * keep[cell]
            values.append(kept + row_of(home, cell, sub)[...] * home_theta[cell])
        for i in range(batch):
            row_of(base, first + i, sub)[...] = values[i]
        return carry

    lax.fori_loop(0, cells // batch, body, 0)


def land_rows(sizes, scale, land, received, base):
    cells, nodes, branches, cap, sub = sizes
    batch = 8
    core = lax.axis_index("dest") % 2
    for side, rows in enumerate(received):
        offset = jnp.where(core == side % 2, 0, 2 * padded(cap)) + side // 2 * padded(cap)

        def body(step, carry, side=side, rows=rows, offset=offset):
            first = step * batch
            stores = []
            for i in range(batch):
                at = row_of(base, land[side * padded(cap) + first + i], sub)
                value = row_of(rows, first + i, sub)[...] * scale[offset + first + i]
                stores.append((at, at[...] + value))
            for at, value in stores:
                at[...] = value
            return carry

        lax.fori_loop(0, cap // batch, body, 0)


def finish_kernel(sizes, chunk, scale, land, *rest):
    cells, nodes, branches, cap, sub = sizes
    received, (base_in, out, base, staged, sems) = rest[:4], rest[4:]
    land_rows(sizes, scale, land, received, base)
    copies = []
    for number in range(cells // chunk):

        def body(step, carry, number=number):
            for half in range(2):
                first = number * chunk + step * 16 + half * 8
                for q in range(sub):
                    staged[
                        pl.ds(pl.multiple_of(first, 8), 8), q * LANES : (q + 1) * LANES
                    ] = base[pl.ds(first * sub + q, 8, stride=sub), :]
            return carry

        lax.fori_loop(0, chunk // 16, body, 0)
        at = pl.ds(number * chunk, chunk)
        copies.append(
            pltpu.make_async_copy(staged.at[at, :], out.at[at, :], sems.at[number])
        )
        copies[-1].start()
    for copy in copies:
        copy.wait()


def on_device(occupancy, capacity, jam, wave, node_in, node_out, send_list, recv_list, turn):
    cells, width = occupancy.shape
    branches, nodes = node_in.shape
    cap = send_list.shape[1]
    sub = width // LANES
    sizes = (cells, nodes, branches, cap, sub)
    regions = lax.axis_size("region")
    commodities = width * lax.axis_size("dest")
    height = cells // LANES
    per_cell = (height, LANES)
    list_shape = (4 * padded(cap) // LANES, LANES)
    chunk = 128
    row_bytes = width * 4
    occupancy = pltpu.with_memory_space_constraint(occupancy, pltpu.HBM)
    turn = pltpu.with_memory_space_constraint(turn, pltpu.HBM)

    local_sum, rows = pl.pallas_call(
        functools.partial(cell_sum_kernel, chunk, sub),
        in_specs=[ANYWHERE],
        out_specs=[VMEM_WHOLE] * 2,
        out_shape=[
            jax.ShapeDtypeStruct(per_cell, F32),
            pltpu.VMEM(((cells + 1) * sub, LANES), F32),
        ],
        scratch_shapes=[
            pltpu.VMEM((cells, width), F32),
            pltpu.VMEM((cells, LANES), F32),
            pltpu.SemaphoreType.DMA((cells // chunk,)),
        ],
        compiler_params=params(14),
        cost_estimate=cost(cells * width, cells * row_bytes),
        name="cell_sum",
    )(occupancy)

    sums = partners(local_sum, "dest")

    turns, *lists = pl.pallas_call(
        functools.partial(turn_rows_kernel, sizes, chunk),
        in_specs=[ANYWHERE] * 2 + [VMEM_WHOLE] * 4,
        out_specs=[VMEM_WHOLE] * 7,
        out_shape=[
            pltpu.VMEM((nodes * sub, LANES), I32),
            jax.ShapeDtypeStruct((branches * nodes // LANES, LANES), I32),
        ]
        + [jax.ShapeDtypeStruct(list_shape, I32)] * 3
        + [jax.ShapeDtypeStruct(per_cell, I32)] * 2,
        scratch_shapes=[
            pltpu.VMEM((nodes, width), I32),
            pltpu.SemaphoreType.DMA((nodes // chunk,)),
        ],
        compiler_params=params(8),
        cost_estimate=cost(0, nodes * row_bytes),
        name="turn_rows",
    )(turn, local_sum, node_in, node_out, send_list, recv_list)
    in_cell, send_node, send_outlet, land, source_node, source_outlet = (
        x.reshape(-1) for x in lists
    )

    turns, *sums = lax.optimization_barrier((turns, *sums))
    vehicles = tree_sum(sums) / commodities
    cap_of = capacity.reshape(per_cell)
    fraction = jnp.minimum(vehicles, cap_of) / vehicles
    supply = jnp.minimum(cap_of, wave.reshape(per_cell) * (jam.reshape(per_cell) - vehicles))
    rows_shape = pltpu.VMEM(((cells + 1) * sub, LANES), F32)
    parts = tuple((side, 0, cap) for side in range(4))

    def send_shape(part):
        return pltpu.VMEM((part[2] * sub, LANES), F32)


    supply_there = to_neighbours(supply)
    weights = jnp.concatenate([fraction.reshape(-1), jnp.zeros((LANES,), F32)])
    (ahead,) = pl.pallas_call(
        functools.partial(send_kernel, sizes, parts[2:3]),
        in_specs=[SMEM_WHOLE] * 4 + [VMEM_WHOLE] * 2,
        out_specs=[VMEM_WHOLE],
        out_shape=[send_shape(parts[2])],
        compiler_params=params(4),
        cost_estimate=cost(1, 1),
        name="send_ahead",
    )(weights, in_cell, send_node, send_outlet, rows, turns)
    ahead, supply_there = lax.optimization_barrier((ahead, supply_there))
    scaled = pl.pallas_call(
        functools.partial(scale_kernel, sizes),
        in_specs=[SMEM_WHOLE, VMEM_WHOLE, ANYWHERE, ANYWHERE],
        out_specs=VMEM_WHOLE,
        out_shape=rows_shape,
        compiler_params=params(4),
        cost_estimate=cost(1, 1),
        name="scale_rows",
    )(fraction.reshape(-1), rows, ahead, supply_there)
    near = pl.pallas_call(
        functools.partial(send_kernel, sizes, (parts[0], parts[1], parts[3]), None),
        in_specs=[SMEM_WHOLE] * 3 + [VMEM_WHOLE] * 2,
        out_specs=[VMEM_WHOLE] * 3,
        out_shape=[send_shape(part) for part in (parts[0], parts[1], parts[3])],
        compiler_params=params(4),
        cost_estimate=cost(1, 1),
        name="send_near",
    )(in_cell, send_node, send_outlet, scaled, turns)
    arrived = [
        shifted(send, "region", SHIFTS[side]) for side, send in enumerate([near[0], near[1], ahead, near[2]])
    ]

    flow, demand = pl.pallas_call(
        functools.partial(node_flow_kernel, sizes),
        in_specs=[SMEM_WHOLE] + [VMEM_WHOLE] * 2 + [ANYWHERE],
        out_specs=[VMEM_WHOLE] * 2,
        out_shape=[
            pltpu.VMEM((nodes * sub, LANES), F32),
            jax.ShapeDtypeStruct((branches * nodes // LANES, LANES), F32),
        ],
        scratch_shapes=[pltpu.VMEM((branches, nodes, LANES), F32)],
        compiler_params=params(8),
        cost_estimate=cost(1, 1),
        name="node_flow",
    )(in_cell, scaled, turns, near[0])

    joined = jnp.concatenate([demand, supply_there])
    shared = lax.all_gather(joined, "dest", axis=0, tiled=True)
    theta, slot_theta = pl.pallas_call(
        functools.partial(theta_kernel, sizes, regions, commodities),
        in_specs=[VMEM_WHOLE] * 4,
        out_specs=[VMEM_WHOLE] * 2,
        out_shape=[
            jax.ShapeDtypeStruct((nodes // LANES, LANES), F32),
            jax.ShapeDtypeStruct((2 * padded(cap) // LANES, LANES), F32),
        ],
        compiler_params=params(8),
        cost_estimate=cost(1, 1),
        name="theta",
    )(supply, shared, node_out, send_list)
    slot_theta, arrived[2] = lax.optimization_barrier((slot_theta, arrived[2]))
    per_side = padded(cap) // LANES
    theta_there = [to_two(slot_theta[:per_side], 0), to_two(slot_theta[per_side:], 2)]

    home = pl.pallas_call(
        functools.partial(home_kernel, sizes),
        in_specs=[SMEM_WHOLE] * 2 + [VMEM_WHOLE] * 2 + [ANYWHERE],
        out_specs=VMEM_WHOLE,
        out_shape=rows_shape,
        compiler_params=params(4),
        cost_estimate=cost(1, 1),
        name="home_rows",
    )(source_node, source_outlet, turns, flow, slot_theta)
    keep, home_theta = pl.pallas_call(
        functools.partial(keep_kernel, sizes),
        in_specs=[VMEM_WHOLE] * 4 + [ANYWHERE],
        out_specs=[VMEM_WHOLE] * 2,
        out_shape=[jax.ShapeDtypeStruct(per_cell, F32)] * 2,
        compiler_params=params(8),
        cost_estimate=cost(10000000, 1),
        name="keep",
    )(theta, node_in, node_out, fraction, home)
    base = pl.pallas_call(
        functools.partial(base_kernel, sizes),
        in_specs=[SMEM_WHOLE] * 2 + [VMEM_WHOLE] * 2,
        out_specs=VMEM_WHOLE,
        out_shape=rows_shape,
        compiler_params=params(4),
        cost_estimate=cost(10000000, 1),
        name="base_rows",
    )(keep.reshape(-1), home_theta.reshape(-1), rows, home)

    base, *rest = lax.optimization_barrier((base, *theta_there, *arrived))
    theta_there, arrived = rest[:2], rest[2:]
    got = jnp.concatenate(theta_there)
    members = lax.axis_size("dest")
    other = lax.ppermute(got, "dest", [(i, i ^ 1) for i in range(members)])
    scale = jnp.concatenate([got, other])

    out, _ = pl.pallas_call(
        functools.partial(finish_kernel, sizes, chunk),
        in_specs=[SMEM_WHOLE] * 2 + [VMEM_WHOLE] * 5,
        out_specs=[ANYWHERE, VMEM_WHOLE],
        out_shape=[jax.ShapeDtypeStruct((cells, width), F32), rows_shape],
        scratch_shapes=[
            pltpu.VMEM((cells, width), F32),
            pltpu.SemaphoreType.DMA((cells // chunk,)),
        ],
        input_output_aliases={6: 1},
        compiler_params=params(12),
        cost_estimate=cost(cells * width, cells * row_bytes),
        name="finish",
    )(scale.reshape(-1), land, *arrived, base)
    return out


def solution(mesh):
    return jax.shard_map(
        on_device,
        mesh=mesh,
        in_specs=(
            P("region", "dest"),
            P("region"),
            P("region"),
            P("region"),
            P(None, "region"),
            P(None, "region"),
            P("region", None),
            P("region", None),
            P("region", "dest"),
        ),
        out_specs=P("region", "dest"),
        check_vma=False,
    )
```

```python
import functools

import jax
import jax.numpy as jnp
from jax import lax
from jax.experimental import pallas as pl
from jax.experimental.pallas import tpu as pltpu
from jax.sharding import PartitionSpec as P

SHIFTS = (1, -1, 2, -2)
LANES = 128
MIB = 1 << 20
F32 = jnp.float32
I32 = jnp.int32
VMEM_WHOLE = pl.BlockSpec(memory_space=pltpu.VMEM)
SMEM_WHOLE = pl.BlockSpec(memory_space=pltpu.SMEM)
ANYWHERE = pl.BlockSpec(memory_space=pl.ANY)


def to_neighbours(block):
    regions, members = lax.axis_size("region"), lax.axis_size("dest")
    route = [
        (r * members + d, (r + SHIFTS[d % 4]) % regions * members + d)
        for r in range(regions)
        for d in range(members)
    ]
    return lax.ppermute(block, ("region", "dest"), route)


def to_two(block, first):
    regions, members = lax.axis_size("region"), lax.axis_size("dest")
    route = [
        (r * members + d, (r + SHIFTS[first + d % 2]) % regions * members + d)
        for r in range(regions)
        for d in range(members)
    ]
    return lax.ppermute(block, ("region", "dest"), route)


def shifted(block, axis, distance):
    devices = range(lax.axis_size(axis))
    route = [((i - distance) % len(devices), i) for i in devices]
    return lax.ppermute(block, axis, route)


def partners(block, axis):
    count = lax.axis_size(axis)
    return [block] + [
        lax.ppermute(block, axis, [(i, i ^ other) for i in range(count)])
        for other in range(1, count)
    ]


def tree_sum(parts):
    while len(parts) > 1:
        parts = [parts[k] + parts[k + 1] for k in range(0, len(parts), 2)]
    return parts[0]


def params(mib):
    return pltpu.CompilerParams(vmem_limit_bytes=mib * MIB)


def cost(flops, moved):
    return pl.CostEstimate(flops=flops, bytes_accessed=moved, transcendentals=0)


def lane_sums(partial):
    count = partial.shape[0]
    parts = jnp.dot(
        in_parts(partial), jnp.ones((LANES, LANES), jnp.bfloat16), preferred_element_type=F32
    )
    sums = parts[:count, :] + parts[count : 2 * count, :] + parts[2 * count :, :]
    row = lax.broadcasted_iota(I32, (LANES, LANES), 0)
    lane = lax.broadcasted_iota(I32, (LANES, LANES), 1)
    pieces = [
        jnp.sum(jnp.where(row == lane, sums[k : k + LANES, :], 0.0), axis=0, keepdims=True)
        for k in range(0, partial.shape[0], LANES)
    ]
    return jnp.concatenate(pieces, axis=0)


def stacked(row):
    return jnp.concatenate(
        [row[:, k : k + LANES] for k in range(0, row.shape[1], LANES)], axis=0
    )


def strung(rows):
    return jnp.concatenate([rows[k : k + 1, :] for k in range(rows.shape[0])], axis=1)


def row_of(ref, number, sub):
    if sub % 8 == 0:
        return ref.reshape(ref.shape[0] // sub, sub, LANES).at[number]
    return ref.at[pl.ds(pl.multiple_of(number * sub, sub), sub), :]


def padded(cap):
    return -(-cap // LANES) * LANES


def put_row(ref, row, value, fill):
    width = value.shape[1]
    for q in range(-(-width // LANES)):
        piece = value[:, q * LANES : min((q + 1) * LANES, width)]
        lack = LANES - piece.shape[1]
        if lack:
            piece = jnp.concatenate([piece, jnp.full((1, lack), fill, piece.dtype)], axis=1)
        ref[row + q : row + q + 1, :] = piece


def one_hot(index, count):
    rows = lax.broadcasted_iota(I32, (count, index.shape[1]), 0)
    return jnp.where(rows == index, 1.0, 0.0)


def in_parts(x):
    high = x.astype(jnp.bfloat16)
    rest = x - high.astype(F32)
    middle = rest.astype(jnp.bfloat16)
    low = (rest - middle.astype(F32)).astype(jnp.bfloat16)
    return jnp.concatenate([high, middle, low], axis=0)


def selected(values, choice, dims):
    count = values.shape[0]
    product = lax.dot_general(
        in_parts(values), choice.astype(jnp.bfloat16), (dims, ((), ())),
        preferred_element_type=F32,
    )
    return product[:count, :] + product[count : 2 * count, :] + product[2 * count :, :]


def look_up(table, index):
    picked = selected(table.T, one_hot(index // LANES, table.shape[0]), ((1,), (0,)))
    return jnp.sum(picked * one_hot(index % LANES, LANES), axis=0, keepdims=True)


def scatter(index, values, height):
    high = jnp.where(index >= 0, index // LANES, -1)
    low = jnp.where(index >= 0, index % LANES, -1)
    return selected(one_hot(high, height) * values, one_hot(low, LANES), ((1,), (1,)))


def home_cells(node_out, region_no, cells):
    here = (node_out >= 0) & (node_out // cells == region_no)
    return jnp.where(here, node_out % cells, -1)


def rows_of_group(x_ref, rows_ref, first, sub):
    total = None
    for q in range(sub):
        piece = x_ref[pl.ds(pl.multiple_of(first, 8), 8), q * LANES : (q + 1) * LANES]
        rows_ref[pl.ds(first * sub + q, 8, stride=sub), :] = piece
        total = piece if total is None else total + piece
    return total


def copies_in(source, target, sems, chunk):
    copies = [
        pltpu.make_async_copy(
            source.at[pl.ds(i * chunk, chunk), :], target.at[pl.ds(i * chunk, chunk), :], sems.at[i]
        )
        for i in range(target.shape[0] // chunk)
    ]
    for copy in copies:
        copy.start()
    return copies


def make_lists(
    sizes, node_in, node_out, send_list, recv_list,
    in_cell, send_node, send_outlet, land, source_node, source_outlet,
):
    cells, nodes, branches, cap, sub = sizes
    height = cells // LANES
    region_no = lax.axis_index("region")
    ids = lax.broadcasted_iota(I32, (1, nodes), 1).astype(F32) + 1.0
    number = jnp.zeros((height, LANES), F32)
    slot = jnp.zeros((height, LANES), F32)
    for j in range(branches):
        ins = node_in[j : j + 1, :]
        put_row(in_cell, j * (nodes // LANES), jnp.where(ins >= 0, ins, cells), cells)
        home = home_cells(node_out[j : j + 1, :], region_no, cells)
        here = scatter(home, ids, height)
        number = number + here
        slot = slot + jnp.where(here > 0.0, j + 1.0, 0.0)
    source_node[...] = jnp.maximum(number.astype(I32) - 1, 0)
    source_outlet[...] = slot.astype(I32) - 1
    per_side = padded(cap) // LANES
    for side in range(4):
        slots = send_list[side : side + 1, :]
        lands = recv_list[side : side + 1, :]
        put_row(send_node, side * per_side, jnp.where(slots >= 0, slots % nodes, 0), 0)
        put_row(send_outlet, side * per_side, jnp.where(slots >= 0, slots // nodes, -1), -1)
        put_row(land, side * per_side, jnp.where(lands >= 0, lands, cells), cells)


def cell_sum_kernel(chunk, sub, x_hbm, sum_ref, rows_ref, x, partial, sems):
    copies = copies_in(x_hbm, x, sems, chunk)
    zeros = rows_ref.shape[0] - sub
    rows_ref[zeros:, :] = jnp.zeros((sub, LANES), F32)
    for number, copy in enumerate(copies):
        copy.wait()

        def body(step, carry, number=number):
            for half in range(2):
                first = number * chunk + step * 16 + half * 8
                total = rows_of_group(x, rows_ref, first, sub)
                partial[pl.ds(pl.multiple_of(first, 8), 8), :] = total
            return carry

        lax.fori_loop(0, chunk // 16, body, 0)
    sum_ref[...] = lane_sums(partial[...])


def turn_rows_kernel(sizes, chunk, x_hbm, after_ref, *rest):
    cells, nodes, branches, cap, sub = sizes
    lists, rows_ref, made, (x, sems) = rest[:4], rest[4], rest[5:11], rest[11:]
    copies = copies_in(x_hbm, x, sems, chunk)
    make_lists(sizes, *lists, *made)
    for number, copy in enumerate(copies):
        copy.wait()

        def body(step, carry, number=number):
            for half in range(2):
                rows_of_group(x, rows_ref, number * chunk + step * 16 + half * 8, sub)
            return carry

        lax.fori_loop(0, chunk // 16, body, 0)


def gathered_flow(node, in_cell, fraction, rows, sizes):
    cells, nodes, branches, cap, sub = sizes
    parts = []
    for i in range(branches):
        cell = in_cell[i * nodes + node]
        part = row_of(rows, cell, sub)[...]
        parts.append(part if fraction is None else part * fraction[cell])
    return tree_sum(parts)


def scale_kernel(sizes, fraction, rows, sent_ref, supply_ref, scaled):
    cells, nodes, branches, cap, sub = sizes

    def body(step, carry):
        first = step * 16
        values = [
            row_of(rows, first + i, sub)[...] * fraction[first + i] for i in range(16)
        ]
        for i in range(16):
            row_of(scaled, first + i, sub)[...] = values[i]
        return carry

    lax.fori_loop(0, cells // 16, body, 0)
    row_of(scaled, cells, sub)[...] = jnp.zeros((sub, LANES), F32)


def send_kernel(sizes, sides, fraction, in_cell, send_node, send_outlet, rows, turns, *sends):
    cells, nodes, branches, cap, sub = sizes
    batch = 16
    for side, send in zip(sides, sends):

        def body(step, carry, side=side, send=send):
            first = step * batch
            values = []
            for i in range(batch):
                slot = side * padded(cap) + first + i
                node = send_node[slot]
                value = gathered_flow(node, in_cell, fraction, rows, sizes)
                choice = row_of(turns, node, sub)[...]
                values.append(jnp.where(choice == send_outlet[slot], value, 0.0))
            for i in range(batch):
                row_of(send, first + i, sub)[...] = values[i]
            return carry

        lax.fori_loop(0, cap // batch, body, 0)


def scaled_send_kernel(sizes, side, theta, send_node, send_outlet, flow, turns, send):
    cells, nodes, branches, cap, sub = sizes
    batch = 16

    def body(step, carry):
        first = step * batch
        values = []
        for i in range(batch):
            slot = side * padded(cap) + first + i
            node = send_node[slot]
            value = row_of(flow, node, sub)[...] * theta[node]
            choice = row_of(turns, node, sub)[...]
            values.append(jnp.where(choice == send_outlet[slot], value, 0.0))
        for i in range(batch):
            row_of(send, first + i, sub)[...] = values[i]
        return carry

    lax.fori_loop(0, cap // batch, body, 0)


def node_flow_kernel(sizes, in_cell, scaled, turns, after_ref, flow, demand, partial):
    cells, nodes, branches, cap, sub = sizes

    def gather(step, carry):
        first = step * 16
        values = [
            gathered_flow(first + i, in_cell, None, scaled, sizes) for i in range(16)
        ]
        for i in range(16):
            row_of(flow, first + i, sub)[...] = values[i]
        return carry

    def measure(step, carry):
        for half in range(2):
            first = step * 16 + half * 8
            totals = [jnp.zeros((8, LANES), F32)] * branches
            for q in range(sub):
                at = pl.ds(first * sub + q, 8, stride=sub)
                value = flow[at, :]
                choice = turns[at, :]
                totals = [
                    total + jnp.where(choice == j, value, 0.0) for j, total in enumerate(totals)
                ]
            for j in range(branches):
                partial[j, pl.ds(pl.multiple_of(first, 8), 8), :] = totals[j]
        return carry

    lax.fori_loop(0, nodes // 16, gather, 0)
    lax.fori_loop(0, nodes // 16, measure, 0)
    per_outlet = nodes // LANES
    for j in range(branches):
        demand[j * per_outlet : (j + 1) * per_outlet, :] = lane_sums(partial[j])


def theta_kernel(
    sizes, regions, commodities, supply, shared, node_out, send_list, theta_out, slot_theta
):
    cells, nodes, branches, cap, sub = sizes
    per_outlet = nodes // LANES
    height = cells // LANES
    block = branches * per_outlet + height
    region_no = lax.axis_index("region")
    members = shared.shape[0] // block
    parts = [
        shared[d * block : d * block + branches * per_outlet, :] for d in range(members)
    ]
    demand = tree_sum(parts) * (1.0 / commodities)
    table = jnp.concatenate(
        [supply[...]]
        + [
            shared[d * block + branches * per_outlet : (d + 1) * block, :] for d in range(4)
        ],
        axis=0,
    )
    tall = jnp.ones((per_outlet, LANES), F32)
    for j in range(branches):
        outs = node_out[j : j + 1, :]
        cell = jnp.maximum(outs, 0)
        offset = (cell // cells + regions - region_no) % regions
        sector = jnp.zeros_like(offset)
        for d in range(4):
            sector = jnp.where(offset == (-SHIFTS[d]) % regions, d + 1, sector)
        room = stacked(look_up(table, sector * cells + cell % cells))
        ratio = room / jnp.maximum(demand[j * per_outlet : (j + 1) * per_outlet, :], room)
        tall = jnp.minimum(tall, jnp.where(stacked(outs) >= 0, ratio, 1.0))
    theta_out[...] = tall
    per_side = padded(cap) // LANES
    for k in range(2):
        slots = send_list[pl.ds(2 * k + lax.axis_index("dest") % 2, 1), :]
        there = look_up(tall, jnp.where(slots >= 0, slots % nodes, 0))
        put_row(slot_theta, k * per_side, there, 0.0)


def keep_kernel(
    sizes, theta_ref, node_in, node_out, fraction, sent_ref, arrived_ref, keep, home_theta
):
    cells, nodes, branches, cap, sub = sizes
    height = cells // LANES
    region_no = lax.axis_index("region")
    theta = strung(theta_ref[...])
    cell_theta = jnp.zeros((height, LANES), F32)
    into = jnp.zeros((height, LANES), F32)
    for j in range(branches):
        home = home_cells(node_out[j : j + 1, :], region_no, cells)
        cell_theta = cell_theta + scatter(node_in[j : j + 1, :], theta, height)
        into = into + scatter(home, theta, height)
    keep[...] = 1.0 - cell_theta * fraction[...]
    home_theta[...] = into


def home_kernel(sizes, source, outlet, turns, flow, after_ref, home):
    cells, nodes, branches, cap, sub = sizes
    batch = 16

    def body(step, carry):
        first = step * batch
        values = []
        for i in range(batch):
            node = source[first + i]
            choice = row_of(turns, node, sub)[...]
            moved = row_of(flow, node, sub)[...]
            values.append(jnp.where(choice == outlet[first + i], moved, 0.0))
        for i in range(batch):
            row_of(home, first + i, sub)[...] = values[i]
        return carry

    lax.fori_loop(0, cells // batch, body, 0)


def base_kernel(sizes, keep, home_theta, rows, home, base):
    cells, nodes, branches, cap, sub = sizes
    batch = 16

    def body(step, carry):
        first = step * batch
        values = []
        for i in range(batch):
            cell = first + i
            kept = row_of(rows, cell, sub)[...] * keep[cell]
            values.append(kept + row_of(home, cell, sub)[...] * home_theta[cell])
        for i in range(batch):
            row_of(base, first + i, sub)[...] = values[i]
        return carry

    lax.fori_loop(0, cells // batch, body, 0)


def land_rows(sizes, sides, scale, land, received, base):
    cells, nodes, branches, cap, sub = sizes
    batch = 16
    core = lax.axis_index("dest") % 2
    for side, rows in zip(sides, received):
        offset = jnp.where(core == side % 2, 0, 2 * padded(cap)) + side // 2 * padded(cap)

        def body(step, carry, side=side, rows=rows, offset=offset):
            first = step * batch
            stores = []
            for i in range(batch):
                at = row_of(base, land[side * padded(cap) + first + i], sub)
                value = row_of(rows, first + i, sub)[...]
                if scale is not None:
                    value = value * scale[offset + first + i]
                stores.append((at, at[...] + value))
            for at, value in stores:
                at[...] = value
            return carry

        lax.fori_loop(0, cap // batch, body, 0)


def land_kernel(sizes, sides, scale, land, *rest):
    received, (base_in, base) = rest[: len(sides)], rest[len(sides) :]
    land_rows(sizes, sides, scale, land, received, base)


def finish_kernel(sizes, sides, chunk, land, *rest):
    cells, nodes, branches, cap, sub = sizes
    received, (base_in, out, base, staged, sems) = rest[: len(sides)], rest[len(sides) :]
    land_rows(sizes, sides, None, land, received, base)
    copies = []
    for number in range(cells // chunk):

        def body(step, carry, number=number):
            for half in range(2):
                first = number * chunk + step * 16 + half * 8
                for q in range(sub):
                    staged[
                        pl.ds(pl.multiple_of(first, 8), 8), q * LANES : (q + 1) * LANES
                    ] = base[pl.ds(first * sub + q, 8, stride=sub), :]
            return carry

        lax.fori_loop(0, chunk // 16, body, 0)
        at = pl.ds(number * chunk, chunk)
        copies.append(
            pltpu.make_async_copy(staged.at[at, :], out.at[at, :], sems.at[number])
        )
        copies[-1].start()
    for copy in copies:
        copy.wait()


def on_device(occupancy, capacity, jam, wave, node_in, node_out, send_list, recv_list, turn):
    cells, width = occupancy.shape
    branches, nodes = node_in.shape
    cap = send_list.shape[1]
    sub = width // LANES
    sizes = (cells, nodes, branches, cap, sub)
    regions = lax.axis_size("region")
    commodities = width * lax.axis_size("dest")
    height = cells // LANES
    per_cell = (height, LANES)
    list_shape = (4 * padded(cap) // LANES, LANES)
    chunk = 128
    row_bytes = width * 4
    occupancy = pltpu.with_memory_space_constraint(occupancy, pltpu.HBM)
    turn = pltpu.with_memory_space_constraint(turn, pltpu.HBM)

    local_sum, rows = pl.pallas_call(
        functools.partial(cell_sum_kernel, chunk, sub),
        in_specs=[ANYWHERE],
        out_specs=[VMEM_WHOLE] * 2,
        out_shape=[
            jax.ShapeDtypeStruct(per_cell, F32),
            pltpu.VMEM(((cells + 1) * sub, LANES), F32),
        ],
        scratch_shapes=[
            pltpu.VMEM((cells, width), F32),
            pltpu.VMEM((cells, LANES), F32),
            pltpu.SemaphoreType.DMA((cells // chunk,)),
        ],
        compiler_params=params(14),
        cost_estimate=cost(cells * width, cells * row_bytes),
        name="cell_sum",
    )(occupancy)

    sums = partners(local_sum, "dest")

    turns, *lists = pl.pallas_call(
        functools.partial(turn_rows_kernel, sizes, chunk),
        in_specs=[ANYWHERE] * 2 + [VMEM_WHOLE] * 4,
        out_specs=[VMEM_WHOLE] * 7,
        out_shape=[
            pltpu.VMEM((nodes * sub, LANES), I32),
            jax.ShapeDtypeStruct((branches * nodes // LANES, LANES), I32),
        ]
        + [jax.ShapeDtypeStruct(list_shape, I32)] * 3
        + [jax.ShapeDtypeStruct(per_cell, I32)] * 2,
        scratch_shapes=[
            pltpu.VMEM((nodes, width), I32),
            pltpu.SemaphoreType.DMA((nodes // chunk,)),
        ],
        compiler_params=params(8),
        cost_estimate=cost(0, nodes * row_bytes),
        name="turn_rows",
    )(turn, local_sum, node_in, node_out, send_list, recv_list)
    in_cell, send_node, send_outlet, land, source_node, source_outlet = (
        x.reshape(-1) for x in lists
    )

    turns, *sums = lax.optimization_barrier((turns, *sums))
    vehicles = tree_sum(sums) / commodities
    cap_of = capacity.reshape(per_cell)
    fraction = jnp.minimum(vehicles, cap_of) / vehicles
    supply = jnp.minimum(cap_of, wave.reshape(per_cell) * (jam.reshape(per_cell) - vehicles))
    rows_shape = pltpu.VMEM(((cells + 1) * sub, LANES), F32)
    send_shape = pltpu.VMEM((cap * sub, LANES), F32)

    supply_there = to_neighbours(supply)
    weights = jnp.concatenate([fraction.reshape(-1), jnp.zeros((LANES,), F32)])
    (ahead,) = pl.pallas_call(
        functools.partial(send_kernel, sizes, (2,)),
        in_specs=[SMEM_WHOLE] * 4 + [VMEM_WHOLE] * 2,
        out_specs=[VMEM_WHOLE],
        out_shape=[send_shape],
        compiler_params=params(4),
        cost_estimate=cost(1, 1),
        name="send_ahead",
    )(weights, in_cell, send_node, send_outlet, rows, turns)
    ahead, supply_there = lax.optimization_barrier((ahead, supply_there))
    scaled = pl.pallas_call(
        functools.partial(scale_kernel, sizes),
        in_specs=[SMEM_WHOLE, VMEM_WHOLE, ANYWHERE, ANYWHERE],
        out_specs=VMEM_WHOLE,
        out_shape=rows_shape,
        compiler_params=params(4),
        cost_estimate=cost(1, 1),
        name="scale_rows",
    )(fraction.reshape(-1), rows, ahead, supply_there)
    near = pl.pallas_call(
        functools.partial(send_kernel, sizes, (0, 1), None),
        in_specs=[SMEM_WHOLE] * 3 + [VMEM_WHOLE] * 2,
        out_specs=[VMEM_WHOLE] * 2,
        out_shape=[send_shape] * 2,
        compiler_params=params(4),
        cost_estimate=cost(1, 1),
        name="send_near",
    )(in_cell, send_node, send_outlet, scaled, turns)
    arrived = [
        shifted(send, "region", SHIFTS[side]) for side, send in enumerate([*near, ahead])
    ]

    flow, demand = pl.pallas_call(
        functools.partial(node_flow_kernel, sizes),
        in_specs=[SMEM_WHOLE] + [VMEM_WHOLE] * 2 + [ANYWHERE],
        out_specs=[VMEM_WHOLE] * 2,
        out_shape=[
            pltpu.VMEM((nodes * sub, LANES), F32),
            jax.ShapeDtypeStruct((branches * nodes // LANES, LANES), F32),
        ],
        scratch_shapes=[pltpu.VMEM((branches, nodes, LANES), F32)],
        compiler_params=params(8),
        cost_estimate=cost(1, 1),
        name="node_flow",
    )(in_cell, scaled, turns, near[0])

    joined = jnp.concatenate([demand, supply_there])
    shared = lax.all_gather(joined, "dest", axis=0, tiled=True)
    theta, slot_theta = pl.pallas_call(
        functools.partial(theta_kernel, sizes, regions, commodities),
        in_specs=[VMEM_WHOLE] * 4,
        out_specs=[VMEM_WHOLE] * 2,
        out_shape=[
            jax.ShapeDtypeStruct((nodes // LANES, LANES), F32),
            jax.ShapeDtypeStruct((2 * padded(cap) // LANES, LANES), F32),
        ],
        compiler_params=params(8),
        cost_estimate=cost(1, 1),
        name="theta",
    )(supply, shared, node_out, send_list)
    theta, slot_theta, arrived[2] = lax.optimization_barrier((theta, slot_theta, arrived[2]))
    per_side = padded(cap) // LANES
    theta_there = [to_two(slot_theta[:per_side], 0), to_two(slot_theta[per_side:], 2)]

    (behind,) = pl.pallas_call(
        functools.partial(scaled_send_kernel, sizes, 3),
        in_specs=[SMEM_WHOLE] * 3 + [VMEM_WHOLE] * 2,
        out_specs=[VMEM_WHOLE],
        out_shape=[send_shape],
        compiler_params=params(4),
        cost_estimate=cost(1, 1),
        name="send_scaled",
    )(theta.reshape(-1), send_node, send_outlet, flow, turns)
    home = pl.pallas_call(
        functools.partial(home_kernel, sizes),
        in_specs=[SMEM_WHOLE] * 2 + [VMEM_WHOLE] * 2 + [ANYWHERE],
        out_specs=VMEM_WHOLE,
        out_shape=rows_shape,
        compiler_params=params(4),
        cost_estimate=cost(4000000000, 1),
        name="home_rows",
    )(source_node, source_outlet, turns, flow, behind)
    keep, home_theta = pl.pallas_call(
        functools.partial(keep_kernel, sizes),
        in_specs=[VMEM_WHOLE] * 4 + [ANYWHERE] * 2,
        out_specs=[VMEM_WHOLE] * 2,
        out_shape=[jax.ShapeDtypeStruct(per_cell, F32)] * 2,
        compiler_params=params(8),
        cost_estimate=cost(10000000, 1),
        name="keep",
    )(theta, node_in, node_out, fraction, behind, arrived[2])
    base = pl.pallas_call(
        functools.partial(base_kernel, sizes),
        in_specs=[SMEM_WHOLE] * 2 + [VMEM_WHOLE] * 2,
        out_specs=VMEM_WHOLE,
        out_shape=rows_shape,
        compiler_params=params(4),
        cost_estimate=cost(10000000, 1),
        name="base_rows",
    )(keep.reshape(-1), home_theta.reshape(-1), rows, home)

    base, *rest = lax.optimization_barrier((base, *theta_there, *arrived))
    theta_there, arrived = rest[:2], rest[2:]
    last = shifted(behind, "region", SHIFTS[3])
    got = jnp.concatenate(theta_there)
    members = lax.axis_size("dest")
    other = lax.ppermute(got, "dest", [(i, i ^ 1) for i in range(members)])
    scale = jnp.concatenate([got, other])

    base = pl.pallas_call(
        functools.partial(land_kernel, sizes, (0, 1, 2)),
        in_specs=[SMEM_WHOLE] * 2 + [VMEM_WHOLE] * 4,
        out_specs=VMEM_WHOLE,
        out_shape=rows_shape,
        input_output_aliases={5: 0},
        compiler_params=params(4),
        cost_estimate=cost(4000000000, 1),
        name="land_first",
    )(scale.reshape(-1), land, *arrived, base)

    out, _ = pl.pallas_call(
        functools.partial(finish_kernel, sizes, (3,), chunk),
        in_specs=[SMEM_WHOLE] + [VMEM_WHOLE] * 2,
        out_specs=[ANYWHERE, VMEM_WHOLE],
        out_shape=[jax.ShapeDtypeStruct((cells, width), F32), rows_shape],
        scratch_shapes=[
            pltpu.VMEM((cells, width), F32),
            pltpu.SemaphoreType.DMA((cells // chunk,)),
        ],
        input_output_aliases={2: 1},
        compiler_params=params(12),
        cost_estimate=cost(cells * width, cells * row_bytes),
        name="finish",
    )(land, last, base)
    return out


def solution(mesh):
    return jax.shard_map(
        on_device,
        mesh=mesh,
        in_specs=(
            P("region", "dest"),
            P("region"),
            P("region"),
            P("region"),
            P(None, "region"),
            P(None, "region"),
            P("region", None),
            P("region", None),
            P("region", "dest"),
        ),
        out_specs=P("region", "dest"),
        check_vma=False,
    )
```

```python
import functools

import jax
import jax.numpy as jnp
from jax import lax
from jax.experimental import pallas as pl
from jax.experimental.pallas import tpu as pltpu
from jax.sharding import PartitionSpec as P

SHIFTS = (1, -1, 2, -2)
LANES = 128
MIB = 1 << 20
F32 = jnp.float32
I32 = jnp.int32
VMEM_WHOLE = pl.BlockSpec(memory_space=pltpu.VMEM)
SMEM_WHOLE = pl.BlockSpec(memory_space=pltpu.SMEM)
ANYWHERE = pl.BlockSpec(memory_space=pl.ANY)


def to_neighbours(block):
    regions, members = lax.axis_size("region"), lax.axis_size("dest")
    route = [
        (r * members + d, (r + SHIFTS[d % 4]) % regions * members + d)
        for r in range(regions)
        for d in range(members)
    ]
    return lax.ppermute(block, ("region", "dest"), route)


def to_two(block, first):
    regions, members = lax.axis_size("region"), lax.axis_size("dest")
    route = [
        (r * members + d, (r + SHIFTS[first + d % 2]) % regions * members + d)
        for r in range(regions)
        for d in range(members)
    ]
    return lax.ppermute(block, ("region", "dest"), route)


def shifted(block, axis, distance):
    devices = range(lax.axis_size(axis))
    route = [((i - distance) % len(devices), i) for i in devices]
    return lax.ppermute(block, axis, route)


def partners(block, axis):
    count = lax.axis_size(axis)
    return [block] + [
        lax.ppermute(block, axis, [(i, i ^ other) for i in range(count)])
        for other in range(1, count)
    ]


def tree_sum(parts):
    while len(parts) > 1:
        parts = [parts[k] + parts[k + 1] for k in range(0, len(parts), 2)]
    return parts[0]


def params(mib):
    return pltpu.CompilerParams(vmem_limit_bytes=mib * MIB)


def cost(flops, moved):
    return pl.CostEstimate(flops=flops, bytes_accessed=moved, transcendentals=0)


def lane_sums(partial):
    count = partial.shape[0]
    parts = jnp.dot(
        in_parts(partial), jnp.ones((LANES, LANES), jnp.bfloat16), preferred_element_type=F32
    )
    sums = parts[:count, :] + parts[count : 2 * count, :] + parts[2 * count :, :]
    row = lax.broadcasted_iota(I32, (LANES, LANES), 0)
    lane = lax.broadcasted_iota(I32, (LANES, LANES), 1)
    pieces = [
        jnp.sum(jnp.where(row == lane, sums[k : k + LANES, :], 0.0), axis=0, keepdims=True)
        for k in range(0, partial.shape[0], LANES)
    ]
    return jnp.concatenate(pieces, axis=0)


def stacked(row):
    return jnp.concatenate(
        [row[:, k : k + LANES] for k in range(0, row.shape[1], LANES)], axis=0
    )


def strung(rows):
    return jnp.concatenate([rows[k : k + 1, :] for k in range(rows.shape[0])], axis=1)


def row_of(ref, number, sub):
    if sub % 8 == 0:
        return ref.reshape(ref.shape[0] // sub, sub, LANES).at[number]
    return ref.at[pl.ds(pl.multiple_of(number * sub, sub), sub), :]


def padded(cap):
    return -(-cap // LANES) * LANES


def put_row(ref, row, value, fill):
    width = value.shape[1]
    for q in range(-(-width // LANES)):
        piece = value[:, q * LANES : min((q + 1) * LANES, width)]
        lack = LANES - piece.shape[1]
        if lack:
            piece = jnp.concatenate([piece, jnp.full((1, lack), fill, piece.dtype)], axis=1)
        ref[row + q : row + q + 1, :] = piece


def one_hot(index, count):
    rows = lax.broadcasted_iota(I32, (count, index.shape[1]), 0)
    return jnp.where(rows == index, 1.0, 0.0)


def in_parts(x):
    high = x.astype(jnp.bfloat16)
    rest = x - high.astype(F32)
    middle = rest.astype(jnp.bfloat16)
    low = (rest - middle.astype(F32)).astype(jnp.bfloat16)
    return jnp.concatenate([high, middle, low], axis=0)


def selected(values, choice, dims):
    count = values.shape[0]
    product = lax.dot_general(
        in_parts(values), choice.astype(jnp.bfloat16), (dims, ((), ())),
        preferred_element_type=F32,
    )
    return product[:count, :] + product[count : 2 * count, :] + product[2 * count :, :]


def look_up(table, index):
    picked = selected(table.T, one_hot(index // LANES, table.shape[0]), ((1,), (0,)))
    return jnp.sum(picked * one_hot(index % LANES, LANES), axis=0, keepdims=True)


def scatter(index, values, height):
    high = jnp.where(index >= 0, index // LANES, -1)
    low = jnp.where(index >= 0, index % LANES, -1)
    return selected(one_hot(high, height) * values, one_hot(low, LANES), ((1,), (1,)))


def home_cells(node_out, region_no, cells):
    here = (node_out >= 0) & (node_out // cells == region_no)
    return jnp.where(here, node_out % cells, -1)


def rows_of_group(x_ref, rows_ref, first, sub):
    total = None
    for q in range(sub):
        piece = x_ref[pl.ds(pl.multiple_of(first, 8), 8), q * LANES : (q + 1) * LANES]
        rows_ref[pl.ds(first * sub + q, 8, stride=sub), :] = piece
        total = piece if total is None else total + piece
    return total


def copies_in(source, target, sems, chunk):
    copies = [
        pltpu.make_async_copy(
            source.at[pl.ds(i * chunk, chunk), :], target.at[pl.ds(i * chunk, chunk), :], sems.at[i]
        )
        for i in range(target.shape[0] // chunk)
    ]
    for copy in copies:
        copy.start()
    return copies


def make_lists(
    sizes, node_in, node_out, send_list, recv_list,
    in_cell, send_node, send_outlet, land, source_node, source_outlet,
):
    cells, nodes, branches, cap, sub = sizes
    height = cells // LANES
    region_no = lax.axis_index("region")
    ids = lax.broadcasted_iota(I32, (1, nodes), 1).astype(F32) + 1.0
    number = jnp.zeros((height, LANES), F32)
    slot = jnp.zeros((height, LANES), F32)
    for j in range(branches):
        ins = node_in[j : j + 1, :]
        put_row(in_cell, j * (nodes // LANES), jnp.where(ins >= 0, ins, cells), cells)
        home = home_cells(node_out[j : j + 1, :], region_no, cells)
        here = scatter(home, ids, height)
        number = number + here
        slot = slot + jnp.where(here > 0.0, j + 1.0, 0.0)
    source_node[...] = jnp.maximum(number.astype(I32) - 1, 0)
    source_outlet[...] = slot.astype(I32) - 1
    per_side = padded(cap) // LANES
    for side in range(4):
        slots = send_list[side : side + 1, :]
        lands = recv_list[side : side + 1, :]
        put_row(send_node, side * per_side, jnp.where(slots >= 0, slots % nodes, 0), 0)
        put_row(send_outlet, side * per_side, jnp.where(slots >= 0, slots // nodes, -1), -1)
        put_row(land, side * per_side, jnp.where(lands >= 0, lands, cells), cells)


def cell_sum_kernel(chunk, sub, x_hbm, sum_ref, rows_ref, x, partial, sems):
    copies = copies_in(x_hbm, x, sems, chunk)
    zeros = rows_ref.shape[0] - sub
    rows_ref[zeros:, :] = jnp.zeros((sub, LANES), F32)
    for number, copy in enumerate(copies):
        copy.wait()

        def body(step, carry, number=number):
            for half in range(2):
                first = number * chunk + step * 16 + half * 8
                total = rows_of_group(x, rows_ref, first, sub)
                partial[pl.ds(pl.multiple_of(first, 8), 8), :] = total
            return carry

        lax.fori_loop(0, chunk // 16, body, 0)
    sum_ref[...] = lane_sums(partial[...])


def turn_rows_kernel(sizes, chunk, x_hbm, after_ref, *rest):
    cells, nodes, branches, cap, sub = sizes
    lists, rows_ref, made, (x, sems) = rest[:4], rest[4], rest[5:11], rest[11:]
    copies = copies_in(x_hbm, x, sems, chunk)
    make_lists(sizes, *lists, *made)
    for number, copy in enumerate(copies):
        copy.wait()

        def body(step, carry, number=number):
            for half in range(2):
                rows_of_group(x, rows_ref, number * chunk + step * 16 + half * 8, sub)
            return carry

        lax.fori_loop(0, chunk // 16, body, 0)


def gathered_flow(node, in_cell, fraction, rows, sizes):
    cells, nodes, branches, cap, sub = sizes
    parts = []
    for i in range(branches):
        cell = in_cell[i * nodes + node]
        part = row_of(rows, cell, sub)[...]
        parts.append(part if fraction is None else part * fraction[cell])
    return tree_sum(parts)


def scale_kernel(sizes, fraction, rows, sent_ref, supply_ref, scaled):
    cells, nodes, branches, cap, sub = sizes

    def body(step, carry):
        first = step * 16
        values = [
            row_of(rows, first + i, sub)[...] * fraction[first + i] for i in range(16)
        ]
        for i in range(16):
            row_of(scaled, first + i, sub)[...] = values[i]
        return carry

    lax.fori_loop(0, cells // 16, body, 0)
    row_of(scaled, cells, sub)[...] = jnp.zeros((sub, LANES), F32)


def send_kernel(sizes, sides, fraction, in_cell, send_node, send_outlet, rows, turns, *sends):
    cells, nodes, branches, cap, sub = sizes
    batch = 16
    for side, send in zip(sides, sends):

        def body(step, carry, side=side, send=send):
            first = step * batch
            values = []
            for i in range(batch):
                slot = side * padded(cap) + first + i
                node = send_node[slot]
                value = gathered_flow(node, in_cell, fraction, rows, sizes)
                choice = row_of(turns, node, sub)[...]
                values.append(jnp.where(choice == send_outlet[slot], value, 0.0))
            for i in range(batch):
                row_of(send, first + i, sub)[...] = values[i]
            return carry

        lax.fori_loop(0, cap // batch, body, 0)


def scaled_send_kernel(sizes, side, theta, send_node, send_outlet, flow, turns, send):
    cells, nodes, branches, cap, sub = sizes
    batch = 16

    def body(step, carry):
        first = step * batch
        values = []
        for i in range(batch):
            slot = side * padded(cap) + first + i
            node = send_node[slot]
            value = row_of(flow, node, sub)[...] * theta[node]
            choice = row_of(turns, node, sub)[...]
            values.append(jnp.where(choice == send_outlet[slot], value, 0.0))
        for i in range(batch):
            row_of(send, first + i, sub)[...] = values[i]
        return carry

    lax.fori_loop(0, cap // batch, body, 0)


def node_flow_kernel(sizes, in_cell, scaled, turns, after_ref, flow, demand, partial):
    cells, nodes, branches, cap, sub = sizes

    def gather(step, carry):
        first = step * 16
        values = [
            gathered_flow(first + i, in_cell, None, scaled, sizes) for i in range(16)
        ]
        for i in range(16):
            row_of(flow, first + i, sub)[...] = values[i]
        return carry

    def measure(step, carry):
        for half in range(2):
            first = step * 16 + half * 8
            totals = [jnp.zeros((8, LANES), F32)] * branches
            for q in range(sub):
                at = pl.ds(first * sub + q, 8, stride=sub)
                value = flow[at, :]
                choice = turns[at, :]
                totals = [
                    total + jnp.where(choice == j, value, 0.0) for j, total in enumerate(totals)
                ]
            for j in range(branches):
                partial[j, pl.ds(pl.multiple_of(first, 8), 8), :] = totals[j]
        return carry

    lax.fori_loop(0, nodes // 16, gather, 0)
    lax.fori_loop(0, nodes // 16, measure, 0)
    per_outlet = nodes // LANES
    for j in range(branches):
        demand[j * per_outlet : (j + 1) * per_outlet, :] = lane_sums(partial[j])


def theta_kernel(
    sizes, regions, commodities, supply, shared, node_out, send_list, theta_out, slot_theta
):
    cells, nodes, branches, cap, sub = sizes
    per_outlet = nodes // LANES
    height = cells // LANES
    block = branches * per_outlet + height
    region_no = lax.axis_index("region")
    members = shared.shape[0] // block
    parts = [
        shared[d * block : d * block + branches * per_outlet, :] for d in range(members)
    ]
    demand = tree_sum(parts) * (1.0 / commodities)
    table = jnp.concatenate(
        [supply[...]]
        + [
            shared[d * block + branches * per_outlet : (d + 1) * block, :] for d in range(4)
        ],
        axis=0,
    )
    tall = jnp.ones((per_outlet, LANES), F32)
    for j in range(branches):
        outs = node_out[j : j + 1, :]
        cell = jnp.maximum(outs, 0)
        offset = (cell // cells + regions - region_no) % regions
        sector = jnp.zeros_like(offset)
        for d in range(4):
            sector = jnp.where(offset == (-SHIFTS[d]) % regions, d + 1, sector)
        room = stacked(look_up(table, sector * cells + cell % cells))
        ratio = room / jnp.maximum(demand[j * per_outlet : (j + 1) * per_outlet, :], room)
        tall = jnp.minimum(tall, jnp.where(stacked(outs) >= 0, ratio, 1.0))
    theta_out[...] = tall
    per_side = padded(cap) // LANES
    for k in range(2):
        slots = send_list[pl.ds(2 * k + lax.axis_index("dest") % 2, 1), :]
        there = look_up(tall, jnp.where(slots >= 0, slots % nodes, 0))
        put_row(slot_theta, k * per_side, there, 0.0)


def keep_kernel(
    sizes, theta_ref, node_in, node_out, fraction, sent_ref, arrived_ref, keep, home_theta
):
    cells, nodes, branches, cap, sub = sizes
    height = cells // LANES
    region_no = lax.axis_index("region")
    theta = strung(theta_ref[...])
    cell_theta = jnp.zeros((height, LANES), F32)
    into = jnp.zeros((height, LANES), F32)
    for j in range(branches):
        home = home_cells(node_out[j : j + 1, :], region_no, cells)
        cell_theta = cell_theta + scatter(node_in[j : j + 1, :], theta, height)
        into = into + scatter(home, theta, height)
    keep[...] = 1.0 - cell_theta * fraction[...]
    home_theta[...] = into


def home_kernel(sizes, source, outlet, turns, flow, after_ref, home):
    cells, nodes, branches, cap, sub = sizes
    batch = 16

    def body(step, carry):
        first = step * batch
        values = []
        for i in range(batch):
            node = source[first + i]
            choice = row_of(turns, node, sub)[...]
            moved = row_of(flow, node, sub)[...]
            values.append(jnp.where(choice == outlet[first + i], moved, 0.0))
        for i in range(batch):
            row_of(home, first + i, sub)[...] = values[i]
        return carry

    lax.fori_loop(0, cells // batch, body, 0)


def base_kernel(sizes, keep, home_theta, rows, home, base):
    cells, nodes, branches, cap, sub = sizes
    batch = 16

    def body(step, carry):
        first = step * batch
        values = []
        for i in range(batch):
            cell = first + i
            kept = row_of(rows, cell, sub)[...] * keep[cell]
            values.append(kept + row_of(home, cell, sub)[...] * home_theta[cell])
        for i in range(batch):
            row_of(base, first + i, sub)[...] = values[i]
        return carry

    lax.fori_loop(0, cells // batch, body, 0)


def land_rows(sizes, sides, scale, land, received, base):
    cells, nodes, branches, cap, sub = sizes
    batch = 16
    core = lax.axis_index("dest") % 2
    for side, rows in zip(sides, received):
        offset = jnp.where(core == side % 2, 0, 2 * padded(cap)) + side // 2 * padded(cap)

        def body(step, carry, side=side, rows=rows, offset=offset):
            first = step * batch
            stores = []
            for i in range(batch):
                at = row_of(base, land[side * padded(cap) + first + i], sub)
                value = row_of(rows, first + i, sub)[...]
                if scale is not None:
                    value = value * scale[offset + first + i]
                stores.append((at, at[...] + value))
            for at, value in stores:
                at[...] = value
            return carry

        lax.fori_loop(0, cap // batch, body, 0)


def land_kernel(sizes, sides, scale, land, *rest):
    received, (base_in, base) = rest[: len(sides)], rest[len(sides) :]
    land_rows(sizes, sides, scale, land, received, base)


def finish_kernel(sizes, sides, chunk, land, *rest):
    cells, nodes, branches, cap, sub = sizes
    received, (base_in, out, base, staged, sems) = rest[: len(sides)], rest[len(sides) :]
    land_rows(sizes, sides, None, land, received, base)
    copies = []
    for number in range(cells // chunk):

        def body(step, carry, number=number):
            for half in range(2):
                first = number * chunk + step * 16 + half * 8
                for q in range(sub):
                    staged[
                        pl.ds(pl.multiple_of(first, 8), 8), q * LANES : (q + 1) * LANES
                    ] = base[pl.ds(first * sub + q, 8, stride=sub), :]
            return carry

        lax.fori_loop(0, chunk // 16, body, 0)
        at = pl.ds(number * chunk, chunk)
        copies.append(
            pltpu.make_async_copy(staged.at[at, :], out.at[at, :], sems.at[number])
        )
        copies[-1].start()
    for copy in copies:
        copy.wait()


def on_device(occupancy, capacity, jam, wave, node_in, node_out, send_list, recv_list, turn):
    cells, width = occupancy.shape
    branches, nodes = node_in.shape
    cap = send_list.shape[1]
    sub = width // LANES
    sizes = (cells, nodes, branches, cap, sub)
    regions = lax.axis_size("region")
    commodities = width * lax.axis_size("dest")
    height = cells // LANES
    per_cell = (height, LANES)
    list_shape = (4 * padded(cap) // LANES, LANES)
    chunk = 128
    row_bytes = width * 4
    occupancy = pltpu.with_memory_space_constraint(occupancy, pltpu.HBM)
    turn = pltpu.with_memory_space_constraint(turn, pltpu.HBM)

    local_sum, rows = pl.pallas_call(
        functools.partial(cell_sum_kernel, chunk, sub),
        in_specs=[ANYWHERE],
        out_specs=[VMEM_WHOLE] * 2,
        out_shape=[
            jax.ShapeDtypeStruct(per_cell, F32),
            pltpu.VMEM(((cells + 1) * sub, LANES), F32),
        ],
        scratch_shapes=[
            pltpu.VMEM((cells, width), F32),
            pltpu.VMEM((cells, LANES), F32),
            pltpu.SemaphoreType.DMA((cells // chunk,)),
        ],
        compiler_params=params(14),
        cost_estimate=cost(cells * width, cells * row_bytes),
        name="cell_sum",
    )(occupancy)

    sums = partners(local_sum, "dest")

    turns, *lists = pl.pallas_call(
        functools.partial(turn_rows_kernel, sizes, chunk),
        in_specs=[ANYWHERE] * 2 + [VMEM_WHOLE] * 4,
        out_specs=[VMEM_WHOLE] * 7,
        out_shape=[
            pltpu.VMEM((nodes * sub, LANES), I32),
            jax.ShapeDtypeStruct((branches * nodes // LANES, LANES), I32),
        ]
        + [jax.ShapeDtypeStruct(list_shape, I32)] * 3
        + [jax.ShapeDtypeStruct(per_cell, I32)] * 2,
        scratch_shapes=[
            pltpu.VMEM((nodes, width), I32),
            pltpu.SemaphoreType.DMA((nodes // chunk,)),
        ],
        compiler_params=params(8),
        cost_estimate=cost(0, nodes * row_bytes),
        name="turn_rows",
    )(turn, local_sum, node_in, node_out, send_list, recv_list)
    in_cell, send_node, send_outlet, land, source_node, source_outlet = (
        x.reshape(-1) for x in lists
    )

    turns, *sums = lax.optimization_barrier((turns, *sums))
    vehicles = tree_sum(sums) / commodities
    cap_of = capacity.reshape(per_cell)
    fraction = jnp.minimum(vehicles, cap_of) / vehicles
    supply = jnp.minimum(cap_of, wave.reshape(per_cell) * (jam.reshape(per_cell) - vehicles))
    rows_shape = pltpu.VMEM(((cells + 1) * sub, LANES), F32)
    send_shape = pltpu.VMEM((cap * sub, LANES), F32)

    supply_there = to_neighbours(supply)
    weights = jnp.concatenate([fraction.reshape(-1), jnp.zeros((LANES,), F32)])
    (ahead,) = pl.pallas_call(
        functools.partial(send_kernel, sizes, (2,)),
        in_specs=[SMEM_WHOLE] * 4 + [VMEM_WHOLE] * 2,
        out_specs=[VMEM_WHOLE],
        out_shape=[send_shape],
        compiler_params=params(4),
        cost_estimate=cost(1, 1),
        name="send_ahead",
    )(weights, in_cell, send_node, send_outlet, rows, turns)
    scaled = pl.pallas_call(
        functools.partial(scale_kernel, sizes),
        in_specs=[SMEM_WHOLE, VMEM_WHOLE, ANYWHERE, ANYWHERE],
        out_specs=VMEM_WHOLE,
        out_shape=rows_shape,
        compiler_params=params(4),
        cost_estimate=cost(10000000000, 1),
        name="scale_rows",
    )(fraction.reshape(-1), rows, ahead, supply_there)
    near = pl.pallas_call(
        functools.partial(send_kernel, sizes, (0, 1), None),
        in_specs=[SMEM_WHOLE] * 3 + [VMEM_WHOLE] * 2,
        out_specs=[VMEM_WHOLE] * 2,
        out_shape=[send_shape] * 2,
        compiler_params=params(4),
        cost_estimate=cost(1, 1),
        name="send_near",
    )(in_cell, send_node, send_outlet, scaled, turns)
    arrived = [
        shifted(send, "region", SHIFTS[side]) for side, send in enumerate([*near, ahead])
    ]

    flow, demand = pl.pallas_call(
        functools.partial(node_flow_kernel, sizes),
        in_specs=[SMEM_WHOLE] + [VMEM_WHOLE] * 2 + [ANYWHERE],
        out_specs=[VMEM_WHOLE] * 2,
        out_shape=[
            pltpu.VMEM((nodes * sub, LANES), F32),
            jax.ShapeDtypeStruct((branches * nodes // LANES, LANES), F32),
        ],
        scratch_shapes=[pltpu.VMEM((branches, nodes, LANES), F32)],
        compiler_params=params(8),
        cost_estimate=cost(1, 1),
        name="node_flow",
    )(in_cell, scaled, turns, near[0])

    joined = jnp.concatenate([demand, supply_there])
    shared = lax.all_gather(joined, "dest", axis=0, tiled=True)
    theta, slot_theta = pl.pallas_call(
        functools.partial(theta_kernel, sizes, regions, commodities),
        in_specs=[VMEM_WHOLE] * 4,
        out_specs=[VMEM_WHOLE] * 2,
        out_shape=[
            jax.ShapeDtypeStruct((nodes // LANES, LANES), F32),
            jax.ShapeDtypeStruct((2 * padded(cap) // LANES, LANES), F32),
        ],
        compiler_params=params(8),
        cost_estimate=cost(1, 1),
        name="theta",
    )(supply, shared, node_out, send_list)
    theta, slot_theta, arrived[2] = lax.optimization_barrier((theta, slot_theta, arrived[2]))
    per_side = padded(cap) // LANES
    theta_there = [to_two(slot_theta[:per_side], 0), to_two(slot_theta[per_side:], 2)]

    (behind,) = pl.pallas_call(
        functools.partial(scaled_send_kernel, sizes, 3),
        in_specs=[SMEM_WHOLE] * 3 + [VMEM_WHOLE] * 2,
        out_specs=[VMEM_WHOLE],
        out_shape=[send_shape],
        compiler_params=params(4),
        cost_estimate=cost(1, 1),
        name="send_scaled",
    )(theta.reshape(-1), send_node, send_outlet, flow, turns)
    home = pl.pallas_call(
        functools.partial(home_kernel, sizes),
        in_specs=[SMEM_WHOLE] * 2 + [VMEM_WHOLE] * 2 + [ANYWHERE],
        out_specs=VMEM_WHOLE,
        out_shape=rows_shape,
        compiler_params=params(4),
        cost_estimate=cost(4000000000, 1),
        name="home_rows",
    )(source_node, source_outlet, turns, flow, behind)
    keep, home_theta = pl.pallas_call(
        functools.partial(keep_kernel, sizes),
        in_specs=[VMEM_WHOLE] * 4 + [ANYWHERE] * 2,
        out_specs=[VMEM_WHOLE] * 2,
        out_shape=[jax.ShapeDtypeStruct(per_cell, F32)] * 2,
        compiler_params=params(8),
        cost_estimate=cost(10000000, 1),
        name="keep",
    )(theta, node_in, node_out, fraction, behind, arrived[2])
    base = pl.pallas_call(
        functools.partial(base_kernel, sizes),
        in_specs=[SMEM_WHOLE] * 2 + [VMEM_WHOLE] * 2,
        out_specs=VMEM_WHOLE,
        out_shape=rows_shape,
        compiler_params=params(4),
        cost_estimate=cost(10000000, 1),
        name="base_rows",
    )(keep.reshape(-1), home_theta.reshape(-1), rows, home)

    base, *rest = lax.optimization_barrier((base, *theta_there, *arrived))
    theta_there, arrived = rest[:2], rest[2:]
    last = shifted(behind, "region", SHIFTS[3])
    got = jnp.concatenate(theta_there)
    members = lax.axis_size("dest")
    other = lax.ppermute(got, "dest", [(i, i ^ 1) for i in range(members)])
    scale = jnp.concatenate([got, other])

    base = pl.pallas_call(
        functools.partial(land_kernel, sizes, (0, 1, 2)),
        in_specs=[SMEM_WHOLE] * 2 + [VMEM_WHOLE] * 4,
        out_specs=VMEM_WHOLE,
        out_shape=rows_shape,
        input_output_aliases={5: 0},
        compiler_params=params(4),
        cost_estimate=cost(4000000000, 1),
        name="land_first",
    )(scale.reshape(-1), land, *arrived, base)

    out, _ = pl.pallas_call(
        functools.partial(finish_kernel, sizes, (3,), chunk),
        in_specs=[SMEM_WHOLE] + [VMEM_WHOLE] * 2,
        out_specs=[ANYWHERE, VMEM_WHOLE],
        out_shape=[jax.ShapeDtypeStruct((cells, width), F32), rows_shape],
        scratch_shapes=[
            pltpu.VMEM((cells, width), F32),
            pltpu.SemaphoreType.DMA((cells // chunk,)),
        ],
        input_output_aliases={2: 1},
        compiler_params=params(12),
        cost_estimate=cost(cells * width, cells * row_bytes),
        name="finish",
    )(land, last, base)
    return out


def solution(mesh):
    return jax.shard_map(
        on_device,
        mesh=mesh,
        in_specs=(
            P("region", "dest"),
            P("region"),
            P("region"),
            P("region"),
            P(None, "region"),
            P(None, "region"),
            P("region", None),
            P("region", None),
            P("region", "dest"),
        ),
        out_specs=P("region", "dest"),
        check_vma=False,
    )
```

```python
import functools

import jax
import jax.numpy as jnp
from jax import lax
from jax.experimental import pallas as pl
from jax.experimental.pallas import tpu as pltpu
from jax.sharding import PartitionSpec as P

SHIFTS = (1, -1, 2, -2)
LANES = 128
MIB = 1 << 20
F32 = jnp.float32
I32 = jnp.int32
VMEM_WHOLE = pl.BlockSpec(memory_space=pltpu.VMEM)
SMEM_WHOLE = pl.BlockSpec(memory_space=pltpu.SMEM)
ANYWHERE = pl.BlockSpec(memory_space=pl.ANY)


def to_neighbours(block):
    regions, members = lax.axis_size("region"), lax.axis_size("dest")
    route = [
        (r * members + d, (r + SHIFTS[d % 4]) % regions * members + d)
        for r in range(regions)
        for d in range(members)
    ]
    return lax.ppermute(block, ("region", "dest"), route)


def to_two(block, first):
    regions, members = lax.axis_size("region"), lax.axis_size("dest")
    route = [
        (r * members + d, (r + SHIFTS[first + d % 2]) % regions * members + d)
        for r in range(regions)
        for d in range(members)
    ]
    return lax.ppermute(block, ("region", "dest"), route)


def shifted(block, axis, distance):
    devices = range(lax.axis_size(axis))
    route = [((i - distance) % len(devices), i) for i in devices]
    return lax.ppermute(block, axis, route)


def partners(block, axis):
    count = lax.axis_size(axis)
    return [block] + [
        lax.ppermute(block, axis, [(i, i ^ other) for i in range(count)])
        for other in range(1, count)
    ]


def tree_sum(parts):
    while len(parts) > 1:
        parts = [parts[k] + parts[k + 1] for k in range(0, len(parts), 2)]
    return parts[0]


def params(mib):
    return pltpu.CompilerParams(vmem_limit_bytes=mib * MIB)


def cost(flops, moved):
    return pl.CostEstimate(flops=flops, bytes_accessed=moved, transcendentals=0)


def lane_sums(partial):
    count = partial.shape[0]
    parts = jnp.dot(
        in_parts(partial), jnp.ones((LANES, LANES), jnp.bfloat16), preferred_element_type=F32
    )
    sums = parts[:count, :] + parts[count : 2 * count, :] + parts[2 * count :, :]
    row = lax.broadcasted_iota(I32, (LANES, LANES), 0)
    lane = lax.broadcasted_iota(I32, (LANES, LANES), 1)
    pieces = [
        jnp.sum(jnp.where(row == lane, sums[k : k + LANES, :], 0.0), axis=0, keepdims=True)
        for k in range(0, partial.shape[0], LANES)
    ]
    return jnp.concatenate(pieces, axis=0)


def stacked(row):
    return jnp.concatenate(
        [row[:, k : k + LANES] for k in range(0, row.shape[1], LANES)], axis=0
    )


def strung(rows):
    return jnp.concatenate([rows[k : k + 1, :] for k in range(rows.shape[0])], axis=1)


def row_of(ref, number, sub):
    if sub % 8 == 0:
        return ref.reshape(ref.shape[0] // sub, sub, LANES).at[number]
    return ref.at[pl.ds(pl.multiple_of(number * sub, sub), sub), :]


def padded(cap):
    return -(-cap // LANES) * LANES


def put_row(ref, row, value, fill):
    width = value.shape[1]
    for q in range(-(-width // LANES)):
        piece = value[:, q * LANES : min((q + 1) * LANES, width)]
        lack = LANES - piece.shape[1]
        if lack:
            piece = jnp.concatenate([piece, jnp.full((1, lack), fill, piece.dtype)], axis=1)
        ref[row + q : row + q + 1, :] = piece


def one_hot(index, count):
    rows = lax.broadcasted_iota(I32, (count, index.shape[1]), 0)
    return jnp.where(rows == index, 1.0, 0.0)


def in_parts(x):
    high = x.astype(jnp.bfloat16)
    rest = x - high.astype(F32)
    middle = rest.astype(jnp.bfloat16)
    low = (rest - middle.astype(F32)).astype(jnp.bfloat16)
    return jnp.concatenate([high, middle, low], axis=0)


def selected(values, choice, dims):
    count = values.shape[0]
    product = lax.dot_general(
        in_parts(values), choice.astype(jnp.bfloat16), (dims, ((), ())),
        preferred_element_type=F32,
    )
    return product[:count, :] + product[count : 2 * count, :] + product[2 * count :, :]


def look_up(table, index):
    picked = selected(table.T, one_hot(index // LANES, table.shape[0]), ((1,), (0,)))
    return jnp.sum(picked * one_hot(index % LANES, LANES), axis=0, keepdims=True)


def scatter(index, values, height):
    high = jnp.where(index >= 0, index // LANES, -1)
    low = jnp.where(index >= 0, index % LANES, -1)
    return selected(one_hot(high, height) * values, one_hot(low, LANES), ((1,), (1,)))


def home_cells(node_out, region_no, cells):
    here = (node_out >= 0) & (node_out // cells == region_no)
    return jnp.where(here, node_out % cells, -1)


def rows_of_group(x_ref, rows_ref, first, sub):
    total = None
    for q in range(sub):
        piece = x_ref[pl.ds(pl.multiple_of(first, 8), 8), q * LANES : (q + 1) * LANES]
        rows_ref[pl.ds(first * sub + q, 8, stride=sub), :] = piece
        total = piece if total is None else total + piece
    return total


def copies_in(source, target, sems, chunk):
    copies = [
        pltpu.make_async_copy(
            source.at[pl.ds(i * chunk, chunk), :], target.at[pl.ds(i * chunk, chunk), :], sems.at[i]
        )
        for i in range(target.shape[0] // chunk)
    ]
    for copy in copies:
        copy.start()
    return copies


def make_lists(
    sizes, node_in, node_out, send_list, recv_list,
    in_cell, send_node, send_outlet, land, source_node, source_outlet,
):
    cells, nodes, branches, cap, sub = sizes
    height = cells // LANES
    region_no = lax.axis_index("region")
    ids = lax.broadcasted_iota(I32, (1, nodes), 1).astype(F32) + 1.0
    number = jnp.zeros((height, LANES), F32)
    slot = jnp.zeros((height, LANES), F32)
    for j in range(branches):
        ins = node_in[j : j + 1, :]
        put_row(in_cell, j * (nodes // LANES), jnp.where(ins >= 0, ins, cells), cells)
        home = home_cells(node_out[j : j + 1, :], region_no, cells)
        here = scatter(home, ids, height)
        number = number + here
        slot = slot + jnp.where(here > 0.0, j + 1.0, 0.0)
    source_node[...] = jnp.maximum(number.astype(I32) - 1, 0)
    source_outlet[...] = slot.astype(I32) - 1
    per_side = padded(cap) // LANES
    for side in range(4):
        slots = send_list[side : side + 1, :]
        lands = recv_list[side : side + 1, :]
        put_row(send_node, side * per_side, jnp.where(slots >= 0, slots % nodes, 0), 0)
        put_row(send_outlet, side * per_side, jnp.where(slots >= 0, slots // nodes, -1), -1)
        put_row(land, side * per_side, jnp.where(lands >= 0, lands, cells), cells)


def cell_sum_kernel(chunk, sub, x_hbm, sum_ref, rows_ref, x, partial, sems):
    copies = copies_in(x_hbm, x, sems, chunk)
    zeros = rows_ref.shape[0] - sub
    rows_ref[zeros:, :] = jnp.zeros((sub, LANES), F32)
    for number, copy in enumerate(copies):
        copy.wait()

        def body(step, carry, number=number):
            for half in range(2):
                first = number * chunk + step * 16 + half * 8
                total = rows_of_group(x, rows_ref, first, sub)
                partial[pl.ds(pl.multiple_of(first, 8), 8), :] = total
            return carry

        lax.fori_loop(0, chunk // 16, body, 0)
    sum_ref[...] = lane_sums(partial[...])


def turn_rows_kernel(sizes, chunk, x_hbm, after_ref, *rest):
    cells, nodes, branches, cap, sub = sizes
    lists, rows_ref, made, (x, sems) = rest[:4], rest[4], rest[5:11], rest[11:]
    copies = copies_in(x_hbm, x, sems, chunk)
    make_lists(sizes, *lists, *made)
    for number, copy in enumerate(copies):
        copy.wait()

        def body(step, carry, number=number):
            for half in range(2):
                rows_of_group(x, rows_ref, number * chunk + step * 16 + half * 8, sub)
            return carry

        lax.fori_loop(0, chunk // 16, body, 0)


def gathered_flow(node, in_cell, fraction, rows, sizes):
    cells, nodes, branches, cap, sub = sizes
    parts = []
    for i in range(branches):
        cell = in_cell[i * nodes + node]
        part = row_of(rows, cell, sub)[...]
        parts.append(part if fraction is None else part * fraction[cell])
    return tree_sum(parts)


def scale_kernel(sizes, fraction, rows, sent_ref, supply_ref, scaled):
    cells, nodes, branches, cap, sub = sizes

    def body(step, carry):
        first = step * 16
        values = [
            row_of(rows, first + i, sub)[...] * fraction[first + i] for i in range(16)
        ]
        for i in range(16):
            row_of(scaled, first + i, sub)[...] = values[i]
        return carry

    lax.fori_loop(0, cells // 16, body, 0)
    row_of(scaled, cells, sub)[...] = jnp.zeros((sub, LANES), F32)


def send_kernel(sizes, parts, fraction, in_cell, send_node, send_outlet, rows, turns, *sends):
    cells, nodes, branches, cap, sub = sizes
    batch = 16
    for (side, start, count), send in zip(parts, sends):

        def body(step, carry, side=side, start=start, send=send):
            first = step * batch
            values = []
            for i in range(batch):
                slot = side * padded(cap) + start + first + i
                node = send_node[slot]
                value = gathered_flow(node, in_cell, fraction, rows, sizes)
                choice = row_of(turns, node, sub)[...]
                values.append(jnp.where(choice == send_outlet[slot], value, 0.0))
            for i in range(batch):
                row_of(send, first + i, sub)[...] = values[i]
            return carry

        lax.fori_loop(0, count // batch, body, 0)


def scaled_send_kernel(sizes, part, theta, send_node, send_outlet, flow, turns, send):
    cells, nodes, branches, cap, sub = sizes
    side, start, count = part
    batch = 16

    def body(step, carry):
        first = step * batch
        values = []
        for i in range(batch):
            slot = side * padded(cap) + start + first + i
            node = send_node[slot]
            value = row_of(flow, node, sub)[...] * theta[node]
            choice = row_of(turns, node, sub)[...]
            values.append(jnp.where(choice == send_outlet[slot], value, 0.0))
        for i in range(batch):
            row_of(send, first + i, sub)[...] = values[i]
        return carry

    lax.fori_loop(0, count // batch, body, 0)


def node_flow_kernel(sizes, in_cell, scaled, turns, after_ref, flow, demand, partial):
    cells, nodes, branches, cap, sub = sizes

    def gather(step, carry):
        first = step * 16
        values = [
            gathered_flow(first + i, in_cell, None, scaled, sizes) for i in range(16)
        ]
        for i in range(16):
            row_of(flow, first + i, sub)[...] = values[i]
        return carry

    def measure(step, carry):
        for half in range(2):
            first = step * 16 + half * 8
            totals = [jnp.zeros((8, LANES), F32)] * branches
            for q in range(sub):
                at = pl.ds(first * sub + q, 8, stride=sub)
                value = flow[at, :]
                choice = turns[at, :]
                totals = [
                    total + jnp.where(choice == j, value, 0.0) for j, total in enumerate(totals)
                ]
            for j in range(branches):
                partial[j, pl.ds(pl.multiple_of(first, 8), 8), :] = totals[j]
        return carry

    lax.fori_loop(0, nodes // 16, gather, 0)
    lax.fori_loop(0, nodes // 16, measure, 0)
    per_outlet = nodes // LANES
    for j in range(branches):
        demand[j * per_outlet : (j + 1) * per_outlet, :] = lane_sums(partial[j])


def theta_kernel(
    sizes, regions, commodities, supply, shared, node_out, send_list, theta_out, slot_theta
):
    cells, nodes, branches, cap, sub = sizes
    per_outlet = nodes // LANES
    height = cells // LANES
    block = branches * per_outlet + height
    region_no = lax.axis_index("region")
    members = shared.shape[0] // block
    parts = [
        shared[d * block : d * block + branches * per_outlet, :] for d in range(members)
    ]
    demand = tree_sum(parts) * (1.0 / commodities)
    table = jnp.concatenate(
        [supply[...]]
        + [
            shared[d * block + branches * per_outlet : (d + 1) * block, :] for d in range(4)
        ],
        axis=0,
    )
    tall = jnp.ones((per_outlet, LANES), F32)
    for j in range(branches):
        outs = node_out[j : j + 1, :]
        cell = jnp.maximum(outs, 0)
        offset = (cell // cells + regions - region_no) % regions
        sector = jnp.zeros_like(offset)
        for d in range(4):
            sector = jnp.where(offset == (-SHIFTS[d]) % regions, d + 1, sector)
        room = stacked(look_up(table, sector * cells + cell % cells))
        ratio = room / jnp.maximum(demand[j * per_outlet : (j + 1) * per_outlet, :], room)
        tall = jnp.minimum(tall, jnp.where(stacked(outs) >= 0, ratio, 1.0))
    theta_out[...] = tall
    per_side = padded(cap) // LANES
    for k in range(2):
        slots = send_list[pl.ds(2 * k + lax.axis_index("dest") % 2, 1), :]
        there = look_up(tall, jnp.where(slots >= 0, slots % nodes, 0))
        put_row(slot_theta, k * per_side, there, 0.0)


def keep_kernel(
    sizes, theta_ref, node_in, node_out, fraction, sent_ref, arrived_ref, keep, home_theta
):
    cells, nodes, branches, cap, sub = sizes
    height = cells // LANES
    region_no = lax.axis_index("region")
    theta = strung(theta_ref[...])
    cell_theta = jnp.zeros((height, LANES), F32)
    into = jnp.zeros((height, LANES), F32)
    for j in range(branches):
        home = home_cells(node_out[j : j + 1, :], region_no, cells)
        cell_theta = cell_theta + scatter(node_in[j : j + 1, :], theta, height)
        into = into + scatter(home, theta, height)
    keep[...] = 1.0 - cell_theta * fraction[...]
    home_theta[...] = into


def home_kernel(sizes, source, outlet, turns, flow, after_ref, home):
    cells, nodes, branches, cap, sub = sizes
    batch = 16

    def body(step, carry):
        first = step * batch
        values = []
        for i in range(batch):
            node = source[first + i]
            choice = row_of(turns, node, sub)[...]
            moved = row_of(flow, node, sub)[...]
            values.append(jnp.where(choice == outlet[first + i], moved, 0.0))
        for i in range(batch):
            row_of(home, first + i, sub)[...] = values[i]
        return carry

    lax.fori_loop(0, cells // batch, body, 0)


def base_kernel(sizes, keep, home_theta, rows, home, base):
    cells, nodes, branches, cap, sub = sizes
    batch = 16

    def body(step, carry):
        first = step * batch
        values = []
        for i in range(batch):
            cell = first + i
            kept = row_of(rows, cell, sub)[...] * keep[cell]
            values.append(kept + row_of(home, cell, sub)[...] * home_theta[cell])
        for i in range(batch):
            row_of(base, first + i, sub)[...] = values[i]
        return carry

    lax.fori_loop(0, cells // batch, body, 0)


def land_rows(sizes, parts, scale, land, received, base):
    cells, nodes, branches, cap, sub = sizes
    batch = 16
    core = lax.axis_index("dest") % 2
    for (side, start, count), rows in zip(parts, received):
        offset = jnp.where(core == side % 2, 0, 2 * padded(cap)) + side // 2 * padded(cap)
        offset = offset + start

        def body(step, carry, side=side, start=start, rows=rows, offset=offset):
            first = step * batch
            stores = []
            for i in range(batch):
                at = row_of(base, land[side * padded(cap) + start + first + i], sub)
                value = row_of(rows, first + i, sub)[...]
                if scale is not None:
                    value = value * scale[offset + first + i]
                stores.append((at, at[...] + value))
            for at, value in stores:
                at[...] = value
            return carry

        lax.fori_loop(0, count // batch, body, 0)


def land_kernel(sizes, parts, scale, land, *rest):
    received, (base_in, base) = rest[: len(parts)], rest[len(parts) :]
    land_rows(sizes, parts, scale, land, received, base)


def finish_kernel(sizes, parts, chunk, land, *rest):
    cells, nodes, branches, cap, sub = sizes
    received, (base_in, out, base, staged, sems) = rest[: len(parts)], rest[len(parts) :]
    land_rows(sizes, parts, None, land, received, base)
    copies = []
    for number in range(cells // chunk):

        def body(step, carry, number=number):
            for half in range(2):
                first = number * chunk + step * 16 + half * 8
                for q in range(sub):
                    staged[
                        pl.ds(pl.multiple_of(first, 8), 8), q * LANES : (q + 1) * LANES
                    ] = base[pl.ds(first * sub + q, 8, stride=sub), :]
            return carry

        lax.fori_loop(0, chunk // 16, body, 0)
        at = pl.ds(number * chunk, chunk)
        copies.append(
            pltpu.make_async_copy(staged.at[at, :], out.at[at, :], sems.at[number])
        )
        copies[-1].start()
    for copy in copies:
        copy.wait()


def on_device(occupancy, capacity, jam, wave, node_in, node_out, send_list, recv_list, turn):
    cells, width = occupancy.shape
    branches, nodes = node_in.shape
    cap = send_list.shape[1]
    sub = width // LANES
    sizes = (cells, nodes, branches, cap, sub)
    regions = lax.axis_size("region")
    commodities = width * lax.axis_size("dest")
    height = cells // LANES
    per_cell = (height, LANES)
    list_shape = (4 * padded(cap) // LANES, LANES)
    chunk = 128
    row_bytes = width * 4
    occupancy = pltpu.with_memory_space_constraint(occupancy, pltpu.HBM)
    turn = pltpu.with_memory_space_constraint(turn, pltpu.HBM)

    local_sum, rows = pl.pallas_call(
        functools.partial(cell_sum_kernel, chunk, sub),
        in_specs=[ANYWHERE],
        out_specs=[VMEM_WHOLE] * 2,
        out_shape=[
            jax.ShapeDtypeStruct(per_cell, F32),
            pltpu.VMEM(((cells + 1) * sub, LANES), F32),
        ],
        scratch_shapes=[
            pltpu.VMEM((cells, width), F32),
            pltpu.VMEM((cells, LANES), F32),
            pltpu.SemaphoreType.DMA((cells // chunk,)),
        ],
        compiler_params=params(14),
        cost_estimate=cost(cells * width, cells * row_bytes),
        name="cell_sum",
    )(occupancy)

    sums = partners(local_sum, "dest")

    turns, *lists = pl.pallas_call(
        functools.partial(turn_rows_kernel, sizes, chunk),
        in_specs=[ANYWHERE] * 2 + [VMEM_WHOLE] * 4,
        out_specs=[VMEM_WHOLE] * 7,
        out_shape=[
            pltpu.VMEM((nodes * sub, LANES), I32),
            jax.ShapeDtypeStruct((branches * nodes // LANES, LANES), I32),
        ]
        + [jax.ShapeDtypeStruct(list_shape, I32)] * 3
        + [jax.ShapeDtypeStruct(per_cell, I32)] * 2,
        scratch_shapes=[
            pltpu.VMEM((nodes, width), I32),
            pltpu.SemaphoreType.DMA((nodes // chunk,)),
        ],
        compiler_params=params(8),
        cost_estimate=cost(0, nodes * row_bytes),
        name="turn_rows",
    )(turn, local_sum, node_in, node_out, send_list, recv_list)
    in_cell, send_node, send_outlet, land, source_node, source_outlet = (
        x.reshape(-1) for x in lists
    )

    turns, *sums = lax.optimization_barrier((turns, *sums))
    vehicles = tree_sum(sums) / commodities
    cap_of = capacity.reshape(per_cell)
    fraction = jnp.minimum(vehicles, cap_of) / vehicles
    supply = jnp.minimum(cap_of, wave.reshape(per_cell) * (jam.reshape(per_cell) - vehicles))
    rows_shape = pltpu.VMEM(((cells + 1) * sub, LANES), F32)
    early = cap // 2 // 16 * 16
    parts = (*((side, 0, cap) for side in range(3)), (3, 0, early))
    last_part = (3, early, cap - early)

    def send_shape(part):
        return pltpu.VMEM((part[2] * sub, LANES), F32)


    supply_there = to_neighbours(supply)
    weights = jnp.concatenate([fraction.reshape(-1), jnp.zeros((LANES,), F32)])
    (ahead,) = pl.pallas_call(
        functools.partial(send_kernel, sizes, parts[2:3]),
        in_specs=[SMEM_WHOLE] * 4 + [VMEM_WHOLE] * 2,
        out_specs=[VMEM_WHOLE],
        out_shape=[send_shape(parts[2])],
        compiler_params=params(4),
        cost_estimate=cost(1, 1),
        name="send_ahead",
    )(weights, in_cell, send_node, send_outlet, rows, turns)
    scaled = pl.pallas_call(
        functools.partial(scale_kernel, sizes),
        in_specs=[SMEM_WHOLE, VMEM_WHOLE, ANYWHERE, ANYWHERE],
        out_specs=VMEM_WHOLE,
        out_shape=rows_shape,
        compiler_params=params(4),
        cost_estimate=cost(10000000000, 1),
        name="scale_rows",
    )(fraction.reshape(-1), rows, ahead, supply_there)
    near = pl.pallas_call(
        functools.partial(send_kernel, sizes, (*parts[:2], parts[3]), None),
        in_specs=[SMEM_WHOLE] * 3 + [VMEM_WHOLE] * 2,
        out_specs=[VMEM_WHOLE] * 3,
        out_shape=[send_shape(part) for part in (*parts[:2], parts[3])],
        compiler_params=params(4),
        cost_estimate=cost(1, 1),
        name="send_near",
    )(in_cell, send_node, send_outlet, scaled, turns)
    arrived = [
        shifted(send, "region", SHIFTS[side]) for side, send in enumerate([*near[:2], ahead, near[2]])
    ]

    flow, demand = pl.pallas_call(
        functools.partial(node_flow_kernel, sizes),
        in_specs=[SMEM_WHOLE] + [VMEM_WHOLE] * 2 + [ANYWHERE],
        out_specs=[VMEM_WHOLE] * 2,
        out_shape=[
            pltpu.VMEM((nodes * sub, LANES), F32),
            jax.ShapeDtypeStruct((branches * nodes // LANES, LANES), F32),
        ],
        scratch_shapes=[pltpu.VMEM((branches, nodes, LANES), F32)],
        compiler_params=params(8),
        cost_estimate=cost(1, 1),
        name="node_flow",
    )(in_cell, scaled, turns, near[0])

    joined = jnp.concatenate([demand, supply_there])
    shared = lax.all_gather(joined, "dest", axis=0, tiled=True)
    theta, slot_theta = pl.pallas_call(
        functools.partial(theta_kernel, sizes, regions, commodities),
        in_specs=[VMEM_WHOLE] * 4,
        out_specs=[VMEM_WHOLE] * 2,
        out_shape=[
            jax.ShapeDtypeStruct((nodes // LANES, LANES), F32),
            jax.ShapeDtypeStruct((2 * padded(cap) // LANES, LANES), F32),
        ],
        compiler_params=params(8),
        cost_estimate=cost(1, 1),
        name="theta",
    )(supply, shared, node_out, send_list)
    theta, slot_theta, arrived[2] = lax.optimization_barrier((theta, slot_theta, arrived[2]))
    per_side = padded(cap) // LANES
    theta_there = [to_two(slot_theta[:per_side], 0), to_two(slot_theta[per_side:], 2)]

    (behind,) = pl.pallas_call(
        functools.partial(scaled_send_kernel, sizes, last_part),
        in_specs=[SMEM_WHOLE] * 3 + [VMEM_WHOLE] * 2,
        out_specs=[VMEM_WHOLE],
        out_shape=[send_shape(last_part)],
        compiler_params=params(4),
        cost_estimate=cost(1, 1),
        name="send_scaled",
    )(theta.reshape(-1), send_node, send_outlet, flow, turns)
    behind, arrived[3] = lax.optimization_barrier((behind, arrived[3]))
    last = shifted(behind, "region", SHIFTS[3])
    home = pl.pallas_call(
        functools.partial(home_kernel, sizes),
        in_specs=[SMEM_WHOLE] * 2 + [VMEM_WHOLE] * 2 + [ANYWHERE],
        out_specs=VMEM_WHOLE,
        out_shape=rows_shape,
        compiler_params=params(4),
        cost_estimate=cost(2000000000, 1),
        name="home_rows",
    )(source_node, source_outlet, turns, flow, behind)
    keep, home_theta = pl.pallas_call(
        functools.partial(keep_kernel, sizes),
        in_specs=[VMEM_WHOLE] * 4 + [ANYWHERE] * 2,
        out_specs=[VMEM_WHOLE] * 2,
        out_shape=[jax.ShapeDtypeStruct(per_cell, F32)] * 2,
        compiler_params=params(8),
        cost_estimate=cost(10000000, 1),
        name="keep",
    )(theta, node_in, node_out, fraction, behind, arrived[2])
    base = pl.pallas_call(
        functools.partial(base_kernel, sizes),
        in_specs=[SMEM_WHOLE] * 2 + [VMEM_WHOLE] * 2,
        out_specs=VMEM_WHOLE,
        out_shape=rows_shape,
        compiler_params=params(4),
        cost_estimate=cost(10000000, 1),
        name="base_rows",
    )(keep.reshape(-1), home_theta.reshape(-1), rows, home)

    base, *rest = lax.optimization_barrier((base, *theta_there, *arrived))
    theta_there, arrived = rest[:2], rest[2:]
    got = jnp.concatenate(theta_there)
    members = lax.axis_size("dest")
    other = lax.ppermute(got, "dest", [(i, i ^ 1) for i in range(members)])
    scale = jnp.concatenate([got, other])

    base = pl.pallas_call(
        functools.partial(land_kernel, sizes, parts),
        in_specs=[SMEM_WHOLE] * 2 + [VMEM_WHOLE] * 5,
        out_specs=VMEM_WHOLE,
        out_shape=rows_shape,
        input_output_aliases={6: 0},
        compiler_params=params(4),
        cost_estimate=cost(2000000000, 1),
        name="land_first",
    )(scale.reshape(-1), land, *arrived, base)

    out, _ = pl.pallas_call(
        functools.partial(finish_kernel, sizes, (last_part,), chunk),
        in_specs=[SMEM_WHOLE] + [VMEM_WHOLE] * 2,
        out_specs=[ANYWHERE, VMEM_WHOLE],
        out_shape=[jax.ShapeDtypeStruct((cells, width), F32), rows_shape],
        scratch_shapes=[
            pltpu.VMEM((cells, width), F32),
            pltpu.SemaphoreType.DMA((cells // chunk,)),
        ],
        input_output_aliases={2: 1},
        compiler_params=params(12),
        cost_estimate=cost(cells * width, cells * row_bytes),
        name="finish",
    )(land, last, base)
    return out


def solution(mesh):
    return jax.shard_map(
        on_device,
        mesh=mesh,
        in_specs=(
            P("region", "dest"),
            P("region"),
            P("region"),
            P("region"),
            P(None, "region"),
            P(None, "region"),
            P("region", None),
            P("region", None),
            P("region", "dest"),
        ),
        out_specs=P("region", "dest"),
        check_vma=False,
    )
```

```python
import functools

import jax
import jax.numpy as jnp
from jax import lax
from jax.experimental import pallas as pl
from jax.experimental.pallas import tpu as pltpu
from jax.sharding import PartitionSpec as P

SHIFTS = (1, -1, 2, -2)
AHEAD = 2
LANES = 128
MIB = 1 << 20
F32 = jnp.float32
I32 = jnp.int32
VMEM_WHOLE = pl.BlockSpec(memory_space=pltpu.VMEM)
SMEM_WHOLE = pl.BlockSpec(memory_space=pltpu.SMEM)
ANYWHERE = pl.BlockSpec(memory_space=pl.ANY)


def to_neighbours(block):
    regions, members = lax.axis_size("region"), lax.axis_size("dest")
    route = [
        (r * members + d, (r + SHIFTS[d % 4]) % regions * members + d)
        for r in range(regions)
        for d in range(members)
    ]
    return lax.ppermute(block, ("region", "dest"), route)


def to_two(block, first):
    regions, members = lax.axis_size("region"), lax.axis_size("dest")
    route = [
        (r * members + d, (r + SHIFTS[first + d % 2]) % regions * members + d)
        for r in range(regions)
        for d in range(members)
    ]
    return lax.ppermute(block, ("region", "dest"), route)


def shifted(block, axis, distance):
    devices = range(lax.axis_size(axis))
    route = [((i - distance) % len(devices), i) for i in devices]
    return lax.ppermute(block, axis, route)


def partners(block, axis):
    count = lax.axis_size(axis)
    return [block] + [
        lax.ppermute(block, axis, [(i, i ^ other) for i in range(count)])
        for other in range(1, count)
    ]


def tree_sum(parts):
    while len(parts) > 1:
        parts = [parts[k] + parts[k + 1] for k in range(0, len(parts), 2)]
    return parts[0]


def params(mib):
    return pltpu.CompilerParams(vmem_limit_bytes=mib * MIB)


def cost(flops, moved):
    return pl.CostEstimate(flops=flops, bytes_accessed=moved, transcendentals=0)


def lane_sums(partial):
    count = partial.shape[0]
    parts = jnp.dot(
        in_parts(partial), jnp.ones((LANES, LANES), jnp.bfloat16), preferred_element_type=F32
    )
    sums = parts[:count, :] + parts[count : 2 * count, :] + parts[2 * count :, :]
    row = lax.broadcasted_iota(I32, (LANES, LANES), 0)
    lane = lax.broadcasted_iota(I32, (LANES, LANES), 1)
    pieces = [
        jnp.sum(jnp.where(row == lane, sums[k : k + LANES, :], 0.0), axis=0, keepdims=True)
        for k in range(0, partial.shape[0], LANES)
    ]
    return jnp.concatenate(pieces, axis=0)


def stacked(row):
    return jnp.concatenate(
        [row[:, k : k + LANES] for k in range(0, row.shape[1], LANES)], axis=0
    )


def strung(rows):
    return jnp.concatenate([rows[k : k + 1, :] for k in range(rows.shape[0])], axis=1)


def row_of(ref, number, sub):
    if sub % 8 == 0:
        return ref.reshape(ref.shape[0] // sub, sub, LANES).at[number]
    return ref.at[pl.ds(pl.multiple_of(number * sub, sub), sub), :]


def padded(cap):
    return -(-cap // LANES) * LANES


def put_row(ref, row, value, fill):
    width = value.shape[1]
    for q in range(-(-width // LANES)):
        piece = value[:, q * LANES : min((q + 1) * LANES, width)]
        lack = LANES - piece.shape[1]
        if lack:
            piece = jnp.concatenate([piece, jnp.full((1, lack), fill, piece.dtype)], axis=1)
        ref[row + q : row + q + 1, :] = piece


def one_hot(index, count):
    rows = lax.broadcasted_iota(I32, (count, index.shape[1]), 0)
    return jnp.where(rows == index, 1.0, 0.0)


def in_parts(x):
    high = x.astype(jnp.bfloat16)
    rest = x - high.astype(F32)
    middle = rest.astype(jnp.bfloat16)
    low = (rest - middle.astype(F32)).astype(jnp.bfloat16)
    return jnp.concatenate([high, middle, low], axis=0)


def selected(values, choice, dims):
    count = values.shape[0]
    product = lax.dot_general(
        in_parts(values), choice.astype(jnp.bfloat16), (dims, ((), ())),
        preferred_element_type=F32,
    )
    return product[:count, :] + product[count : 2 * count, :] + product[2 * count :, :]


def look_up(table, index):
    picked = selected(table.T, one_hot(index // LANES, table.shape[0]), ((1,), (0,)))
    return jnp.sum(picked * one_hot(index % LANES, LANES), axis=0, keepdims=True)


def scatter(index, values, height):
    high = jnp.where(index >= 0, index // LANES, -1)
    low = jnp.where(index >= 0, index % LANES, -1)
    return selected(one_hot(high, height) * values, one_hot(low, LANES), ((1,), (1,)))


def home_cells(node_out, region_no, cells):
    here = (node_out >= 0) & (node_out // cells == region_no)
    return jnp.where(here, node_out % cells, -1)


def rows_of_group(x_ref, rows_ref, first, sub):
    total = None
    for q in range(sub):
        piece = x_ref[pl.ds(pl.multiple_of(first, 8), 8), q * LANES : (q + 1) * LANES]
        rows_ref[pl.ds(first * sub + q, 8, stride=sub), :] = piece
        total = piece if total is None else total + piece
    return total


def copies_in(source, target, sems, chunk):
    copies = [
        pltpu.make_async_copy(
            source.at[pl.ds(i * chunk, chunk), :], target.at[pl.ds(i * chunk, chunk), :], sems.at[i]
        )
        for i in range(target.shape[0] // chunk)
    ]
    for copy in copies:
        copy.start()
    return copies


def make_lists(
    sizes, node_in, node_out, send_list, recv_list,
    in_cell, send_node, send_outlet, land, ahead, source_node, source_outlet,
):
    cells, nodes, branches, cap, sub = sizes
    height = cells // LANES
    region_no = lax.axis_index("region")
    ids = lax.broadcasted_iota(I32, (1, nodes), 1).astype(F32) + 1.0
    number = jnp.zeros((height, LANES), F32)
    slot = jnp.zeros((height, LANES), F32)
    for j in range(branches):
        ins = node_in[j : j + 1, :]
        put_row(in_cell, j * (nodes // LANES), jnp.where(ins >= 0, ins, cells), cells)
        home = home_cells(node_out[j : j + 1, :], region_no, cells)
        here = scatter(home, ids, height)
        number = number + here
        slot = slot + jnp.where(here > 0.0, j + 1.0, 0.0)
    source_node[...] = jnp.maximum(number.astype(I32) - 1, 0)
    source_outlet[...] = slot.astype(I32) - 1
    per_side = padded(cap) // LANES
    for side in range(4):
        slots = send_list[side : side + 1, :]
        lands = recv_list[side : side + 1, :]
        node = jnp.where(slots >= 0, slots % nodes, 0)
        outlet = jnp.where(slots >= 0, slots // nodes, -1)
        put_row(send_node, side * per_side, node, 0)
        put_row(send_outlet, side * per_side, outlet, -1)
        put_row(land, side * per_side, jnp.where(lands >= 0, lands, cells), cells)
        if side == AHEAD:
            for j in range(branches):
                ins = node_in[j : j + 1, :]
                table = stacked(jnp.where(ins >= 0, ins, cells)).astype(F32)
                put_row(ahead, j * per_side, (look_up(table, node) + 0.5).astype(I32), cells)
            put_row(ahead, branches * per_side, node, 0)
            put_row(ahead, (branches + 1) * per_side, outlet, -1)


def cell_sum_kernel(chunk, sub, x_hbm, sum_ref, rows_ref, x, partial, sems):
    copies = copies_in(x_hbm, x, sems, chunk)
    zeros = rows_ref.shape[0] - sub
    rows_ref[zeros:, :] = jnp.zeros((sub, LANES), F32)
    for number, copy in enumerate(copies):
        copy.wait()

        def body(step, carry, number=number):
            for half in range(2):
                first = number * chunk + step * 16 + half * 8
                total = rows_of_group(x, rows_ref, first, sub)
                partial[pl.ds(pl.multiple_of(first, 8), 8), :] = total
            return carry

        lax.fori_loop(0, chunk // 16, body, 0)
    sum_ref[...] = lane_sums(partial[...])


def turn_rows_kernel(sizes, chunk, x_hbm, after_ref, *rest):
    cells, nodes, branches, cap, sub = sizes
    lists, rows_ref, made, (x, sems) = rest[:4], rest[4], rest[5:12], rest[12:]
    copies = copies_in(x_hbm, x, sems, chunk)
    make_lists(sizes, *lists, *made)
    for number, copy in enumerate(copies):
        copy.wait()

        def body(step, carry, number=number):
            for half in range(2):
                rows_of_group(x, rows_ref, number * chunk + step * 16 + half * 8, sub)
            return carry

        lax.fori_loop(0, chunk // 16, body, 0)


def gathered_flow(node, in_cell, scaled, sizes):
    cells, nodes, branches, cap, sub = sizes
    return tree_sum(
        [row_of(scaled, in_cell[i * nodes + node], sub)[...] for i in range(branches)]
    )


def send_ahead_kernel(sizes, fraction, slots, rows, turns, send):
    cells, nodes, branches, cap, sub = sizes
    batch = 16

    def body(step, carry):
        first = step * batch
        values = []
        for i in range(batch):
            slot = first + i
            parts = []
            for j in range(branches):
                cell = slots[j * padded(cap) + slot]
                parts.append(row_of(rows, cell, sub)[...] * fraction[cell])
            node = slots[branches * padded(cap) + slot]
            choice = row_of(turns, node, sub)[...]
            outlet = slots[(branches + 1) * padded(cap) + slot]
            values.append(jnp.where(choice == outlet, tree_sum(parts), 0.0))
        for i in range(batch):
            row_of(send, first + i, sub)[...] = values[i]
        return carry

    lax.fori_loop(0, cap // batch, body, 0)


def scale_kernel(sizes, fraction, rows, sent_ref, supply_ref, scaled):
    cells, nodes, branches, cap, sub = sizes

    def body(step, carry):
        first = step * 16
        values = [
            row_of(rows, first + i, sub)[...] * fraction[first + i] for i in range(16)
        ]
        for i in range(16):
            row_of(scaled, first + i, sub)[...] = values[i]
        return carry

    lax.fori_loop(0, cells // 16, body, 0)
    row_of(scaled, cells, sub)[...] = jnp.zeros((sub, LANES), F32)


def send_kernel(sizes, sides, in_cell, send_node, send_outlet, scaled, turns, *sends):
    cells, nodes, branches, cap, sub = sizes
    batch = 16
    for side, send in zip(sides, sends):

        def body(step, carry, side=side, send=send):
            first = step * batch
            values = []
            for i in range(batch):
                slot = side * padded(cap) + first + i
                node = send_node[slot]
                value = gathered_flow(node, in_cell, scaled, sizes)
                choice = row_of(turns, node, sub)[...]
                values.append(jnp.where(choice == send_outlet[slot], value, 0.0))
            for i in range(batch):
                row_of(send, first + i, sub)[...] = values[i]
            return carry

        lax.fori_loop(0, cap // batch, body, 0)


def scaled_send_kernel(sizes, side, theta, send_node, send_outlet, flow, turns, send):
    cells, nodes, branches, cap, sub = sizes
    batch = 16

    def body(step, carry):
        first = step * batch
        values = []
        for i in range(batch):
            slot = side * padded(cap) + first + i
            node = send_node[slot]
            value = row_of(flow, node, sub)[...] * theta[node]
            choice = row_of(turns, node, sub)[...]
            values.append(jnp.where(choice == send_outlet[slot], value, 0.0))
        for i in range(batch):
            row_of(send, first + i, sub)[...] = values[i]
        return carry

    lax.fori_loop(0, cap // batch, body, 0)


def node_flow_kernel(sizes, in_cell, scaled, turns, after_ref, flow, demand, partial):
    cells, nodes, branches, cap, sub = sizes

    def gather(step, carry):
        first = step * 16
        values = [
            gathered_flow(first + i, in_cell, scaled, sizes) for i in range(16)
        ]
        for i in range(16):
            row_of(flow, first + i, sub)[...] = values[i]
        return carry

    def measure(step, carry):
        for half in range(2):
            first = step * 16 + half * 8
            totals = [jnp.zeros((8, LANES), F32)] * branches
            for q in range(sub):
                at = pl.ds(first * sub + q, 8, stride=sub)
                value = flow[at, :]
                choice = turns[at, :]
                totals = [
                    total + jnp.where(choice == j, value, 0.0) for j, total in enumerate(totals)
                ]
            for j in range(branches):
                partial[j, pl.ds(pl.multiple_of(first, 8), 8), :] = totals[j]
        return carry

    lax.fori_loop(0, nodes // 16, gather, 0)
    lax.fori_loop(0, nodes // 16, measure, 0)
    per_outlet = nodes // LANES
    for j in range(branches):
        demand[j * per_outlet : (j + 1) * per_outlet, :] = lane_sums(partial[j])


def theta_kernel(
    sizes, regions, commodities, supply, shared, node_out, send_list, theta_out, slot_theta
):
    cells, nodes, branches, cap, sub = sizes
    per_outlet = nodes // LANES
    height = cells // LANES
    block = branches * per_outlet + height
    region_no = lax.axis_index("region")
    members = shared.shape[0] // block
    parts = [
        shared[d * block : d * block + branches * per_outlet, :] for d in range(members)
    ]
    demand = tree_sum(parts) * (1.0 / commodities)
    table = jnp.concatenate(
        [supply[...]]
        + [
            shared[d * block + branches * per_outlet : (d + 1) * block, :] for d in range(4)
        ],
        axis=0,
    )
    tall = jnp.ones((per_outlet, LANES), F32)
    for j in range(branches):
        outs = node_out[j : j + 1, :]
        cell = jnp.maximum(outs, 0)
        offset = (cell // cells + regions - region_no) % regions
        sector = jnp.zeros_like(offset)
        for d in range(4):
            sector = jnp.where(offset == (-SHIFTS[d]) % regions, d + 1, sector)
        room = stacked(look_up(table, sector * cells + cell % cells))
        ratio = room / jnp.maximum(demand[j * per_outlet : (j + 1) * per_outlet, :], room)
        tall = jnp.minimum(tall, jnp.where(stacked(outs) >= 0, ratio, 1.0))
    theta_out[...] = tall
    per_side = padded(cap) // LANES
    for k in range(2):
        slots = send_list[pl.ds(2 * k + lax.axis_index("dest") % 2, 1), :]
        there = look_up(tall, jnp.where(slots >= 0, slots % nodes, 0))
        put_row(slot_theta, k * per_side, there, 0.0)


def keep_kernel(
    sizes, theta_ref, node_in, node_out, fraction, sent_ref, arrived_ref, keep, home_theta
):
    cells, nodes, branches, cap, sub = sizes
    height = cells // LANES
    region_no = lax.axis_index("region")
    theta = strung(theta_ref[...])
    cell_theta = jnp.zeros((height, LANES), F32)
    into = jnp.zeros((height, LANES), F32)
    for j in range(branches):
        home = home_cells(node_out[j : j + 1, :], region_no, cells)
        cell_theta = cell_theta + scatter(node_in[j : j + 1, :], theta, height)
        into = into + scatter(home, theta, height)
    keep[...] = 1.0 - cell_theta * fraction[...]
    home_theta[...] = into


def home_kernel(sizes, source, outlet, turns, flow, after_ref, home):
    cells, nodes, branches, cap, sub = sizes
    batch = 16

    def body(step, carry):
        first = step * batch
        values = []
        for i in range(batch):
            node = source[first + i]
            choice = row_of(turns, node, sub)[...]
            moved = row_of(flow, node, sub)[...]
            values.append(jnp.where(choice == outlet[first + i], moved, 0.0))
        for i in range(batch):
            row_of(home, first + i, sub)[...] = values[i]
        return carry

    lax.fori_loop(0, cells // batch, body, 0)


def base_kernel(sizes, keep, home_theta, rows, home, base):
    cells, nodes, branches, cap, sub = sizes
    batch = 16

    def body(step, carry):
        first = step * batch
        values = []
        for i in range(batch):
            cell = first + i
            kept = row_of(rows, cell, sub)[...] * keep[cell]
            values.append(kept + row_of(home, cell, sub)[...] * home_theta[cell])
        for i in range(batch):
            row_of(base, first + i, sub)[...] = values[i]
        return carry

    lax.fori_loop(0, cells // batch, body, 0)


def land_rows(sizes, sides, scale, land, received, base):
    cells, nodes, branches, cap, sub = sizes
    batch = 16
    core = lax.axis_index("dest") % 2
    for side, rows in zip(sides, received):
        offset = jnp.where(core == side % 2, 0, 2 * padded(cap)) + side // 2 * padded(cap)

        def body(step, carry, side=side, rows=rows, offset=offset):
            first = step * batch
            stores = []
            for i in range(batch):
                at = row_of(base, land[side * padded(cap) + first + i], sub)
                value = row_of(rows, first + i, sub)[...]
                if scale is not None:
                    value = value * scale[offset + first + i]
                stores.append((at, at[...] + value))
            for at, value in stores:
                at[...] = value
            return carry

        lax.fori_loop(0, cap // batch, body, 0)


def land_kernel(sizes, sides, scale, land, *rest):
    received, (base_in, base) = rest[: len(sides)], rest[len(sides) :]
    land_rows(sizes, sides, scale, land, received, base)


def finish_kernel(sizes, sides, chunk, land, *rest):
    cells, nodes, branches, cap, sub = sizes
    received, (base_in, out, base, staged, sems) = rest[: len(sides)], rest[len(sides) :]
    land_rows(sizes, sides, None, land, received, base)
    copies = []
    for number in range(cells // chunk):

        def body(step, carry, number=number):
            for half in range(2):
                first = number * chunk + step * 16 + half * 8
                for q in range(sub):
                    staged[
                        pl.ds(pl.multiple_of(first, 8), 8), q * LANES : (q + 1) * LANES
                    ] = base[pl.ds(first * sub + q, 8, stride=sub), :]
            return carry

        lax.fori_loop(0, chunk // 16, body, 0)
        at = pl.ds(number * chunk, chunk)
        copies.append(
            pltpu.make_async_copy(staged.at[at, :], out.at[at, :], sems.at[number])
        )
        copies[-1].start()
    for copy in copies:
        copy.wait()


def on_device(occupancy, capacity, jam, wave, node_in, node_out, send_list, recv_list, turn):
    cells, width = occupancy.shape
    branches, nodes = node_in.shape
    cap = send_list.shape[1]
    sub = width // LANES
    sizes = (cells, nodes, branches, cap, sub)
    regions = lax.axis_size("region")
    commodities = width * lax.axis_size("dest")
    height = cells // LANES
    per_cell = (height, LANES)
    list_shape = (4 * padded(cap) // LANES, LANES)
    ahead_rows = -(-(branches + 2) * padded(cap) // LANES // 8) * 8
    chunk = 128
    row_bytes = width * 4
    occupancy = pltpu.with_memory_space_constraint(occupancy, pltpu.HBM)
    turn = pltpu.with_memory_space_constraint(turn, pltpu.HBM)

    local_sum, rows = pl.pallas_call(
        functools.partial(cell_sum_kernel, chunk, sub),
        in_specs=[ANYWHERE],
        out_specs=[VMEM_WHOLE] * 2,
        out_shape=[
            jax.ShapeDtypeStruct(per_cell, F32),
            pltpu.VMEM(((cells + 1) * sub, LANES), F32),
        ],
        scratch_shapes=[
            pltpu.VMEM((cells, width), F32),
            pltpu.VMEM((cells, LANES), F32),
            pltpu.SemaphoreType.DMA((cells // chunk,)),
        ],
        compiler_params=params(14),
        cost_estimate=cost(cells * width, cells * row_bytes),
        name="cell_sum",
    )(occupancy)

    sums = partners(local_sum, "dest")

    turns, *lists = pl.pallas_call(
        functools.partial(turn_rows_kernel, sizes, chunk),
        in_specs=[ANYWHERE] * 2 + [VMEM_WHOLE] * 4,
        out_specs=[VMEM_WHOLE] * 8,
        out_shape=[
            pltpu.VMEM((nodes * sub, LANES), I32),
            jax.ShapeDtypeStruct((branches * nodes // LANES, LANES), I32),
        ]
        + [jax.ShapeDtypeStruct(list_shape, I32)] * 3
        + [jax.ShapeDtypeStruct((ahead_rows, LANES), I32)]
        + [jax.ShapeDtypeStruct(per_cell, I32)] * 2,
        scratch_shapes=[
            pltpu.VMEM((nodes, width), I32),
            pltpu.SemaphoreType.DMA((nodes // chunk,)),
        ],
        compiler_params=params(8),
        cost_estimate=cost(0, nodes * row_bytes),
        name="turn_rows",
    )(turn, local_sum, node_in, node_out, send_list, recv_list)
    in_cell, send_node, send_outlet, land, ahead_list, source_node, source_outlet = (
        x.reshape(-1) for x in lists
    )

    turns, *sums = lax.optimization_barrier((turns, *sums))
    vehicles = tree_sum(sums) / commodities
    cap_of = capacity.reshape(per_cell)
    fraction = jnp.minimum(vehicles, cap_of) / vehicles
    supply = jnp.minimum(cap_of, wave.reshape(per_cell) * (jam.reshape(per_cell) - vehicles))
    rows_shape = pltpu.VMEM(((cells + 1) * sub, LANES), F32)
    send_shape = pltpu.VMEM((cap * sub, LANES), F32)

    supply_there = to_neighbours(supply)
    weights = jnp.concatenate([fraction.reshape(-1), jnp.zeros((LANES,), F32)])
    (ahead,) = pl.pallas_call(
        functools.partial(send_ahead_kernel, sizes),
        in_specs=[SMEM_WHOLE] * 2 + [VMEM_WHOLE] * 2,
        out_specs=[VMEM_WHOLE],
        out_shape=[send_shape],
        compiler_params=params(4),
        cost_estimate=cost(1, 1),
        name="send_ahead",
    )(weights, ahead_list, rows, turns)
    scaled = pl.pallas_call(
        functools.partial(scale_kernel, sizes),
        in_specs=[SMEM_WHOLE, VMEM_WHOLE, ANYWHERE, ANYWHERE],
        out_specs=VMEM_WHOLE,
        out_shape=rows_shape,
        compiler_params=params(4),
        cost_estimate=cost(10000000000, 1),
        name="scale_rows",
    )(fraction.reshape(-1), rows, ahead, supply_there)
    near = pl.pallas_call(
        functools.partial(send_kernel, sizes, (0, 1)),
        in_specs=[SMEM_WHOLE] * 3 + [VMEM_WHOLE] * 2,
        out_specs=[VMEM_WHOLE] * 2,
        out_shape=[send_shape] * 2,
        compiler_params=params(4),
        cost_estimate=cost(1, 1),
        name="send_near",
    )(in_cell, send_node, send_outlet, scaled, turns)
    arrived = [
        shifted(send, "region", SHIFTS[side]) for side, send in enumerate([*near, ahead])
    ]

    flow, demand = pl.pallas_call(
        functools.partial(node_flow_kernel, sizes),
        in_specs=[SMEM_WHOLE] + [VMEM_WHOLE] * 2 + [ANYWHERE],
        out_specs=[VMEM_WHOLE] * 2,
        out_shape=[
            pltpu.VMEM((nodes * sub, LANES), F32),
            jax.ShapeDtypeStruct((branches * nodes // LANES, LANES), F32),
        ],
        scratch_shapes=[pltpu.VMEM((branches, nodes, LANES), F32)],
        compiler_params=params(8),
        cost_estimate=cost(1, 1),
        name="node_flow",
    )(in_cell, scaled, turns, near[0])

    joined = jnp.concatenate([demand, supply_there])
    shared = lax.all_gather(joined, "dest", axis=0, tiled=True)
    theta, slot_theta = pl.pallas_call(
        functools.partial(theta_kernel, sizes, regions, commodities),
        in_specs=[VMEM_WHOLE] * 4,
        out_specs=[VMEM_WHOLE] * 2,
        out_shape=[
            jax.ShapeDtypeStruct((nodes // LANES, LANES), F32),
            jax.ShapeDtypeStruct((2 * padded(cap) // LANES, LANES), F32),
        ],
        compiler_params=params(8),
        cost_estimate=cost(1, 1),
        name="theta",
    )(supply, shared, node_out, send_list)
    theta, slot_theta, arrived[2] = lax.optimization_barrier((theta, slot_theta, arrived[2]))
    per_side = padded(cap) // LANES
    theta_there = [to_two(slot_theta[:per_side], 0), to_two(slot_theta[per_side:], 2)]

    (behind,) = pl.pallas_call(
        functools.partial(scaled_send_kernel, sizes, 3),
        in_specs=[SMEM_WHOLE] * 3 + [VMEM_WHOLE] * 2,
        out_specs=[VMEM_WHOLE],
        out_shape=[send_shape],
        compiler_params=params(4),
        cost_estimate=cost(1, 1),
        name="send_scaled",
    )(theta.reshape(-1), send_node, send_outlet, flow, turns)
    home = pl.pallas_call(
        functools.partial(home_kernel, sizes),
        in_specs=[SMEM_WHOLE] * 2 + [VMEM_WHOLE] * 2 + [ANYWHERE],
        out_specs=VMEM_WHOLE,
        out_shape=rows_shape,
        compiler_params=params(4),
        cost_estimate=cost(4000000000, 1),
        name="home_rows",
    )(source_node, source_outlet, turns, flow, behind)
    keep, home_theta = pl.pallas_call(
        functools.partial(keep_kernel, sizes),
        in_specs=[VMEM_WHOLE] * 4 + [ANYWHERE] * 2,
        out_specs=[VMEM_WHOLE] * 2,
        out_shape=[jax.ShapeDtypeStruct(per_cell, F32)] * 2,
        compiler_params=params(8),
        cost_estimate=cost(10000000, 1),
        name="keep",
    )(theta, node_in, node_out, fraction, behind, arrived[2])
    base = pl.pallas_call(
        functools.partial(base_kernel, sizes),
        in_specs=[SMEM_WHOLE] * 2 + [VMEM_WHOLE] * 2,
        out_specs=VMEM_WHOLE,
        out_shape=rows_shape,
        compiler_params=params(4),
        cost_estimate=cost(10000000, 1),
        name="base_rows",
    )(keep.reshape(-1), home_theta.reshape(-1), rows, home)

    base, *rest = lax.optimization_barrier((base, *theta_there, *arrived))
    theta_there, arrived = rest[:2], rest[2:]
    last = shifted(behind, "region", SHIFTS[3])
    got = jnp.concatenate(theta_there)
    members = lax.axis_size("dest")
    other = lax.ppermute(got, "dest", [(i, i ^ 1) for i in range(members)])
    scale = jnp.concatenate([got, other])

    base = pl.pallas_call(
        functools.partial(land_kernel, sizes, (0, 1, 2)),
        in_specs=[SMEM_WHOLE] * 2 + [VMEM_WHOLE] * 4,
        out_specs=VMEM_WHOLE,
        out_shape=rows_shape,
        input_output_aliases={5: 0},
        compiler_params=params(4),
        cost_estimate=cost(4000000000, 1),
        name="land_first",
    )(scale.reshape(-1), land, *arrived, base)

    out, _ = pl.pallas_call(
        functools.partial(finish_kernel, sizes, (3,), chunk),
        in_specs=[SMEM_WHOLE] + [VMEM_WHOLE] * 2,
        out_specs=[ANYWHERE, VMEM_WHOLE],
        out_shape=[jax.ShapeDtypeStruct((cells, width), F32), rows_shape],
        scratch_shapes=[
            pltpu.VMEM((cells, width), F32),
            pltpu.SemaphoreType.DMA((cells // chunk,)),
        ],
        input_output_aliases={2: 1},
        compiler_params=params(12),
        cost_estimate=cost(cells * width, cells * row_bytes),
        name="finish",
    )(land, last, base)
    return out


def solution(mesh):
    return jax.shard_map(
        on_device,
        mesh=mesh,
        in_specs=(
            P("region", "dest"),
            P("region"),
            P("region"),
            P("region"),
            P(None, "region"),
            P(None, "region"),
            P("region", None),
            P("region", None),
            P("region", "dest"),
        ),
        out_specs=P("region", "dest"),
        check_vma=False,
    )
```

```python
import functools

import jax
import jax.numpy as jnp
from jax import lax
from jax.experimental import pallas as pl
from jax.experimental.pallas import tpu as pltpu
from jax.sharding import PartitionSpec as P

SHIFTS = (1, -1, 2, -2)
AHEAD = 2
BATCH = 32
LANES = 128
MIB = 1 << 20
F32 = jnp.float32
I32 = jnp.int32
VMEM_WHOLE = pl.BlockSpec(memory_space=pltpu.VMEM)
SMEM_WHOLE = pl.BlockSpec(memory_space=pltpu.SMEM)
ANYWHERE = pl.BlockSpec(memory_space=pl.ANY)


def to_neighbours(block):
    regions, members = lax.axis_size("region"), lax.axis_size("dest")
    route = [
        (r * members + d, (r + SHIFTS[d % 4]) % regions * members + d)
        for r in range(regions)
        for d in range(members)
    ]
    return lax.ppermute(block, ("region", "dest"), route)


def to_two(block, first):
    regions, members = lax.axis_size("region"), lax.axis_size("dest")
    route = [
        (r * members + d, (r + SHIFTS[first + d % 2]) % regions * members + d)
        for r in range(regions)
        for d in range(members)
    ]
    return lax.ppermute(block, ("region", "dest"), route)


def shifted(block, axis, distance):
    devices = range(lax.axis_size(axis))
    route = [((i - distance) % len(devices), i) for i in devices]
    return lax.ppermute(block, axis, route)


def partners(block, axis):
    count = lax.axis_size(axis)
    return [block] + [
        lax.ppermute(block, axis, [(i, i ^ other) for i in range(count)])
        for other in range(1, count)
    ]


def tree_sum(parts):
    while len(parts) > 1:
        parts = [parts[k] + parts[k + 1] for k in range(0, len(parts), 2)]
    return parts[0]


def params(mib):
    return pltpu.CompilerParams(vmem_limit_bytes=mib * MIB)


def cost(flops, moved):
    return pl.CostEstimate(flops=flops, bytes_accessed=moved, transcendentals=0)


def lane_sums(partial):
    count = partial.shape[0]
    parts = jnp.dot(
        in_parts(partial), jnp.ones((LANES, LANES), jnp.bfloat16), preferred_element_type=F32
    )
    sums = parts[:count, :] + parts[count : 2 * count, :] + parts[2 * count :, :]
    row = lax.broadcasted_iota(I32, (LANES, LANES), 0)
    lane = lax.broadcasted_iota(I32, (LANES, LANES), 1)
    pieces = [
        jnp.sum(jnp.where(row == lane, sums[k : k + LANES, :], 0.0), axis=0, keepdims=True)
        for k in range(0, partial.shape[0], LANES)
    ]
    return jnp.concatenate(pieces, axis=0)


def stacked(row):
    return jnp.concatenate(
        [row[:, k : k + LANES] for k in range(0, row.shape[1], LANES)], axis=0
    )


def strung(rows):
    return jnp.concatenate([rows[k : k + 1, :] for k in range(rows.shape[0])], axis=1)


def row_of(ref, number, sub):
    if sub % 8 == 0:
        return ref.reshape(ref.shape[0] // sub, sub, LANES).at[number]
    return ref.at[pl.ds(pl.multiple_of(number * sub, sub), sub), :]


def padded(cap):
    return -(-cap // LANES) * LANES


def put_row(ref, row, value, fill):
    width = value.shape[1]
    for q in range(-(-width // LANES)):
        piece = value[:, q * LANES : min((q + 1) * LANES, width)]
        lack = LANES - piece.shape[1]
        if lack:
            piece = jnp.concatenate([piece, jnp.full((1, lack), fill, piece.dtype)], axis=1)
        ref[row + q : row + q + 1, :] = piece


def one_hot(index, count):
    rows = lax.broadcasted_iota(I32, (count, index.shape[1]), 0)
    return jnp.where(rows == index, 1.0, 0.0)


def in_parts(x):
    high = x.astype(jnp.bfloat16)
    rest = x - high.astype(F32)
    middle = rest.astype(jnp.bfloat16)
    low = (rest - middle.astype(F32)).astype(jnp.bfloat16)
    return jnp.concatenate([high, middle, low], axis=0)


def selected(values, choice, dims):
    count = values.shape[0]
    product = lax.dot_general(
        in_parts(values), choice.astype(jnp.bfloat16), (dims, ((), ())),
        preferred_element_type=F32,
    )
    return product[:count, :] + product[count : 2 * count, :] + product[2 * count :, :]


def look_up(table, index):
    picked = selected(table.T, one_hot(index // LANES, table.shape[0]), ((1,), (0,)))
    return jnp.sum(picked * one_hot(index % LANES, LANES), axis=0, keepdims=True)


def scatter(index, values, height):
    high = jnp.where(index >= 0, index // LANES, -1)
    low = jnp.where(index >= 0, index % LANES, -1)
    return selected(one_hot(high, height) * values, one_hot(low, LANES), ((1,), (1,)))


def home_cells(node_out, region_no, cells):
    here = (node_out >= 0) & (node_out // cells == region_no)
    return jnp.where(here, node_out % cells, -1)


def rows_of_group(x_ref, rows_ref, first, sub):
    total = None
    for q in range(sub):
        piece = x_ref[pl.ds(pl.multiple_of(first, 8), 8), q * LANES : (q + 1) * LANES]
        rows_ref[pl.ds(first * sub + q, 8, stride=sub), :] = piece
        total = piece if total is None else total + piece
    return total


def copies_in(source, target, sems, chunk):
    copies = [
        pltpu.make_async_copy(
            source.at[pl.ds(i * chunk, chunk), :], target.at[pl.ds(i * chunk, chunk), :], sems.at[i]
        )
        for i in range(target.shape[0] // chunk)
    ]
    for copy in copies:
        copy.start()
    return copies


def make_lists(
    sizes, node_in, node_out, send_list, recv_list,
    in_cell, send_node, send_outlet, land, ahead, source_node, source_outlet,
):
    cells, nodes, branches, cap, sub = sizes
    height = cells // LANES
    region_no = lax.axis_index("region")
    ids = lax.broadcasted_iota(I32, (1, nodes), 1).astype(F32) + 1.0
    number = jnp.zeros((height, LANES), F32)
    slot = jnp.zeros((height, LANES), F32)
    for j in range(branches):
        ins = node_in[j : j + 1, :]
        put_row(in_cell, j * (nodes // LANES), jnp.where(ins >= 0, ins, cells), cells)
        home = home_cells(node_out[j : j + 1, :], region_no, cells)
        here = scatter(home, ids, height)
        number = number + here
        slot = slot + jnp.where(here > 0.0, j + 1.0, 0.0)
    source_node[...] = jnp.maximum(number.astype(I32) - 1, 0)
    source_outlet[...] = slot.astype(I32) - 1
    per_side = padded(cap) // LANES
    for side in range(4):
        slots = send_list[side : side + 1, :]
        lands = recv_list[side : side + 1, :]
        node = jnp.where(slots >= 0, slots % nodes, 0)
        outlet = jnp.where(slots >= 0, slots // nodes, -1)
        put_row(send_node, side * per_side, node, 0)
        put_row(send_outlet, side * per_side, outlet, -1)
        put_row(land, side * per_side, jnp.where(lands >= 0, lands, cells), cells)
        if side == AHEAD:
            for j in range(branches):
                ins = node_in[j : j + 1, :]
                table = stacked(jnp.where(ins >= 0, ins, cells)).astype(F32)
                put_row(ahead, j * per_side, (look_up(table, node) + 0.5).astype(I32), cells)
            put_row(ahead, branches * per_side, node, 0)
            put_row(ahead, (branches + 1) * per_side, outlet, -1)


def cell_sum_kernel(chunk, sub, x_hbm, sum_ref, rows_ref, x, partial, sems):
    copies = copies_in(x_hbm, x, sems, chunk)
    zeros = rows_ref.shape[0] - sub
    rows_ref[zeros:, :] = jnp.zeros((sub, LANES), F32)
    for number, copy in enumerate(copies):
        copy.wait()

        def body(step, carry, number=number):
            for half in range(2):
                first = number * chunk + step * 16 + half * 8
                total = rows_of_group(x, rows_ref, first, sub)
                partial[pl.ds(pl.multiple_of(first, 8), 8), :] = total
            return carry

        lax.fori_loop(0, chunk // 16, body, 0)
    sum_ref[...] = lane_sums(partial[...])


def turn_rows_kernel(sizes, chunk, x_hbm, after_ref, *rest):
    cells, nodes, branches, cap, sub = sizes
    lists, rows_ref, made, (x, sems) = rest[:4], rest[4], rest[5:12], rest[12:]
    copies = copies_in(x_hbm, x, sems, chunk)
    make_lists(sizes, *lists, *made)
    for number, copy in enumerate(copies):
        copy.wait()

        def body(step, carry, number=number):
            for half in range(2):
                rows_of_group(x, rows_ref, number * chunk + step * 16 + half * 8, sub)
            return carry

        lax.fori_loop(0, chunk // 16, body, 0)


def gathered_flow(node, in_cell, scaled, sizes):
    cells, nodes, branches, cap, sub = sizes
    return tree_sum(
        [row_of(scaled, in_cell[i * nodes + node], sub)[...] for i in range(branches)]
    )


def send_ahead_kernel(sizes, fraction, slots, rows, turns, send):
    cells, nodes, branches, cap, sub = sizes
    batch = BATCH

    def body(step, carry):
        first = step * batch
        values = []
        for i in range(batch):
            slot = first + i
            parts = []
            for j in range(branches):
                cell = slots[j * padded(cap) + slot]
                parts.append(row_of(rows, cell, sub)[...] * fraction[cell])
            node = slots[branches * padded(cap) + slot]
            choice = row_of(turns, node, sub)[...]
            outlet = slots[(branches + 1) * padded(cap) + slot]
            values.append(jnp.where(choice == outlet, tree_sum(parts), 0.0))
        for i in range(batch):
            row_of(send, first + i, sub)[...] = values[i]
        return carry

    lax.fori_loop(0, cap // batch, body, 0)


def scale_rows(sizes, fraction, rows, scaled):
    cells, nodes, branches, cap, sub = sizes

    def body(step, carry):
        first = step * BATCH
        values = [
            row_of(rows, first + i, sub)[...] * fraction[first + i] for i in range(BATCH)
        ]
        for i in range(BATCH):
            row_of(scaled, first + i, sub)[...] = values[i]
        return carry

    lax.fori_loop(0, cells // BATCH, body, 0)
    row_of(scaled, cells, sub)[...] = jnp.zeros((sub, LANES), F32)


def scale_send_kernel(
    sizes, sides, fraction, in_cell, send_node, send_outlet, rows, turns, sent_ref, supply_ref,
    scaled, *sends,
):
    cells, nodes, branches, cap, sub = sizes
    scale_rows(sizes, fraction, rows, scaled)
    batch = BATCH
    for side, send in zip(sides, sends):

        def body(step, carry, side=side, send=send):
            first = step * batch
            values = []
            for i in range(batch):
                slot = side * padded(cap) + first + i
                node = send_node[slot]
                value = gathered_flow(node, in_cell, scaled, sizes)
                choice = row_of(turns, node, sub)[...]
                values.append(jnp.where(choice == send_outlet[slot], value, 0.0))
            for i in range(batch):
                row_of(send, first + i, sub)[...] = values[i]
            return carry

        lax.fori_loop(0, cap // batch, body, 0)


def scaled_send_kernel(sizes, side, theta, send_node, send_outlet, flow, turns, send):
    cells, nodes, branches, cap, sub = sizes
    batch = BATCH

    def body(step, carry):
        first = step * batch
        values = []
        for i in range(batch):
            slot = side * padded(cap) + first + i
            node = send_node[slot]
            value = row_of(flow, node, sub)[...] * theta[node]
            choice = row_of(turns, node, sub)[...]
            values.append(jnp.where(choice == send_outlet[slot], value, 0.0))
        for i in range(batch):
            row_of(send, first + i, sub)[...] = values[i]
        return carry

    lax.fori_loop(0, cap // batch, body, 0)


def node_flow_kernel(sizes, in_cell, scaled, turns, after_ref, flow, demand, partial):
    cells, nodes, branches, cap, sub = sizes

    def gather(step, carry):
        first = step * BATCH
        values = [
            gathered_flow(first + i, in_cell, scaled, sizes) for i in range(BATCH)
        ]
        for i in range(BATCH):
            row_of(flow, first + i, sub)[...] = values[i]
        return carry

    def measure(step, carry):
        for half in range(2):
            first = step * 16 + half * 8
            totals = [jnp.zeros((8, LANES), F32)] * branches
            for q in range(sub):
                at = pl.ds(first * sub + q, 8, stride=sub)
                value = flow[at, :]
                choice = turns[at, :]
                totals = [
                    total + jnp.where(choice == j, value, 0.0) for j, total in enumerate(totals)
                ]
            for j in range(branches):
                partial[j, pl.ds(pl.multiple_of(first, 8), 8), :] = totals[j]
        return carry

    lax.fori_loop(0, nodes // BATCH, gather, 0)
    lax.fori_loop(0, nodes // 16, measure, 0)
    per_outlet = nodes // LANES
    for j in range(branches):
        demand[j * per_outlet : (j + 1) * per_outlet, :] = lane_sums(partial[j])


def theta_kernel(
    sizes, regions, commodities, supply, shared, node_out, send_list, theta_out, slot_theta
):
    cells, nodes, branches, cap, sub = sizes
    per_outlet = nodes // LANES
    height = cells // LANES
    block = branches * per_outlet + height
    region_no = lax.axis_index("region")
    members = shared.shape[0] // block
    parts = [
        shared[d * block : d * block + branches * per_outlet, :] for d in range(members)
    ]
    demand = tree_sum(parts) * (1.0 / commodities)
    table = jnp.concatenate(
        [supply[...]]
        + [
            shared[d * block + branches * per_outlet : (d + 1) * block, :] for d in range(4)
        ],
        axis=0,
    )
    tall = jnp.ones((per_outlet, LANES), F32)
    for j in range(branches):
        outs = node_out[j : j + 1, :]
        cell = jnp.maximum(outs, 0)
        offset = (cell // cells + regions - region_no) % regions
        sector = jnp.zeros_like(offset)
        for d in range(4):
            sector = jnp.where(offset == (-SHIFTS[d]) % regions, d + 1, sector)
        room = stacked(look_up(table, sector * cells + cell % cells))
        ratio = room / jnp.maximum(demand[j * per_outlet : (j + 1) * per_outlet, :], room)
        tall = jnp.minimum(tall, jnp.where(stacked(outs) >= 0, ratio, 1.0))
    theta_out[...] = tall
    per_side = padded(cap) // LANES
    for k in range(2):
        slots = send_list[pl.ds(2 * k + lax.axis_index("dest") % 2, 1), :]
        there = look_up(tall, jnp.where(slots >= 0, slots % nodes, 0))
        put_row(slot_theta, k * per_side, there, 0.0)


def keep_kernel(
    sizes, theta_ref, node_in, node_out, fraction, sent_ref, arrived_ref, keep, home_theta
):
    cells, nodes, branches, cap, sub = sizes
    height = cells // LANES
    region_no = lax.axis_index("region")
    theta = strung(theta_ref[...])
    cell_theta = jnp.zeros((height, LANES), F32)
    into = jnp.zeros((height, LANES), F32)
    for j in range(branches):
        home = home_cells(node_out[j : j + 1, :], region_no, cells)
        cell_theta = cell_theta + scatter(node_in[j : j + 1, :], theta, height)
        into = into + scatter(home, theta, height)
    keep[...] = 1.0 - cell_theta * fraction[...]
    home_theta[...] = into


def home_kernel(sizes, source, outlet, turns, flow, after_ref, home):
    cells, nodes, branches, cap, sub = sizes
    batch = BATCH

    def body(step, carry):
        first = step * batch
        values = []
        for i in range(batch):
            node = source[first + i]
            choice = row_of(turns, node, sub)[...]
            moved = row_of(flow, node, sub)[...]
            values.append(jnp.where(choice == outlet[first + i], moved, 0.0))
        for i in range(batch):
            row_of(home, first + i, sub)[...] = values[i]
        return carry

    lax.fori_loop(0, cells // batch, body, 0)


def base_kernel(sizes, keep, home_theta, rows, home, base):
    cells, nodes, branches, cap, sub = sizes
    batch = BATCH

    def body(step, carry):
        first = step * batch
        values = []
        for i in range(batch):
            cell = first + i
            kept = row_of(rows, cell, sub)[...] * keep[cell]
            values.append(kept + row_of(home, cell, sub)[...] * home_theta[cell])
        for i in range(batch):
            row_of(base, first + i, sub)[...] = values[i]
        return carry

    lax.fori_loop(0, cells // batch, body, 0)


def land_rows(sizes, sides, scale, land, received, base):
    cells, nodes, branches, cap, sub = sizes
    batch = BATCH
    core = lax.axis_index("dest") % 2
    for side, rows in zip(sides, received):
        offset = jnp.where(core == side % 2, 0, 2 * padded(cap)) + side // 2 * padded(cap)

        def body(step, carry, side=side, rows=rows, offset=offset):
            first = step * batch
            stores = []
            for i in range(batch):
                at = row_of(base, land[side * padded(cap) + first + i], sub)
                value = row_of(rows, first + i, sub)[...]
                if scale is not None:
                    value = value * scale[offset + first + i]
                stores.append((at, at[...] + value))
            for at, value in stores:
                at[...] = value
            return carry

        lax.fori_loop(0, cap // batch, body, 0)


def land_kernel(sizes, sides, scale, land, *rest):
    received, (base_in, base) = rest[: len(sides)], rest[len(sides) :]
    land_rows(sizes, sides, scale, land, received, base)


def finish_kernel(sizes, sides, chunk, land, *rest):
    cells, nodes, branches, cap, sub = sizes
    received, (base_in, out, base, staged, sems) = rest[: len(sides)], rest[len(sides) :]
    land_rows(sizes, sides, None, land, received, base)
    copies = []
    for number in range(cells // chunk):

        def body(step, carry, number=number):
            for half in range(2):
                first = number * chunk + step * 16 + half * 8
                for q in range(sub):
                    staged[
                        pl.ds(pl.multiple_of(first, 8), 8), q * LANES : (q + 1) * LANES
                    ] = base[pl.ds(first * sub + q, 8, stride=sub), :]
            return carry

        lax.fori_loop(0, chunk // 16, body, 0)
        at = pl.ds(number * chunk, chunk)
        copies.append(
            pltpu.make_async_copy(staged.at[at, :], out.at[at, :], sems.at[number])
        )
        copies[-1].start()
    for copy in copies:
        copy.wait()


def on_device(occupancy, capacity, jam, wave, node_in, node_out, send_list, recv_list, turn):
    cells, width = occupancy.shape
    branches, nodes = node_in.shape
    cap = send_list.shape[1]
    sub = width // LANES
    sizes = (cells, nodes, branches, cap, sub)
    regions = lax.axis_size("region")
    commodities = width * lax.axis_size("dest")
    height = cells // LANES
    per_cell = (height, LANES)
    list_shape = (4 * padded(cap) // LANES, LANES)
    ahead_rows = -(-(branches + 2) * padded(cap) // LANES // 8) * 8
    chunk = 128
    row_bytes = width * 4
    occupancy = pltpu.with_memory_space_constraint(occupancy, pltpu.HBM)
    turn = pltpu.with_memory_space_constraint(turn, pltpu.HBM)

    local_sum, rows = pl.pallas_call(
        functools.partial(cell_sum_kernel, chunk, sub),
        in_specs=[ANYWHERE],
        out_specs=[VMEM_WHOLE] * 2,
        out_shape=[
            jax.ShapeDtypeStruct(per_cell, F32),
            pltpu.VMEM(((cells + 1) * sub, LANES), F32),
        ],
        scratch_shapes=[
            pltpu.VMEM((cells, width), F32),
            pltpu.VMEM((cells, LANES), F32),
            pltpu.SemaphoreType.DMA((cells // chunk,)),
        ],
        compiler_params=params(14),
        cost_estimate=cost(cells * width, cells * row_bytes),
        name="cell_sum",
    )(occupancy)

    sums = partners(local_sum, "dest")

    turns, *lists = pl.pallas_call(
        functools.partial(turn_rows_kernel, sizes, chunk),
        in_specs=[ANYWHERE] * 2 + [VMEM_WHOLE] * 4,
        out_specs=[VMEM_WHOLE] * 8,
        out_shape=[
            pltpu.VMEM((nodes * sub, LANES), I32),
            jax.ShapeDtypeStruct((branches * nodes // LANES, LANES), I32),
        ]
        + [jax.ShapeDtypeStruct(list_shape, I32)] * 3
        + [jax.ShapeDtypeStruct((ahead_rows, LANES), I32)]
        + [jax.ShapeDtypeStruct(per_cell, I32)] * 2,
        scratch_shapes=[
            pltpu.VMEM((nodes, width), I32),
            pltpu.SemaphoreType.DMA((nodes // chunk,)),
        ],
        compiler_params=params(8),
        cost_estimate=cost(0, nodes * row_bytes),
        name="turn_rows",
    )(turn, local_sum, node_in, node_out, send_list, recv_list)
    in_cell, send_node, send_outlet, land, ahead_list, source_node, source_outlet = (
        x.reshape(-1) for x in lists
    )

    turns, *sums = lax.optimization_barrier((turns, *sums))
    vehicles = tree_sum(sums) / commodities
    cap_of = capacity.reshape(per_cell)
    fraction = jnp.minimum(vehicles, cap_of) / vehicles
    supply = jnp.minimum(cap_of, wave.reshape(per_cell) * (jam.reshape(per_cell) - vehicles))
    rows_shape = pltpu.VMEM(((cells + 1) * sub, LANES), F32)
    send_shape = pltpu.VMEM((cap * sub, LANES), F32)

    supply_there = to_neighbours(supply)
    weights = jnp.concatenate([fraction.reshape(-1), jnp.zeros((LANES,), F32)])
    (ahead,) = pl.pallas_call(
        functools.partial(send_ahead_kernel, sizes),
        in_specs=[SMEM_WHOLE] * 2 + [VMEM_WHOLE] * 2,
        out_specs=[VMEM_WHOLE],
        out_shape=[send_shape],
        compiler_params=params(4),
        cost_estimate=cost(1, 1),
        name="send_ahead",
    )(weights, ahead_list, rows, turns)
    scaled, *near = pl.pallas_call(
        functools.partial(scale_send_kernel, sizes, (0, 1)),
        in_specs=[SMEM_WHOLE] * 4 + [VMEM_WHOLE] * 2 + [ANYWHERE] * 2,
        out_specs=[VMEM_WHOLE] * 3,
        out_shape=[rows_shape] + [send_shape] * 2,
        compiler_params=params(4),
        cost_estimate=cost(10000000000, 1),
        name="scale_send",
    )(fraction.reshape(-1), in_cell, send_node, send_outlet, rows, turns, ahead, supply_there)
    arrived = [
        shifted(send, "region", SHIFTS[side]) for side, send in enumerate([*near, ahead])
    ]

    flow, demand = pl.pallas_call(
        functools.partial(node_flow_kernel, sizes),
        in_specs=[SMEM_WHOLE] + [VMEM_WHOLE] * 2 + [ANYWHERE],
        out_specs=[VMEM_WHOLE] * 2,
        out_shape=[
            pltpu.VMEM((nodes * sub, LANES), F32),
            jax.ShapeDtypeStruct((branches * nodes // LANES, LANES), F32),
        ],
        scratch_shapes=[pltpu.VMEM((branches, nodes, LANES), F32)],
        compiler_params=params(8),
        cost_estimate=cost(1, 1),
        name="node_flow",
    )(in_cell, scaled, turns, near[0])

    joined = jnp.concatenate([demand, supply_there])
    shared = lax.all_gather(joined, "dest", axis=0, tiled=True)
    theta, slot_theta = pl.pallas_call(
        functools.partial(theta_kernel, sizes, regions, commodities),
        in_specs=[VMEM_WHOLE] * 4,
        out_specs=[VMEM_WHOLE] * 2,
        out_shape=[
            jax.ShapeDtypeStruct((nodes // LANES, LANES), F32),
            jax.ShapeDtypeStruct((2 * padded(cap) // LANES, LANES), F32),
        ],
        compiler_params=params(8),
        cost_estimate=cost(1, 1),
        name="theta",
    )(supply, shared, node_out, send_list)
    theta, slot_theta, arrived[2] = lax.optimization_barrier((theta, slot_theta, arrived[2]))
    per_side = padded(cap) // LANES
    theta_there = [to_two(slot_theta[:per_side], 0), to_two(slot_theta[per_side:], 2)]

    (behind,) = pl.pallas_call(
        functools.partial(scaled_send_kernel, sizes, 3),
        in_specs=[SMEM_WHOLE] * 3 + [VMEM_WHOLE] * 2,
        out_specs=[VMEM_WHOLE],
        out_shape=[send_shape],
        compiler_params=params(4),
        cost_estimate=cost(1, 1),
        name="send_scaled",
    )(theta.reshape(-1), send_node, send_outlet, flow, turns)
    home = pl.pallas_call(
        functools.partial(home_kernel, sizes),
        in_specs=[SMEM_WHOLE] * 2 + [VMEM_WHOLE] * 2 + [ANYWHERE],
        out_specs=VMEM_WHOLE,
        out_shape=rows_shape,
        compiler_params=params(4),
        cost_estimate=cost(4000000000, 1),
        name="home_rows",
    )(source_node, source_outlet, turns, flow, behind)
    keep, home_theta = pl.pallas_call(
        functools.partial(keep_kernel, sizes),
        in_specs=[VMEM_WHOLE] * 4 + [ANYWHERE] * 2,
        out_specs=[VMEM_WHOLE] * 2,
        out_shape=[jax.ShapeDtypeStruct(per_cell, F32)] * 2,
        compiler_params=params(8),
        cost_estimate=cost(10000000, 1),
        name="keep",
    )(theta, node_in, node_out, fraction, behind, arrived[2])
    base = pl.pallas_call(
        functools.partial(base_kernel, sizes),
        in_specs=[SMEM_WHOLE] * 2 + [VMEM_WHOLE] * 2,
        out_specs=VMEM_WHOLE,
        out_shape=rows_shape,
        compiler_params=params(4),
        cost_estimate=cost(10000000, 1),
        name="base_rows",
    )(keep.reshape(-1), home_theta.reshape(-1), rows, home)

    base, *rest = lax.optimization_barrier((base, *theta_there, *arrived))
    theta_there, arrived = rest[:2], rest[2:]
    last = shifted(behind, "region", SHIFTS[3])
    got = jnp.concatenate(theta_there)
    members = lax.axis_size("dest")
    other = lax.ppermute(got, "dest", [(i, i ^ 1) for i in range(members)])
    scale = jnp.concatenate([got, other])

    base = pl.pallas_call(
        functools.partial(land_kernel, sizes, (0, 1, 2)),
        in_specs=[SMEM_WHOLE] * 2 + [VMEM_WHOLE] * 4,
        out_specs=VMEM_WHOLE,
        out_shape=rows_shape,
        input_output_aliases={5: 0},
        compiler_params=params(4),
        cost_estimate=cost(4000000000, 1),
        name="land_first",
    )(scale.reshape(-1), land, *arrived, base)

    out, _ = pl.pallas_call(
        functools.partial(finish_kernel, sizes, (3,), chunk),
        in_specs=[SMEM_WHOLE] + [VMEM_WHOLE] * 2,
        out_specs=[ANYWHERE, VMEM_WHOLE],
        out_shape=[jax.ShapeDtypeStruct((cells, width), F32), rows_shape],
        scratch_shapes=[
            pltpu.VMEM((cells, width), F32),
            pltpu.SemaphoreType.DMA((cells // chunk,)),
        ],
        input_output_aliases={2: 1},
        compiler_params=params(12),
        cost_estimate=cost(cells * width, cells * row_bytes),
        name="finish",
    )(land, last, base)
    return out


def solution(mesh):
    return jax.shard_map(
        on_device,
        mesh=mesh,
        in_specs=(
            P("region", "dest"),
            P("region"),
            P("region"),
            P("region"),
            P(None, "region"),
            P(None, "region"),
            P("region", None),
            P("region", None),
            P("region", "dest"),
        ),
        out_specs=P("region", "dest"),
        check_vma=False,
    )
```

```python
import functools

import jax
import jax.numpy as jnp
from jax import lax
from jax.experimental import pallas as pl
from jax.experimental.pallas import tpu as pltpu
from jax.sharding import PartitionSpec as P

SHIFTS = (1, -1, 2, -2)
AHEAD = 2
LANES = 128
MIB = 1 << 20
F32 = jnp.float32
I32 = jnp.int32
VMEM_WHOLE = pl.BlockSpec(memory_space=pltpu.VMEM)
SMEM_WHOLE = pl.BlockSpec(memory_space=pltpu.SMEM)
ANYWHERE = pl.BlockSpec(memory_space=pl.ANY)


def to_neighbours(block):
    regions, members = lax.axis_size("region"), lax.axis_size("dest")
    route = [
        (r * members + d, (r + SHIFTS[d % 4]) % regions * members + d)
        for r in range(regions)
        for d in range(members)
    ]
    return lax.ppermute(block, ("region", "dest"), route)


def to_two(block, first):
    regions, members = lax.axis_size("region"), lax.axis_size("dest")
    route = [
        (r * members + d, (r + SHIFTS[first + d % 2]) % regions * members + d)
        for r in range(regions)
        for d in range(members)
    ]
    return lax.ppermute(block, ("region", "dest"), route)


def shifted(block, axis, distance):
    devices = range(lax.axis_size(axis))
    route = [((i - distance) % len(devices), i) for i in devices]
    return lax.ppermute(block, axis, route)


def partners(block, axis):
    count = lax.axis_size(axis)
    return [block] + [
        lax.ppermute(block, axis, [(i, i ^ other) for i in range(count)])
        for other in range(1, count)
    ]


def tree_sum(parts):
    while len(parts) > 1:
        parts = [parts[k] + parts[k + 1] for k in range(0, len(parts), 2)]
    return parts[0]


def params(mib):
    return pltpu.CompilerParams(vmem_limit_bytes=mib * MIB)


def cost(flops, moved):
    return pl.CostEstimate(flops=flops, bytes_accessed=moved, transcendentals=0)


def lane_sums(partial):
    count = partial.shape[0]
    parts = jnp.dot(
        in_parts(partial), jnp.ones((LANES, LANES), jnp.bfloat16), preferred_element_type=F32
    )
    sums = parts[:count, :] + parts[count : 2 * count, :] + parts[2 * count :, :]
    row = lax.broadcasted_iota(I32, (LANES, LANES), 0)
    lane = lax.broadcasted_iota(I32, (LANES, LANES), 1)
    pieces = [
        jnp.sum(jnp.where(row == lane, sums[k : k + LANES, :], 0.0), axis=0, keepdims=True)
        for k in range(0, partial.shape[0], LANES)
    ]
    return jnp.concatenate(pieces, axis=0)


def stacked(row):
    return jnp.concatenate(
        [row[:, k : k + LANES] for k in range(0, row.shape[1], LANES)], axis=0
    )


def strung(rows):
    return jnp.concatenate([rows[k : k + 1, :] for k in range(rows.shape[0])], axis=1)


def row_of(ref, number, sub):
    if sub % 8 == 0:
        return ref.reshape(ref.shape[0] // sub, sub, LANES).at[number]
    return ref.at[pl.ds(pl.multiple_of(number * sub, sub), sub), :]


def padded(cap):
    return -(-cap // LANES) * LANES


def put_row(ref, row, value, fill):
    width = value.shape[1]
    for q in range(-(-width // LANES)):
        piece = value[:, q * LANES : min((q + 1) * LANES, width)]
        lack = LANES - piece.shape[1]
        if lack:
            piece = jnp.concatenate([piece, jnp.full((1, lack), fill, piece.dtype)], axis=1)
        ref[row + q : row + q + 1, :] = piece


def one_hot(index, count):
    rows = lax.broadcasted_iota(I32, (count, index.shape[1]), 0)
    return jnp.where(rows == index, 1.0, 0.0)


def in_parts(x):
    high = x.astype(jnp.bfloat16)
    rest = x - high.astype(F32)
    middle = rest.astype(jnp.bfloat16)
    low = (rest - middle.astype(F32)).astype(jnp.bfloat16)
    return jnp.concatenate([high, middle, low], axis=0)


def selected(values, choice, dims):
    count = values.shape[0]
    product = lax.dot_general(
        in_parts(values), choice.astype(jnp.bfloat16), (dims, ((), ())),
        preferred_element_type=F32,
    )
    return product[:count, :] + product[count : 2 * count, :] + product[2 * count :, :]


def look_up(table, index):
    picked = selected(table.T, one_hot(index // LANES, table.shape[0]), ((1,), (0,)))
    return jnp.sum(picked * one_hot(index % LANES, LANES), axis=0, keepdims=True)


def scatter(index, values, height):
    high = jnp.where(index >= 0, index // LANES, -1)
    low = jnp.where(index >= 0, index % LANES, -1)
    return selected(one_hot(high, height) * values, one_hot(low, LANES), ((1,), (1,)))


def home_cells(node_out, region_no, cells):
    here = (node_out >= 0) & (node_out // cells == region_no)
    return jnp.where(here, node_out % cells, -1)


def rows_of_group(x_ref, rows_ref, first, sub):
    total = None
    for q in range(sub):
        piece = x_ref[pl.ds(pl.multiple_of(first, 8), 8), q * LANES : (q + 1) * LANES]
        rows_ref[pl.ds(first * sub + q, 8, stride=sub), :] = piece
        total = piece if total is None else total + piece
    return total


def copies_in(source, target, sems, chunk):
    copies = [
        pltpu.make_async_copy(
            source.at[pl.ds(i * chunk, chunk), :], target.at[pl.ds(i * chunk, chunk), :], sems.at[i]
        )
        for i in range(target.shape[0] // chunk)
    ]
    for copy in copies:
        copy.start()
    return copies


def make_lists(
    sizes, node_in, node_out, send_list, recv_list,
    in_cell, send_node, send_outlet, land, ahead, source_node, source_outlet,
):
    cells, nodes, branches, cap, sub = sizes
    height = cells // LANES
    region_no = lax.axis_index("region")
    ids = lax.broadcasted_iota(I32, (1, nodes), 1).astype(F32) + 1.0
    number = jnp.zeros((height, LANES), F32)
    slot = jnp.zeros((height, LANES), F32)
    for j in range(branches):
        ins = node_in[j : j + 1, :]
        put_row(in_cell, j * (nodes // LANES), jnp.where(ins >= 0, ins, cells), cells)
        home = home_cells(node_out[j : j + 1, :], region_no, cells)
        here = scatter(home, ids, height)
        number = number + here
        slot = slot + jnp.where(here > 0.0, j + 1.0, 0.0)
    source_node[...] = jnp.maximum(number.astype(I32) - 1, 0)
    source_outlet[...] = slot.astype(I32) - 1
    per_side = padded(cap) // LANES
    for side in range(4):
        slots = send_list[side : side + 1, :]
        lands = recv_list[side : side + 1, :]
        node = jnp.where(slots >= 0, slots % nodes, 0)
        outlet = jnp.where(slots >= 0, slots // nodes, -1)
        put_row(send_node, side * per_side, node, 0)
        put_row(send_outlet, side * per_side, outlet, -1)
        put_row(land, side * per_side, jnp.where(lands >= 0, lands, cells), cells)
        if side == AHEAD:
            for j in range(branches):
                ins = node_in[j : j + 1, :]
                table = stacked(jnp.where(ins >= 0, ins, cells)).astype(F32)
                put_row(ahead, j * per_side, (look_up(table, node) + 0.5).astype(I32), cells)
            put_row(ahead, branches * per_side, node, 0)
            put_row(ahead, (branches + 1) * per_side, outlet, -1)


def cell_sum_kernel(chunk, sub, x_hbm, sum_ref, rows_ref, x, partial, sems):
    copies = copies_in(x_hbm, x, sems, chunk)
    zeros = rows_ref.shape[0] - sub
    rows_ref[zeros:, :] = jnp.zeros((sub, LANES), F32)
    for number, copy in enumerate(copies):
        copy.wait()

        def body(step, carry, number=number):
            for part in range(4):
                first = number * chunk + step * 32 + part * 8
                total = rows_of_group(x, rows_ref, first, sub)
                partial[pl.ds(pl.multiple_of(first, 8), 8), :] = total
            return carry

        lax.fori_loop(0, chunk // 32, body, 0)
    sum_ref[...] = lane_sums(partial[...])


def turn_rows_kernel(sizes, chunk, x_hbm, after_ref, *rest):
    cells, nodes, branches, cap, sub = sizes
    lists, rows_ref, made, (x, sems) = rest[:4], rest[4], rest[5:12], rest[12:]
    copies = copies_in(x_hbm, x, sems, chunk)
    make_lists(sizes, *lists, *made)
    for number, copy in enumerate(copies):
        copy.wait()

        def body(step, carry, number=number):
            for part in range(4):
                rows_of_group(x, rows_ref, number * chunk + step * 32 + part * 8, sub)
            return carry

        lax.fori_loop(0, chunk // 32, body, 0)


def gathered_flow(node, in_cell, scaled, sizes):
    cells, nodes, branches, cap, sub = sizes
    return tree_sum(
        [row_of(scaled, in_cell[i * nodes + node], sub)[...] for i in range(branches)]
    )


def send_ahead_kernel(sizes, fraction, slots, rows, turns, send):
    cells, nodes, branches, cap, sub = sizes
    batch = 16

    def body(step, carry):
        first = step * batch
        values = []
        for i in range(batch):
            slot = first + i
            parts = []
            for j in range(branches):
                cell = slots[j * padded(cap) + slot]
                parts.append(row_of(rows, cell, sub)[...] * fraction[cell])
            node = slots[branches * padded(cap) + slot]
            choice = row_of(turns, node, sub)[...]
            outlet = slots[(branches + 1) * padded(cap) + slot]
            values.append(jnp.where(choice == outlet, tree_sum(parts), 0.0))
        for i in range(batch):
            row_of(send, first + i, sub)[...] = values[i]
        return carry

    lax.fori_loop(0, cap // batch, body, 0)


def scale_kernel(sizes, fraction, rows, sent_ref, supply_ref, scaled):
    cells, nodes, branches, cap, sub = sizes

    def body(step, carry):
        first = step * 16
        values = [
            row_of(rows, first + i, sub)[...] * fraction[first + i] for i in range(16)
        ]
        for i in range(16):
            row_of(scaled, first + i, sub)[...] = values[i]
        return carry

    lax.fori_loop(0, cells // 16, body, 0)
    row_of(scaled, cells, sub)[...] = jnp.zeros((sub, LANES), F32)


def send_kernel(sizes, sides, in_cell, send_node, send_outlet, scaled, turns, *sends):
    cells, nodes, branches, cap, sub = sizes
    batch = 16
    for side, send in zip(sides, sends):

        def body(step, carry, side=side, send=send):
            first = step * batch
            values = []
            for i in range(batch):
                slot = side * padded(cap) + first + i
                node = send_node[slot]
                value = gathered_flow(node, in_cell, scaled, sizes)
                choice = row_of(turns, node, sub)[...]
                values.append(jnp.where(choice == send_outlet[slot], value, 0.0))
            for i in range(batch):
                row_of(send, first + i, sub)[...] = values[i]
            return carry

        lax.fori_loop(0, cap // batch, body, 0)


def scaled_send_kernel(sizes, side, theta, send_node, send_outlet, flow, turns, send):
    cells, nodes, branches, cap, sub = sizes
    batch = 16

    def body(step, carry):
        first = step * batch
        values = []
        for i in range(batch):
            slot = side * padded(cap) + first + i
            node = send_node[slot]
            value = row_of(flow, node, sub)[...] * theta[node]
            choice = row_of(turns, node, sub)[...]
            values.append(jnp.where(choice == send_outlet[slot], value, 0.0))
        for i in range(batch):
            row_of(send, first + i, sub)[...] = values[i]
        return carry

    lax.fori_loop(0, cap // batch, body, 0)


def node_flow_kernel(sizes, in_cell, scaled, turns, after_ref, flow, demand, partial):
    cells, nodes, branches, cap, sub = sizes

    def gather(step, carry):
        first = step * 16
        values = [
            gathered_flow(first + i, in_cell, scaled, sizes) for i in range(16)
        ]
        for i in range(16):
            row_of(flow, first + i, sub)[...] = values[i]
        return carry

    def measure(step, carry):
        for part in range(4):
            first = step * 32 + part * 8
            totals = [jnp.zeros((8, LANES), F32)] * branches
            for q in range(sub):
                at = pl.ds(first * sub + q, 8, stride=sub)
                value = flow[at, :]
                choice = turns[at, :]
                totals = [
                    total + jnp.where(choice == j, value, 0.0) for j, total in enumerate(totals)
                ]
            for j in range(branches):
                partial[j, pl.ds(pl.multiple_of(first, 8), 8), :] = totals[j]
        return carry

    lax.fori_loop(0, nodes // 16, gather, 0)
    lax.fori_loop(0, nodes // 32, measure, 0)
    per_outlet = nodes // LANES
    for j in range(branches):
        demand[j * per_outlet : (j + 1) * per_outlet, :] = lane_sums(partial[j])


def theta_kernel(
    sizes, regions, commodities, supply, shared, node_out, send_list, theta_out, slot_theta
):
    cells, nodes, branches, cap, sub = sizes
    per_outlet = nodes // LANES
    height = cells // LANES
    block = branches * per_outlet + height
    region_no = lax.axis_index("region")
    members = shared.shape[0] // block
    parts = [
        shared[d * block : d * block + branches * per_outlet, :] for d in range(members)
    ]
    demand = tree_sum(parts) * (1.0 / commodities)
    table = jnp.concatenate(
        [supply[...]]
        + [
            shared[d * block + branches * per_outlet : (d + 1) * block, :] for d in range(4)
        ],
        axis=0,
    )
    tall = jnp.ones((per_outlet, LANES), F32)
    for j in range(branches):
        outs = node_out[j : j + 1, :]
        cell = jnp.maximum(outs, 0)
        offset = (cell // cells + regions - region_no) % regions
        sector = jnp.zeros_like(offset)
        for d in range(4):
            sector = jnp.where(offset == (-SHIFTS[d]) % regions, d + 1, sector)
        room = stacked(look_up(table, sector * cells + cell % cells))
        ratio = room / jnp.maximum(demand[j * per_outlet : (j + 1) * per_outlet, :], room)
        tall = jnp.minimum(tall, jnp.where(stacked(outs) >= 0, ratio, 1.0))
    theta_out[...] = tall
    per_side = padded(cap) // LANES
    for k in range(2):
        slots = send_list[pl.ds(2 * k + lax.axis_index("dest") % 2, 1), :]
        there = look_up(tall, jnp.where(slots >= 0, slots % nodes, 0))
        put_row(slot_theta, k * per_side, there, 0.0)


def keep_kernel(
    sizes, theta_ref, node_in, node_out, fraction, sent_ref, arrived_ref, keep, home_theta
):
    cells, nodes, branches, cap, sub = sizes
    height = cells // LANES
    region_no = lax.axis_index("region")
    theta = strung(theta_ref[...])
    cell_theta = jnp.zeros((height, LANES), F32)
    into = jnp.zeros((height, LANES), F32)
    for j in range(branches):
        home = home_cells(node_out[j : j + 1, :], region_no, cells)
        cell_theta = cell_theta + scatter(node_in[j : j + 1, :], theta, height)
        into = into + scatter(home, theta, height)
    keep[...] = 1.0 - cell_theta * fraction[...]
    home_theta[...] = into


def home_kernel(sizes, source, outlet, turns, flow, after_ref, home):
    cells, nodes, branches, cap, sub = sizes
    batch = 16

    def body(step, carry):
        first = step * batch
        values = []
        for i in range(batch):
            node = source[first + i]
            choice = row_of(turns, node, sub)[...]
            moved = row_of(flow, node, sub)[...]
            values.append(jnp.where(choice == outlet[first + i], moved, 0.0))
        for i in range(batch):
            row_of(home, first + i, sub)[...] = values[i]
        return carry

    lax.fori_loop(0, cells // batch, body, 0)


def base_kernel(sizes, keep, home_theta, rows, home, base):
    cells, nodes, branches, cap, sub = sizes
    batch = 16

    def body(step, carry):
        first = step * batch
        values = []
        for i in range(batch):
            cell = first + i
            kept = row_of(rows, cell, sub)[...] * keep[cell]
            values.append(kept + row_of(home, cell, sub)[...] * home_theta[cell])
        for i in range(batch):
            row_of(base, first + i, sub)[...] = values[i]
        return carry

    lax.fori_loop(0, cells // batch, body, 0)


def land_rows(sizes, sides, scale, land, received, base):
    cells, nodes, branches, cap, sub = sizes
    batch = 16
    core = lax.axis_index("dest") % 2
    for side, rows in zip(sides, received):
        offset = jnp.where(core == side % 2, 0, 2 * padded(cap)) + side // 2 * padded(cap)

        def body(step, carry, side=side, rows=rows, offset=offset):
            first = step * batch
            stores = []
            for i in range(batch):
                at = row_of(base, land[side * padded(cap) + first + i], sub)
                value = row_of(rows, first + i, sub)[...]
                if scale is not None:
                    value = value * scale[offset + first + i]
                stores.append((at, at[...] + value))
            for at, value in stores:
                at[...] = value
            return carry

        lax.fori_loop(0, cap // batch, body, 0)


def land_kernel(sizes, sides, scale, land, *rest):
    received, (base_in, base) = rest[: len(sides)], rest[len(sides) :]
    land_rows(sizes, sides, scale, land, received, base)


def finish_kernel(sizes, sides, chunk, land, *rest):
    cells, nodes, branches, cap, sub = sizes
    received, (base_in, out, base, staged, sems) = rest[: len(sides)], rest[len(sides) :]
    land_rows(sizes, sides, None, land, received, base)
    copies = []
    for number in range(cells // chunk):

        def body(step, carry, number=number):
            for part in range(4):
                first = number * chunk + step * 32 + part * 8
                for q in range(sub):
                    staged[
                        pl.ds(pl.multiple_of(first, 8), 8), q * LANES : (q + 1) * LANES
                    ] = base[pl.ds(first * sub + q, 8, stride=sub), :]
            return carry

        lax.fori_loop(0, chunk // 32, body, 0)
        at = pl.ds(number * chunk, chunk)
        copies.append(
            pltpu.make_async_copy(staged.at[at, :], out.at[at, :], sems.at[number])
        )
        copies[-1].start()
    for copy in copies:
        copy.wait()


def on_device(occupancy, capacity, jam, wave, node_in, node_out, send_list, recv_list, turn):
    cells, width = occupancy.shape
    branches, nodes = node_in.shape
    cap = send_list.shape[1]
    sub = width // LANES
    sizes = (cells, nodes, branches, cap, sub)
    regions = lax.axis_size("region")
    commodities = width * lax.axis_size("dest")
    height = cells // LANES
    per_cell = (height, LANES)
    list_shape = (4 * padded(cap) // LANES, LANES)
    ahead_rows = -(-(branches + 2) * padded(cap) // LANES // 8) * 8
    chunk = 128
    row_bytes = width * 4
    occupancy = pltpu.with_memory_space_constraint(occupancy, pltpu.HBM)
    turn = pltpu.with_memory_space_constraint(turn, pltpu.HBM)

    local_sum, rows = pl.pallas_call(
        functools.partial(cell_sum_kernel, chunk, sub),
        in_specs=[ANYWHERE],
        out_specs=[VMEM_WHOLE] * 2,
        out_shape=[
            jax.ShapeDtypeStruct(per_cell, F32),
            pltpu.VMEM(((cells + 1) * sub, LANES), F32),
        ],
        scratch_shapes=[
            pltpu.VMEM((cells, width), F32),
            pltpu.VMEM((cells, LANES), F32),
            pltpu.SemaphoreType.DMA((cells // chunk,)),
        ],
        compiler_params=params(14),
        cost_estimate=cost(cells * width, cells * row_bytes),
        name="cell_sum",
    )(occupancy)

    sums = partners(local_sum, "dest")

    turns, *lists = pl.pallas_call(
        functools.partial(turn_rows_kernel, sizes, chunk),
        in_specs=[ANYWHERE] * 2 + [VMEM_WHOLE] * 4,
        out_specs=[VMEM_WHOLE] * 8,
        out_shape=[
            pltpu.VMEM((nodes * sub, LANES), I32),
            jax.ShapeDtypeStruct((branches * nodes // LANES, LANES), I32),
        ]
        + [jax.ShapeDtypeStruct(list_shape, I32)] * 3
        + [jax.ShapeDtypeStruct((ahead_rows, LANES), I32)]
        + [jax.ShapeDtypeStruct(per_cell, I32)] * 2,
        scratch_shapes=[
            pltpu.VMEM((nodes, width), I32),
            pltpu.SemaphoreType.DMA((nodes // chunk,)),
        ],
        compiler_params=params(8),
        cost_estimate=cost(0, nodes * row_bytes),
        name="turn_rows",
    )(turn, local_sum, node_in, node_out, send_list, recv_list)
    in_cell, send_node, send_outlet, land, ahead_list, source_node, source_outlet = (
        x.reshape(-1) for x in lists
    )

    turns, *sums = lax.optimization_barrier((turns, *sums))
    vehicles = tree_sum(sums) / commodities
    cap_of = capacity.reshape(per_cell)
    fraction = jnp.minimum(vehicles, cap_of) / vehicles
    supply = jnp.minimum(cap_of, wave.reshape(per_cell) * (jam.reshape(per_cell) - vehicles))
    rows_shape = pltpu.VMEM(((cells + 1) * sub, LANES), F32)
    send_shape = pltpu.VMEM((cap * sub, LANES), F32)

    supply_there = to_neighbours(supply)
    weights = jnp.concatenate([fraction.reshape(-1), jnp.zeros((LANES,), F32)])
    (ahead,) = pl.pallas_call(
        functools.partial(send_ahead_kernel, sizes),
        in_specs=[SMEM_WHOLE] * 2 + [VMEM_WHOLE] * 2,
        out_specs=[VMEM_WHOLE],
        out_shape=[send_shape],
        compiler_params=params(4),
        cost_estimate=cost(1, 1),
        name="send_ahead",
    )(weights, ahead_list, rows, turns)
    scaled = pl.pallas_call(
        functools.partial(scale_kernel, sizes),
        in_specs=[SMEM_WHOLE, VMEM_WHOLE, ANYWHERE, ANYWHERE],
        out_specs=VMEM_WHOLE,
        out_shape=rows_shape,
        compiler_params=params(4),
        cost_estimate=cost(10000000000, 1),
        name="scale_rows",
    )(fraction.reshape(-1), rows, ahead, supply_there)
    near = pl.pallas_call(
        functools.partial(send_kernel, sizes, (0, 1)),
        in_specs=[SMEM_WHOLE] * 3 + [VMEM_WHOLE] * 2,
        out_specs=[VMEM_WHOLE] * 2,
        out_shape=[send_shape] * 2,
        compiler_params=params(4),
        cost_estimate=cost(1, 1),
        name="send_near",
    )(in_cell, send_node, send_outlet, scaled, turns)
    arrived = [
        shifted(send, "region", SHIFTS[side]) for side, send in enumerate([*near, ahead])
    ]

    flow, demand = pl.pallas_call(
        functools.partial(node_flow_kernel, sizes),
        in_specs=[SMEM_WHOLE] + [VMEM_WHOLE] * 2 + [ANYWHERE],
        out_specs=[VMEM_WHOLE] * 2,
        out_shape=[
            pltpu.VMEM((nodes * sub, LANES), F32),
            jax.ShapeDtypeStruct((branches * nodes // LANES, LANES), F32),
        ],
        scratch_shapes=[pltpu.VMEM((branches, nodes, LANES), F32)],
        compiler_params=params(8),
        cost_estimate=cost(1, 1),
        name="node_flow",
    )(in_cell, scaled, turns, near[0])

    joined = jnp.concatenate([demand, supply_there])
    shared = lax.all_gather(joined, "dest", axis=0, tiled=True)
    theta, slot_theta = pl.pallas_call(
        functools.partial(theta_kernel, sizes, regions, commodities),
        in_specs=[VMEM_WHOLE] * 4,
        out_specs=[VMEM_WHOLE] * 2,
        out_shape=[
            jax.ShapeDtypeStruct((nodes // LANES, LANES), F32),
            jax.ShapeDtypeStruct((2 * padded(cap) // LANES, LANES), F32),
        ],
        compiler_params=params(8),
        cost_estimate=cost(1, 1),
        name="theta",
    )(supply, shared, node_out, send_list)
    theta, slot_theta, arrived[2] = lax.optimization_barrier((theta, slot_theta, arrived[2]))
    per_side = padded(cap) // LANES
    theta_there = [to_two(slot_theta[:per_side], 0), to_two(slot_theta[per_side:], 2)]

    (behind,) = pl.pallas_call(
        functools.partial(scaled_send_kernel, sizes, 3),
        in_specs=[SMEM_WHOLE] * 3 + [VMEM_WHOLE] * 2,
        out_specs=[VMEM_WHOLE],
        out_shape=[send_shape],
        compiler_params=params(4),
        cost_estimate=cost(1, 1),
        name="send_scaled",
    )(theta.reshape(-1), send_node, send_outlet, flow, turns)
    home = pl.pallas_call(
        functools.partial(home_kernel, sizes),
        in_specs=[SMEM_WHOLE] * 2 + [VMEM_WHOLE] * 2 + [ANYWHERE],
        out_specs=VMEM_WHOLE,
        out_shape=rows_shape,
        compiler_params=params(4),
        cost_estimate=cost(4000000000, 1),
        name="home_rows",
    )(source_node, source_outlet, turns, flow, behind)
    keep, home_theta = pl.pallas_call(
        functools.partial(keep_kernel, sizes),
        in_specs=[VMEM_WHOLE] * 4 + [ANYWHERE] * 2,
        out_specs=[VMEM_WHOLE] * 2,
        out_shape=[jax.ShapeDtypeStruct(per_cell, F32)] * 2,
        compiler_params=params(8),
        cost_estimate=cost(10000000, 1),
        name="keep",
    )(theta, node_in, node_out, fraction, behind, arrived[2])
    base = pl.pallas_call(
        functools.partial(base_kernel, sizes),
        in_specs=[SMEM_WHOLE] * 2 + [VMEM_WHOLE] * 2,
        out_specs=VMEM_WHOLE,
        out_shape=rows_shape,
        compiler_params=params(4),
        cost_estimate=cost(10000000, 1),
        name="base_rows",
    )(keep.reshape(-1), home_theta.reshape(-1), rows, home)

    base, *rest = lax.optimization_barrier((base, *theta_there, *arrived))
    theta_there, arrived = rest[:2], rest[2:]
    last = shifted(behind, "region", SHIFTS[3])
    got = jnp.concatenate(theta_there)
    members = lax.axis_size("dest")
    other = lax.ppermute(got, "dest", [(i, i ^ 1) for i in range(members)])
    scale = jnp.concatenate([got, other])

    base = pl.pallas_call(
        functools.partial(land_kernel, sizes, (0, 1, 2)),
        in_specs=[SMEM_WHOLE] * 2 + [VMEM_WHOLE] * 4,
        out_specs=VMEM_WHOLE,
        out_shape=rows_shape,
        input_output_aliases={5: 0},
        compiler_params=params(4),
        cost_estimate=cost(4000000000, 1),
        name="land_first",
    )(scale.reshape(-1), land, *arrived, base)

    out, _ = pl.pallas_call(
        functools.partial(finish_kernel, sizes, (3,), chunk),
        in_specs=[SMEM_WHOLE] + [VMEM_WHOLE] * 2,
        out_specs=[ANYWHERE, VMEM_WHOLE],
        out_shape=[jax.ShapeDtypeStruct((cells, width), F32), rows_shape],
        scratch_shapes=[
            pltpu.VMEM((cells, width), F32),
            pltpu.SemaphoreType.DMA((cells // chunk,)),
        ],
        input_output_aliases={2: 1},
        compiler_params=params(12),
        cost_estimate=cost(cells * width, cells * row_bytes),
        name="finish",
    )(land, last, base)
    return out


def solution(mesh):
    return jax.shard_map(
        on_device,
        mesh=mesh,
        in_specs=(
            P("region", "dest"),
            P("region"),
            P("region"),
            P("region"),
            P(None, "region"),
            P(None, "region"),
            P("region", None),
            P("region", None),
            P("region", "dest"),
        ),
        out_specs=P("region", "dest"),
        check_vma=False,
    )
```

```python
import functools

import jax
import jax.numpy as jnp
from jax import lax
from jax.experimental import pallas as pl
from jax.experimental.pallas import tpu as pltpu
from jax.sharding import PartitionSpec as P

SHIFTS = (1, -1, 2, -2)
AHEAD = 2
LANES = 128
MIB = 1 << 20
F32 = jnp.float32
I32 = jnp.int32
VMEM_WHOLE = pl.BlockSpec(memory_space=pltpu.VMEM)
SMEM_WHOLE = pl.BlockSpec(memory_space=pltpu.SMEM)
ANYWHERE = pl.BlockSpec(memory_space=pl.ANY)


def to_neighbours(block):
    regions, members = lax.axis_size("region"), lax.axis_size("dest")
    route = [
        (r * members + d, (r + SHIFTS[d % 4]) % regions * members + d)
        for r in range(regions)
        for d in range(members)
    ]
    return lax.ppermute(block, ("region", "dest"), route)


def to_two(block, first):
    regions, members = lax.axis_size("region"), lax.axis_size("dest")
    route = [
        (r * members + d, (r + SHIFTS[first + d % 2]) % regions * members + d)
        for r in range(regions)
        for d in range(members)
    ]
    return lax.ppermute(block, ("region", "dest"), route)


def shifted(block, axis, distance):
    devices = range(lax.axis_size(axis))
    route = [((i - distance) % len(devices), i) for i in devices]
    return lax.ppermute(block, axis, route)


def partners(block, axis):
    count = lax.axis_size(axis)
    return [block] + [
        lax.ppermute(block, axis, [(i, i ^ other) for i in range(count)])
        for other in range(1, count)
    ]


def tree_sum(parts):
    while len(parts) > 1:
        parts = [parts[k] + parts[k + 1] for k in range(0, len(parts), 2)]
    return parts[0]


def params(mib):
    return pltpu.CompilerParams(vmem_limit_bytes=mib * MIB)


def cost(flops, moved):
    return pl.CostEstimate(flops=flops, bytes_accessed=moved, transcendentals=0)


def lane_sums(partial):
    count = partial.shape[0]
    parts = jnp.dot(
        in_parts(partial), jnp.ones((LANES, LANES), jnp.bfloat16), preferred_element_type=F32
    )
    sums = parts[:count, :] + parts[count : 2 * count, :] + parts[2 * count :, :]
    row = lax.broadcasted_iota(I32, (LANES, LANES), 0)
    lane = lax.broadcasted_iota(I32, (LANES, LANES), 1)
    pieces = [
        jnp.sum(jnp.where(row == lane, sums[k : k + LANES, :], 0.0), axis=0, keepdims=True)
        for k in range(0, partial.shape[0], LANES)
    ]
    return jnp.concatenate(pieces, axis=0)


def stacked(row):
    return jnp.concatenate(
        [row[:, k : k + LANES] for k in range(0, row.shape[1], LANES)], axis=0
    )


def strung(rows):
    return jnp.concatenate([rows[k : k + 1, :] for k in range(rows.shape[0])], axis=1)


def row_of(ref, number, sub):
    if sub % 8 == 0:
        return ref.reshape(ref.shape[0] // sub, sub, LANES).at[number]
    return ref.at[pl.ds(pl.multiple_of(number * sub, sub), sub), :]


def padded(cap):
    return -(-cap // LANES) * LANES


def put_row(ref, row, value, fill):
    width = value.shape[1]
    for q in range(-(-width // LANES)):
        piece = value[:, q * LANES : min((q + 1) * LANES, width)]
        lack = LANES - piece.shape[1]
        if lack:
            piece = jnp.concatenate([piece, jnp.full((1, lack), fill, piece.dtype)], axis=1)
        ref[row + q : row + q + 1, :] = piece


def one_hot(index, count):
    rows = lax.broadcasted_iota(I32, (count, index.shape[1]), 0)
    return jnp.where(rows == index, 1.0, 0.0)


def in_parts(x):
    high = x.astype(jnp.bfloat16)
    rest = x - high.astype(F32)
    middle = rest.astype(jnp.bfloat16)
    low = (rest - middle.astype(F32)).astype(jnp.bfloat16)
    return jnp.concatenate([high, middle, low], axis=0)


def selected(values, choice, dims):
    count = values.shape[0]
    product = lax.dot_general(
        in_parts(values), choice.astype(jnp.bfloat16), (dims, ((), ())),
        preferred_element_type=F32,
    )
    return product[:count, :] + product[count : 2 * count, :] + product[2 * count :, :]


def look_up(table, index):
    picked = selected(table.T, one_hot(index // LANES, table.shape[0]), ((1,), (0,)))
    return jnp.sum(picked * one_hot(index % LANES, LANES), axis=0, keepdims=True)


def scatter(index, values, height):
    high = jnp.where(index >= 0, index // LANES, -1)
    low = jnp.where(index >= 0, index % LANES, -1)
    return selected(one_hot(high, height) * values, one_hot(low, LANES), ((1,), (1,)))


def home_cells(node_out, region_no, cells):
    here = (node_out >= 0) & (node_out // cells == region_no)
    return jnp.where(here, node_out % cells, -1)


def rows_of_group(x_ref, rows_ref, first, sub):
    total = None
    for q in range(sub):
        piece = x_ref[pl.ds(pl.multiple_of(first, 8), 8), q * LANES : (q + 1) * LANES]
        rows_ref[pl.ds(first * sub + q, 8, stride=sub), :] = piece
        total = piece if total is None else total + piece
    return total


def copies_in(source, target, sems, chunk):
    copies = [
        pltpu.make_async_copy(
            source.at[pl.ds(i * chunk, chunk), :], target.at[pl.ds(i * chunk, chunk), :], sems.at[i]
        )
        for i in range(target.shape[0] // chunk)
    ]
    for copy in copies:
        copy.start()
    return copies


def make_lists(
    sizes, node_in, node_out, send_list, recv_list,
    in_cell, send_node, send_outlet, land, ahead, source_node, source_outlet,
):
    cells, nodes, branches, cap, sub = sizes
    height = cells // LANES
    region_no = lax.axis_index("region")
    ids = lax.broadcasted_iota(I32, (1, nodes), 1).astype(F32) + 1.0
    number = jnp.zeros((height, LANES), F32)
    slot = jnp.zeros((height, LANES), F32)
    for j in range(branches):
        ins = node_in[j : j + 1, :]
        put_row(in_cell, j * (nodes // LANES), jnp.where(ins >= 0, ins, cells), cells)
        home = home_cells(node_out[j : j + 1, :], region_no, cells)
        here = scatter(home, ids, height)
        number = number + here
        slot = slot + jnp.where(here > 0.0, j + 1.0, 0.0)
    source_node[...] = jnp.maximum(number.astype(I32) - 1, 0)
    source_outlet[...] = slot.astype(I32) - 1
    per_side = padded(cap) // LANES
    for side in range(4):
        slots = send_list[side : side + 1, :]
        lands = recv_list[side : side + 1, :]
        node = jnp.where(slots >= 0, slots % nodes, 0)
        outlet = jnp.where(slots >= 0, slots // nodes, -1)
        put_row(send_node, side * per_side, node, 0)
        put_row(send_outlet, side * per_side, outlet, -1)
        put_row(land, side * per_side, jnp.where(lands >= 0, lands, cells), cells)
        if side == AHEAD:
            for j in range(branches):
                ins = node_in[j : j + 1, :]
                table = stacked(jnp.where(ins >= 0, ins, cells)).astype(F32)
                put_row(ahead, j * per_side, (look_up(table, node) + 0.5).astype(I32), cells)
            put_row(ahead, branches * per_side, node, 0)
            put_row(ahead, (branches + 1) * per_side, outlet, -1)


def cell_sum_kernel(chunk, sub, x_hbm, sum_ref, rows_ref, x, partial, sems):
    copies = copies_in(x_hbm, x, sems, chunk)
    zeros = rows_ref.shape[0] - sub
    rows_ref[zeros:, :] = jnp.zeros((sub, LANES), F32)
    for number, copy in enumerate(copies):
        copy.wait()

        def body(step, carry, number=number):
            for part in range(4):
                first = number * chunk + step * 32 + part * 8
                total = rows_of_group(x, rows_ref, first, sub)
                partial[pl.ds(pl.multiple_of(first, 8), 8), :] = total
            return carry

        lax.fori_loop(0, chunk // 32, body, 0)
    sum_ref[...] = lane_sums(partial[...])


def turn_rows_kernel(sizes, chunk, x_hbm, after_ref, *rest):
    cells, nodes, branches, cap, sub = sizes
    lists, rows_ref, made, (x, sems) = rest[:4], rest[4], rest[5:12], rest[12:]
    copies = copies_in(x_hbm, x, sems, chunk)
    make_lists(sizes, *lists, *made)
    for number, copy in enumerate(copies):
        copy.wait()

        def body(step, carry, number=number):
            for part in range(4):
                rows_of_group(x, rows_ref, number * chunk + step * 32 + part * 8, sub)
            return carry

        lax.fori_loop(0, chunk // 32, body, 0)


def gathered_flow(node, in_cell, scaled, sizes):
    cells, nodes, branches, cap, sub = sizes
    return tree_sum(
        [row_of(scaled, in_cell[i * nodes + node], sub)[...] for i in range(branches)]
    )


def send_ahead_kernel(sizes, fraction, slots, rows, turns, send):
    cells, nodes, branches, cap, sub = sizes
    batch = 16

    def body(step, carry):
        first = step * batch
        values = []
        for i in range(batch):
            slot = first + i
            parts = []
            for j in range(branches):
                cell = slots[j * padded(cap) + slot]
                parts.append(row_of(rows, cell, sub)[...] * fraction[cell])
            node = slots[branches * padded(cap) + slot]
            choice = row_of(turns, node, sub)[...]
            outlet = slots[(branches + 1) * padded(cap) + slot]
            values.append(jnp.where(choice == outlet, tree_sum(parts), 0.0))
        for i in range(batch):
            row_of(send, first + i, sub)[...] = values[i]
        return carry

    lax.fori_loop(0, cap // batch, body, 0)


def scale_kernel(sizes, fraction, rows, sent_ref, supply_ref, scaled):
    cells, nodes, branches, cap, sub = sizes

    def body(step, carry):
        first = step * 16
        values = [
            row_of(rows, first + i, sub)[...] * fraction[first + i] for i in range(16)
        ]
        for i in range(16):
            row_of(scaled, first + i, sub)[...] = values[i]
        return carry

    lax.fori_loop(0, cells // 16, body, 0)
    row_of(scaled, cells, sub)[...] = jnp.zeros((sub, LANES), F32)


def send_kernel(sizes, sides, in_cell, send_node, send_outlet, scaled, turns, *sends):
    cells, nodes, branches, cap, sub = sizes
    batch = 16
    for side, send in zip(sides, sends):

        def body(step, carry, side=side, send=send):
            first = step * batch
            values = []
            for i in range(batch):
                slot = side * padded(cap) + first + i
                node = send_node[slot]
                value = gathered_flow(node, in_cell, scaled, sizes)
                choice = row_of(turns, node, sub)[...]
                values.append(jnp.where(choice == send_outlet[slot], value, 0.0))
            for i in range(batch):
                row_of(send, first + i, sub)[...] = values[i]
            return carry

        lax.fori_loop(0, cap // batch, body, 0)


def scaled_send_kernel(sizes, side, theta, send_node, send_outlet, flow, turns, send):
    cells, nodes, branches, cap, sub = sizes
    batch = 16

    def body(step, carry):
        first = step * batch
        values = []
        for i in range(batch):
            slot = side * padded(cap) + first + i
            node = send_node[slot]
            value = row_of(flow, node, sub)[...] * theta[node]
            choice = row_of(turns, node, sub)[...]
            values.append(jnp.where(choice == send_outlet[slot], value, 0.0))
        for i in range(batch):
            row_of(send, first + i, sub)[...] = values[i]
        return carry

    lax.fori_loop(0, cap // batch, body, 0)


def node_flow_kernel(sizes, in_cell, scaled, turns, after_ref, flow, demand, partial):
    cells, nodes, branches, cap, sub = sizes

    def gather(step, carry):
        first = step * 16
        values = [
            gathered_flow(first + i, in_cell, scaled, sizes) for i in range(16)
        ]
        for i in range(16):
            row_of(flow, first + i, sub)[...] = values[i]
        return carry

    def measure(step, carry):
        for part in range(4):
            first = step * 32 + part * 8
            totals = [jnp.zeros((8, LANES), F32)] * branches
            for q in range(sub):
                at = pl.ds(first * sub + q, 8, stride=sub)
                value = flow[at, :]
                choice = turns[at, :]
                totals = [
                    total + jnp.where(choice == j, value, 0.0) for j, total in enumerate(totals)
                ]
            for j in range(branches):
                partial[j, pl.ds(pl.multiple_of(first, 8), 8), :] = totals[j]
        return carry

    lax.fori_loop(0, nodes // 16, gather, 0)
    lax.fori_loop(0, nodes // 32, measure, 0)
    per_outlet = nodes // LANES
    for j in range(branches):
        demand[j * per_outlet : (j + 1) * per_outlet, :] = lane_sums(partial[j])


def theta_kernel(
    sizes, regions, commodities, supply, shared, node_out, send_list, theta_out, slot_theta
):
    cells, nodes, branches, cap, sub = sizes
    per_outlet = nodes // LANES
    height = cells // LANES
    block = branches * per_outlet + height
    region_no = lax.axis_index("region")
    members = shared.shape[0] // block
    parts = [
        shared[d * block : d * block + branches * per_outlet, :] for d in range(members)
    ]
    demand = tree_sum(parts) * (1.0 / commodities)
    table = jnp.concatenate(
        [supply[...]]
        + [
            shared[d * block + branches * per_outlet : (d + 1) * block, :] for d in range(4)
        ],
        axis=0,
    )
    tall = jnp.ones((per_outlet, LANES), F32)
    for j in range(branches):
        outs = node_out[j : j + 1, :]
        cell = jnp.maximum(outs, 0)
        offset = (cell // cells + regions - region_no) % regions
        sector = jnp.zeros_like(offset)
        for d in range(4):
            sector = jnp.where(offset == (-SHIFTS[d]) % regions, d + 1, sector)
        room = stacked(look_up(table, sector * cells + cell % cells))
        ratio = room / jnp.maximum(demand[j * per_outlet : (j + 1) * per_outlet, :], room)
        tall = jnp.minimum(tall, jnp.where(stacked(outs) >= 0, ratio, 1.0))
    theta_out[...] = tall
    per_side = padded(cap) // LANES
    for k in range(2):
        slots = send_list[pl.ds(2 * k + lax.axis_index("dest") % 2, 1), :]
        there = look_up(tall, jnp.where(slots >= 0, slots % nodes, 0))
        put_row(slot_theta, k * per_side, there, 0.0)


def keep_kernel(
    sizes, theta_ref, node_in, node_out, fraction, sent_ref, arrived_ref, keep, home_theta
):
    cells, nodes, branches, cap, sub = sizes
    height = cells // LANES
    region_no = lax.axis_index("region")
    theta = strung(theta_ref[...])
    cell_theta = jnp.zeros((height, LANES), F32)
    into = jnp.zeros((height, LANES), F32)
    for j in range(branches):
        home = home_cells(node_out[j : j + 1, :], region_no, cells)
        cell_theta = cell_theta + scatter(node_in[j : j + 1, :], theta, height)
        into = into + scatter(home, theta, height)
    keep[...] = 1.0 - cell_theta * fraction[...]
    home_theta[...] = into


def home_kernel(sizes, source, outlet, turns, flow, after_ref, home):
    cells, nodes, branches, cap, sub = sizes
    batch = 16

    def body(step, carry):
        first = step * batch
        values = []
        for i in range(batch):
            node = source[first + i]
            choice = row_of(turns, node, sub)[...]
            moved = row_of(flow, node, sub)[...]
            values.append(jnp.where(choice == outlet[first + i], moved, 0.0))
        for i in range(batch):
            row_of(home, first + i, sub)[...] = values[i]
        return carry

    lax.fori_loop(0, cells // batch, body, 0)


def base_kernel(sizes, keep, home_theta, rows, home, base):
    cells, nodes, branches, cap, sub = sizes
    batch = 16

    def body(step, carry):
        first = step * batch
        values = []
        for i in range(batch):
            cell = first + i
            kept = row_of(rows, cell, sub)[...] * keep[cell]
            values.append(kept + row_of(home, cell, sub)[...] * home_theta[cell])
        for i in range(batch):
            row_of(base, first + i, sub)[...] = values[i]
        return carry

    lax.fori_loop(0, cells // batch, body, 0)


def land_rows(sizes, sides, scale, land, received, base):
    cells, nodes, branches, cap, sub = sizes
    batch = 16
    core = lax.axis_index("dest") % 2
    for side, rows in zip(sides, received):
        offset = jnp.where(core == side % 2, 0, 2 * padded(cap)) + side // 2 * padded(cap)

        def body(step, carry, side=side, rows=rows, offset=offset):
            first = step * batch
            stores = []
            for i in range(batch):
                at = row_of(base, land[side * padded(cap) + first + i], sub)
                value = row_of(rows, first + i, sub)[...]
                if scale is not None:
                    value = value * scale[offset + first + i]
                stores.append((at, at[...] + value))
            for at, value in stores:
                at[...] = value
            return carry

        lax.fori_loop(0, cap // batch, body, 0)


def land_kernel(sizes, sides, scale, land, *rest):
    received, (base_in, base) = rest[: len(sides)], rest[len(sides) :]
    land_rows(sizes, sides, scale, land, received, base)


def finish_kernel(sizes, sides, chunk, land, *rest):
    cells, nodes, branches, cap, sub = sizes
    received, (base_in, out, base, staged, sems) = rest[: len(sides)], rest[len(sides) :]
    land_rows(sizes, sides, None, land, received, base)
    copies = []
    for number in range(cells // chunk):

        def body(step, carry, number=number):
            for part in range(4):
                first = number * chunk + step * 32 + part * 8
                for q in range(sub):
                    staged[
                        pl.ds(pl.multiple_of(first, 8), 8), q * LANES : (q + 1) * LANES
                    ] = base[pl.ds(first * sub + q, 8, stride=sub), :]
            return carry

        lax.fori_loop(0, chunk // 32, body, 0)
        at = pl.ds(number * chunk, chunk)
        copies.append(
            pltpu.make_async_copy(staged.at[at, :], out.at[at, :], sems.at[number])
        )
        copies[-1].start()
    for copy in copies:
        copy.wait()


def on_device(occupancy, capacity, jam, wave, node_in, node_out, send_list, recv_list, turn):
    cells, width = occupancy.shape
    branches, nodes = node_in.shape
    cap = send_list.shape[1]
    sub = width // LANES
    sizes = (cells, nodes, branches, cap, sub)
    regions = lax.axis_size("region")
    commodities = width * lax.axis_size("dest")
    height = cells // LANES
    per_cell = (height, LANES)
    list_shape = (4 * padded(cap) // LANES, LANES)
    ahead_rows = -(-(branches + 2) * padded(cap) // LANES // 8) * 8
    chunk = 256
    row_bytes = width * 4
    occupancy = pltpu.with_memory_space_constraint(occupancy, pltpu.HBM)
    turn = pltpu.with_memory_space_constraint(turn, pltpu.HBM)

    local_sum, rows = pl.pallas_call(
        functools.partial(cell_sum_kernel, chunk, sub),
        in_specs=[ANYWHERE],
        out_specs=[VMEM_WHOLE] * 2,
        out_shape=[
            jax.ShapeDtypeStruct(per_cell, F32),
            pltpu.VMEM(((cells + 1) * sub, LANES), F32),
        ],
        scratch_shapes=[
            pltpu.VMEM((cells, width), F32),
            pltpu.VMEM((cells, LANES), F32),
            pltpu.SemaphoreType.DMA((cells // chunk,)),
        ],
        compiler_params=params(14),
        cost_estimate=cost(cells * width, cells * row_bytes),
        name="cell_sum",
    )(occupancy)

    sums = partners(local_sum, "dest")

    turns, *lists = pl.pallas_call(
        functools.partial(turn_rows_kernel, sizes, chunk),
        in_specs=[ANYWHERE] * 2 + [VMEM_WHOLE] * 4,
        out_specs=[VMEM_WHOLE] * 8,
        out_shape=[
            pltpu.VMEM((nodes * sub, LANES), I32),
            jax.ShapeDtypeStruct((branches * nodes // LANES, LANES), I32),
        ]
        + [jax.ShapeDtypeStruct(list_shape, I32)] * 3
        + [jax.ShapeDtypeStruct((ahead_rows, LANES), I32)]
        + [jax.ShapeDtypeStruct(per_cell, I32)] * 2,
        scratch_shapes=[
            pltpu.VMEM((nodes, width), I32),
            pltpu.SemaphoreType.DMA((nodes // chunk,)),
        ],
        compiler_params=params(8),
        cost_estimate=cost(0, nodes * row_bytes),
        name="turn_rows",
    )(turn, local_sum, node_in, node_out, send_list, recv_list)
    in_cell, send_node, send_outlet, land, ahead_list, source_node, source_outlet = (
        x.reshape(-1) for x in lists
    )

    turns, *sums = lax.optimization_barrier((turns, *sums))
    vehicles = tree_sum(sums) / commodities
    cap_of = capacity.reshape(per_cell)
    fraction = jnp.minimum(vehicles, cap_of) / vehicles
    supply = jnp.minimum(cap_of, wave.reshape(per_cell) * (jam.reshape(per_cell) - vehicles))
    rows_shape = pltpu.VMEM(((cells + 1) * sub, LANES), F32)
    send_shape = pltpu.VMEM((cap * sub, LANES), F32)

    supply_there = to_neighbours(supply)
    weights = jnp.concatenate([fraction.reshape(-1), jnp.zeros((LANES,), F32)])
    (ahead,) = pl.pallas_call(
        functools.partial(send_ahead_kernel, sizes),
        in_specs=[SMEM_WHOLE] * 2 + [VMEM_WHOLE] * 2,
        out_specs=[VMEM_WHOLE],
        out_shape=[send_shape],
        compiler_params=params(4),
        cost_estimate=cost(1, 1),
        name="send_ahead",
    )(weights, ahead_list, rows, turns)
    scaled = pl.pallas_call(
        functools.partial(scale_kernel, sizes),
        in_specs=[SMEM_WHOLE, VMEM_WHOLE, ANYWHERE, ANYWHERE],
        out_specs=VMEM_WHOLE,
        out_shape=rows_shape,
        compiler_params=params(4),
        cost_estimate=cost(10000000000, 1),
        name="scale_rows",
    )(fraction.reshape(-1), rows, ahead, supply_there)
    near = pl.pallas_call(
        functools.partial(send_kernel, sizes, (0, 1)),
        in_specs=[SMEM_WHOLE] * 3 + [VMEM_WHOLE] * 2,
        out_specs=[VMEM_WHOLE] * 2,
        out_shape=[send_shape] * 2,
        compiler_params=params(4),
        cost_estimate=cost(1, 1),
        name="send_near",
    )(in_cell, send_node, send_outlet, scaled, turns)
    arrived = [
        shifted(send, "region", SHIFTS[side]) for side, send in enumerate([*near, ahead])
    ]

    flow, demand = pl.pallas_call(
        functools.partial(node_flow_kernel, sizes),
        in_specs=[SMEM_WHOLE] + [VMEM_WHOLE] * 2 + [ANYWHERE],
        out_specs=[VMEM_WHOLE] * 2,
        out_shape=[
            pltpu.VMEM((nodes * sub, LANES), F32),
            jax.ShapeDtypeStruct((branches * nodes // LANES, LANES), F32),
        ],
        scratch_shapes=[pltpu.VMEM((branches, nodes, LANES), F32)],
        compiler_params=params(8),
        cost_estimate=cost(1, 1),
        name="node_flow",
    )(in_cell, scaled, turns, near[0])

    joined = jnp.concatenate([demand, supply_there])
    shared = lax.all_gather(joined, "dest", axis=0, tiled=True)
    theta, slot_theta = pl.pallas_call(
        functools.partial(theta_kernel, sizes, regions, commodities),
        in_specs=[VMEM_WHOLE] * 4,
        out_specs=[VMEM_WHOLE] * 2,
        out_shape=[
            jax.ShapeDtypeStruct((nodes // LANES, LANES), F32),
            jax.ShapeDtypeStruct((2 * padded(cap) // LANES, LANES), F32),
        ],
        compiler_params=params(8),
        cost_estimate=cost(1, 1),
        name="theta",
    )(supply, shared, node_out, send_list)
    theta, slot_theta, arrived[2] = lax.optimization_barrier((theta, slot_theta, arrived[2]))
    per_side = padded(cap) // LANES
    theta_there = [to_two(slot_theta[:per_side], 0), to_two(slot_theta[per_side:], 2)]

    (behind,) = pl.pallas_call(
        functools.partial(scaled_send_kernel, sizes, 3),
        in_specs=[SMEM_WHOLE] * 3 + [VMEM_WHOLE] * 2,
        out_specs=[VMEM_WHOLE],
        out_shape=[send_shape],
        compiler_params=params(4),
        cost_estimate=cost(1, 1),
        name="send_scaled",
    )(theta.reshape(-1), send_node, send_outlet, flow, turns)
    home = pl.pallas_call(
        functools.partial(home_kernel, sizes),
        in_specs=[SMEM_WHOLE] * 2 + [VMEM_WHOLE] * 2 + [ANYWHERE],
        out_specs=VMEM_WHOLE,
        out_shape=rows_shape,
        compiler_params=params(4),
        cost_estimate=cost(4000000000, 1),
        name="home_rows",
    )(source_node, source_outlet, turns, flow, behind)
    keep, home_theta = pl.pallas_call(
        functools.partial(keep_kernel, sizes),
        in_specs=[VMEM_WHOLE] * 4 + [ANYWHERE] * 2,
        out_specs=[VMEM_WHOLE] * 2,
        out_shape=[jax.ShapeDtypeStruct(per_cell, F32)] * 2,
        compiler_params=params(8),
        cost_estimate=cost(10000000, 1),
        name="keep",
    )(theta, node_in, node_out, fraction, behind, arrived[2])
    base = pl.pallas_call(
        functools.partial(base_kernel, sizes),
        in_specs=[SMEM_WHOLE] * 2 + [VMEM_WHOLE] * 2,
        out_specs=VMEM_WHOLE,
        out_shape=rows_shape,
        compiler_params=params(4),
        cost_estimate=cost(10000000, 1),
        name="base_rows",
    )(keep.reshape(-1), home_theta.reshape(-1), rows, home)

    base, *rest = lax.optimization_barrier((base, *theta_there, *arrived))
    theta_there, arrived = rest[:2], rest[2:]
    last = shifted(behind, "region", SHIFTS[3])
    got = jnp.concatenate(theta_there)
    members = lax.axis_size("dest")
    other = lax.ppermute(got, "dest", [(i, i ^ 1) for i in range(members)])
    scale = jnp.concatenate([got, other])

    base = pl.pallas_call(
        functools.partial(land_kernel, sizes, (0, 1, 2)),
        in_specs=[SMEM_WHOLE] * 2 + [VMEM_WHOLE] * 4,
        out_specs=VMEM_WHOLE,
        out_shape=rows_shape,
        input_output_aliases={5: 0},
        compiler_params=params(4),
        cost_estimate=cost(4000000000, 1),
        name="land_first",
    )(scale.reshape(-1), land, *arrived, base)

    out, _ = pl.pallas_call(
        functools.partial(finish_kernel, sizes, (3,), chunk),
        in_specs=[SMEM_WHOLE] + [VMEM_WHOLE] * 2,
        out_specs=[ANYWHERE, VMEM_WHOLE],
        out_shape=[jax.ShapeDtypeStruct((cells, width), F32), rows_shape],
        scratch_shapes=[
            pltpu.VMEM((cells, width), F32),
            pltpu.SemaphoreType.DMA((cells // chunk,)),
        ],
        input_output_aliases={2: 1},
        compiler_params=params(12),
        cost_estimate=cost(cells * width, cells * row_bytes),
        name="finish",
    )(land, last, base)
    return out


def solution(mesh):
    return jax.shard_map(
        on_device,
        mesh=mesh,
        in_specs=(
            P("region", "dest"),
            P("region"),
            P("region"),
            P("region"),
            P(None, "region"),
            P(None, "region"),
            P("region", None),
            P("region", None),
            P("region", "dest"),
        ),
        out_specs=P("region", "dest"),
        check_vma=False,
    )
```
